32 devices in a mesh: dp: 8 (over z, x), tensor: 4 (over y, core).
Axes of the slice: x: 2, y: 2, z: 4, core: 2. Of those that a mesh axis runs over, the one named last changes fastest.
Arguments:
- layer_input: bfloat16 [32768, 767], P(('dp', 'tensor')), may hold values from -6 to 6
- segments: int32 [32, 1024], P(('dp', 'tensor')), may hold values from 0 to 7, never falling along the last dimension, each value on 1 to 512 neighbouring positions
- cotangent: bfloat16 [32768, 767], P(('dp', 'tensor')), may hold values from -6 to 6
- gain_one: float32 [767], replicated, may hold values from 0.1 to 1.9
- w_qkv: bfloat16 [3, 767, 768], P(None, None, 'tensor'), may hold values from -0.21875 to 0.21875
- b_qv: bfloat16 [2, 768], P(None, 'tensor'), may hold values from -1.796875 to 1.796875
- w_out: bfloat16 [768, 767], P('tensor'), may hold values from -0.625 to 0.625
- b_out: bfloat16 [767], replicated, may hold values from -1.796875 to 1.796875
- gain_two: float32 [767], replicated, may hold values from 0.1 to 1.9
- w_up: bfloat16 [767, 3072], P(None, 'tensor'), may hold values from -0.21875 to 0.21875
- b_up: bfloat16 [3072], P('tensor'), may hold values from -1.796875 to 1.796875
- w_down: bfloat16 [3072, 767], P('tensor'), may hold values from -0.15625 to 0.15625
- b_down: bfloat16 [767], replicated, may hold values from -1.796875 to 1.796875
Outputs:
- output: bfloat16 [32768, 767], P(('dp', 'tensor'))
- input_grad: bfloat16 [32768, 767], P(('dp', 'tensor'))
- grad_gain_one: float32 [767], replicated
- grad_qkv: float32 [3, 767, 768], P(None, None, 'tensor')
- grad_bqv: float32 [2, 768], P(None, 'tensor')
- grad_out: float32 [768, 767], P('tensor')
- grad_bout: float32 [767], replicated
- grad_gain_two: float32 [767], replicated
- grad_up: float32 [767, 3072], P(None, 'tensor')
- grad_bup: float32 [3072], P('tensor')
- grad_down: float32 [3072, 767], P('tensor')
- grad_bdown: float32 [767], replicated
The draws below stay inside these ranges and needn't reach their ends.
Inputs may be any that keep to these rules, and one draw needn't show every extreme that they name: `segments`: along each row of 1024 positions the document number never falls; every row holds 8 documents of 1 to 512 tokens, one of exactly 512.
All inputs are finite; a program needn't handle non-finite values.
Results may differ from the reference program's by a relative error of at most 0.018.
Values may be sent and summed in bfloat16 or wider, within the bound.
A program may use at most 192 MiB of HBM per device.

```python
import math
import jax
import jax.numpy as jnp
import numpy as np
from jax import lax

D_MODEL = 768
HEADS = 12
HEAD_DIM = 64
FF = 3072
SEQ = 1024
SEGS = 8
ROWS_DEV = 1
DC = 767
NROWS = 32
TOKENS = 32768
N_TENSOR = 4


def levels(rng, dims, cuts, smallest, largest):
    loudness = 1.0
    for position, shards_of in cuts:
        draws = jax.random.uniform(jax.random.fold_in(jax.random.fold_in(rng, 6), position), (shards_of,), jnp.float32, smallest / len(cuts), largest / len(cuts))
        loudness = loudness * jnp.repeat(jnp.exp(draws), dims[position] // shards_of).reshape((-1,) + (1,) * (len(dims) - 1 - position))
    return loudness


def length_profile(count, total, most, skew):
    weights = [(1 << 20) // math.isqrt(standing ** skew) + 1 for standing in range(2, count + 1)]
    surplus, holding = total - most - (count - 1), [1] * (count - 1)
    while surplus > 0:
        candidates = [i for i in range(count - 1) if holding[i] < most]
        whole, remaining = sum([weights[i] for i in candidates]), surplus
        for i in candidates:
            extra = min(most - holding[i], max(1, remaining * weights[i] // whole), surplus)
            holding[i] = holding[i] + extra
            surplus = surplus - extra
    return np.array([most] + holding)


def ragged(key, amount, total, limit, lean):
    if amount == 2:
        one = jax.random.randint(key, (), max(1, total - limit), min(limit, total - 1) + 1)
        return jnp.stack([one, total - one])
    lengths = jnp.asarray(length_profile(amount, total, limit, lean), jnp.int32)
    twos = (amount - 1) // 2
    source_of, receiver = lengths[1:1 + 2 * twos:2], lengths[2:2 + 2 * twos:2]
    slack = jnp.minimum(source_of - 1, limit - receiver)
    moved = jax.random.randint(jax.random.fold_in(key, 1), (twos,), 0, 1 << 20) % (slack + 1)
    lengths = lengths.at[1:1 + 2 * twos:2].set(source_of - moved).at[2:2 + 2 * twos:2].set(receiver + moved)
    return lengths[jax.random.permutation(jax.random.fold_in(key, 2), amount)]


def gaussian(rng, dims, scale, limit, cuts=(), held_as=jnp.bfloat16):
    entries = jax.random.normal(rng, dims, jnp.float32) * scale
    if len(cuts) > 0:
        entries = levels(rng, dims, cuts, -0.22, 0.18) * entries
    return jnp.clip(entries, min=-limit, max=limit).astype(held_as)


def setup_inputs(seed: int = 0) -> dict:
    streams_of = jax.random.split(jax.random.key(seed), 14)
    layer_input = gaussian(streams_of[0], (TOKENS, DC), 1.0, 6.0, ((0, 32),))
    segments = jax.vmap(lambda own: jnp.searchsorted(jnp.cumsum(ragged(own, SEGS, SEQ, SEQ // 2, 2)), jnp.arange(SEQ), side="right"))(jax.random.split(streams_of[1], NROWS)).reshape((NROWS, SEQ)).astype(jnp.int32)
    cotangent = gaussian(streams_of[2], (TOKENS, DC), 1.0, 6.0, ((0, 32),))
    gain_one = jnp.clip(1.0 + 0.18 * jax.random.normal(streams_of[3], (DC,), jnp.float32), 0.1, 1.9)
    w_qkv = gaussian(streams_of[4], (3, DC, D_MODEL), DC ** -0.5, 0.21875, ((2, 4),))
    b_qv = gaussian(streams_of[5], (2, D_MODEL), 0.3, 1.796875, ((1, 4),))
    w_out = gaussian(streams_of[6], (D_MODEL, DC), (D_MODEL // 8) ** -0.5, 0.625, ((0, 4),))
    b_out = gaussian(streams_of[7], (DC,), 0.3, 1.796875)
    gain_two = jnp.clip(1.0 + 0.18 * jax.random.normal(streams_of[8], (DC,), jnp.float32), 0.1, 1.9)
    w_up = gaussian(streams_of[9], (DC, FF), DC ** -0.5, 0.21875, ((1, 4),))
    b_up = gaussian(streams_of[10], (FF,), 0.3, 1.796875, ((0, 4),))
    w_down = gaussian(streams_of[11], (FF, DC), (FF // 2) ** -0.5, 0.15625, ((0, 4),))
    b_down = gaussian(streams_of[12], (DC,), 0.3, 1.796875)
    return {"layer_input": layer_input, "segments": segments, "cotangent": cotangent, "gain_one": gain_one, "w_qkv": w_qkv, "b_qv": b_qv, "w_out": w_out, "b_out": b_out, "gain_two": gain_two, "w_up": w_up, "b_up": b_up, "w_down": w_down, "b_down": b_down}


EPSILON = 1e-05
MASKED_SCORE = -1e+30
HIGHEST = lax.Precision.HIGHEST

@jax.custom_vjp
def low(v):
    return lax.optimization_barrier(v.astype(jnp.bfloat16)).astype(jnp.float32)

@jax.custom_vjp
def low_back(v):
    return v

def low_keep(v):
    return (low(v), None)

def low_pass(kept, grad):
    return (grad,)

def back_keep(v):
    return (v, None)

def back_low(kept, grad):
    return (low(grad),)
low.defvjp(low_keep, low_pass)
low_back.defvjp(back_keep, back_low)

def norm_rows(values, gain):
    total = lax.optimization_barrier(jnp.sum(values, axis=-1, keepdims=True))
    square = lax.optimization_barrier(jnp.sum(values * values, axis=-1, keepdims=True))
    return values * lax.rsqrt((square + total * total) / (values.shape[-1] + 1) + EPSILON) * gain

def attend(query, key_proj, value_proj, seg_rows):
    row_count, length = seg_rows.shape
    extent = min(512, length)
    pieces = length // extent
    scale = HEAD_DIM ** (-0.5)
    query = query.reshape(row_count, pieces, extent, HEADS, HEAD_DIM).transpose(1, 0, 2, 3, 4)
    key_proj = key_proj.reshape(row_count, length, HEADS, HEAD_DIM)
    value_proj = value_proj.reshape(row_count, length, HEADS, HEAD_DIM)
    offsets = (jnp.arange(pieces) * extent).astype(jnp.int32)

    def one_piece(inputs):
        query_part, offset = inputs
        scores = jnp.einsum('rbhe,rkhe->rhbk', query_part, key_proj, precision=HIGHEST) * scale
        scores = low_back(scores)
        query_pos = offset + jnp.arange(extent).astype(jnp.int32)
        key_pos = jnp.arange(length).astype(jnp.int32)
        query_seg = lax.dynamic_slice_in_dim(seg_rows, offset, extent, 1)
        allowed = (key_pos[None, None, :] <= query_pos[None, :, None]) & (query_seg[:, :, None] == seg_rows[:, None, :])
        scores = jnp.where(allowed[:, None], scores, MASKED_SCORE)
        highest = lax.optimization_barrier(jnp.max(scores, axis=-1, keepdims=True))
        exponent = jnp.exp(scores - highest)
        probs = low(exponent / lax.optimization_barrier(jnp.sum(exponent, axis=-1, keepdims=True)))
        return jnp.einsum('rhbk,rkhe->rbhe', probs, value_proj, precision=HIGHEST)
    result = lax.map(jax.checkpoint(one_piece), (query, offsets))
    return result.transpose(1, 0, 2, 3, 4).reshape(row_count * length, HEADS * HEAD_DIM)

def layer(inputs, seg_rows, gain_one, w_qkv, b_qv, w_out, b_out, gain_two, w_up, b_up, w_down, b_down):
    normed_one = low(norm_rows(inputs, gain_one))
    projected = jnp.einsum('tc,jcd->jtd', normed_one, w_qkv, precision=HIGHEST)
    query = low_back(low(projected[0] + b_qv[0]))
    key_proj = low_back(low(projected[1]))
    value_proj = low_back(low(projected[2] + b_qv[1]))
    attended = low_back(low(attend(query, key_proj, value_proj, seg_rows)))
    branch_one = low_back(jnp.dot(attended, w_out, precision=HIGHEST) + b_out)
    resid = inputs + branch_one
    normed_two = low(norm_rows(resid, gain_two))
    pre_act = low_back(jnp.dot(normed_two, w_up, precision=HIGHEST) + b_up)
    hidden = low(jax.nn.gelu(pre_act))
    return resid + (jnp.dot(hidden, w_down, precision=HIGHEST) + b_down)

def reference(layer_input, segments, cotangent, gain_one, w_qkv, b_qv, w_out, b_out, gain_two, w_up, b_up, w_down, b_down):
    group = ROWS_DEV * N_TENSOR
    steps_count = NROWS // group
    group_tokens = group * SEQ
    stored = layer_input.shape[-1]
    params = tuple((item.astype(jnp.float32) for item in (gain_one, w_qkv, b_qv, w_out, b_out, gain_two, w_up, b_up, w_down, b_down)))
    inputs = (layer_input.reshape(steps_count, group_tokens, stored), segments.reshape(steps_count, group, SEQ), cotangent.reshape(steps_count, group_tokens, stored))

    def one_group(carry, item):
        input_group, seg_group, cot_group = item

        def forward(values, *weights):
            return layer(values, seg_group, *weights)
        result, pull = jax.vjp(forward, input_group.astype(jnp.float32), *params)
        gradients = pull(cot_group.astype(jnp.float32))
        carry = tuple((left + right for left, right in zip(carry, gradients[1:])))
        return (carry, (result.astype(jnp.bfloat16), gradients[0].astype(jnp.bfloat16)))
    zeros = tuple((jnp.zeros_like(item) for item in params))
    totals, (results, input_grads) = lax.scan(one_group, zeros, inputs)
    output = results.reshape(TOKENS, stored)
    input_grad = input_grads.reshape(TOKENS, stored)
    return (output, input_grad, totals[0], totals[1], totals[2], totals[3], totals[4], totals[5], totals[6], totals[7], totals[8], totals[9])
```

```python
import functools

import jax
import jax.numpy as jnp
from jax import lax
from jax.experimental import pallas as pl
from jax.experimental.pallas import tpu as pltpu
from jax.sharding import PartitionSpec as P

HEAD_DIM = 64
LANES = 128
EPSILON = 1e-05
MASKED_SCORE = -1e30
LONGEST = 512
BLOCK = 256
F32 = jnp.float32
BF16 = jnp.bfloat16
NN = (((1,), (0,)), ((), ()))
NT = (((1,), (1,)), ((), ()))
TN = (((0,), (0,)), ((), ()))
GELU_A = 0.7978845608028654
GELU_B = 0.044715
MIB = 1024 * 1024


def dot(a, b, dims=NN):
    return lax.dot_general(a, b, dims, preferred_element_type=F32)


def attn_fwd_kernel(q_ref, k_ref, v_ref, qh_ref, kn_ref, o_ref, lse_ref):
    length = q_ref.shape[0]
    first = lax.broadcasted_iota(jnp.int32, (1, LANES), 1) < HEAD_DIM
    causal = lax.broadcasted_iota(jnp.int32, (BLOCK, BLOCK), 0) <= lax.broadcasted_iota(
        jnp.int32, (BLOCK, BLOCK), 1
    )
    for hi in range(BLOCK, length + 1, BLOCK):
        lo = max(0, hi - BLOCK - LONGEST)
        at = slice(hi - BLOCK, hi)
        parts = []
        for h in range(2):
            sel = first if h == 0 else ~first
            qa = jnp.where(sel, q_ref[at, :] * 0.125, qh_ref[at, :])
            ka = jnp.where(sel, k_ref[lo:hi, :], kn_ref[lo:hi, :])
            s = dot(ka, qa, NT)
            tail = jnp.where(causal, s[hi - BLOCK - lo :, :], MASKED_SCORE)
            s = tail if hi == BLOCK else jnp.concatenate([s[: hi - BLOCK - lo, :], tail], axis=0)
            m = jnp.max(s, axis=0, keepdims=True)
            p = jnp.exp(s - m)
            total = jnp.sum(p, axis=0, keepdims=True)
            weights = (p * (1.0 / total)).astype(BF16)
            parts.append(dot(weights, v_ref[lo:hi, :], TN))
            lse_ref[h : h + 1, at] = m + jnp.log(total)
        o_ref[at, :] = jnp.where(first, parts[0], parts[1]).astype(BF16)


def attn_fwd(qkv, qh, kn, rows):
    tokens = qkv.shape[0]
    length = tokens // rows
    pairs = qkv.shape[1] // (3 * LANES)

    def cols(j):
        return pl.BlockSpec((length, LANES), lambda r, p: (r, j * pairs + p))

    seg = pl.BlockSpec((length, LANES), lambda r, p: (r, 0))
    return pl.pallas_call(
        attn_fwd_kernel,
        grid=(rows, pairs),
        in_specs=[cols(0), cols(1), cols(2), seg, seg],
        out_specs=[cols(0), pl.BlockSpec((None, None, 2, length), lambda r, p: (r, p, 0, 0))],
        out_shape=[
            jax.ShapeDtypeStruct((tokens, pairs * LANES), BF16),
            jax.ShapeDtypeStruct((rows, pairs, 2, length), F32),
        ],
        compiler_params=pltpu.CompilerParams(vmem_limit_bytes=32 * MIB),
        name="attn_fwd",
    )(qkv, qkv, qkv, qh, kn)


def attn_bwd_kernel(
    q_ref, k_ref, v_ref, do_ref, lse_ref, qh_ref, kn_ref, out_ref, dk_acc, dv_acc, *, pairs
):
    length = q_ref.shape[0]
    first = lax.broadcasted_iota(jnp.int32, (1, LANES), 1) < HEAD_DIM
    causal = lax.broadcasted_iota(jnp.int32, (BLOCK, BLOCK), 0) <= lax.broadcasted_iota(
        jnp.int32, (BLOCK, BLOCK), 1
    )
    dk_acc[...] = jnp.zeros_like(dk_acc)
    dv_acc[...] = jnp.zeros_like(dv_acc)
    zero = jnp.zeros((), BF16)

    def cols(j):
        return pl.ds(pl.multiple_of((j * pairs + pl.program_id(1)) * LANES, LANES), LANES)

    for hi in range(BLOCK, length + 1, BLOCK):
        lo = max(0, hi - BLOCK - LONGEST)
        at = slice(hi - BLOCK, hi)
        dq = None
        for h in range(2):
            sel = first if h == 0 else ~first
            q = q_ref[at, :] * 0.125
            k = k_ref[lo:hi, :]
            qa = jnp.where(sel, q, qh_ref[at, :])
            ka = jnp.where(sel, k, kn_ref[lo:hi, :])
            qm = jnp.where(sel, q, zero)
            km = jnp.where(sel, k, zero)
            dom = jnp.where(sel, do_ref[at, :], zero)
            s = dot(ka, qa, NT)
            tail = jnp.where(causal, s[hi - BLOCK - lo :, :], MASKED_SCORE)
            s = tail if hi == BLOCK else jnp.concatenate([s[: hi - BLOCK - lo, :], tail], axis=0)
            p = jnp.exp(s - lse_ref[h : h + 1, at])
            dp = dot(v_ref[lo:hi, :], dom, NT)
            t = p * dp
            inner = jnp.sum(t, axis=0, keepdims=True)
            ds = (t - p * inner).astype(BF16)
            dv_acc[lo:hi, :] += dot(p.astype(BF16), dom)
            dk_acc[lo:hi, :] += dot(ds, qm)
            part = dot(ds, km, TN)
            dq = part if dq is None else dq + part
        out_ref[at, cols(0)] = (dq * 0.125).astype(BF16)
    out_ref[:, cols(1)] = dk_acc[...].astype(BF16)
    out_ref[:, cols(2)] = dv_acc[...].astype(BF16)


def attn_bwd(qkv, grad, lse, qh, kn, rows):
    tokens, width = qkv.shape
    length = tokens // rows
    pairs = width // (3 * LANES)

    def cols(j):
        return pl.BlockSpec((length, LANES), lambda r, p: (r, j * pairs + p))

    seg = pl.BlockSpec((length, LANES), lambda r, p: (r, 0))
    return pl.pallas_call(
        functools.partial(attn_bwd_kernel, pairs=pairs),
        grid=(rows, pairs),
        in_specs=[
            cols(0),
            cols(1),
            cols(2),
            cols(0),
            pl.BlockSpec((None, None, 2, length), lambda r, p: (r, p, 0, 0)),
            seg,
            seg,
        ],
        out_specs=pl.BlockSpec((length, width), lambda r, p: (r, 0)),
        out_shape=jax.ShapeDtypeStruct((tokens, width), BF16),
        scratch_shapes=[pltpu.VMEM((length, LANES), F32), pltpu.VMEM((length, LANES), F32)],
        compiler_params=pltpu.CompilerParams(vmem_limit_bytes=32 * MIB),
        name="attn_bwd",
    )(qkv, qkv, qkv, grad, lse, qh, kn)


def ffn_kernel(
    n_ref, c_ref, nt_ref, ct_ref, up_ref, down_ref, bias_ref, out0_ref, back0_ref,
    out_ref, back_ref, gup_ref, gdown_ref, gbias_ref, acc_up, acc_down, *, chunk
):
    @pl.when(pl.program_id(0) == 0)
    def _():
        out_ref[...] = out0_ref[...]
        back_ref[...] = back0_ref[...]

    acc_up[...] = jnp.zeros_like(acc_up)
    acc_down[...] = jnp.zeros_like(acc_down)
    gbias_ref[...] = jnp.zeros_like(gbias_ref)

    @pl.loop(0, n_ref.shape[0] // chunk)
    def _(i):
        r = pl.ds(pl.multiple_of(i * chunk, chunk), chunk)
        pre = dot(n_ref[r, :], up_ref[...]) + bias_ref[...]
        dh = dot(c_ref[r, :], down_ref[...], NT)
        sq = pre * pre
        th = jnp.tanh(pre * (GELU_A + (GELU_A * GELU_B) * sq))
        half = 0.5 + 0.5 * th
        hidden = (pre * half).astype(BF16)
        slope = half + (0.5 * pre) * (1.0 - th * th) * (GELU_A + (3.0 * GELU_A * GELU_B) * sq)
        dpre = (dh * slope).astype(BF16)
        out_ref[r, :] += dot(hidden, down_ref[...])
        back_ref[r, :] += dot(dpre, up_ref[...], NT)
        acc_up[...] += dot(nt_ref[:, r], dpre)
        acc_down[...] += dot(ct_ref[:, r], hidden)
        gbias_ref[...] += jnp.sum(dpre.astype(F32), axis=0, keepdims=True)

    gup_ref[...] = acc_up[...].astype(BF16)
    gdown_ref[...] = acc_down[...].astype(BF16)


def ffn(n, c, nt, ct, up, down, bias, out0, back0, block=384, chunk=512):
    tokens, model = n.shape
    count, _, units = up.shape
    inner = units // block

    def whole(rows, cols):
        return pl.BlockSpec((rows, cols), lambda i: (0, 0))

    tall = pl.BlockSpec((None, model, block), lambda i: (i // inner, 0, i % inner))
    wide = pl.BlockSpec((None, block, model), lambda i: (i // inner, i % inner, 0))
    line = pl.BlockSpec((None, 1, block), lambda i: (i // inner, 0, i % inner))
    big = whole(tokens, model)
    return pl.pallas_call(
        functools.partial(ffn_kernel, chunk=chunk),
        grid=(count * inner,),
        in_specs=[big, big, whole(model, tokens), whole(model, tokens), tall, wide, line, big, big],
        out_specs=[big, big, tall, tall, line],
        out_shape=[
            jax.ShapeDtypeStruct((tokens, model), F32),
            jax.ShapeDtypeStruct((tokens, model), F32),
            jax.ShapeDtypeStruct((count, model, units), BF16),
            jax.ShapeDtypeStruct((count, model, units), BF16),
            jax.ShapeDtypeStruct((count, 1, units), F32),
        ],
        scratch_shapes=[pltpu.VMEM((model, block), F32), pltpu.VMEM((model, block), F32)],
        input_output_aliases={7: 0, 8: 1},
        compiler_params=pltpu.CompilerParams(vmem_limit_bytes=58 * MIB),
        name="ffn",
    )(n, c, nt, ct, up, down, bias, out0, back0)


def norm_scale(values):
    total = jnp.sum(values, axis=-1, keepdims=True)
    square = jnp.sum(values * values, axis=-1, keepdims=True)
    return lax.rsqrt((square + total * total) / values.shape[-1] + EPSILON), total


def norm_back(values, gain, upstream):
    scale, total = norm_scale(values)
    weighted = upstream * values
    spread = jnp.sum(weighted * gain, axis=-1, keepdims=True)
    grad = upstream * gain * scale - (spread * scale * scale * scale / values.shape[-1]) * (
        values + total
    )
    return grad, jnp.sum(weighted * scale, axis=0)


def solution(mesh):
    n_dp, n_tensor = mesh.shape["dp"], mesh.shape["tensor"]
    assert n_tensor == 4 and n_dp & (n_dp - 1) == 0
    bits = [1 << i for i in range(n_dp.bit_length() - 1)]

    def to_core(v):
        return lax.ppermute(v, "tensor", [(i, i ^ 1) for i in range(4)])

    def to_y(v):
        return lax.ppermute(v, "tensor", [(i, i ^ 2) for i in range(4)])

    def to_dp(v, bit):
        return lax.ppermute(v, "dp", [(i, i ^ bit) for i in range(n_dp)])

    def odd(bit):
        return (lax.axis_index("dp") & bit) != 0

    def joined(mine, other, bit):
        upper = odd(bit)
        return jnp.concatenate(
            [jnp.where(upper, other, mine), jnp.where(upper, mine, other)], axis=0
        )

    def halves(v, bit):
        half = v.shape[0] // 2
        upper = odd(bit)
        return (
            jnp.where(upper, v[half:], v[:half]),
            jnp.where(upper, v[:half], v[half:]),
        )

    def gather(part):
        core = to_core(part)
        if bits:
            mine = to_y(halves(part, bits[0])[0])
            over = joined(mine, to_dp(mine, bits[0]), bits[0])
        else:
            over = to_y(part)
        return part, core, over, to_core(over)

    def add(a, b):
        return (a.astype(F32) + b.astype(F32)).astype(a.dtype)

    def reduce_y(over, diagonal):
        return to_y(add(over, to_core(diagonal)))

    def reduce_rest(own, core, from_y):
        v = (own.astype(F32) + to_core(core).astype(F32) + from_y.astype(F32)).astype(own.dtype)
        for bit in bits:
            keep, send = halves(v, bit)
            v = add(keep, to_dp(send, bit))
        for bit in bits[::-1]:
            v = joined(v, to_dp(v, bit), bit)
        return v

    def reduce_small(own, core, over, diagonal):
        v = own + to_core(core) + reduce_y(over, diagonal)
        for bit in bits:
            v = v + to_dp(v, bit)
        return v

    def local(
        layer_input, segments, cotangent, gain_one, w_qkv, b_qv, w_out, b_out, gain_two,
        w_up, b_up, w_down, b_down,
    ):
        rows = segments.shape[0]
        stored = layer_input.shape[1]
        model = stored + 1
        width = w_qkv.shape[2]
        units = w_up.shape[1]

        def pad(v, size=model):
            return jnp.pad(v, [(0, 0)] * (v.ndim - 1) + [(0, size - v.shape[-1])])

        misc = jnp.concatenate(
            [pad(b_up[None], units), pad(b_qv, units), jnp.zeros((29, units), BF16)], axis=0
        )
        part_attn = jnp.concatenate(
            [
                pad(w_qkv.transpose(0, 2, 1)).reshape(3 * width, model),
                pad(w_out),
                misc,
            ],
            axis=0,
        )
        part_up = jnp.pad(w_up, [(0, 1), (0, 0)])
        part_down = pad(w_down)
        quarters = gather(part_attn)
        ups = gather(part_up)
        downs = gather(part_down)

        def pair(first):
            a, b = quarters[first], quarters[first + 1]
            both = jnp.stack([a, b])
            qkv = both[:, : 3 * width].reshape(2, 3, width, model).transpose(1, 0, 2, 3)
            qkv = qkv.reshape(6 * width, model)
            out = both[:, 3 * width : 4 * width].reshape(2 * width, model)
            bias_q = both[:, 4 * width + 1, :width].reshape(2 * width)
            bias_v = both[:, 4 * width + 2, :width].reshape(2 * width)
            bias = jnp.concatenate([bias_q, jnp.zeros_like(bias_q), bias_v]).astype(F32)
            bias_up = both[:, 4 * width, :].reshape(2, 1, units).astype(F32)
            return qkv, out, bias, bias_up

        weights = [pair(0), pair(2)]

        gain_one_f, gain_two_f = pad(gain_one), pad(gain_two)
        x = pad(layer_input).astype(F32)
        n_one = (x * norm_scale(x)[0] * gain_one_f).astype(BF16)
        lane = jnp.arange(LANES) % HEAD_DIM
        hot = segments.reshape(-1, 1) == lane[None, :]
        qh = jnp.where(hot, 1.0, 0.0).astype(BF16)
        kn = jnp.where(hot | (lane >= 8)[None, :], 0.0, MASKED_SCORE).astype(BF16)
        qkvs, atts, lses = [], [], []
        for w, _, bias, _ in weights:
            qkv = (dot(n_one, w, NT) + bias).astype(BF16)
            att, lse = attn_fwd(qkv, qh, kn, rows)
            qkvs.append(qkv)
            atts.append(att)
            lses.append(lse)
        branch = dot(atts[0], weights[0][1]) + dot(atts[1], weights[1][1])
        resid = x + (branch + pad(b_out).astype(F32))
        n_two = (resid * norm_scale(resid)[0] * gain_two_f).astype(BF16)

        cot = pad(cotangent)
        n_t, c_t = n_two.T, cot.T
        out_sum = jnp.zeros(resid.shape, F32)
        back = jnp.zeros(resid.shape, F32)
        grads = []
        for first, w in ((2, weights[1]), (0, weights[0])):
            out_sum, back, g_up, g_down, g_bias = ffn(
                n_two, cot, n_t, c_t,
                jnp.stack(ups[first : first + 2]), jnp.stack(downs[first : first + 2]),
                w[3], out_sum, back,
            )
            grads.append((g_up, g_down, g_bias))
        output = (resid + (out_sum + pad(b_down).astype(F32))).astype(BF16)
        far, near = grads
        grad_up = reduce_rest(near[0][0], near[0][1], reduce_y(far[0][0], far[0][1]))
        grad_down = reduce_rest(near[1][0], near[1][1], reduce_y(far[1][0], far[1][1]))

        cot_f = cot.astype(F32)
        d_norm, grad_gain_two = norm_back(resid, gain_two_f, back)
        d_resid = cot_f + d_norm
        d_branch = d_resid.astype(BF16)
        grad_bout = jnp.sum(d_branch.astype(F32), axis=0)
        grad_bdown = jnp.sum(cot_f, axis=0)

        back = 0.0
        grads = []
        for i in (1, 0):
            w, out = weights[i][0], weights[i][1]
            d_att = dot(d_branch, out, NT).astype(BF16)
            g_out = dot(atts[i], d_branch, TN).astype(BF16)
            d_qkv = attn_bwd(qkvs[i], d_att, lses[i], qh, kn, rows)
            g_qkv = dot(d_qkv, n_one, TN).astype(BF16)
            sums = jnp.sum(d_qkv.astype(F32), axis=0)
            back = back + dot(d_qkv, w)
            g_qkv = g_qkv.reshape(3, 2, width, model).transpose(1, 0, 2, 3)
            g = jnp.concatenate(
                [g_qkv.reshape(2, 3 * width, model), g_out.reshape(2, width, model)], axis=1
            )
            sums = sums.reshape(3, 2, width)
            grads.append((g, pad(sums[::2].transpose(1, 0, 2), units)))
        far_a, near_a = grads
        grad_attn = reduce_rest(near_a[0][0], near_a[0][1], reduce_y(far_a[0][0], far_a[0][1]))

        d_norm, grad_gain_one = norm_back(x, gain_one_f, back)
        input_grad = (d_resid + d_norm).astype(BF16)

        common = jnp.stack([grad_bdown, grad_bout, grad_gain_two, grad_gain_one])
        small = [
            jnp.concatenate([source[2][i], source_a[1][i], common], axis=0)
            for source, source_a, i in ((near, near_a, 0), (near, near_a, 1), (far, far_a, 0), (far, far_a, 1))
        ]
        small = reduce_small(*small)

        grad_attn = grad_attn.astype(F32)
        return (
            output[:, :stored],
            input_grad[:, :stored],
            small[6, :stored],
            grad_attn[: 3 * width].reshape(3, width, model).transpose(0, 2, 1)[:, :stored],
            small[1:3, :width],
            grad_attn[3 * width :, :stored],
            small[4, :stored],
            small[5, :stored],
            grad_up.astype(F32)[:stored],
            small[0],
            grad_down.T.astype(F32)[:, :stored],
            small[3, :stored],
        )

    return jax.shard_map(
        local,
        mesh=mesh,
        in_specs=(
            P(("dp", "tensor"), None),
            P(("dp", "tensor"), None),
            P(("dp", "tensor"), None),
            P(),
            P(None, None, "tensor"),
            P(None, "tensor"),
            P("tensor", None),
            P(),
            P(),
            P(None, "tensor"),
            P("tensor"),
            P("tensor", None),
            P(),
        ),
        out_specs=(
            P(("dp", "tensor"), None),
            P(("dp", "tensor"), None),
            P(),
            P(None, None, "tensor"),
            P(None, "tensor"),
            P("tensor", None),
            P(),
            P(),
            P(None, "tensor"),
            P("tensor"),
            P("tensor", None),
            P(),
        ),
        check_vma=False,
    )
```

```python
import functools

import jax
import jax.numpy as jnp
from jax import lax
from jax.experimental import pallas as pl
from jax.experimental.pallas import tpu as pltpu
from jax.sharding import PartitionSpec as P

HEAD_DIM = 64
LANES = 128
EPSILON = 1e-05
MASKED_SCORE = -1e30
LONGEST = 512
BLOCK = 256
CHUNK = 256
F32 = jnp.float32
BF16 = jnp.bfloat16
NN = (((1,), (0,)), ((), ()))
NT = (((1,), (1,)), ((), ()))
TN = (((0,), (0,)), ((), ()))
GELU_A = 0.7978845608028654
GELU_B = 0.044715
MIB = 1024 * 1024
MESH = pl.DeviceIdType.MESH


def dot(a, b, dims=NN):
    return lax.dot_general(a, b, dims, preferred_element_type=F32)


def params(mib, **more):
    return pltpu.CompilerParams(vmem_limit_bytes=mib * MIB, **more)


def full(shape):
    return pl.BlockSpec(shape, lambda *_: (0,) * len(shape))


def widen(ref, wide):
    wide[:, wide.shape[1] - LANES :] = jnp.zeros((wide.shape[0], LANES), F32)
    wide[:, : ref.shape[1]] = ref[...].astype(F32)
    return wide[...]


def norm_scale(values):
    total = jnp.sum(values, axis=-1, keepdims=True)
    square = jnp.sum(values * values, axis=-1, keepdims=True)
    return lax.rsqrt((square + total * total) / values.shape[-1] + EPSILON), total


def norm_back(values, gain, upstream):
    scale, total = norm_scale(values)
    weighted = upstream * values
    spread = jnp.sum(weighted * gain, axis=-1, keepdims=True)
    grad = upstream * gain * scale - (spread * scale * scale * scale / values.shape[-1]) * (
        values + total
    )
    return grad, jnp.sum(weighted * scale, axis=0, keepdims=True)


def add_up(ref, value):
    @pl.when(pl.program_id(0) == 0)
    def _():
        ref[...] = jnp.zeros_like(ref)

    ref[...] += value


def prep_kernel(x_ref, c_ref, gain_ref, n_ref, cot_ref, sum_ref, wide):
    x = widen(x_ref, wide)
    n_ref[...] = (x * norm_scale(x)[0] * gain_ref[...]).astype(BF16)
    c = widen(c_ref, wide)
    cot_ref[...] = c.astype(BF16)
    add_up(sum_ref, jnp.sum(c, axis=0, keepdims=True))


def mid_kernel(x_ref, branch_ref, bias_ref, gain_ref, resid_ref, n_ref, wide):
    resid = widen(x_ref, wide) + (branch_ref[...] + bias_ref[...])
    resid_ref[...] = resid
    n_ref[...] = (resid * norm_scale(resid)[0] * gain_ref[...]).astype(BF16)


def turn_kernel(
    out_ref, back_ref, resid_ref, cot_ref, bias_ref, gain_ref,
    output_ref, d_resid_ref, d_branch_ref, gain_sum_ref, branch_sum_ref,
):
    resid = resid_ref[...]
    output = (resid + (out_ref[...] + bias_ref[...])).astype(BF16)
    output_ref[...] = output[:, : output_ref.shape[1]]
    d_norm, gain_sum = norm_back(resid, gain_ref[...], back_ref[...])
    d_resid = cot_ref[...].astype(F32) + d_norm
    d_resid_ref[...] = d_resid
    d_branch = d_resid.astype(BF16)
    d_branch_ref[...] = d_branch
    add_up(gain_sum_ref, gain_sum)
    add_up(branch_sum_ref, jnp.sum(d_branch.astype(F32), axis=0, keepdims=True))


def last_kernel(x_ref, back_ref, d_resid_ref, gain_ref, grad_ref, gain_sum_ref, wide):
    d_norm, gain_sum = norm_back(widen(x_ref, wide), gain_ref[...], back_ref[...])
    grad = (d_resid_ref[...] + d_norm).astype(BF16)
    grad_ref[...] = grad[:, : grad_ref.shape[1]]
    add_up(gain_sum_ref, gain_sum)


def over_tokens(kernel, inputs, outputs, wide=None, block=256, name=None):
    tokens = inputs[0].shape[0]

    def spec(shape):
        if shape[0] == 1:
            return full(shape)
        return pl.BlockSpec((block, shape[1]), lambda i: (i, 0))

    return pl.pallas_call(
        kernel,
        grid=(tokens // block,),
        in_specs=[spec(v.shape) for v in inputs],
        out_specs=[spec(shape) for shape, _ in outputs],
        out_shape=[jax.ShapeDtypeStruct(*o) for o in outputs],
        scratch_shapes=[pltpu.VMEM((block, wide), F32)] if wide else [],
        compiler_params=params(32),
        name=name,
    )(*inputs)


def scores_of(q_ref, k_ref, qh_ref, kn_ref, sel, at, span):
    q = q_ref[at, :] * 0.125
    qa = jnp.where(sel, q, qh_ref[at, :])
    ka = jnp.where(sel, k_ref[span, :], kn_ref[span, :])
    s = dot(ka, qa, NT)
    causal = lax.broadcasted_iota(jnp.int32, (BLOCK, BLOCK), 0) <= lax.broadcasted_iota(
        jnp.int32, (BLOCK, BLOCK), 1
    )
    early = s.shape[0] - BLOCK
    tail = jnp.where(causal, s[early:, :], MASKED_SCORE)
    return (tail if early == 0 else jnp.concatenate([s[:early, :], tail], axis=0)), q


def spans(length, row):
    for end in range(BLOCK, length + 1, BLOCK):
        start = max(0, end - BLOCK - LONGEST)
        base = row * length
        yield slice(base + end - BLOCK, base + end), slice(base + start, base + end)


def fwd_kernel(
    n_ref, w_ref, wo_ref, bias_ref, qh_ref, kn_ref, branch0_ref, *refs, rows, kept
):
    qkv_ref, att_ref, lse_ref, branch_ref = refs[kept:]

    @pl.when(pl.program_id(0) == 0)
    def _():
        branch_ref[...] = branch0_ref[...]

    length = n_ref.shape[0] // rows
    first = lax.broadcasted_iota(jnp.int32, (1, LANES), 1) < HEAD_DIM
    qkv_ref[...] = (dot(n_ref[...], w_ref[...], NT) + bias_ref[...]).astype(BF16)
    q_ref, k_ref, v_ref = (qkv_ref.at[:, j * LANES : (j + 1) * LANES] for j in range(3))
    for row in range(rows):
        for at, span in spans(length, row):
            parts = []
            for h in range(2):
                sel = first if h == 0 else ~first
                s, _ = scores_of(q_ref, k_ref, qh_ref, kn_ref, sel, at, span)
                m = jnp.max(s, axis=0, keepdims=True)
                p = jnp.exp(s - m)
                total = jnp.sum(p, axis=0, keepdims=True)
                weights = (p * (1.0 / total)).astype(BF16)
                parts.append(dot(weights, v_ref[span, :], TN))
                lse_ref[h : h + 1, at] = m + jnp.log(total)
            att_ref[at, :] = jnp.where(first, parts[0], parts[1]).astype(BF16)
    branch_ref[...] += dot(att_ref[...], wo_ref[...])


def attn_fwd(n, w, wo, bias, qh, kn, branch, kept, rows, start, pairs):
    tokens, model = n.shape
    count = w.shape[0]

    def of(shape, at):
        return pl.BlockSpec((None, *shape), lambda p: (p + at, 0, 0))

    out_specs = [of((tokens, 3 * LANES), start), of((tokens, LANES), start), of((2, tokens), start)]
    return pl.pallas_call(
        functools.partial(fwd_kernel, rows=rows, kept=len(kept)),
        grid=(count,),
        in_specs=[
            full((tokens, model)), of((3 * LANES, model), 0), of((LANES, model), 0),
            of((1, 3 * LANES), 0), full((tokens, LANES)), full((tokens, LANES)),
            full((tokens, model)),
        ] + [pl.BlockSpec(memory_space=pl.ANY)] * len(kept),
        out_specs=out_specs + [full((tokens, model))],
        out_shape=[
            jax.ShapeDtypeStruct((pairs, tokens, 3 * LANES), BF16),
            jax.ShapeDtypeStruct((pairs, tokens, LANES), BF16),
            jax.ShapeDtypeStruct((pairs, 2, tokens), F32),
            jax.ShapeDtypeStruct((tokens, model), F32),
        ],
        input_output_aliases={7 + i: i for i in range(len(kept))} | {6: 3},
        compiler_params=params(48),
        name="attn_fwd",
    )(n, w, wo, bias, qh, kn, branch, *kept)


def ffn_kernel(
    n_ref, c_ref, up_ref, down_ref, bias_ref,
    out_ref, back_ref, gup_ref, gdown_ref, gbias_ref, nt, ct, *, chunk
):
    tokens = n_ref.shape[0]

    @pl.when(pl.program_id(0) == 0)
    def _():
        out_ref[...] = jnp.zeros_like(out_ref)
        back_ref[...] = jnp.zeros_like(back_ref)
        for i in range(0, tokens, 256):
            nt[:, i : i + 256] = n_ref[i : i + 256, :].T
            ct[:, i : i + 256] = c_ref[i : i + 256, :].T

    gup = gdown = gbias = None
    for i in range(0, tokens, chunk):
        r = slice(i, i + chunk)
        pre = dot(n_ref[r, :], up_ref[...]) + bias_ref[...]
        dh = dot(c_ref[r, :], down_ref[...], NT)
        sq = pre * pre
        th = jnp.tanh(pre * (GELU_A + (GELU_A * GELU_B) * sq))
        half = 0.5 + 0.5 * th
        hidden = (pre * half).astype(BF16)
        slope = half + (0.5 * pre) * (1.0 - th * th) * (GELU_A + (3.0 * GELU_A * GELU_B) * sq)
        dpre = (dh * slope).astype(BF16)
        out_ref[r, :] += dot(hidden, down_ref[...])
        back_ref[r, :] += dot(dpre, up_ref[...], NT)
        a, b = dot(nt[:, r], dpre), dot(ct[:, r], hidden)
        s = jnp.sum(dpre.astype(F32), axis=0, keepdims=True)
        gup, gdown, gbias = (a, b, s) if i == 0 else (gup + a, gdown + b, gbias + s)
    for i in range(gup_ref.shape[0]):
        gup_ref[i] = gup[CHUNK * i : CHUNK * (i + 1)].astype(BF16)
        gdown_ref[i] = gdown[CHUNK * i : CHUNK * (i + 1)].astype(BF16)
    gbias_ref[...] = gbias


def ffn(n, c, up, down, bias, chunk=1024):
    tokens, model = n.shape
    count, _, units = up.shape
    block = units // 2

    tall = pl.BlockSpec((None, model, block), lambda i: (i // 2, 0, i % 2))
    wide = pl.BlockSpec((None, block, model), lambda i: (i // 2, i % 2, 0))
    line = pl.BlockSpec((None, 1, block), lambda i: (i // 2, 0, i % 2))
    grad = pl.BlockSpec((None, model // CHUNK, None, CHUNK, block), lambda i: (i // 2, 0, i % 2, 0, 0))
    big = full((tokens, model))
    return pl.pallas_call(
        functools.partial(ffn_kernel, chunk=chunk),
        grid=(count * 2,),
        in_specs=[big, big, tall, wide, line],
        out_specs=[big, big, grad, grad, line],
        out_shape=[jax.ShapeDtypeStruct((tokens, model), F32)] * 2
        + [jax.ShapeDtypeStruct((count, model // CHUNK, 2, CHUNK, block), BF16)] * 2
        + [jax.ShapeDtypeStruct((count, 1, units), F32)],
        scratch_shapes=[pltpu.VMEM((model, tokens), BF16)] * 2,
        compiler_params=params(60),
        name="ffn",
    )(n, c, up, down, bias)


def bwd_kernel(
    n_ref, db_ref, qkv_ref, att_ref, lse_ref, w_ref, wo_ref, qh_ref, kn_ref, gup_ref, gdown_ref,
    back_ref, sums_ref, red_ref,
    da, dqkv, dk_acc, dv_acc, g, core_in, y_in, x_in, z_in, ag, xag_in,
    core_s, core_r, y_s, y_r, x_s, x_r, z_s, z_r, a_s, a_r, xa_s, xa_r, load_s, out_s,
    *, rows, pairs, group, steps
):
    t = pl.program_id(0)
    tokens = n_ref.shape[0]
    length = tokens // rows
    early = gup_ref.shape[1] + gdown_ref.shape[1]
    chunks = early + pairs // 2
    others = group // 2
    keep = CHUNK // others
    dp, tensor = lax.axis_index("dp"), lax.axis_index("tensor")
    side, place = dp % 2, (dp % group) // 2
    mine = pl.ds(pl.multiple_of(place * keep, keep), keep)
    to_core = (dp, tensor + 1 - 2 * (tensor % 2))
    to_y = (dp, (tensor + 2) % 4)
    to_x = (dp + 1 - 2 * side, tensor)

    def place_of(o):
        return (place + o) % others

    def to_z(o):
        return (dp - dp % group + place_of(o) * 2 + side, tensor)

    def remote(src, dst, send, recv, device):
        return pltpu.make_async_remote_copy(
            src_ref=src, dst_ref=dst, send_sem=send, recv_sem=recv, device_id=device,
            device_id_type=MESH,
        )

    late = pairs // 2

    def early_source(which, k):
        ref, at = (gup_ref, k) if k < gup_ref.shape[1] else (gdown_ref, k - gup_ref.shape[1])
        return ref.at[which, at]

    def core_copy(which, k, src):
        return remote(src, core_in.at[which, k], core_s.at[which, k], core_r.at[which, k], to_core)

    def y_copy(k):
        return remote(g.at[chunks + k], y_in.at[k], y_s.at[k], y_r.at[k], to_y)

    def x_copy(k):
        return remote(g.at[k, 1 - side], x_in.at[k], x_s.at[k], x_r.at[k], to_x)

    def z_copy(k, o):
        rows_of = pl.ds(pl.multiple_of(place_of(o) * keep, keep), keep)
        return remote(
            g.at[k, side, rows_of], z_in.at[k, o - 1], z_s.at[k, o - 1], z_r.at[k, o - 1], to_z(o)
        )

    def a_copy(k, o):
        return remote(ag.at[k, mine], ag.at[k, mine], a_s.at[k, o - 1], a_r.at[k, o - 1], to_z(o))

    def a_wait(k, o):
        rows_of = pl.ds(pl.multiple_of(place_of(others - o) * keep, keep), keep)
        part = ag.at[k, rows_of]
        remote(part, part, a_s.at[k, o - 1], a_r.at[k, o - 1], to_z(o)).wait_recv()

    def xa_copy(k):
        return remote(ag.at[k], xag_in.at[k], xa_s.at[k], xa_r.at[k], to_x)

    def out_copies(k):
        return (
            pltpu.make_async_copy(ag.at[k], red_ref.at[k, side], out_s.at[k, 0]),
            pltpu.make_async_copy(xag_in.at[k], red_ref.at[k, 1 - side], out_s.at[k, 1]),
        )

    def load(which, k):
        return pltpu.make_async_copy(
            early_source(2 * which, k), g.at[which * chunks + k], load_s.at[which, k]
        )

    def load_wait(which, k):
        pltpu.make_async_copy(
            gup_ref.at[0, 0], g.at[which * chunks + k], load_s.at[which, k]
        ).wait()

    def stage(lag):
        def run(body):
            k = t - lag

            @pl.when((k >= 0) & (k < chunks))
            def _():
                body(k)

        return run

    def send_y():
        @stage(0)
        def _(k):
            core_copy(0, k, g.at[0]).wait_recv()

            @pl.when(k < early)
            def _():
                load_wait(1, k)

            g[chunks + k] = (g[chunks + k].astype(F32) + core_in[0, k].astype(F32)).astype(BF16)
            y_copy(k).start()

    def send_x():
        @stage(1)
        def _(k):
            core_copy(1, k, g.at[0]).wait_recv()

            @pl.when(k < early)
            def _():
                load_wait(0, k)

            y_copy(k).wait_recv()
            g[k] = (
                g[k].astype(F32) + core_in[1, k].astype(F32) + y_in[k].astype(F32)
            ).astype(BF16)
            x_copy(k).start()

    def send_z():
        @stage(2)
        def _(k):
            x_copy(k).wait_recv()
            g[k, side] = (g[k, side].astype(F32) + x_in[k].astype(F32)).astype(BF16)
            for o in range(1, others):
                z_copy(k, o).start()

    def send_back():
        @stage(2)
        def _(k):
            total = g[k, side, mine].astype(F32)
            for o in range(1, others):
                z_copy(k, o).wait_recv()
                total += z_in[k, o - 1].astype(F32)
            ag[k, mine] = total.astype(BF16)
            for o in range(1, others):
                a_copy(k, o).start()

    def send_back_x():
        @stage(3)
        def _(k):
            for o in range(1, others):
                a_wait(k, o)
            xa_copy(k).start()

    def finish():
        @stage(3)
        def _(k):
            xa_copy(k).wait_recv()
            for c in out_copies(k):
                c.start()

    first = lax.broadcasted_iota(jnp.int32, (1, LANES), 1) < HEAD_DIM
    zero = jnp.zeros((), BF16)
    q_ref, k_ref, v_ref = (qkv_ref.at[:, j * LANES : (j + 1) * LANES] for j in range(3))
    computing = t < pairs

    def attend(row, at, span):
        dq = None
        for h in range(2):
            sel = first if h == 0 else ~first
            s, q = scores_of(q_ref, k_ref, qh_ref, kn_ref, sel, at, span)
            qm = jnp.where(sel, q, zero)
            km = jnp.where(sel, k_ref[span, :], zero)
            dom = jnp.where(sel, da[at, :], zero)
            p = jnp.exp(s - lse_ref[h : h + 1, at])
            dp_ = dot(v_ref[span, :], dom, NT)
            u = p * dp_
            inner = jnp.sum(u, axis=0, keepdims=True)
            ds = (u - p * inner).astype(BF16)
            dv_acc[span, :] += dot(p.astype(BF16), dom)
            dk_acc[span, :] += dot(ds, qm)
            part = dot(ds, km, TN)
            dq = part if dq is None else dq + part
        dqkv[at, :LANES] = (dq * 0.125).astype(BF16)

    @pl.when(t == 0)
    def _():
        barrier = pltpu.get_barrier_semaphore()
        partners = [to_core, to_y, to_x] + [to_z(o) for o in range(1, others)]
        for device in partners:
            pl.semaphore_signal(barrier, inc=1, device_id=device, device_id_type=MESH)
        pl.semaphore_wait(barrier, len(partners))
        for k in range(early):
            core_copy(0, k, early_source(3, k)).start()
            load(1, k).start()
        for k in range(early):
            core_copy(1, k, early_source(1, k)).start()
            load(0, k).start()

    @pl.when(computing)
    def _():
        da[...] = dot(db_ref[...], wo_ref[...], NT).astype(BF16)
        dk_acc[...] = jnp.zeros_like(dk_acc)
        dv_acc[...] = jnp.zeros_like(dv_acc)

    events = [[send_z, send_y], [send_back_x], [send_x], [send_back], [finish]]
    for event in events.pop(0):
        event()
    for row in range(rows):
        for at, span in spans(length, row):
            pl.when(computing)(functools.partial(attend, row, at, span))
            for event in events.pop(0) if events else ():
                event()
    for left in events:
        for event in left:
            event()

    @pl.when(computing)
    def _():
        dqkv[:, LANES : 2 * LANES] = dk_acc[...].astype(BF16)
        dqkv[:, 2 * LANES :] = dv_acc[...].astype(BF16)
        sums_ref[...] = jnp.sum(dqkv[...].astype(F32), axis=0, keepdims=True)
        grown = dot(dqkv[...], w_ref[...])

        @pl.when(t == 0)
        def _():
            back_ref[...] = grown

        @pl.when(t > 0)
        def _():
            back_ref[...] += grown

        grads = dot(dqkv[...], n_ref[...], TN).astype(BF16)
        grads_out = dot(att_ref[...], db_ref[...], TN).astype(BF16)
        wide = grads.shape[1] // 2
        for h in range(2):
            unit = 2 * (pairs - 1 - t) + h
            quarter, j = unit // late, unit % late
            odd, half = quarter % 2, quarter // 2
            base = (1 - odd) * (half * chunks + early) + odd * (2 * chunks + late * half) + j
            for side_ in range(2):
                cols = slice(side_ * wide, (side_ + 1) * wide)
                for i in range(3):
                    lines = slice(LANES * i + HEAD_DIM * h, LANES * i + HEAD_DIM * (h + 1))
                    g[base, side_, HEAD_DIM * i : HEAD_DIM * (i + 1), :] = grads[lines, cols]
                g[base, side_, 3 * HEAD_DIM :, :] = grads_out[
                    HEAD_DIM * h : HEAD_DIM * (h + 1), cols
                ]

            @pl.when(odd == 1)
            def _():
                core_copy(1 - half, early + j, g.at[base]).start()

    @pl.when(t == steps - 1)
    def _():
        @pl.loop(0, chunks)
        def _(k):
            for which in range(2):
                core_copy(which, k, g.at[0]).wait_send()
            y_copy(k).wait_send()
            x_copy(k).wait_send()
            for o in range(1, others):
                z_copy(k, o).wait_send()
                a_copy(k, o).wait_send()
            xa_copy(k).wait_send()
            for c in out_copies(k):
                c.wait()


def attn_bwd(n, db, qkv, att, lse, w, wo, qh, kn, gup, gdown, rows, group):
    tokens, model = n.shape
    pairs = qkv.shape[0]
    early, late = gup.shape[1] + gdown.shape[1], pairs // 2
    chunks = early + late
    steps = max(pairs, chunks + 3)
    others = group // 2
    wide = model // 2

    def of(shape):
        return pl.BlockSpec((None, *shape), lambda p: (jnp.maximum(pairs - 1 - p, 0), 0, 0))

    anywhere = pl.BlockSpec(memory_space=pl.ANY)
    sems = pltpu.SemaphoreType.DMA
    many = (chunks, max(others - 1, 1))
    return pl.pallas_call(
        functools.partial(bwd_kernel, rows=rows, pairs=pairs, group=group, steps=steps),
        grid=(steps,),
        in_specs=[
            full((tokens, model)), full((tokens, model)), of((tokens, 3 * LANES)),
            of((tokens, LANES)), of((2, tokens)), of((3 * LANES, model)), of((LANES, model)),
            full((tokens, LANES)), full((tokens, LANES)), anywhere, anywhere,
        ],
        out_specs=[full((tokens, model)), of((1, 3 * LANES)), anywhere],
        out_shape=[
            jax.ShapeDtypeStruct((tokens, model), F32),
            jax.ShapeDtypeStruct((pairs, 1, 3 * LANES), F32),
            jax.ShapeDtypeStruct((chunks, 2, CHUNK, wide), BF16),
        ],
        scratch_shapes=[
            pltpu.VMEM((tokens, LANES), BF16),
            pltpu.VMEM((tokens, 3 * LANES), BF16),
            pltpu.VMEM((tokens, LANES), F32),
            pltpu.VMEM((tokens, LANES), F32),
            pltpu.VMEM((2 * chunks + 2 * late, 2, CHUNK, wide), BF16),
            pltpu.VMEM((2, chunks, 2, CHUNK, wide), BF16),
            pltpu.VMEM((chunks, 2, CHUNK, wide), BF16),
            pltpu.VMEM((chunks, CHUNK, wide), BF16),
            pltpu.VMEM((*many, CHUNK // others, wide), BF16),
            pltpu.VMEM((chunks, CHUNK, wide), BF16),
            pltpu.VMEM((chunks, CHUNK, wide), BF16),
            sems((2, chunks)), sems((2, chunks)), sems((chunks,)), sems((chunks,)),
            sems((chunks,)), sems((chunks,)), sems(many), sems(many), sems(many), sems(many),
            sems((chunks,)), sems((chunks,)), sems((2, early)), sems((chunks, 2)),
        ],
        compiler_params=params(60, collective_id=0, has_side_effects=True),
        name="attn_bwd",
    )(n, db, qkv, att, lse, w, wo, qh, kn, gup, gdown)


def solution(mesh):
    n_dp, n_tensor = mesh.shape["dp"], mesh.shape["tensor"]
    assert n_tensor == 4 and n_dp % 2 == 0 and n_dp & (n_dp - 1) == 0
    bits = [1 << i for i in range(n_dp.bit_length() - 1)]
    group = min(n_dp, 8)

    def to_core(v):
        return lax.ppermute(v, "tensor", [(i, i ^ 1) for i in range(4)])

    def to_y(v):
        return lax.ppermute(v, "tensor", [(i, i ^ 2) for i in range(4)])

    def to_dp(v, bit):
        return lax.ppermute(v, "dp", [(i, i ^ bit) for i in range(n_dp)])

    def gather(part):
        core = to_core(part)
        upper = lax.axis_index("dp") % 2 != 0
        half = part.shape[0] // 2
        mine = to_y(jnp.where(upper, part[half:], part[:half]))
        other = to_dp(mine, 1)
        over = jnp.concatenate([jnp.where(upper, other, mine), jnp.where(upper, mine, other)])
        return part, core, over, to_core(over)

    def reduce_small(own, core, over, diagonal):
        v = own + to_core(core) + to_y(over + to_core(diagonal))
        for bit in bits:
            v = v + to_dp(v, bit)
        return v

    def local(
        layer_input, segments, cotangent, gain_one, w_qkv, b_qv, w_out, b_out, gain_two,
        w_up, b_up, w_down, b_down,
    ):
        rows = segments.shape[0]
        tokens, stored = layer_input.shape
        model = stored + 1
        heads = w_qkv.shape[2] // HEAD_DIM
        units = w_up.shape[1]

        def pad(v, size=model):
            return jnp.pad(v, [(0, 0)] * (v.ndim - 1) + [(0, size - v.shape[-1])])

        def line(v):
            return pad(v.astype(F32))[None]

        split = w_qkv.reshape(3, stored, heads, HEAD_DIM).transpose(2, 0, 3, 1)
        split = jnp.concatenate([split, w_out.reshape(heads, 1, HEAD_DIM, stored)], axis=1)
        part_attn = pad(split).reshape(heads * 4 * HEAD_DIM, model)
        bias = b_qv.reshape(2, heads, HEAD_DIM)
        bias = jnp.stack([bias[0], jnp.zeros_like(bias[0]), bias[1]], axis=1)
        misc = jnp.concatenate(
            [pad(b_up[None], units), pad(bias.reshape(1, -1), units), jnp.zeros((30, units), BF16)]
        )
        miscs = gather(misc)
        attns = gather(part_attn)
        ups = gather(jnp.pad(w_up, [(0, 1), (0, 0)]))
        downs = gather(pad(w_down))

        def paired(two, two_misc):
            both = jnp.stack(two).reshape(heads, 2, 4, HEAD_DIM, model).transpose(0, 2, 1, 3, 4)
            both = both.reshape(heads, 4, LANES, model)
            w, wo = both[:, :3].reshape(heads, 3 * LANES, model), both[:, 3]
            b = jnp.stack([m[1, : heads * 3 * HEAD_DIM] for m in two_misc]).astype(F32)
            b = b.reshape(heads, 2, 3, HEAD_DIM).transpose(0, 2, 1, 3)
            return w, wo, b.reshape(heads, 1, 3 * LANES)

        gain_one_f, gain_two_f = line(gain_one), line(gain_two)
        n_one, cot, grad_bdown = over_tokens(
            prep_kernel,
            [layer_input, cotangent, gain_one_f],
            [((tokens, model), BF16), ((tokens, model), BF16), ((1, model), F32)],
            wide=model,
            name="prep",
        )
        lane = jnp.arange(LANES) % HEAD_DIM
        hot = segments.reshape(-1, 1) == lane[None, :]
        qh = jnp.where(hot, 1.0, 0.0).astype(BF16)
        kn = jnp.where(hot | (lane >= 8)[None, :], 0.0, MASKED_SCORE).astype(BF16)
        near = paired(attns[:2], miscs[:2])
        branch = jnp.zeros((tokens, model), F32)
        *kept, branch = attn_fwd(n_one, *near, qh, kn, branch, (), rows, 0, 2 * heads)
        far_parts, branch = lax.optimization_barrier(((attns[2:], miscs[2:]), branch))
        far = paired(*far_parts)
        *kept, branch = attn_fwd(n_one, *far, qh, kn, branch, kept, rows, heads, 2 * heads)
        resid, n_two = over_tokens(
            mid_kernel,
            [layer_input, branch, line(b_out), gain_two_f],
            [((tokens, model), F32), ((tokens, model), BF16)],
            wide=model,
            name="mid",
        )

        up_all, down_all, bias_all, n_two = lax.optimization_barrier((ups, downs, miscs, n_two))
        bias_up = jnp.stack([m[:1] for m in bias_all]).astype(F32)
        out_sum, back, g_up, g_down, g_bias = ffn(
            n_two, cot, jnp.stack(up_all), jnp.stack(down_all), bias_up
        )
        output, d_resid, d_branch, grad_gain_two, grad_bout = over_tokens(
            turn_kernel,
            [out_sum, back, resid, cot, line(b_down), gain_two_f],
            [
                ((tokens, stored), BF16), ((tokens, model), F32), ((tokens, model), BF16),
                ((1, model), F32), ((1, model), F32),
            ],
            name="turn",
        )

        w_all = jnp.concatenate([near[0], far[0]])
        wo_all = jnp.concatenate([near[1], far[1]])
        back, sums, reduced = attn_bwd(
            n_one, d_branch, *kept, w_all, wo_all, qh, kn, g_up, g_down, rows, group
        )
        input_grad, grad_gain_one = over_tokens(
            last_kernel,
            [layer_input, back, d_resid, gain_one_f],
            [((tokens, stored), BF16), ((1, model), F32)],
            wide=model,
            name="last",
        )

        sums = sums.reshape(2 * heads, 3, 2, HEAD_DIM).transpose(0, 2, 1, 3)
        sums = sums.reshape(4, heads, 3, HEAD_DIM)[:, :, ::2].transpose(0, 2, 1, 3)
        sums = pad(sums.reshape(4, 2, heads * HEAD_DIM), units)
        common = jnp.concatenate([grad_bdown, grad_bout, grad_gain_two, grad_gain_one])
        small = reduce_small(*(jnp.concatenate([g_bias[i], sums[i], common]) for i in range(4)))

        for bit in bits:
            if bit >= group:
                reduced = (reduced.astype(F32) + to_dp(reduced, bit).astype(F32)).astype(BF16)
        n_up, n_down = g_up.shape[1], g_down.shape[1]
        reduced = reduced.transpose(0, 2, 1, 3).reshape(-1, CHUNK, model)
        grad_up = reduced[:n_up].reshape(model, units)
        grad_down = reduced[n_up : n_up + n_down].reshape(model, units)
        grad_attn = reduced[n_up + n_down :].reshape(heads, 4, HEAD_DIM, model)
        grad_qkv = grad_attn[:, :3].transpose(1, 3, 0, 2).reshape(3, model, heads * HEAD_DIM)
        return (
            output,
            input_grad,
            small[6, :stored],
            grad_qkv[:, :stored].astype(F32),
            small[1:3, : heads * HEAD_DIM],
            grad_attn[:, 3, :, :stored].reshape(heads * HEAD_DIM, stored).astype(F32),
            small[4, :stored],
            small[5, :stored],
            grad_up[:stored].astype(F32),
            small[0],
            grad_down.T[:, :stored].astype(F32),
            small[3, :stored],
        )

    return jax.shard_map(
        local,
        mesh=mesh,
        in_specs=(
            P(("dp", "tensor"), None),
            P(("dp", "tensor"), None),
            P(("dp", "tensor"), None),
            P(),
            P(None, None, "tensor"),
            P(None, "tensor"),
            P("tensor", None),
            P(),
            P(),
            P(None, "tensor"),
            P("tensor"),
            P("tensor", None),
            P(),
        ),
        out_specs=(
            P(("dp", "tensor"), None),
            P(("dp", "tensor"), None),
            P(),
            P(None, None, "tensor"),
            P(None, "tensor"),
            P("tensor", None),
            P(),
            P(),
            P(None, "tensor"),
            P("tensor"),
            P("tensor", None),
            P(),
        ),
        check_vma=False,
    )
```

```python
import functools

import jax
import jax.numpy as jnp
from jax import lax
from jax.experimental import pallas as pl
from jax.experimental.pallas import tpu as pltpu
from jax.sharding import PartitionSpec as P

HEAD_DIM = 64
LANES = 128
EPSILON = 1e-05
MASKED_SCORE = -1e30
LONGEST = 512
BLOCK = 256
CHUNK = 256
F32 = jnp.float32
BF16 = jnp.bfloat16
NN = (((1,), (0,)), ((), ()))
NT = (((1,), (1,)), ((), ()))
TN = (((0,), (0,)), ((), ()))
GELU_A = 0.7978845608028654
GELU_B = 0.044715
MIB = 1024 * 1024
MESH = pl.DeviceIdType.MESH


def dot(a, b, dims=NN):
    return lax.dot_general(a, b, dims, preferred_element_type=F32)


def params(mib, **more):
    return pltpu.CompilerParams(vmem_limit_bytes=mib * MIB, **more)


def full(shape):
    return pl.BlockSpec(shape, lambda *_: (0,) * len(shape))


def once(shape):
    return pl.BlockSpec(shape, lambda *_: (0,) * len(shape), pipeline_mode=pl.Buffered(1))


def widen(ref, wide):
    wide[:, wide.shape[1] - LANES :] = jnp.zeros((wide.shape[0], LANES), F32)
    wide[:, : ref.shape[1]] = ref[...].astype(F32)
    return wide[...]


def norm_scale(values):
    total = jnp.sum(values, axis=-1, keepdims=True)
    square = jnp.sum(values * values, axis=-1, keepdims=True)
    return lax.rsqrt((square + total * total) / values.shape[-1] + EPSILON), total


def norm_back(values, gain, upstream):
    scale, total = norm_scale(values)
    weighted = upstream * values
    spread = jnp.sum(weighted * gain, axis=-1, keepdims=True)
    grad = upstream * gain * scale - (spread * scale * scale * scale / values.shape[-1]) * (
        values + total
    )
    return grad, jnp.sum(weighted * scale, axis=0, keepdims=True)


def add_up(ref, value):
    @pl.when(pl.program_id(0) == 0)
    def _():
        ref[...] = jnp.zeros_like(ref)

    ref[...] += value


def prep_kernel(x_ref, c_ref, gain_ref, n_ref, cot_ref, sum_ref, wide):
    x = widen(x_ref, wide)
    n_ref[...] = (x * norm_scale(x)[0] * gain_ref[...]).astype(BF16)
    c = widen(c_ref, wide)
    cot_ref[...] = c.astype(BF16)
    add_up(sum_ref, jnp.sum(c, axis=0, keepdims=True))


def mid_kernel(x_ref, branch_ref, bias_ref, gain_ref, resid_ref, n_ref, wide):
    resid = widen(x_ref, wide) + (branch_ref[...] + bias_ref[...])
    resid_ref[...] = resid
    n_ref[...] = (resid * norm_scale(resid)[0] * gain_ref[...]).astype(BF16)


def over_tokens(kernel, inputs, outputs, wide=None, block=256, name=None):
    tokens = inputs[0].shape[0]

    def spec(shape):
        if shape[0] == 1:
            return full(shape)
        return pl.BlockSpec((block, shape[1]), lambda i: (i, 0))

    return pl.pallas_call(
        kernel,
        grid=(tokens // block,),
        in_specs=[spec(v.shape) for v in inputs],
        out_specs=[spec(shape) for shape, _ in outputs],
        out_shape=[jax.ShapeDtypeStruct(*o) for o in outputs],
        scratch_shapes=[pltpu.VMEM((block, wide), F32)] if wide else [],
        compiler_params=params(32),
        name=name,
    )(*inputs)


def scores_of(q_ref, k_ref, qh_ref, kn_ref, sel, at, span):
    q = q_ref[at, :] * 0.125
    qa = jnp.where(sel, q, qh_ref[at, :])
    ka = jnp.where(sel, k_ref[span, :], kn_ref[span, :])
    s = dot(ka, qa, NT)
    causal = lax.broadcasted_iota(jnp.int32, (BLOCK, BLOCK), 0) <= lax.broadcasted_iota(
        jnp.int32, (BLOCK, BLOCK), 1
    )
    early = s.shape[0] - BLOCK
    tail = jnp.where(causal, s[early:, :], MASKED_SCORE)
    return (tail if early == 0 else jnp.concatenate([s[:early, :], tail], axis=0)), q


def spans(length, row):
    for end in range(BLOCK, length + 1, BLOCK):
        start = max(0, end - BLOCK - LONGEST)
        base = row * length
        yield slice(base + end - BLOCK, base + end), slice(base + start, base + end)


def fwd_kernel(
    n_ref, w_ref, wo_ref, bias_ref, qh_ref, kn_ref, branch0_ref, *refs, rows, kept
):
    qkv_ref, att_ref, lse_ref, branch_ref = refs[kept:]

    @pl.when(pl.program_id(0) == 0)
    def _():
        branch_ref[...] = branch0_ref[...]

    length = n_ref.shape[0] // rows
    first = lax.broadcasted_iota(jnp.int32, (1, LANES), 1) < HEAD_DIM
    qkv_ref[...] = (dot(n_ref[...], w_ref[...], NT) + bias_ref[...]).astype(BF16)
    q_ref, k_ref, v_ref = (qkv_ref.at[:, j * LANES : (j + 1) * LANES] for j in range(3))
    for row in range(rows):
        for at, span in spans(length, row):
            parts = []
            for h in range(2):
                sel = first if h == 0 else ~first
                s, _ = scores_of(q_ref, k_ref, qh_ref, kn_ref, sel, at, span)
                m = jnp.max(s, axis=0, keepdims=True)
                p = jnp.exp(s - m)
                total = jnp.sum(p, axis=0, keepdims=True)
                weights = (p * (1.0 / total)).astype(BF16)
                parts.append(dot(weights, v_ref[span, :], TN))
                lse_ref[h : h + 1, at] = m + jnp.log(total)
            att_ref[at, :] = jnp.where(first, parts[0], parts[1]).astype(BF16)
    branch_ref[...] += dot(att_ref[...], wo_ref[...])


def attn_fwd(n, w, wo, bias, qh, kn, branch, kept, rows, start, pairs):
    tokens, model = n.shape
    count = w.shape[0]

    def of(shape, at):
        return pl.BlockSpec((None, *shape), lambda p: (p + at, 0, 0))

    out_specs = [of((tokens, 3 * LANES), start), of((tokens, LANES), start), of((2, tokens), start)]
    return pl.pallas_call(
        functools.partial(fwd_kernel, rows=rows, kept=len(kept)),
        grid=(count,),
        in_specs=[
            full((tokens, model)), of((3 * LANES, model), 0), of((LANES, model), 0),
            of((1, 3 * LANES), 0), full((tokens, LANES)), full((tokens, LANES)),
            full((tokens, model)),
        ] + [pl.BlockSpec(memory_space=pl.ANY)] * len(kept),
        out_specs=out_specs + [full((tokens, model))],
        out_shape=[
            jax.ShapeDtypeStruct((pairs, tokens, 3 * LANES), BF16),
            jax.ShapeDtypeStruct((pairs, tokens, LANES), BF16),
            jax.ShapeDtypeStruct((pairs, 2, tokens), F32),
            jax.ShapeDtypeStruct((tokens, model), F32),
        ],
        input_output_aliases={7 + i: i for i in range(len(kept))} | {6: 3},
        compiler_params=params(48),
        name="attn_fwd",
    )(n, w, wo, bias, qh, kn, branch, *kept)


def ffn_kernel(
    n_ref, c_ref, resid_ref, up_ref, down_ref, bias_ref, bias_out_ref, gain_ref,
    gup_ref, gdown_ref, gbias_ref, output_ref, d_resid_ref, d_branch_ref, gain_sum_ref, branch_sum_ref,
    out, back, nt, ct, *, chunk
):
    tokens = n_ref.shape[0]
    step, last = pl.program_id(0), pl.num_programs(0) - 1

    @pl.when(step == 0)
    def _():
        out[...] = jnp.zeros_like(out)
        back[...] = jnp.zeros_like(back)
        for i in range(0, tokens, 256):
            nt[:, i : i + 256] = n_ref[i : i + 256, :].T
            ct[:, i : i + 256] = c_ref[i : i + 256, :].T

    gup = gdown = gbias = None
    for i in range(0, tokens, chunk):
        r = slice(i, i + chunk)
        pre = dot(n_ref[r, :], up_ref[...]) + bias_ref[...]
        dh = dot(c_ref[r, :], down_ref[...], NT)
        sq = pre * pre
        th = jnp.tanh(pre * (GELU_A + (GELU_A * GELU_B) * sq))
        half = 0.5 + 0.5 * th
        hidden = (pre * half).astype(BF16)
        slope = half + (0.5 * pre) * (1.0 - th * th) * (GELU_A + (3.0 * GELU_A * GELU_B) * sq)
        dpre = (dh * slope).astype(BF16)
        out[r, :] += dot(hidden, down_ref[...])
        back[r, :] += dot(dpre, up_ref[...], NT)
        a, b = dot(nt[:, r], dpre), dot(ct[:, r], hidden)
        s = jnp.sum(dpre.astype(F32), axis=0, keepdims=True)
        gup, gdown, gbias = (a, b, s) if i == 0 else (gup + a, gdown + b, gbias + s)
    wide = gup_ref.shape[3]
    for i in range(gup_ref.shape[0]):
        for h in range(2):
            at = slice(CHUNK * i, CHUNK * (i + 1)), slice(wide * h, wide * (h + 1))
            gup_ref[i, h] = gup[at].astype(BF16)
            gdown_ref[i, h] = gdown[at].astype(BF16)
    gbias_ref[...] = gbias

    @pl.when(step == last)
    def _():
        gain_sum_ref[...] = jnp.zeros_like(gain_sum_ref)
        branch_sum_ref[...] = jnp.zeros_like(branch_sum_ref)

        @pl.loop(0, tokens // 256)
        def _(i):
            r = pl.ds(pl.multiple_of(i * 256, 256), 256)
            resid = resid_ref[r, :]
            output = (resid + (out[r, :] + bias_out_ref[...])).astype(BF16)
            output_ref[r, :] = output[:, : output_ref.shape[1]]
            d_norm, gain_sum = norm_back(resid, gain_ref[...], back[r, :])
            d_resid = c_ref[r, :].astype(F32) + d_norm
            d_resid_ref[r, :] = d_resid
            d_branch = d_resid.astype(BF16)
            d_branch_ref[r, :] = d_branch
            gain_sum_ref[...] += gain_sum
            branch_sum_ref[...] += jnp.sum(d_branch.astype(F32), axis=0, keepdims=True)


def ffn(n, c, resid, up, down, bias, bias_out, gain, stored, chunk=512):
    tokens, model = n.shape
    count, _, units = up.shape
    wide = units // 2

    def of(*shape):
        return pl.BlockSpec((None, *shape), lambda i: (i,) + (0,) * len(shape))

    grad = of(model // CHUNK, 2, CHUNK, wide)
    big, row = once((tokens, model)), full((1, model))
    grads = jax.ShapeDtypeStruct((count, model // CHUNK, 2, CHUNK, wide), BF16)
    return pl.pallas_call(
        functools.partial(ffn_kernel, chunk=chunk),
        grid=(count,),
        in_specs=[big, big, big, of(model, units), of(units, model), of(1, units), row, row],
        out_specs=[grad, grad, of(1, units), once((tokens, stored)), big, big, row, row],
        out_shape=[
            grads,
            grads,
            jax.ShapeDtypeStruct((count, 1, units), F32),
            jax.ShapeDtypeStruct((tokens, stored), BF16),
            jax.ShapeDtypeStruct((tokens, model), F32),
            jax.ShapeDtypeStruct((tokens, model), BF16),
            jax.ShapeDtypeStruct((1, model), F32),
            jax.ShapeDtypeStruct((1, model), F32),
        ],
        scratch_shapes=[pltpu.VMEM((tokens, model), F32)] * 2
        + [pltpu.VMEM((model, tokens), BF16)] * 2,
        compiler_params=params(60),
        name="ffn",
    )(n, c, resid, up, down, bias, bias_out, gain)


def bwd_kernel(
    n_ref, db_ref, qkv_ref, att_ref, lse_ref, w_ref, wo_ref, qh_ref, kn_ref, x_ref, d_resid_ref,
    gain_ref, small_ref, gup_ref, gdown_ref,
    grad_in_ref, grad_up_ref, grad_down_ref, grad_qkv_ref, grad_out_ref, total_ref,
    da, dqkv, dk_acc, dv_acc, back, wide_x, g, core_in, y_in, x_in, z_in, ag, xag_in, sv, sv_in, sv_z,
    core_s, core_r, y_s, y_r, x_s, x_r, z_s, z_r, a_s, a_r, xa_s, xa_r, load_s, sv_s, sv_r, svz_s, svz_r,
    *, rows, pairs, group, steps
):
    t = pl.program_id(0)
    tokens = n_ref.shape[0]
    length = tokens // rows
    early = gup_ref.shape[1] + gdown_ref.shape[1]
    chunks = early + pairs // 2
    others = group // 2
    keep = CHUNK // others
    dp, tensor = lax.axis_index("dp"), lax.axis_index("tensor")
    side, place = dp % 2, (dp % group) // 2
    mine = pl.ds(pl.multiple_of(place * keep, keep), keep)
    to_core = (dp, tensor + 1 - 2 * (tensor % 2))
    to_y = (dp, (tensor + 2) % 4)
    to_x = (dp + 1 - 2 * side, tensor)

    def place_of(o):
        return (place + o) % others

    def to_z(o):
        return (dp - dp % group + place_of(o) * 2 + side, tensor)

    def remote(src, dst, send, recv, device):
        return pltpu.make_async_remote_copy(
            src_ref=src, dst_ref=dst, send_sem=send, recv_sem=recv, device_id=device,
            device_id_type=MESH,
        )

    late = pairs // 2

    def early_source(which, k):
        ref, at = (gup_ref, k) if k < gup_ref.shape[1] else (gdown_ref, k - gup_ref.shape[1])
        return ref.at[which, at]

    def core_copy(which, k, src):
        return remote(src, core_in.at[which, k], core_s.at[which, k], core_r.at[which, k], to_core)

    def y_copy(k):
        return remote(g.at[chunks + k], y_in.at[k], y_s.at[k], y_r.at[k], to_y)

    def x_copy(k):
        return remote(g.at[k, 1 - side], x_in.at[k], x_s.at[k], x_r.at[k], to_x)

    def z_copy(k, o):
        rows_of = pl.ds(pl.multiple_of(place_of(o) * keep, keep), keep)
        return remote(
            g.at[k, side, rows_of], z_in.at[k, o - 1], z_s.at[k, o - 1], z_r.at[k, o - 1], to_z(o)
        )

    def a_copy(k, o):
        return remote(ag.at[k, mine], ag.at[k, mine], a_s.at[k, o - 1], a_r.at[k, o - 1], to_z(o))

    def a_wait(k, o):
        rows_of = pl.ds(pl.multiple_of(place_of(others - o) * keep, keep), keep)
        part = ag.at[k, rows_of]
        remote(part, part, a_s.at[k, o - 1], a_r.at[k, o - 1], to_z(o)).wait_recv()

    def xa_copy(k):
        return remote(ag.at[k], xag_in.at[k], xa_s.at[k], xa_r.at[k], to_x)

    def load(which, k):
        return pltpu.make_async_copy(
            early_source(2 * which, k), g.at[which * chunks + k], load_s.at[which, k]
        )

    def load_wait(which, k):
        pltpu.make_async_copy(
            gup_ref.at[0, 0], g.at[which * chunks + k], load_s.at[which, k]
        ).wait()

    def stage(lag):
        def run(body):
            k = t - lag

            @pl.when((k >= 0) & (k < chunks))
            def _():
                body(k)

        return run

    def send_y():
        @stage(0)
        def _(k):
            core_copy(0, k, g.at[0]).wait_recv()

            @pl.when(k < early)
            def _():
                load_wait(1, k)

            g[chunks + k] = (g[chunks + k].astype(F32) + core_in[0, k].astype(F32)).astype(BF16)
            y_copy(k).start()

    def send_x():
        @stage(1)
        def _(k):
            core_copy(1, k, g.at[0]).wait_recv()

            @pl.when(k < early)
            def _():
                load_wait(0, k)

            y_copy(k).wait_recv()
            g[k] = (
                g[k].astype(F32) + core_in[1, k].astype(F32) + y_in[k].astype(F32)
            ).astype(BF16)
            x_copy(k).start()

    def send_z():
        @stage(2)
        def _(k):
            x_copy(k).wait_recv()
            g[k, side] = (g[k, side].astype(F32) + x_in[k].astype(F32)).astype(BF16)
            for o in range(1, others):
                z_copy(k, o).start()

    def send_back():
        @stage(2)
        def _(k):
            total = g[k, side, mine].astype(F32)
            for o in range(1, others):
                z_copy(k, o).wait_recv()
                total += z_in[k, o - 1].astype(F32)
            ag[k, mine] = total.astype(BF16)
            for o in range(1, others):
                a_copy(k, o).start()

    def send_back_x():
        @stage(3)
        def _(k):
            for o in range(1, others):
                a_wait(k, o)
            xa_copy(k).start()

    def finish():
        @stage(3)
        def _(k):
            xa_copy(k).wait_recv()
            kept, got = ag[k].astype(F32), xag_in[k].astype(F32)
            halves = jnp.where(side == 0, kept, got), jnp.where(side == 0, got, kept)
            n_up = gup_ref.shape[1]
            wide = kept.shape[1]
            for c in range(chunks):

                @pl.when(k == c)
                def _(c=c):
                    i = c if c < n_up else c - n_up if c < early else c - early
                    for h, value in enumerate(halves):
                        cols = slice(h * wide, (h + 1) * wide)
                        if c < n_up:
                            end = min(CHUNK * (i + 1), grad_up_ref.shape[0])
                            grad_up_ref[CHUNK * i : end, cols] = value[: end - CHUNK * i]
                        elif c < early:
                            end = min(CHUNK * (i + 1), grad_down_ref.shape[1])
                            grad_down_ref[cols, CHUNK * i : end] = value.T[:, : end - CHUNK * i]
                        else:
                            end = min((h + 1) * wide, grad_out_ref.shape[1])
                            head = slice(HEAD_DIM * i, HEAD_DIM * (i + 1))
                            turned = value.T
                            for j in range(3):
                                part = turned[: end - h * wide, HEAD_DIM * j : HEAD_DIM * (j + 1)]
                                grad_qkv_ref[j, h * wide : end, head] = part
                            grad_out_ref[head, h * wide : end] = value[
                                3 * HEAD_DIM :, : end - h * wide
                            ]

    def sv_copy(i, src, device):
        return remote(src, sv_in.at[i], sv_s.at[i], sv_r.at[i], device)

    def svz_copy(o):
        return remote(sv_z.at[place], sv_z.at[place], svz_s.at[o - 1], svz_r.at[o - 1], to_z(o))

    def small_sums():
        @pl.when(t == pairs + 1)
        def _():
            for i in (0, 1):
                sv_copy(i, sv.at[3 - 2 * i], to_core).wait_recv()
            sv[2] += sv_in[0]
            sv_copy(2, sv.at[2], to_y).start()

        @pl.when(t == pairs + 2)
        def _():
            sv_copy(2, sv.at[2], to_y).wait_recv()
            sv[0] = (sv[0] + sv_in[1]) + sv_in[2]
            sv_copy(3, sv.at[0], to_x).start()

        @pl.when(t == pairs + 3)
        def _():
            sv_copy(3, sv.at[0], to_x).wait_recv()
            sv_z[place] = sv[0] + sv_in[3]
            for o in range(1, others):
                svz_copy(o).start()

        @pl.when(t == pairs + 4)
        def _():
            for o in range(1, others):
                part = sv_z.at[place_of(others - o)]
                remote(part, part, svz_s.at[o - 1], svz_r.at[o - 1], to_z(o)).wait_recv()
            total = sv_z[0]
            for i in range(1, others):
                total += sv_z[i]
            total_ref[...] = total

    def norm_one():
        gain_sum = jnp.zeros((1, n_ref.shape[1]), F32)
        for i in range(0, tokens, CHUNK):
            r = slice(i, i + CHUNK)
            d_norm, part = norm_back(widen(x_ref.at[r, :], wide_x), gain_ref[...], back[r, :])
            grad = (d_resid_ref[r, :] + d_norm).astype(BF16)
            grad_in_ref[r, :] = grad[:, : grad_in_ref.shape[1]]
            gain_sum += part
        for i in range(4):
            sv[i, 4:5, :] = gain_sum
        for i in (0, 1):
            sv_copy(i, sv.at[3 - 2 * i], to_core).start()

    first = lax.broadcasted_iota(jnp.int32, (1, LANES), 1) < HEAD_DIM
    zero = jnp.zeros((), BF16)
    q_ref, k_ref, v_ref = (qkv_ref.at[:, j * LANES : (j + 1) * LANES] for j in range(3))
    computing = t < pairs

    def attend(row, at, span):
        dq = None
        for h in range(2):
            sel = first if h == 0 else ~first
            s, q = scores_of(q_ref, k_ref, qh_ref, kn_ref, sel, at, span)
            qm = jnp.where(sel, q, zero)
            km = jnp.where(sel, k_ref[span, :], zero)
            dom = jnp.where(sel, da[at, :], zero)
            p = jnp.exp(s - lse_ref[h : h + 1, at])
            dp_ = dot(v_ref[span, :], dom, NT)
            u = p * dp_
            inner = jnp.sum(u, axis=0, keepdims=True)
            ds = (u - p * inner).astype(BF16)
            dv_acc[span, :] += dot(p.astype(BF16), dom)
            dk_acc[span, :] += dot(ds, qm)
            part = dot(ds, km, TN)
            dq = part if dq is None else dq + part
        dqkv[at, :LANES] = (dq * 0.125).astype(BF16)

    @pl.when(t == 0)
    def _():
        barrier = pltpu.get_barrier_semaphore()
        partners = [to_core, to_y, to_x] + [to_z(o) for o in range(1, others)]
        for device in partners:
            pl.semaphore_signal(barrier, inc=1, device_id=device, device_id_type=MESH)
        pl.semaphore_wait(barrier, len(partners))
        for k in range(early):
            core_copy(0, k, early_source(3, k)).start()
            load(1, k).start()
        for k in range(early):
            core_copy(1, k, early_source(1, k)).start()
            load(0, k).start()
        sv[...] = small_ref[...]

    @pl.when(computing)
    def _():
        da[...] = dot(db_ref[...], wo_ref[...], NT).astype(BF16)
        dk_acc[...] = jnp.zeros_like(dk_acc)
        dv_acc[...] = jnp.zeros_like(dv_acc)

    events = [[send_z, send_y], [send_back_x], [send_x], [send_back], [finish]]
    for event in events.pop(0):
        event()
    for row in range(rows):
        for at, span in spans(length, row):
            pl.when(computing)(functools.partial(attend, row, at, span))
            for event in events.pop(0) if events else ():
                event()
    for left in events:
        for event in left:
            event()
    small_sums()
    pl.when(t == pairs)(norm_one)

    @pl.when(computing)
    def _():
        dqkv[:, LANES : 2 * LANES] = dk_acc[...].astype(BF16)
        dqkv[:, 2 * LANES :] = dv_acc[...].astype(BF16)
        sums = jnp.sum(dqkv[...].astype(F32), axis=0, keepdims=True)
        grown = dot(dqkv[...], w_ref[...])

        @pl.when(t == 0)
        def _():
            back[...] = grown

        @pl.when(t > 0)
        def _():
            back[...] += grown

        grads = dot(dqkv[...], n_ref[...], TN).astype(BF16)
        grads_out = dot(att_ref[...], db_ref[...], TN).astype(BF16)
        wide = grads.shape[1] // 2
        for h in range(2):
            unit = 2 * (pairs - 1 - t) + h
            quarter, j = unit // late, unit % late
            odd, half = quarter % 2, quarter // 2
            for line in range(late):

                @pl.when(j == line)
                def _(line=8 + line, h=h):
                    for i in (0, 2):
                        part = sums[:, LANES * i + HEAD_DIM * h : LANES * i + HEAD_DIM * (h + 1)]
                        sv[quarter, line : line + 1, LANES * i : LANES * i + HEAD_DIM] = part

            base = (1 - odd) * (half * chunks + early) + odd * (2 * chunks + late * half) + j
            for side_ in range(2):
                cols = slice(side_ * wide, (side_ + 1) * wide)
                for i in range(3):
                    lines = slice(LANES * i + HEAD_DIM * h, LANES * i + HEAD_DIM * (h + 1))
                    g[base, side_, HEAD_DIM * i : HEAD_DIM * (i + 1), :] = grads[lines, cols]
                g[base, side_, 3 * HEAD_DIM :, :] = grads_out[
                    HEAD_DIM * h : HEAD_DIM * (h + 1), cols
                ]

            @pl.when(odd == 1)
            def _():
                core_copy(1 - half, early + j, g.at[base]).start()

    @pl.when(t == steps - 1)
    def _():
        @pl.loop(0, chunks)
        def _(k):
            for which in range(2):
                core_copy(which, k, g.at[0]).wait_send()
            y_copy(k).wait_send()
            x_copy(k).wait_send()
            for o in range(1, others):
                z_copy(k, o).wait_send()
                a_copy(k, o).wait_send()
            xa_copy(k).wait_send()

        for i, device in enumerate((to_core, to_core, to_y, to_x)):
            sv_copy(i, sv.at[0], device).wait_send()
        for o in range(1, others):
            svz_copy(o).wait_send()


def attn_bwd(
    n, db, qkv, att, lse, w, wo, qh, kn, x, d_resid, gain, small, gup, gdown, rows, group
):
    tokens, model = n.shape
    stored = x.shape[1]
    pairs = qkv.shape[0]
    early, late = gup.shape[1] + gdown.shape[1], pairs // 2
    chunks = early + late
    steps = max(pairs + 5, chunks + 3)
    others = group // 2
    wide = model // 2
    lines = small.shape[1]

    def of(shape):
        return pl.BlockSpec((None, *shape), lambda p: (jnp.maximum(pairs - 1 - p, 0), 0, 0))

    anywhere = pl.BlockSpec(memory_space=pl.ANY)
    sems = pltpu.SemaphoreType.DMA
    between = max(others - 1, 1)
    many = (chunks, between)
    outs = [
        ((tokens, stored), BF16),
        ((stored, 2 * wide), F32),
        ((2 * wide, stored), F32),
        ((3, stored, late * HEAD_DIM), F32),
        ((late * HEAD_DIM, stored), F32),
        ((lines, model), F32),
    ]
    return pl.pallas_call(
        functools.partial(bwd_kernel, rows=rows, pairs=pairs, group=group, steps=steps),
        grid=(steps,),
        in_specs=[
            once((tokens, model)), once((tokens, model)), of((tokens, 3 * LANES)),
            of((tokens, LANES)), of((2, tokens)), of((3 * LANES, model)), of((LANES, model)),
            once((tokens, LANES)), once((tokens, LANES)), once((tokens, stored)),
            once((tokens, model)), full((1, model)), full(small.shape), anywhere, anywhere,
        ],
        out_specs=[once(shape) for shape, _ in outs],
        out_shape=[jax.ShapeDtypeStruct(*o) for o in outs],
        scratch_shapes=[
            pltpu.VMEM((tokens, LANES), BF16),
            pltpu.VMEM((tokens, 3 * LANES), BF16),
            pltpu.VMEM((tokens, LANES), F32),
            pltpu.VMEM((tokens, LANES), F32),
            pltpu.VMEM((tokens, model), F32),
            pltpu.VMEM((CHUNK, model), F32),
            pltpu.VMEM((2 * chunks + 2 * late, 2, CHUNK, wide), BF16),
            pltpu.VMEM((2, chunks, 2, CHUNK, wide), BF16),
            pltpu.VMEM((chunks, 2, CHUNK, wide), BF16),
            pltpu.VMEM((chunks, CHUNK, wide), BF16),
            pltpu.VMEM((*many, CHUNK // others, wide), BF16),
            pltpu.VMEM((chunks, CHUNK, wide), BF16),
            pltpu.VMEM((chunks, CHUNK, wide), BF16),
            pltpu.VMEM((4, lines, model), F32),
            pltpu.VMEM((4, lines, model), F32),
            pltpu.VMEM((others, lines, model), F32),
            sems((2, chunks)), sems((2, chunks)), sems((chunks,)), sems((chunks,)),
            sems((chunks,)), sems((chunks,)), sems(many), sems(many), sems(many), sems(many),
            sems((chunks,)), sems((chunks,)), sems((2, early)), sems((4,)), sems((4,)),
            sems((between,)), sems((between,)),
        ],
        compiler_params=params(62, collective_id=0, has_side_effects=True),
        name="attn_bwd",
    )(n, db, qkv, att, lse, w, wo, qh, kn, x, d_resid, gain, small, gup, gdown)


def solution(mesh):
    n_dp, n_tensor = mesh.shape["dp"], mesh.shape["tensor"]
    assert n_tensor == 4 and n_dp % 2 == 0 and n_dp & (n_dp - 1) == 0
    bits = [1 << i for i in range(n_dp.bit_length() - 1)]
    group = min(n_dp, 8)

    def to_core(v):
        return lax.ppermute(v, "tensor", [(i, i ^ 1) for i in range(4)])

    def to_y(v):
        return lax.ppermute(v, "tensor", [(i, i ^ 2) for i in range(4)])

    def to_dp(v, bit):
        return lax.ppermute(v, "dp", [(i, i ^ bit) for i in range(n_dp)])

    def gather(part):
        core = to_core(part)
        upper = lax.axis_index("dp") % 2 != 0
        half = part.shape[0] // 2
        mine = to_y(jnp.where(upper, part[half:], part[:half]))
        other = to_dp(mine, 1)
        over = jnp.concatenate([jnp.where(upper, other, mine), jnp.where(upper, mine, other)])
        return part, core, over, to_core(over)

    def local(
        layer_input, segments, cotangent, gain_one, w_qkv, b_qv, w_out, b_out, gain_two,
        w_up, b_up, w_down, b_down,
    ):
        rows = segments.shape[0]
        tokens, stored = layer_input.shape
        model = stored + 1
        heads = w_qkv.shape[2] // HEAD_DIM
        units = w_up.shape[1]

        def pad(v, size=model):
            return jnp.pad(v, [(0, 0)] * (v.ndim - 1) + [(0, size - v.shape[-1])])

        def line(v):
            return pad(v.astype(F32))[None]

        split = w_qkv.reshape(3, stored, heads, HEAD_DIM).transpose(2, 0, 3, 1)
        split = jnp.concatenate([split, w_out.reshape(heads, 1, HEAD_DIM, stored)], axis=1)
        part_attn = pad(split).reshape(heads * 4 * HEAD_DIM, model)
        bias = b_qv.reshape(2, heads, HEAD_DIM)
        bias = jnp.stack([bias[0], jnp.zeros_like(bias[0]), bias[1]], axis=1)
        misc = jnp.concatenate(
            [pad(b_up[None], units), pad(bias.reshape(1, -1), units), jnp.zeros((30, units), BF16)]
        )
        miscs = gather(misc)
        attns = gather(part_attn)
        ups = gather(jnp.pad(w_up, [(0, 1), (0, 0)]))
        downs = gather(pad(w_down))

        def paired(two, two_misc):
            both = jnp.stack(two).reshape(heads, 2, 4, HEAD_DIM, model).transpose(0, 2, 1, 3, 4)
            both = both.reshape(heads, 4, LANES, model)
            w, wo = both[:, :3].reshape(heads, 3 * LANES, model), both[:, 3]
            b = jnp.stack([m[1, : heads * 3 * HEAD_DIM] for m in two_misc]).astype(F32)
            b = b.reshape(heads, 2, 3, HEAD_DIM).transpose(0, 2, 1, 3)
            return w, wo, b.reshape(heads, 1, 3 * LANES)

        gain_one_f, gain_two_f = line(gain_one), line(gain_two)
        n_one, cot, grad_bdown = over_tokens(
            prep_kernel,
            [layer_input, cotangent, gain_one_f],
            [((tokens, model), BF16), ((tokens, model), BF16), ((1, model), F32)],
            wide=model,
            name="prep",
        )
        lane = jnp.arange(LANES) % HEAD_DIM
        hot = segments.reshape(-1, 1) == lane[None, :]
        qh = jnp.where(hot, 1.0, 0.0).astype(BF16)
        kn = jnp.where(hot | (lane >= 8)[None, :], 0.0, MASKED_SCORE).astype(BF16)
        near = paired(attns[:2], miscs[:2])
        branch = jnp.zeros((tokens, model), F32)
        *kept, branch = attn_fwd(n_one, *near, qh, kn, branch, (), rows, 0, 2 * heads)
        far_parts, branch = lax.optimization_barrier(((attns[2:], miscs[2:]), branch))
        far = paired(*far_parts)
        *kept, branch = attn_fwd(n_one, *far, qh, kn, branch, kept, rows, heads, 2 * heads)
        resid, n_two = over_tokens(
            mid_kernel,
            [layer_input, branch, line(b_out), gain_two_f],
            [((tokens, model), F32), ((tokens, model), BF16)],
            wide=model,
            name="mid",
        )

        up_all, down_all, bias_all, n_two = lax.optimization_barrier((ups, downs, miscs, n_two))
        bias_up = jnp.stack([m[:1] for m in bias_all]).astype(F32)
        (
            g_up, g_down, g_bias, output, d_resid, d_branch, grad_gain_two, grad_bout
        ) = ffn(
            n_two, cot, resid, jnp.stack(up_all), jnp.stack(down_all), bias_up, line(b_down),
            gain_two_f, stored,
        )

        w_all = jnp.concatenate([near[0], far[0]])
        wo_all = jnp.concatenate([near[1], far[1]])
        common = jnp.concatenate([grad_bdown, grad_bout, grad_gain_two], axis=0)[None]
        small = jnp.concatenate(
            [g_bias, jnp.broadcast_to(common, (4, 3, model)), jnp.zeros((4, 12, model), F32)], axis=1
        )
        input_grad, grad_up, grad_down, grad_qkv, grad_out, small = attn_bwd(
            n_one, d_branch, *kept, w_all, wo_all, qh, kn, layer_input, d_resid, gain_one_f, small,
            g_up, g_down, rows, group,
        )
        sums = (grad_up, grad_down, grad_qkv, grad_out, small)
        for bit in bits:
            if bit >= group:
                sums = tuple(v + to_dp(v, bit) for v in sums)
        grad_up, grad_down, grad_qkv, grad_out, small = sums
        per_head = small[8 : 8 + heads]
        grad_bqv = jnp.stack(
            [per_head[:, :HEAD_DIM].reshape(-1), per_head[:, 2 * LANES : 2 * LANES + HEAD_DIM].reshape(-1)]
        )
        return (
            output,
            input_grad,
            small[4, :stored],
            grad_qkv,
            grad_bqv,
            grad_out,
            small[2, :stored],
            small[3, :stored],
            grad_up,
            small[0],
            grad_down,
            small[1, :stored],
        )

    return jax.shard_map(
        local,
        mesh=mesh,
        in_specs=(
            P(("dp", "tensor"), None),
            P(("dp", "tensor"), None),
            P(("dp", "tensor"), None),
            P(),
            P(None, None, "tensor"),
            P(None, "tensor"),
            P("tensor", None),
            P(),
            P(),
            P(None, "tensor"),
            P("tensor"),
            P("tensor", None),
            P(),
        ),
        out_specs=(
            P(("dp", "tensor"), None),
            P(("dp", "tensor"), None),
            P(),
            P(None, None, "tensor"),
            P(None, "tensor"),
            P("tensor", None),
            P(),
            P(),
            P(None, "tensor"),
            P("tensor"),
            P("tensor", None),
            P(),
        ),
        check_vma=False,
    )
```

```python
import functools

import jax
import jax.numpy as jnp
from jax import lax
from jax.experimental import pallas as pl
from jax.experimental.pallas import tpu as pltpu
from jax.sharding import PartitionSpec as P

HEAD_DIM = 64
LANES = 128
EPSILON = 1e-05
MASKED_SCORE = -1e30
LONGEST = 512
BLOCK = 256
CHUNK = 256
F32 = jnp.float32
BF16 = jnp.bfloat16
NN = (((1,), (0,)), ((), ()))
NT = (((1,), (1,)), ((), ()))
TN = (((0,), (0,)), ((), ()))
GELU_A = 0.7978845608028654
GELU_B = 0.044715
MIB = 1024 * 1024
MESH = pl.DeviceIdType.MESH


def dot(a, b, dims=NN):
    return lax.dot_general(a, b, dims, preferred_element_type=F32)


def params(mib, **more):
    return pltpu.CompilerParams(vmem_limit_bytes=mib * MIB, **more)


def full(shape):
    return pl.BlockSpec(shape, lambda *_: (0,) * len(shape))


def once(shape):
    return pl.BlockSpec(shape, lambda *_: (0,) * len(shape), pipeline_mode=pl.Buffered(1))


def widen(ref, wide):
    wide[:, wide.shape[1] - LANES :] = jnp.zeros((wide.shape[0], LANES), F32)
    wide[:, : ref.shape[1]] = ref[...].astype(F32)
    return wide[...]


def norm_scale(values):
    total = jnp.sum(values, axis=-1, keepdims=True)
    square = jnp.sum(values * values, axis=-1, keepdims=True)
    return lax.rsqrt((square + total * total) / values.shape[-1] + EPSILON), total


def norm_back(values, gain, upstream):
    scale, total = norm_scale(values)
    weighted = upstream * values
    spread = jnp.sum(weighted * gain, axis=-1, keepdims=True)
    grad = upstream * gain * scale - (spread * scale * scale * scale / values.shape[-1]) * (
        values + total
    )
    return grad, jnp.sum(weighted * scale, axis=0, keepdims=True)


def scores_of(q_ref, k_ref, qh_ref, kn_ref, sel, at, span):
    q = q_ref[at, :] * 0.125
    qa = jnp.where(sel, q, qh_ref[at, :])
    ka = jnp.where(sel, k_ref[span, :], kn_ref[span, :])
    s = dot(ka, qa, NT)
    causal = lax.broadcasted_iota(jnp.int32, (BLOCK, BLOCK), 0) <= lax.broadcasted_iota(
        jnp.int32, (BLOCK, BLOCK), 1
    )
    early = s.shape[0] - BLOCK
    tail = jnp.where(causal, s[early:, :], MASKED_SCORE)
    return (tail if early == 0 else jnp.concatenate([s[:early, :], tail], axis=0)), q


def spans(length, row):
    for end in range(BLOCK, length + 1, BLOCK):
        start = max(0, end - BLOCK - LONGEST)
        base = row * length
        yield slice(base + end - BLOCK, base + end), slice(base + start, base + end)


def remote(src, dst, send, recv, device):
    return pltpu.make_async_remote_copy(
        src_ref=src, dst_ref=dst, send_sem=send, recv_sem=recv, device_id=device,
        device_id_type=MESH,
    )


def greet(partners):
    barrier = pltpu.get_barrier_semaphore()
    for device in partners:
        pl.semaphore_signal(barrier, inc=1, device_id=device, device_id_type=MESH)
    pl.semaphore_wait(barrier, len(partners))


def neighbours():
    dp, tensor = lax.axis_index("dp"), lax.axis_index("tensor")
    side = dp % 2
    to_core = (dp, tensor + 1 - 2 * (tensor % 2))
    return to_core, (dp, (tensor + 2) % 4), (dp + 1 - 2 * side, tensor), side


def pair_weights(even, odd, w, wo):
    for h, unit in enumerate((even, odd)):
        for i in range(3):
            at = LANES * i + HEAD_DIM * h
            w[at : at + HEAD_DIM, :] = unit[HEAD_DIM * i : HEAD_DIM * (i + 1), :]
        wo[HEAD_DIM * h : HEAD_DIM * (h + 1), :] = unit[3 * HEAD_DIM :, :]


def fwd_kernel(
    x_ref, c_ref, wqkv_ref, wout_ref, up_ref, down_ref, misc_ref, gain_one_ref, gain_two_ref,
    bias_out_ref, qh_ref, kn_ref,
    n_ref, cot_ref, c_sum_ref, qkv_ref, att_ref, lse_ref, resid_ref, n_two_ref, wa_ref, wf_ref, misc_all_ref,
    wa, stage, misc, w, wo, branch, wide,
    core_s, core_r, y_s, y_r, x_s, x_r, d_s, d_r, local_s,
    *, rows, pairs
):
    t = pl.program_id(0)
    tokens = x_ref.shape[0]
    length = tokens // rows
    heads = pairs // 2
    stored = x_ref.shape[1]
    model = stored + 1
    early, tail = heads, stage.shape[0]
    to_core, to_y, to_x, side = neighbours()
    half = pl.ds(pl.multiple_of(side * (CHUNK // 2), CHUNK // 2), CHUNK // 2)
    other = pl.ds(pl.multiple_of((1 - side) * (CHUNK // 2), CHUNK // 2), CHUNK // 2)
    last = early + tail

    def held(quarter, k):
        if k == last:
            return misc.at[quarter]
        if k < early:
            return wa.at[quarter, k]
        return wf_ref.at[quarter, k - early]

    def own(k):
        return held(0, k) if k < early or k == last else stage.at[k - early]

    def part(ref, k):
        return ref if k == last else ref.at[half]

    def core_copy(k):
        return remote(own(k), held(1, k), core_s.at[k], core_r.at[k], to_core)

    def y_copy(k):
        return remote(part(own(k), k), part(held(2, k), k), y_s.at[k], y_r.at[k], to_y)

    def x_copy(k):
        ref = held(2, k).at[half]
        return remote(ref, ref, x_s.at[k], x_r.at[k], to_x)

    def d_copy(k):
        return remote(held(2, k), held(3, k), d_s.at[k], d_r.at[k], to_core)

    def keep_copy(k):
        if k == last:
            return pltpu.make_async_copy(misc, misc_all_ref, local_s.at[k])
        if k < early:
            return pltpu.make_async_copy(wa.at[:, k], wa_ref.at[:, k], local_s.at[k])
        return pltpu.make_async_copy(stage.at[k - early], wf_ref.at[0, k - early], local_s.at[k])

    def x_on(k):
        y_copy(k).wait_recv()
        x_copy(k).start()

    def d_on(k):
        if k == last:
            y_copy(k).wait_recv()
        else:
            ref = held(2, k).at[other]
            remote(ref, ref, x_s.at[k], x_r.at[k], to_x).wait_recv()
        d_copy(k).start()

    def start_y(k):
        y_copy(k).start()

    @pl.when(t == 0)
    def _():
        edge = slice(model - LANES, model)
        wa[0, :, :, edge] = jnp.zeros((early, CHUNK, LANES), BF16)
        for j in range(heads):
            head = slice(HEAD_DIM * j, HEAD_DIM * (j + 1))
            for i in range(3):
                wa[0, j, HEAD_DIM * i : HEAD_DIM * (i + 1), :stored] = wqkv_ref[i, head, :]
            wa[0, j, 3 * HEAD_DIM :, :stored] = wout_ref[head, :]
        misc[0] = misc_ref[...]
        greet([to_core, to_y, to_x])
        for k in (last, *range(early)):
            core_copy(k).start()
            y_copy(k).start()
        count = tail // 2
        stage[:, :, edge] = jnp.zeros((tail, CHUNK, LANES), BF16)
        stage[count - 1, CHUNK - 16 :, :] = jnp.zeros((16, model), BF16)
        for i in range(count):
            end = min(CHUNK * (i + 1), stored)
            stage[i, : end - CHUNK * i, :] = up_ref[CHUNK * i : end, :]
            stage[count + i, :, :stored] = down_ref[CHUNK * i : CHUNK * (i + 1), :]
        for k in range(early, last):
            core_copy(k).start()
            keep_copy(k).start()
        branch[...] = jnp.zeros_like(branch)
        c_sum = jnp.zeros((1, model), F32)
        for i in range(0, tokens, CHUNK):
            r = slice(i, i + CHUNK)
            x = widen(x_ref.at[r, :], wide)
            n_ref[r, :] = (x * norm_scale(x)[0] * gain_one_ref[...]).astype(BF16)
            c = widen(c_ref.at[r, :], wide)
            cot_ref[r, :] = c.astype(BF16)
            c_sum += jnp.sum(c, axis=0, keepdims=True)
        c_sum_ref[...] = c_sum
        core_copy(last).wait_recv()

    events = {
        (0, 2): [(start_y, early)], (0, 4): [(d_on, last)],
        (1, 1): [(x_on, 0)], (1, 3): [(start_y, early + 1)],
        (2, 1): [(x_on, 1)], (2, 2): [(start_y, early + 2)], (2, 3): [(d_on, 0)],
        (2, 4): [(d_on, 1)],
        (3, 0): [(x_on, 2)], (3, 2): [(start_y, early + 3)],
        (3, 4): [(d_on, 2)],
        (4, 1): [(x_on, early)], (4, 2): [(start_y, early + 4)],
        (5, 0): [(x_on, early + 1), (d_on, early)], (5, 1): [(start_y, early + 5)],
        (5, 3): [(x_on, early + 2), (d_on, early + 1)],
    }

    def run(slot):
        for (step, at), todo in events.items():
            if at == slot and todo:

                @pl.when(t == step)
                def _(todo=todo):
                    for event, k in todo:
                        event(k)

    for step in range(pairs):
        needed = {divmod(2 * step + h, heads) for h in range(2)}
        seen = {divmod(u, heads) for u in range(2 * step)}

        @pl.when(t == step)
        def _(needed=needed, seen=seen):
            for quarter, j in sorted(needed - seen):
                if quarter == 1:
                    core_copy(j).wait_recv()
                if quarter == 3:
                    d_copy(j).wait_recv()
            if any(quarter == 3 for quarter, _ in needed) and not any(q == 3 for q, _ in seen):
                d_copy(last).wait_recv()

    first = lax.broadcasted_iota(jnp.int32, (1, LANES), 1) < HEAD_DIM
    units = 2 * t, 2 * t + 1
    pair_weights(*(wa.at[u // heads, u % heads] for u in units), w, wo)
    bias = sum(misc[u // heads, u % heads, h, :1, :] for h, u in enumerate(units))
    qkv_ref[...] = (dot(n_ref[...], w[...], NT) + bias).astype(BF16)
    q_ref, k_ref, v_ref = (qkv_ref.at[:, j * LANES : (j + 1) * LANES] for j in range(3))
    run(0)
    slot = 1
    for row in range(rows):
        for at, span in spans(length, row):
            parts = []
            for h in range(2):
                sel = first if h == 0 else ~first
                s, _ = scores_of(q_ref, k_ref, qh_ref, kn_ref, sel, at, span)
                m = jnp.max(s, axis=0, keepdims=True)
                p = jnp.exp(s - m)
                total = jnp.sum(p, axis=0, keepdims=True)
                weights = (p * (1.0 / total)).astype(BF16)
                parts.append(dot(weights, v_ref[span, :], TN))
                lse_ref[h : h + 1, at] = m + jnp.log(total)
            att_ref[at, :] = jnp.where(first, parts[0], parts[1]).astype(BF16)
            if slot < 4:
                run(slot)
                slot += 1
    branch[...] += dot(att_ref[...], wo[...])
    run(4)

    @pl.when(t == pairs - 1)
    def _():
        for i in range(0, tokens, CHUNK):
            r = slice(i, i + CHUNK)
            resid = widen(x_ref.at[r, :], wide) + (branch[r, :] + bias_out_ref[...])
            resid_ref[r, :] = resid
            n_two_ref[r, :] = (resid * norm_scale(resid)[0] * gain_two_ref[...]).astype(BF16)
        for k in range(early + 3, last):
            x_on(k)
        for k in range(early + 2, last):
            d_on(k)
        for k in (*range(early), last):
            keep_copy(k).start()
        for k in range(early, last):
            core_copy(k).wait_recv()
            d_copy(k).wait_recv()
        for k in range(last + 1):
            core_copy(k).wait_send()
            y_copy(k).wait_send()
            if k < last:
                x_copy(k).wait_send()
            d_copy(k).wait_send()
            keep_copy(k).wait()


def forward(x, c, wqkv, wout, up, down, misc, gain_one, gain_two, bias_out, qh, kn, rows):
    tokens, stored = x.shape
    model = stored + 1
    heads = wqkv.shape[1] // HEAD_DIM
    pairs = 2 * heads
    tail = 2 * (model // CHUNK)

    def of(*shape):
        return pl.BlockSpec((None, *shape), lambda p: (p,) + (0,) * len(shape))

    anywhere = pl.BlockSpec(memory_space=pl.ANY)
    sems = pltpu.SemaphoreType.DMA((heads + tail + 1,))
    inputs = [x, c, wqkv, wout, up, down, misc, gain_one, gain_two, bias_out, qh, kn]
    big = once((tokens, model))
    outs = [
        (big, (tokens, model), BF16),
        (big, (tokens, model), BF16),
        (once((1, model)), (1, model), F32),
        (of(tokens, 3 * LANES), (pairs, tokens, 3 * LANES), BF16),
        (of(tokens, LANES), (pairs, tokens, LANES), BF16),
        (of(2, tokens), (pairs, 2, tokens), F32),
        (big, (tokens, model), F32),
        (big, (tokens, model), BF16),
        (anywhere, (4, heads, CHUNK, model), BF16),
        (anywhere, (4, tail, CHUNK, model), BF16),
        (anywhere, (4, *misc.shape), F32),
    ]
    return pl.pallas_call(
        functools.partial(fwd_kernel, rows=rows, pairs=pairs),
        grid=(pairs,),
        in_specs=[once(v.shape) for v in inputs],
        out_specs=[spec for spec, _, _ in outs],
        out_shape=[jax.ShapeDtypeStruct(shape, dtype) for _, shape, dtype in outs],
        scratch_shapes=[
            pltpu.VMEM((4, heads, CHUNK, model), BF16),
            pltpu.VMEM((tail, CHUNK, model), BF16),
            pltpu.VMEM((4, *misc.shape), F32),
            pltpu.VMEM((3 * LANES, model), BF16),
            pltpu.VMEM((LANES, model), BF16),
            pltpu.VMEM((tokens, model), F32),
            pltpu.VMEM((CHUNK, model), F32),
        ]
        + [sems] * 9,
        compiler_params=params(60, collective_id=1, has_side_effects=True),
        name="forward",
    )(*inputs)


def ffn_kernel(
    n_ref, c_ref, resid_ref, up_ref, down_ref, bias_ref, bias_out_ref, gain_ref,
    gup_ref, gdown_ref, gbias_ref, output_ref, d_resid_ref, d_branch_ref, gain_sum_ref, branch_sum_ref,
    out, back, nt, ct, *, chunk
):
    tokens = n_ref.shape[0]
    step, last = pl.program_id(0), pl.num_programs(0) - 1

    @pl.when(step == 0)
    def _():
        out[...] = jnp.zeros_like(out)
        back[...] = jnp.zeros_like(back)
        for i in range(0, tokens, 256):
            nt[:, i : i + 256] = n_ref[i : i + 256, :].T
            ct[:, i : i + 256] = c_ref[i : i + 256, :].T

    model = n_ref.shape[1]
    up, down = (ref[...].reshape(-1, model) for ref in (up_ref, down_ref))
    gup = gdown = gbias = None
    for i in range(0, tokens, chunk):
        r = slice(i, i + chunk)
        pre = dot(n_ref[r, :], up) + bias_ref[...]
        dh = dot(c_ref[r, :], down, NT)
        sq = pre * pre
        th = jnp.tanh(pre * (GELU_A + (GELU_A * GELU_B) * sq))
        half = 0.5 + 0.5 * th
        hidden = (pre * half).astype(BF16)
        slope = half + (0.5 * pre) * (1.0 - th * th) * (GELU_A + (3.0 * GELU_A * GELU_B) * sq)
        dpre = (dh * slope).astype(BF16)
        out[r, :] += dot(hidden, down)
        back[r, :] += dot(dpre, up, NT)
        a, b = dot(nt[:, r], dpre), dot(ct[:, r], hidden)
        s = jnp.sum(dpre.astype(F32), axis=0, keepdims=True)
        gup, gdown, gbias = (a, b, s) if i == 0 else (gup + a, gdown + b, gbias + s)
    wide = gup_ref.shape[3]
    for i in range(gup_ref.shape[0]):
        for h in range(2):
            at = slice(CHUNK * i, CHUNK * (i + 1)), slice(wide * h, wide * (h + 1))
            gup_ref[i, h] = gup[at].astype(BF16)
            gdown_ref[i, h] = gdown[at].astype(BF16)
    gbias_ref[...] = gbias

    @pl.when(step == last)
    def _():
        gain_sum_ref[...] = jnp.zeros_like(gain_sum_ref)
        branch_sum_ref[...] = jnp.zeros_like(branch_sum_ref)

        @pl.loop(0, tokens // 256)
        def _(i):
            r = pl.ds(pl.multiple_of(i * 256, 256), 256)
            resid = resid_ref[r, :]
            output = (resid + (out[r, :] + bias_out_ref[...])).astype(BF16)
            output_ref[r, :] = output[:, : output_ref.shape[1]]
            d_norm, gain_sum = norm_back(resid, gain_ref[...], back[r, :])
            d_resid = c_ref[r, :].astype(F32) + d_norm
            d_resid_ref[r, :] = d_resid
            d_branch = d_resid.astype(BF16)
            d_branch_ref[r, :] = d_branch
            gain_sum_ref[...] += gain_sum
            branch_sum_ref[...] += jnp.sum(d_branch.astype(F32), axis=0, keepdims=True)


def ffn(n, c, resid, weights, bias, bias_out, gain, stored, chunk=512):
    tokens, model = n.shape
    count, _, units = bias.shape
    wide = units // 2

    def chunks(at):
        return pl.BlockSpec((None, model // CHUNK, CHUNK, model), lambda i: (i, at, 0, 0))

    def of(*shape):
        return pl.BlockSpec((None, *shape), lambda i: (i,) + (0,) * len(shape))

    grad = of(model // CHUNK, 2, CHUNK, wide)
    big, row = once((tokens, model)), full((1, model))
    grads = jax.ShapeDtypeStruct((count, model // CHUNK, 2, CHUNK, wide), BF16)
    return pl.pallas_call(
        functools.partial(ffn_kernel, chunk=chunk),
        grid=(count,),
        in_specs=[big, big, big, chunks(0), chunks(1), of(1, units), row, row],
        out_specs=[grad, grad, of(1, units), once((tokens, stored)), big, big, row, row],
        out_shape=[
            grads,
            grads,
            jax.ShapeDtypeStruct((count, 1, units), F32),
            jax.ShapeDtypeStruct((tokens, stored), BF16),
            jax.ShapeDtypeStruct((tokens, model), F32),
            jax.ShapeDtypeStruct((tokens, model), BF16),
            jax.ShapeDtypeStruct((1, model), F32),
            jax.ShapeDtypeStruct((1, model), F32),
        ],
        scratch_shapes=[pltpu.VMEM((tokens, model), F32)] * 2
        + [pltpu.VMEM((model, tokens), BF16)] * 2,
        compiler_params=params(60),
        name="ffn",
    )(n, c, resid, weights, weights, bias, bias_out, gain)


def bwd_kernel(
    n_ref, db_ref, qkv_ref, att_ref, lse_ref, even_ref, odd_ref, qh_ref, kn_ref, x_ref, d_resid_ref,
    gain_ref, small_ref, gup_ref, gdown_ref,
    grad_in_ref, grad_up_ref, grad_down_ref, grad_qkv_ref, grad_out_ref, total_ref,
    w_ref, wo_ref, da, dqkv, dk_acc, dv_acc, back, wide_x, g, core_in, y_in, x_in, z_in, ag, xag_in, sv, sv_in, sv_z,
    core_s, core_r, y_s, y_r, x_s, x_r, z_s, z_r, a_s, a_r, xa_s, xa_r, load_s, sv_s, sv_r, svz_s, svz_r,
    *, rows, pairs, group, steps
):
    t = pl.program_id(0)
    tokens = n_ref.shape[0]
    length = tokens // rows
    early = gup_ref.shape[1] + gdown_ref.shape[1]
    chunks = early + pairs // 2
    others = group // 2
    keep = CHUNK // others
    dp, tensor = lax.axis_index("dp"), lax.axis_index("tensor")
    place = (dp % group) // 2
    mine = pl.ds(pl.multiple_of(place * keep, keep), keep)
    to_core, to_y, to_x, side = neighbours()

    def place_of(o):
        return (place + o) % others

    def to_z(o):
        return (dp - dp % group + place_of(o) * 2 + side, tensor)

    late = pairs // 2

    def early_source(which, k):
        ref, at = (gup_ref, k) if k < gup_ref.shape[1] else (gdown_ref, k - gup_ref.shape[1])
        return ref.at[which, at]

    def core_copy(which, k, src):
        return remote(src, core_in.at[which, k], core_s.at[which, k], core_r.at[which, k], to_core)

    def y_copy(k):
        return remote(g.at[chunks + k], y_in.at[k], y_s.at[k], y_r.at[k], to_y)

    def x_copy(k):
        return remote(g.at[k, 1 - side], x_in.at[k], x_s.at[k], x_r.at[k], to_x)

    def z_copy(k, o):
        rows_of = pl.ds(pl.multiple_of(place_of(o) * keep, keep), keep)
        return remote(
            g.at[k, side, rows_of], z_in.at[k, o - 1], z_s.at[k, o - 1], z_r.at[k, o - 1], to_z(o)
        )

    def a_copy(k, o):
        return remote(ag.at[k, mine], ag.at[k, mine], a_s.at[k, o - 1], a_r.at[k, o - 1], to_z(o))

    def a_wait(k, o):
        rows_of = pl.ds(pl.multiple_of(place_of(others - o) * keep, keep), keep)
        part = ag.at[k, rows_of]
        remote(part, part, a_s.at[k, o - 1], a_r.at[k, o - 1], to_z(o)).wait_recv()

    def xa_copy(k):
        return remote(ag.at[k], xag_in.at[k], xa_s.at[k], xa_r.at[k], to_x)

    def load(which, k):
        return pltpu.make_async_copy(
            early_source(2 * which, k), g.at[which * chunks + k], load_s.at[which, k]
        )

    def load_wait(which, k):
        pltpu.make_async_copy(
            gup_ref.at[0, 0], g.at[which * chunks + k], load_s.at[which, k]
        ).wait()

    def stage(lag):
        def run(body):
            k = t - lag

            @pl.when((k >= 0) & (k < chunks))
            def _():
                body(k)

        return run

    def send_y():
        @stage(0)
        def _(k):
            core_copy(0, k, g.at[0]).wait_recv()

            @pl.when(k < early)
            def _():
                load_wait(1, k)

            g[chunks + k] = (g[chunks + k].astype(F32) + core_in[0, k].astype(F32)).astype(BF16)
            y_copy(k).start()

    def send_x():
        @stage(1)
        def _(k):
            core_copy(1, k, g.at[0]).wait_recv()

            @pl.when(k < early)
            def _():
                load_wait(0, k)

            y_copy(k).wait_recv()
            g[k] = (
                g[k].astype(F32) + core_in[1, k].astype(F32) + y_in[k].astype(F32)
            ).astype(BF16)
            x_copy(k).start()

    def send_z():
        @stage(2)
        def _(k):
            x_copy(k).wait_recv()
            g[k, side] = (g[k, side].astype(F32) + x_in[k].astype(F32)).astype(BF16)
            for o in range(1, others):
                z_copy(k, o).start()

    def send_back():
        @stage(2)
        def _(k):
            total = g[k, side, mine].astype(F32)
            for o in range(1, others):
                z_copy(k, o).wait_recv()
                total += z_in[k, o - 1].astype(F32)
            ag[k, mine] = total.astype(BF16)
            for o in range(1, others):
                a_copy(k, o).start()

    def send_back_x():
        @stage(3)
        def _(k):
            for o in range(1, others):
                a_wait(k, o)
            xa_copy(k).start()

    def finish():
        @stage(3)
        def _(k):
            xa_copy(k).wait_recv()
            kept, got = ag[k].astype(F32), xag_in[k].astype(F32)
            halves = jnp.where(side == 0, kept, got), jnp.where(side == 0, got, kept)
            n_up = gup_ref.shape[1]
            wide = kept.shape[1]
            for c in range(chunks):

                @pl.when(k == c)
                def _(c=c):
                    i = c if c < n_up else c - n_up if c < early else c - early
                    for h, value in enumerate(halves):
                        cols = slice(h * wide, (h + 1) * wide)
                        if c < n_up:
                            end = min(CHUNK * (i + 1), grad_up_ref.shape[0])
                            grad_up_ref[CHUNK * i : end, cols] = value[: end - CHUNK * i]
                        elif c < early:
                            end = min(CHUNK * (i + 1), grad_down_ref.shape[1])
                            grad_down_ref[cols, CHUNK * i : end] = value.T[:, : end - CHUNK * i]
                        else:
                            end = min((h + 1) * wide, grad_out_ref.shape[1])
                            head = slice(HEAD_DIM * i, HEAD_DIM * (i + 1))
                            turned = value.T
                            for j in range(3):
                                part = turned[: end - h * wide, HEAD_DIM * j : HEAD_DIM * (j + 1)]
                                grad_qkv_ref[j, h * wide : end, head] = part
                            grad_out_ref[head, h * wide : end] = value[
                                3 * HEAD_DIM :, : end - h * wide
                            ]

    def sv_copy(i, src, device):
        return remote(src, sv_in.at[i], sv_s.at[i], sv_r.at[i], device)

    def svz_copy(o):
        return remote(sv_z.at[place], sv_z.at[place], svz_s.at[o - 1], svz_r.at[o - 1], to_z(o))

    def small_sums():
        @pl.when(t == pairs + 1)
        def _():
            for i in (0, 1):
                sv_copy(i, sv.at[3 - 2 * i], to_core).wait_recv()
            sv[2] += sv_in[0]
            sv_copy(2, sv.at[2], to_y).start()

        @pl.when(t == pairs + 2)
        def _():
            sv_copy(2, sv.at[2], to_y).wait_recv()
            sv[0] = (sv[0] + sv_in[1]) + sv_in[2]
            sv_copy(3, sv.at[0], to_x).start()

        @pl.when(t == pairs + 3)
        def _():
            sv_copy(3, sv.at[0], to_x).wait_recv()
            sv_z[place] = sv[0] + sv_in[3]
            for o in range(1, others):
                svz_copy(o).start()

        @pl.when(t == pairs + 4)
        def _():
            for o in range(1, others):
                part = sv_z.at[place_of(others - o)]
                remote(part, part, svz_s.at[o - 1], svz_r.at[o - 1], to_z(o)).wait_recv()
            total = sv_z[0]
            for i in range(1, others):
                total += sv_z[i]
            total_ref[...] = total

    def norm_one():
        gain_sum = jnp.zeros((1, n_ref.shape[1]), F32)
        for i in range(0, tokens, CHUNK):
            r = slice(i, i + CHUNK)
            d_norm, part = norm_back(widen(x_ref.at[r, :], wide_x), gain_ref[...], back[r, :])
            grad = (d_resid_ref[r, :] + d_norm).astype(BF16)
            grad_in_ref[r, :] = grad[:, : grad_in_ref.shape[1]]
            gain_sum += part
        for i in range(4):
            sv[i, 4:5, :] = gain_sum
        for i in (0, 1):
            sv_copy(i, sv.at[3 - 2 * i], to_core).start()

    first = lax.broadcasted_iota(jnp.int32, (1, LANES), 1) < HEAD_DIM
    zero = jnp.zeros((), BF16)
    q_ref, k_ref, v_ref = (qkv_ref.at[:, j * LANES : (j + 1) * LANES] for j in range(3))
    computing = t < pairs

    def attend(row, at, span):
        dq = None
        for h in range(2):
            sel = first if h == 0 else ~first
            s, q = scores_of(q_ref, k_ref, qh_ref, kn_ref, sel, at, span)
            qm = jnp.where(sel, q, zero)
            km = jnp.where(sel, k_ref[span, :], zero)
            dom = jnp.where(sel, da[at, :], zero)
            p = jnp.exp(s - lse_ref[h : h + 1, at])
            dp_ = dot(v_ref[span, :], dom, NT)
            u = p * dp_
            inner = jnp.sum(u, axis=0, keepdims=True)
            ds = (u - p * inner).astype(BF16)
            dv_acc[span, :] += dot(p.astype(BF16), dom)
            dk_acc[span, :] += dot(ds, qm)
            part = dot(ds, km, TN)
            dq = part if dq is None else dq + part
        dqkv[at, :LANES] = (dq * 0.125).astype(BF16)

    @pl.when(t == 0)
    def _():
        greet([to_core, to_y, to_x] + [to_z(o) for o in range(1, others)])
        for k in range(early):
            core_copy(0, k, early_source(3, k)).start()
            load(1, k).start()
        for k in range(early):
            core_copy(1, k, early_source(1, k)).start()
            load(0, k).start()
        sv[...] = small_ref[...]

    @pl.when(computing)
    def _():
        pair_weights(even_ref, odd_ref, w_ref, wo_ref)
        da[...] = dot(db_ref[...], wo_ref[...], NT).astype(BF16)
        dk_acc[...] = jnp.zeros_like(dk_acc)
        dv_acc[...] = jnp.zeros_like(dv_acc)

    events = [[send_z, send_y], [send_back_x], [send_x], [send_back], [finish]]
    for event in events.pop(0):
        event()
    for row in range(rows):
        for at, span in spans(length, row):
            pl.when(computing)(functools.partial(attend, row, at, span))
            for event in events.pop(0) if events else ():
                event()
    for left in events:
        for event in left:
            event()
    small_sums()
    pl.when(t == pairs)(norm_one)

    @pl.when(computing)
    def _():
        dqkv[:, LANES : 2 * LANES] = dk_acc[...].astype(BF16)
        dqkv[:, 2 * LANES :] = dv_acc[...].astype(BF16)
        sums = jnp.sum(dqkv[...].astype(F32), axis=0, keepdims=True)
        grown = dot(dqkv[...], w_ref[...])

        @pl.when(t == 0)
        def _():
            back[...] = grown

        @pl.when(t > 0)
        def _():
            back[...] += grown

        grads = dot(dqkv[...], n_ref[...], TN).astype(BF16)
        grads_out = dot(att_ref[...], db_ref[...], TN).astype(BF16)
        wide = grads.shape[1] // 2
        for h in range(2):
            unit = 2 * (pairs - 1 - t) + h
            quarter, j = unit // late, unit % late
            odd, half = quarter % 2, quarter // 2
            for line in range(late):

                @pl.when(j == line)
                def _(line=8 + line, h=h):
                    for i in (0, 2):
                        part = sums[:, LANES * i + HEAD_DIM * h : LANES * i + HEAD_DIM * (h + 1)]
                        sv[quarter, line : line + 1, LANES * i : LANES * i + HEAD_DIM] = part

            base = (1 - odd) * (half * chunks + early) + odd * (2 * chunks + late * half) + j
            for side_ in range(2):
                cols = slice(side_ * wide, (side_ + 1) * wide)
                for i in range(3):
                    lines = slice(LANES * i + HEAD_DIM * h, LANES * i + HEAD_DIM * (h + 1))
                    g[base, side_, HEAD_DIM * i : HEAD_DIM * (i + 1), :] = grads[lines, cols]
                g[base, side_, 3 * HEAD_DIM :, :] = grads_out[
                    HEAD_DIM * h : HEAD_DIM * (h + 1), cols
                ]

            @pl.when(odd == 1)
            def _():
                core_copy(1 - half, early + j, g.at[base]).start()

    @pl.when(t == steps - 1)
    def _():
        @pl.loop(0, chunks)
        def _(k):
            for which in range(2):
                core_copy(which, k, g.at[0]).wait_send()
            y_copy(k).wait_send()
            x_copy(k).wait_send()
            for o in range(1, others):
                z_copy(k, o).wait_send()
                a_copy(k, o).wait_send()
            xa_copy(k).wait_send()

        for i, device in enumerate((to_core, to_core, to_y, to_x)):
            sv_copy(i, sv.at[0], device).wait_send()
        for o in range(1, others):
            svz_copy(o).wait_send()


def attn_bwd(
    n, db, qkv, att, lse, weights, qh, kn, x, d_resid, gain, small, gup, gdown, rows, group
):
    tokens, model = n.shape
    stored = x.shape[1]
    pairs = qkv.shape[0]
    early, late = gup.shape[1] + gdown.shape[1], pairs // 2
    chunks = early + late
    steps = max(pairs + 5, chunks + 3)
    others = group // 2
    wide = model // 2
    lines = small.shape[1]

    def of(shape):
        return pl.BlockSpec((None, *shape), lambda p: (jnp.maximum(pairs - 1 - p, 0), 0, 0))

    def unit(h):
        def at(p):
            u = 2 * jnp.maximum(pairs - 1 - p, 0) + h
            return u // late, u % late, 0, 0

        return pl.BlockSpec((None, None, CHUNK, model), at)

    anywhere = pl.BlockSpec(memory_space=pl.ANY)
    sems = pltpu.SemaphoreType.DMA
    between = max(others - 1, 1)
    many = (chunks, between)
    outs = [
        ((tokens, stored), BF16),
        ((stored, 2 * wide), F32),
        ((2 * wide, stored), F32),
        ((3, stored, late * HEAD_DIM), F32),
        ((late * HEAD_DIM, stored), F32),
        ((lines, model), F32),
    ]
    return pl.pallas_call(
        functools.partial(bwd_kernel, rows=rows, pairs=pairs, group=group, steps=steps),
        grid=(steps,),
        in_specs=[
            once((tokens, model)), once((tokens, model)), of((tokens, 3 * LANES)),
            of((tokens, LANES)), of((2, tokens)), unit(0), unit(1),
            once((tokens, LANES)), once((tokens, LANES)), once((tokens, stored)),
            once((tokens, model)), full((1, model)), full(small.shape), anywhere, anywhere,
        ],
        out_specs=[once(shape) for shape, _ in outs],
        out_shape=[jax.ShapeDtypeStruct(*o) for o in outs],
        scratch_shapes=[
            pltpu.VMEM((3 * LANES, model), BF16),
            pltpu.VMEM((LANES, model), BF16),
            pltpu.VMEM((tokens, LANES), BF16),
            pltpu.VMEM((tokens, 3 * LANES), BF16),
            pltpu.VMEM((tokens, LANES), F32),
            pltpu.VMEM((tokens, LANES), F32),
            pltpu.VMEM((tokens, model), F32),
            pltpu.VMEM((CHUNK, model), F32),
            pltpu.VMEM((2 * chunks + 2 * late, 2, CHUNK, wide), BF16),
            pltpu.VMEM((2, chunks, 2, CHUNK, wide), BF16),
            pltpu.VMEM((chunks, 2, CHUNK, wide), BF16),
            pltpu.VMEM((chunks, CHUNK, wide), BF16),
            pltpu.VMEM((*many, CHUNK // others, wide), BF16),
            pltpu.VMEM((chunks, CHUNK, wide), BF16),
            pltpu.VMEM((chunks, CHUNK, wide), BF16),
            pltpu.VMEM((4, lines, model), F32),
            pltpu.VMEM((4, lines, model), F32),
            pltpu.VMEM((others, lines, model), F32),
            sems((2, chunks)), sems((2, chunks)), sems((chunks,)), sems((chunks,)),
            sems((chunks,)), sems((chunks,)), sems(many), sems(many), sems(many), sems(many),
            sems((chunks,)), sems((chunks,)), sems((2, early)), sems((4,)), sems((4,)),
            sems((between,)), sems((between,)),
        ],
        compiler_params=params(62, collective_id=0, has_side_effects=True),
        name="attn_bwd",
    )(n, db, qkv, att, lse, weights, weights, qh, kn, x, d_resid, gain, small, gup, gdown)


def solution(mesh):
    n_dp, n_tensor = mesh.shape["dp"], mesh.shape["tensor"]
    assert n_tensor == 4 and n_dp % 2 == 0 and n_dp & (n_dp - 1) == 0
    bits = [1 << i for i in range(n_dp.bit_length() - 1)]
    group = min(n_dp, 8)

    def to_dp(v, bit):
        return lax.ppermute(v, "dp", [(i, i ^ bit) for i in range(n_dp)])

    def local(
        layer_input, segments, cotangent, gain_one, w_qkv, b_qv, w_out, b_out, gain_two,
        w_up, b_up, w_down, b_down,
    ):
        rows = segments.shape[0]
        tokens, stored = layer_input.shape
        model = stored + 1
        heads = w_qkv.shape[2] // HEAD_DIM
        units = w_up.shape[1]

        def pad(v, size=model):
            return jnp.pad(v, [(0, 0)] * (v.ndim - 1) + [(0, size - v.shape[-1])])

        def line(v):
            return pad(v.astype(F32))[None]

        bias = b_qv.astype(F32).reshape(2, heads, HEAD_DIM)
        zeros = jnp.zeros((heads, HEAD_DIM), F32)
        places = [
            jnp.concatenate([bias[0], zeros, zeros, zeros, bias[1], zeros], axis=1),
            jnp.concatenate([zeros, bias[0], zeros, zeros, zeros, bias[1]], axis=1),
        ]
        misc = jnp.concatenate(
            [jnp.stack(places, axis=1), b_up.astype(F32).reshape(1, 2, units // 2)]
        )
        misc = jnp.broadcast_to(misc[:, :, None], (heads + 1, 2, 8, units // 2))

        gain_one_f, gain_two_f = line(gain_one), line(gain_two)
        lane = jnp.arange(LANES) % HEAD_DIM
        hot = segments.reshape(-1, 1) == lane[None, :]
        qh = jnp.where(hot, 1.0, 0.0).astype(BF16)
        kn = jnp.where(hot | (lane >= 8)[None, :], 0.0, MASKED_SCORE).astype(BF16)
        (
            n_one, cot, grad_bdown, qkv, att, lse, resid, n_two, w_attn, w_ffn, misc
        ) = forward(
            layer_input, cotangent, w_qkv.transpose(0, 2, 1), w_out, w_up, w_down, misc, gain_one_f,
            gain_two_f, line(b_out), qh, kn, rows,
        )
        bias_up = misc[:, heads, :, 0].reshape(4, 1, units)
        (
            g_up, g_down, g_bias, output, d_resid, d_branch, grad_gain_two, grad_bout
        ) = ffn(n_two, cot, resid, w_ffn, bias_up, line(b_down), gain_two_f, stored)

        common = jnp.concatenate([grad_bdown, grad_bout, grad_gain_two], axis=0)[None]
        small = jnp.concatenate(
            [g_bias, jnp.broadcast_to(common, (4, 3, model)), jnp.zeros((4, 12, model), F32)], axis=1
        )
        input_grad, grad_up, grad_down, grad_qkv, grad_out, small = attn_bwd(
            n_one, d_branch, qkv, att, lse, w_attn, qh, kn, layer_input, d_resid, gain_one_f, small,
            g_up, g_down, rows, group,
        )
        sums = (grad_up, grad_down, grad_qkv, grad_out, small)
        for bit in bits:
            if bit >= group:
                sums = tuple(v + to_dp(v, bit) for v in sums)
        grad_up, grad_down, grad_qkv, grad_out, small = sums
        per_head = small[8 : 8 + heads]
        grad_bqv = jnp.stack(
            [per_head[:, :HEAD_DIM].reshape(-1), per_head[:, 2 * LANES : 2 * LANES + HEAD_DIM].reshape(-1)]
        )
        return (
            output,
            input_grad,
            small[4, :stored],
            grad_qkv,
            grad_bqv,
            grad_out,
            small[2, :stored],
            small[3, :stored],
            grad_up,
            small[0],
            grad_down,
            small[1, :stored],
        )

    return jax.shard_map(
        local,
        mesh=mesh,
        in_specs=(
            P(("dp", "tensor"), None),
            P(("dp", "tensor"), None),
            P(("dp", "tensor"), None),
            P(),
            P(None, None, "tensor"),
            P(None, "tensor"),
            P("tensor", None),
            P(),
            P(),
            P(None, "tensor"),
            P("tensor"),
            P("tensor", None),
            P(),
        ),
        out_specs=(
            P(("dp", "tensor"), None),
            P(("dp", "tensor"), None),
            P(),
            P(None, None, "tensor"),
            P(None, "tensor"),
            P("tensor", None),
            P(),
            P(),
            P(None, "tensor"),
            P("tensor"),
            P("tensor", None),
            P(),
        ),
        check_vma=False,
    )
```

```python
import functools

import jax
import jax.numpy as jnp
from jax import lax
from jax.experimental import pallas as pl
from jax.experimental.pallas import tpu as pltpu
from jax.sharding import PartitionSpec as P

HEAD_DIM = 64
LANES = 128
EPSILON = 1e-05
MASKED_SCORE = -1e30
LONGEST = 512
BLOCK = 256
CHUNK = 256
F32 = jnp.float32
BF16 = jnp.bfloat16
NN = (((1,), (0,)), ((), ()))
NT = (((1,), (1,)), ((), ()))
TN = (((0,), (0,)), ((), ()))
GELU_A = 0.7978845608028654
GELU_B = 0.044715
MIB = 1024 * 1024
MESH = pl.DeviceIdType.MESH


def dot(a, b, dims=NN):
    return lax.dot_general(a, b, dims, preferred_element_type=F32)


def params(mib, **more):
    return pltpu.CompilerParams(vmem_limit_bytes=mib * MIB, **more)


def full(shape):
    return pl.BlockSpec(shape, lambda *_: (0,) * len(shape))


def once(shape):
    return pl.BlockSpec(shape, lambda *_: (0,) * len(shape), pipeline_mode=pl.Buffered(1))


def widen(ref, wide):
    wide[:, wide.shape[1] - LANES :] = jnp.zeros((wide.shape[0], LANES), F32)
    wide[:, : ref.shape[1]] = ref[...].astype(F32)
    return wide[...]


def norm_scale(values):
    total = jnp.sum(values, axis=-1, keepdims=True)
    square = jnp.sum(values * values, axis=-1, keepdims=True)
    return lax.rsqrt((square + total * total) / values.shape[-1] + EPSILON), total


def norm_back(values, gain, upstream):
    scale, total = norm_scale(values)
    weighted = upstream * values
    spread = jnp.sum(weighted * gain, axis=-1, keepdims=True)
    grad = upstream * gain * scale - (spread * scale * scale * scale / values.shape[-1]) * (
        values + total
    )
    return grad, jnp.sum(weighted * scale, axis=0, keepdims=True)


def scores_of(q_ref, k_ref, qh_ref, kn_ref, sel, at, span):
    q = q_ref[at, :] * 0.125
    qa = jnp.where(sel, q, qh_ref[at, :])
    ka = jnp.where(sel, k_ref[span, :], kn_ref[span, :])
    s = dot(ka, qa, NT)
    causal = lax.broadcasted_iota(jnp.int32, (BLOCK, BLOCK), 0) <= lax.broadcasted_iota(
        jnp.int32, (BLOCK, BLOCK), 1
    )
    early = s.shape[0] - BLOCK
    tail = jnp.where(causal, s[early:, :], MASKED_SCORE)
    return (tail if early == 0 else jnp.concatenate([s[:early, :], tail], axis=0)), q


def spans(length, row):
    for end in range(BLOCK, length + 1, BLOCK):
        start = max(0, end - BLOCK - LONGEST)
        base = row * length
        yield slice(base + end - BLOCK, base + end), slice(base + start, base + end)


def remote(src, dst, send, recv, device):
    return pltpu.make_async_remote_copy(
        src_ref=src, dst_ref=dst, send_sem=send, recv_sem=recv, device_id=device,
        device_id_type=MESH,
    )


def greet(partners):
    barrier = pltpu.get_barrier_semaphore()
    for device in partners:
        pl.semaphore_signal(barrier, inc=1, device_id=device, device_id_type=MESH)
    pl.semaphore_wait(barrier, len(partners))


def neighbours():
    dp, tensor = lax.axis_index("dp"), lax.axis_index("tensor")
    side = dp % 2
    to_core = (dp, tensor + 1 - 2 * (tensor % 2))
    return to_core, (dp, (tensor + 2) % 4), (dp + 1 - 2 * side, tensor), side


def pair_weights(even, odd, w, wo):
    for h, unit in enumerate((even, odd)):
        for i in range(3):
            at = LANES * i + HEAD_DIM * h
            w[at : at + HEAD_DIM, :] = unit[HEAD_DIM * i : HEAD_DIM * (i + 1), :]
        wo[HEAD_DIM * h : HEAD_DIM * (h + 1), :] = unit[3 * HEAD_DIM :, :]


def fwd_kernel(
    x_ref, c_ref, wqkv_ref, wout_ref, up_ref, down_ref, misc_ref, gain_one_ref, gain_two_ref,
    bias_out_ref, qh_ref, kn_ref,
    n_ref, cot_ref, c_sum_ref, qkv_ref, att_ref, lse_ref, resid_ref, n_two_ref, wa_ref, wf_ref, misc_all_ref,
    wa, stage, misc, w, wo, branch, wide,
    core_s, core_r, y_s, y_r, x_s, x_r, d_s, d_r, local_s,
    *, rows, pairs
):
    t = pl.program_id(0)
    tokens = x_ref.shape[0]
    length = tokens // rows
    heads = pairs // 2
    stored = x_ref.shape[1]
    model = stored + 1
    early, tail = heads, stage.shape[0]
    to_core, to_y, to_x, side = neighbours()
    half = pl.ds(pl.multiple_of(side * (CHUNK // 2), CHUNK // 2), CHUNK // 2)
    other = pl.ds(pl.multiple_of((1 - side) * (CHUNK // 2), CHUNK // 2), CHUNK // 2)
    last = early + tail

    def held(quarter, k):
        if k == last:
            return misc.at[quarter]
        if k < early:
            return wa.at[quarter, k]
        return wf_ref.at[quarter, k - early]

    def own(k):
        return held(0, k) if k < early or k == last else stage.at[k - early]

    def part(ref, k):
        return ref if k == last else ref.at[half]

    def core_copy(k):
        return remote(own(k), held(1, k), core_s.at[k], core_r.at[k], to_core)

    def y_copy(k):
        return remote(part(own(k), k), part(held(2, k), k), y_s.at[k], y_r.at[k], to_y)

    def x_copy(k):
        ref = held(2, k).at[half]
        return remote(ref, ref, x_s.at[k], x_r.at[k], to_x)

    def d_copy(k):
        return remote(held(2, k), held(3, k), d_s.at[k], d_r.at[k], to_core)

    def keep_copy(k):
        if k == last:
            return pltpu.make_async_copy(misc, misc_all_ref, local_s.at[k])
        if k < early:
            return pltpu.make_async_copy(wa.at[:, k], wa_ref.at[:, k], local_s.at[k])
        return pltpu.make_async_copy(stage.at[k - early], wf_ref.at[0, k - early], local_s.at[k])

    def x_on(k):
        y_copy(k).wait_recv()
        x_copy(k).start()

    def d_on(k):
        if k == last:
            y_copy(k).wait_recv()
        else:
            ref = held(2, k).at[other]
            remote(ref, ref, x_s.at[k], x_r.at[k], to_x).wait_recv()
        d_copy(k).start()

    def start_y(k):
        y_copy(k).start()

    @pl.when(t == 0)
    def _():
        edge = slice(model - LANES, model)
        wa[0, :, :, edge] = jnp.zeros((early, CHUNK, LANES), BF16)
        for j in range(heads):
            head = slice(HEAD_DIM * j, HEAD_DIM * (j + 1))
            for i in range(3):
                wa[0, j, HEAD_DIM * i : HEAD_DIM * (i + 1), :stored] = wqkv_ref[i, head, :]
            wa[0, j, 3 * HEAD_DIM :, :stored] = wout_ref[head, :]
        misc[0] = misc_ref[...]
        greet([to_core, to_y, to_x])
        for k in (last, *range(early)):
            core_copy(k).start()
            y_copy(k).start()
        count = tail // 2
        stage[:, :, edge] = jnp.zeros((tail, CHUNK, LANES), BF16)
        stage[count - 1, CHUNK - 16 :, :] = jnp.zeros((16, model), BF16)
        for i in range(count):
            end = min(CHUNK * (i + 1), stored)
            stage[i, : end - CHUNK * i, :] = up_ref[CHUNK * i : end, :]
            stage[count + i, :, :stored] = down_ref[CHUNK * i : CHUNK * (i + 1), :]
        for k in range(early, last):
            core_copy(k).start()
            keep_copy(k).start()
        branch[...] = jnp.zeros_like(branch)
        c_sum = jnp.zeros((1, model), F32)
        for i in range(0, tokens, CHUNK):
            r = slice(i, i + CHUNK)
            x = widen(x_ref.at[r, :], wide)
            n_ref[r, :] = (x * norm_scale(x)[0] * gain_one_ref[...]).astype(BF16)
            c = widen(c_ref.at[r, :], wide)
            cot_ref[r, :] = c.astype(BF16)
            c_sum += jnp.sum(c, axis=0, keepdims=True)
        c_sum_ref[...] = c_sum
        core_copy(last).wait_recv()

    events = {
        (0, 2): [(start_y, early)], (0, 4): [(d_on, last)],
        (1, 1): [(x_on, 0)], (1, 3): [(start_y, early + 1)],
        (2, 1): [(x_on, 1)], (2, 2): [(start_y, early + 2)], (2, 3): [(d_on, 0)],
        (2, 4): [(d_on, 1)],
        (3, 0): [(x_on, 2)], (3, 2): [(start_y, early + 3)],
        (3, 4): [(d_on, 2)],
        (4, 1): [(x_on, early)], (4, 2): [(start_y, early + 4)],
        (5, 0): [(x_on, early + 1), (d_on, early)], (5, 1): [(start_y, early + 5)],
        (5, 3): [(x_on, early + 2), (d_on, early + 1)],
    }

    def run(slot):
        for (step, at), todo in events.items():
            if at == slot and todo:

                @pl.when(t == step)
                def _(todo=todo):
                    for event, k in todo:
                        event(k)

    for step in range(pairs):
        needed = {divmod(2 * step + h, heads) for h in range(2)}
        seen = {divmod(u, heads) for u in range(2 * step)}

        @pl.when(t == step)
        def _(needed=needed, seen=seen):
            for quarter, j in sorted(needed - seen):
                if quarter == 1:
                    core_copy(j).wait_recv()
                if quarter == 3:
                    d_copy(j).wait_recv()
            if any(quarter == 3 for quarter, _ in needed) and not any(q == 3 for q, _ in seen):
                d_copy(last).wait_recv()

    first = lax.broadcasted_iota(jnp.int32, (1, LANES), 1) < HEAD_DIM
    units = 2 * t, 2 * t + 1
    pair_weights(*(wa.at[u // heads, u % heads] for u in units), w, wo)
    bias = sum(misc[u // heads, u % heads, h, :1, :] for h, u in enumerate(units))
    qkv_ref[...] = (dot(n_ref[...], w[...], NT) + bias).astype(BF16)
    q_ref, k_ref, v_ref = (qkv_ref.at[:, j * LANES : (j + 1) * LANES] for j in range(3))
    run(0)
    slot = 1
    for row in range(rows):
        for at, span in spans(length, row):
            parts = []
            for h in range(2):
                sel = first if h == 0 else ~first
                s, _ = scores_of(q_ref, k_ref, qh_ref, kn_ref, sel, at, span)
                m = jnp.max(s, axis=0, keepdims=True)
                p = jnp.exp(s - m)
                total = jnp.sum(p, axis=0, keepdims=True)
                weights = (p * (1.0 / total)).astype(BF16)
                parts.append(dot(weights, v_ref[span, :], TN))
                lse_ref[h : h + 1, at] = m + jnp.log(total)
            att_ref[at, :] = jnp.where(first, parts[0], parts[1]).astype(BF16)
            if slot < 4:
                run(slot)
                slot += 1
    branch[...] += dot(att_ref[...], wo[...])
    run(4)

    @pl.when(t == pairs - 1)
    def _():
        for i in range(0, tokens, CHUNK):
            r = slice(i, i + CHUNK)
            resid = widen(x_ref.at[r, :], wide) + (branch[r, :] + bias_out_ref[...])
            resid_ref[r, :] = resid
            n_two_ref[r, :] = (resid * norm_scale(resid)[0] * gain_two_ref[...]).astype(BF16)
        for k in range(early + 3, last):
            x_on(k)
        for k in range(early + 2, last):
            d_on(k)
        for k in (*range(early), last):
            keep_copy(k).start()
        for k in range(early, last):
            core_copy(k).wait_recv()
            d_copy(k).wait_recv()
        for k in range(last + 1):
            core_copy(k).wait_send()
            y_copy(k).wait_send()
            if k < last:
                x_copy(k).wait_send()
            d_copy(k).wait_send()
            keep_copy(k).wait()


def forward(x, c, wqkv, wout, up, down, misc, gain_one, gain_two, bias_out, qh, kn, rows):
    tokens, stored = x.shape
    model = stored + 1
    heads = wqkv.shape[1] // HEAD_DIM
    pairs = 2 * heads
    tail = 2 * (model // CHUNK)

    def of(*shape):
        return pl.BlockSpec((None, *shape), lambda p: (p,) + (0,) * len(shape))

    anywhere = pl.BlockSpec(memory_space=pl.ANY)
    sems = pltpu.SemaphoreType.DMA((heads + tail + 1,))
    inputs = [x, c, wqkv, wout, up, down, misc, gain_one, gain_two, bias_out, qh, kn]
    big = once((tokens, model))
    outs = [
        (big, (tokens, model), BF16),
        (big, (tokens, model), BF16),
        (once((1, model)), (1, model), F32),
        (of(tokens, 3 * LANES), (pairs, tokens, 3 * LANES), BF16),
        (of(tokens, LANES), (pairs, tokens, LANES), BF16),
        (of(2, tokens), (pairs, 2, tokens), F32),
        (big, (tokens, model), F32),
        (big, (tokens, model), BF16),
        (anywhere, (4, heads, CHUNK, model), BF16),
        (anywhere, (4, tail, CHUNK, model), BF16),
        (anywhere, (4, *misc.shape), F32),
    ]
    return pl.pallas_call(
        functools.partial(fwd_kernel, rows=rows, pairs=pairs),
        grid=(pairs,),
        in_specs=[once(v.shape) for v in inputs],
        out_specs=[spec for spec, _, _ in outs],
        out_shape=[jax.ShapeDtypeStruct(shape, dtype) for _, shape, dtype in outs],
        scratch_shapes=[
            pltpu.VMEM((4, heads, CHUNK, model), BF16),
            pltpu.VMEM((tail, CHUNK, model), BF16),
            pltpu.VMEM((4, *misc.shape), F32),
            pltpu.VMEM((3 * LANES, model), BF16),
            pltpu.VMEM((LANES, model), BF16),
            pltpu.VMEM((tokens, model), F32),
            pltpu.VMEM((CHUNK, model), F32),
        ]
        + [sems] * 9,
        compiler_params=params(60, collective_id=1, has_side_effects=True),
        name="forward",
    )(*inputs)


def ffn_kernel(
    n_ref, c_ref, resid_ref, up_ref, down_ref, bias_ref, bias_out_ref, gain_ref,
    sum_y_ref, sum_own_ref, got_ref, gbias_ref, output_ref, d_resid_ref, d_branch_ref,
    gain_sum_ref, branch_sum_ref,
    out, back, nt, ct, g, core_in, core_s, core_r, y_s, y_r, out_s, *, chunk
):
    tokens = n_ref.shape[0]
    step, last = pl.program_id(0), pl.num_programs(0) - 1
    to_core, to_y, _, _ = neighbours()
    chunks, sent = core_in.shape[1], got_ref.shape[0]

    def core_copy(which, k):
        return remote(
            g.at[0, k], core_in.at[which, k], core_s.at[which, k], core_r.at[which, k], to_core
        )

    def y_copy(k):
        return remote(g.at[1, k], got_ref.at[k], y_s.at[k], y_r.at[k], to_y)

    def out_copy(which, k):
        dst = sum_own_ref if which else sum_y_ref
        return pltpu.make_async_copy(g.at[1 + which, k], dst.at[k], out_s.at[which, k])

    @pl.when(step == 0)
    def _():
        greet([to_core, to_y])
        out[...] = jnp.zeros_like(out)
        back[...] = jnp.zeros_like(back)
        for i in range(0, tokens, 256):
            nt[:, i : i + 256] = n_ref[i : i + 256, :].T
            ct[:, i : i + 256] = c_ref[i : i + 256, :].T

    model = n_ref.shape[1]
    up, down = (ref[...].reshape(-1, model) for ref in (up_ref, down_ref))
    gup = gdown = gbias = None
    for i in range(0, tokens, chunk):
        r = slice(i, i + chunk)
        pre = dot(n_ref[r, :], up) + bias_ref[...]
        dh = dot(c_ref[r, :], down, NT)
        sq = pre * pre
        th = jnp.tanh(pre * (GELU_A + (GELU_A * GELU_B) * sq))
        half = 0.5 + 0.5 * th
        hidden = (pre * half).astype(BF16)
        slope = half + (0.5 * pre) * (1.0 - th * th) * (GELU_A + (3.0 * GELU_A * GELU_B) * sq)
        dpre = (dh * slope).astype(BF16)
        out[r, :] += dot(hidden, down)
        back[r, :] += dot(dpre, up, NT)
        a, b = dot(nt[:, r], dpre), dot(ct[:, r], hidden)
        s = jnp.sum(dpre.astype(F32), axis=0, keepdims=True)
        gup, gdown, gbias = (a, b, s) if i == 0 else (gup + a, gdown + b, gbias + s)
    gbias_ref[...] = gbias

    @pl.when(step == 2)
    def _():
        for k in range(chunks):
            core_copy(0, k).wait_send()

    wide = g.shape[4]
    place = step % 2 * (1 + step // 2)
    for m, grad in enumerate((gup, gdown)):
        for i in range(chunks // 2):
            for h in range(2):
                at = slice(CHUNK * i, CHUNK * (i + 1)), slice(wide * h, wide * (h + 1))
                g[place, m * (chunks // 2) + i, h] = grad[at].astype(BF16)

    for which in range(2):

        @pl.when(step == 2 * which)
        def _(which=which):
            for k in range(chunks):
                core_copy(which, k).start()

        @pl.when(step == 2 * which + 1)
        def _(which=which):
            for k in range(chunks):
                core_copy(which, k).wait_recv()
                g[1 + which, k] = (
                    g[1 + which, k].astype(F32) + core_in[which, k].astype(F32)
                ).astype(BF16)
                if which == 0 and k < sent:
                    y_copy(k).start()
                else:
                    out_copy(which, k).start()

    @pl.when(step == last)
    def _():
        gain_sum_ref[...] = jnp.zeros_like(gain_sum_ref)
        branch_sum_ref[...] = jnp.zeros_like(branch_sum_ref)

        @pl.loop(0, tokens // 256)
        def _(i):
            r = pl.ds(pl.multiple_of(i * 256, 256), 256)
            resid = resid_ref[r, :]
            output = (resid + (out[r, :] + bias_out_ref[...])).astype(BF16)
            output_ref[r, :] = output[:, : output_ref.shape[1]]
            d_norm, gain_sum = norm_back(resid, gain_ref[...], back[r, :])
            d_resid = c_ref[r, :].astype(F32) + d_norm
            d_resid_ref[r, :] = d_resid
            d_branch = d_resid.astype(BF16)
            d_branch_ref[r, :] = d_branch
            gain_sum_ref[...] += gain_sum
            branch_sum_ref[...] += jnp.sum(d_branch.astype(F32), axis=0, keepdims=True)

        for k in range(chunks):
            core_copy(1, k).wait_send()
            out_copy(1, k).wait()
            if k < sent:
                y_copy(k).wait()
            else:
                out_copy(0, k).wait()


def ffn(n, c, resid, weights, bias, bias_out, gain, stored, sent, chunk=512):
    tokens, model = n.shape
    count, _, units = bias.shape
    wide = units // 2
    each = model // CHUNK

    def chunks(at):
        return pl.BlockSpec((None, each, CHUNK, model), lambda i: (count - 1 - i, at, 0, 0))

    line = pl.BlockSpec((None, 1, units), lambda i: (count - 1 - i, 0, 0))
    anywhere = pl.BlockSpec(memory_space=pl.ANY)
    big, row = once((tokens, model)), full((1, model))
    sems = pltpu.SemaphoreType.DMA
    shape = jax.ShapeDtypeStruct
    return pl.pallas_call(
        functools.partial(ffn_kernel, chunk=chunk),
        grid=(count,),
        in_specs=[big, big, big, chunks(0), chunks(1), line, row, row],
        out_specs=[anywhere] * 3 + [line, once((tokens, stored)), big, big, row, row],
        out_shape=[
            shape((2 * each, 2, CHUNK, wide), BF16),
            shape((2 * each, 2, CHUNK, wide), BF16),
            shape((sent, 2, CHUNK, wide), BF16),
            shape((count, 1, units), F32),
            shape((tokens, stored), BF16),
            shape((tokens, model), F32),
            shape((tokens, model), BF16),
            shape((1, model), F32),
            shape((1, model), F32),
        ],
        scratch_shapes=[pltpu.VMEM((tokens, model), F32)] * 2
        + [pltpu.VMEM((model, tokens), BF16)] * 2
        + [
            pltpu.VMEM((3, 2 * each, 2, CHUNK, wide), BF16),
            pltpu.VMEM((2, 2 * each, 2, CHUNK, wide), BF16),
            sems((2, 2 * each)), sems((2, 2 * each)), sems((sent,)), sems((sent,)),
            sems((2, 2 * each)),
        ],
        compiler_params=params(62, collective_id=2, has_side_effects=True),
        name="ffn",
    )(n, c, resid, weights, weights, bias, bias_out, gain)


def bwd_kernel(
    n_ref, db_ref, qkv_ref, att_ref, lse_ref, even_ref, odd_ref, qh_ref, kn_ref, x_ref, d_resid_ref,
    gain_ref, small_ref, sum_y_ref, sum_own_ref, got_ref,
    grad_in_ref, red_ref, total_ref,
    w, wo, da, dqkv, dk_acc, dv_acc, back, wide_x, g, core_in, y_in, x_in, z_in, ag, xag_in,
    sv, sv_in, sv_z,
    core_s, core_r, y_s, y_r, x_s, x_r, z_s, z_r, a_s, a_r, xa_s, xa_r, load_s, got_s, out_s,
    sv_s, sv_r, svz_s, svz_r,
    *, rows, pairs, group
):
    t = pl.program_id(0)
    tokens = n_ref.shape[0]
    length = tokens // rows
    early, done, late = sum_y_ref.shape[0], got_ref.shape[0], pairs // 2
    chunks = early + late
    others = group // 2
    keep = CHUNK // others
    half = g.shape[3]
    dp, tensor = lax.axis_index("dp"), lax.axis_index("tensor")
    place = (dp % group) // 2
    mine = pl.ds(pl.multiple_of(place * keep, keep), keep)
    to_core, to_y, to_x, side = neighbours()

    def place_of(o):
        return (place + o) % others

    def to_z(o):
        return (dp - dp % group + place_of(o) * 2 + side, tensor)

    def late_at(which, k):
        return chunks + late * which + k - early

    def core_copy(which, i, src):
        return remote(src, core_in.at[which, i], core_s.at[which, i], core_r.at[which, i], to_core)

    def y_copy(k, src):
        return remote(src, y_in.at[k], y_s.at[k], y_r.at[k], to_y)

    def x_copy(k):
        return remote(g.at[k, 1 - side], x_in.at[k], x_s.at[k], x_r.at[k], to_x)

    def z_copy(k, o):
        rows_of = pl.ds(pl.multiple_of(place_of(o) * keep, keep), keep)
        return remote(
            g.at[k, side, rows_of], z_in.at[k, o - 1], z_s.at[k, o - 1], z_r.at[k, o - 1], to_z(o)
        )

    def a_copy(k, o):
        return remote(ag.at[k, mine], ag.at[k, mine], a_s.at[k, o - 1], a_r.at[k, o - 1], to_z(o))

    def a_wait(k, o):
        rows_of = pl.ds(pl.multiple_of(place_of(others - o) * keep, keep), keep)
        part = ag.at[k, rows_of]
        remote(part, part, a_s.at[k, o - 1], a_r.at[k, o - 1], to_z(o)).wait_recv()

    def xa_copy(k):
        return remote(ag.at[k], xag_in.at[k], xa_s.at[k], xa_r.at[k], to_x)

    def out_copy(k, i):
        cols = pl.ds(pl.multiple_of((side + i - 2 * side * i) * half, LANES), half)
        return pltpu.make_async_copy(
            (xag_in if i else ag).at[k], red_ref.at[k, :, cols], out_s.at[k, i]
        )

    def load(k):
        return pltpu.make_async_copy(sum_own_ref.at[k], g.at[k], load_s.at[k])

    def got(k):
        return pltpu.make_async_copy(got_ref.at[k], y_in.at[k], got_s.at[k])

    def send_y(k):
        @pl.when(k < early)
        def _():
            y_copy(k, sum_y_ref.at[jnp.minimum(k, early - 1)]).start()

        @pl.when(k >= early)
        def _():
            at = jnp.maximum(k, early)
            core_copy(0, at - early, g.at[0]).wait_recv()
            i = late_at(0, at)
            g[i] = (g[i].astype(F32) + core_in[0, at - early].astype(F32)).astype(BF16)
            y_copy(at, g.at[i]).start()

    def send_x(k):
        @pl.when(k < early)
        def _():
            load(jnp.minimum(k, early - 1)).wait()

        @pl.when(k >= early)
        def _():
            at = jnp.maximum(k, early)
            core_copy(1, at - early, g.at[0]).wait_recv()
            g[at] = (g[at].astype(F32) + core_in[1, at - early].astype(F32)).astype(BF16)

        @pl.when(k < done)
        def _():
            got(jnp.minimum(k, done - 1)).wait()

        @pl.when(k >= done)
        def _():
            y_copy(jnp.maximum(k, done), g.at[0]).wait_recv()

        g[k] = (g[k].astype(F32) + y_in[k].astype(F32)).astype(BF16)
        x_copy(k).start()

    def send_z(k):
        x_copy(k).wait_recv()
        g[k, side] = (g[k, side].astype(F32) + x_in[k].astype(F32)).astype(BF16)
        for o in range(1, others):
            z_copy(k, o).start()

    def send_back(k):
        total = g[k, side, mine].astype(F32)
        for o in range(1, others):
            z_copy(k, o).wait_recv()
            total += z_in[k, o - 1].astype(F32)
        ag[k, mine] = total.astype(BF16)
        for o in range(1, others):
            a_copy(k, o).start()

    def send_back_x(k):
        for o in range(1, others):
            a_wait(k, o)
        xa_copy(k).start()
        out_copy(k, 0).start()

    def finish(k):
        xa_copy(k).wait_recv()
        out_copy(k, 1).start()

    schedule = [
        (finish, [{}, {3: 0, 4: 2, 5: 4}, {}, {5: 5}, {3: 1, 4: 3}]),
        (send_back_x, [{3: 1, 4: 3, 5: 5}, {2: 0}, {4: 4}, {3: 2}, {}]),
        (send_back, [{}, {2: 1, 3: 3}, {1: 0}, {4: 5}, {2: 2, 3: 4}]),
        (send_z, [{2: 2, 4: 5}, {1: 1, 3: 4}, {}, {2: 3}, {0: 0, 5: 6}]),
        (send_x, [{0: 0, 5: 6}, {0: 1, 1: 2}, {1: 3, 2: 4, 3: 5}, {}, {}]),
        (send_y, [{0: 3, 1: 4, 2: 5, 3: 6, 4: 7, 5: 8}, {}, {}, {}, {}]),
    ]

    def run(slot):
        for event, tables in schedule:
            table = tables[slot]
            if table:
                k = jnp.int32(-1)
                for step, at in table.items():
                    k = jnp.where(t == step, at, k)

                @pl.when(k >= 0)
                def _(event=event, k=k):
                    event(jnp.maximum(k, 0))

    def sv_copy(i, src, device):
        return remote(src, sv_in.at[i], sv_s.at[i], sv_r.at[i], device)

    def svz_copy(o):
        return remote(sv_z.at[place], sv_z.at[place], svz_s.at[o - 1], svz_r.at[o - 1], to_z(o))

    def small_y():
        for i in (0, 1):
            sv_copy(i, sv.at[3 - 2 * i], to_core).wait_recv()
        sv[2] += sv_in[0]
        sv_copy(2, sv.at[2], to_y).start()

    def small_x():
        sv_copy(2, sv.at[2], to_y).wait_recv()
        sv[0] = (sv[0] + sv_in[1]) + sv_in[2]
        sv_copy(3, sv.at[0], to_x).start()

    def small_z():
        sv_copy(3, sv.at[0], to_x).wait_recv()
        sv_z[place] = sv[0] + sv_in[3]
        for o in range(1, others):
            svz_copy(o).start()

    def small_end():
        for o in range(1, others):
            part = sv_z.at[place_of(others - o)]
            remote(part, part, svz_s.at[o - 1], svz_r.at[o - 1], to_z(o)).wait_recv()
        total = sv_z[0]
        for i in range(1, others):
            total += sv_z[i]
        total_ref[...] = total

    def norm_one():
        gain_sum = jnp.zeros((1, n_ref.shape[1]), F32)
        for i in range(0, tokens, CHUNK):
            r = slice(i, i + CHUNK)
            d_norm, part = norm_back(widen(x_ref.at[r, :], wide_x), gain_ref[...], back[r, :])
            grad = (d_resid_ref[r, :] + d_norm).astype(BF16)
            grad_in_ref[r, :] = grad[:, : grad_in_ref.shape[1]]
            gain_sum += part
        for i in range(4):
            sv[i, 4:5, :] = gain_sum
        for i in (0, 1):
            sv_copy(i, sv.at[3 - 2 * i], to_core).start()

    first = lax.broadcasted_iota(jnp.int32, (1, LANES), 1) < HEAD_DIM
    zero = jnp.zeros((), BF16)
    q_ref, k_ref, v_ref = (qkv_ref.at[:, j * LANES : (j + 1) * LANES] for j in range(3))

    def attend(at, span):
        dq = None
        for h in range(2):
            sel = first if h == 0 else ~first
            s, q = scores_of(q_ref, k_ref, qh_ref, kn_ref, sel, at, span)
            qm = jnp.where(sel, q, zero)
            km = jnp.where(sel, k_ref[span, :], zero)
            dom = jnp.where(sel, da[at, :], zero)
            p = jnp.exp(s - lse_ref[h : h + 1, at])
            dp_ = dot(v_ref[span, :], dom, NT)
            u = p * dp_
            inner = jnp.sum(u, axis=0, keepdims=True)
            ds = (u - p * inner).astype(BF16)
            dv_acc[span, :] += dot(p.astype(BF16), dom)
            dk_acc[span, :] += dot(ds, qm)
            part = dot(ds, km, TN)
            dq = part if dq is None else dq + part
        dqkv[at, :LANES] = (dq * 0.125).astype(BF16)

    @pl.when(t == 0)
    def _():
        greet([to_core, to_y, to_x] + [to_z(o) for o in range(1, others)])
        for k in range(early):
            load(k).start()
            if k < done:
                got(k).start()
        sv[...] = small_ref[...]
        back[...] = jnp.zeros_like(back)

    @pl.when(t < pairs)
    def _():
        pair_weights(even_ref, odd_ref, w, wo)
        da[...] = dot(db_ref[...], wo[...], NT).astype(BF16)
        dk_acc[...] = jnp.zeros_like(dk_acc)
        dv_acc[...] = jnp.zeros_like(dv_acc)
        run(0)
        slot = 1
        for row in range(rows):
            for at, span in spans(length, row):
                attend(at, span)
                if slot < 5:
                    run(slot)
                    slot += 1
        dqkv[:, LANES : 2 * LANES] = dk_acc[...].astype(BF16)
        dqkv[:, 2 * LANES :] = dv_acc[...].astype(BF16)
        sums = jnp.sum(dqkv[...].astype(F32), axis=0, keepdims=True)
        back[...] += dot(dqkv[...], w[...])
        grads = dot(dqkv[...], n_ref[...], TN).astype(BF16)
        grads_out = dot(att_ref[...], db_ref[...], TN).astype(BF16)
        for h in range(2):
            unit = 2 * (pairs - 1 - t) + h
            quarter, j = unit // late, unit % late
            for line in range(late):

                @pl.when(j == line)
                def _(line=8 + line, h=h):
                    for i in (0, 2):
                        part = sums[:, LANES * i + HEAD_DIM * h : LANES * i + HEAD_DIM * (h + 1)]
                        sv[quarter, line : line + 1, LANES * i : LANES * i + HEAD_DIM] = part

            i = (j + 1) % late
            odd = quarter % 2
            base = (1 - odd) * (early + (quarter // 2) * late) + odd * (
                chunks + late * (1 + quarter // 2)
            ) + i
            for side_ in range(2):
                cols = slice(side_ * half, (side_ + 1) * half)
                for p in range(3):
                    lines = slice(LANES * p + HEAD_DIM * h, LANES * p + HEAD_DIM * (h + 1))
                    g[base, side_, HEAD_DIM * p : HEAD_DIM * (p + 1), :] = grads[lines, cols]
                g[base, side_, 3 * HEAD_DIM :, :] = grads_out[
                    HEAD_DIM * h : HEAD_DIM * (h + 1), cols
                ]

            @pl.when(odd == 1)
            def _():
                core_copy(1 - quarter // 2, i, g.at[base]).start()

    @pl.when(t == pairs)
    def _():
        left = {
            event: sorted(set(range(done if event == send_y else 0, chunks)) - {k for table in tables for k in table.values()})
            for event, tables in schedule
        }

        def rest(event):
            for k in left[event]:
                event(k)

        rest(send_y)
        rest(send_x)
        norm_one()
        rest(send_z)
        small_y()
        rest(send_back)
        small_x()
        rest(send_back_x)
        small_z()
        rest(finish)
        small_end()

        @pl.loop(0, chunks)
        def _(k):
            x_copy(k).wait_send()
            for o in range(1, others):
                z_copy(k, o).wait_send()
                a_copy(k, o).wait_send()
            xa_copy(k).wait_send()
            for i in range(2):
                out_copy(k, i).wait()

        for k in range(done, chunks):
            y_copy(k, g.at[0]).wait_send()
        for which in range(2):
            for i in range(late):
                core_copy(which, i, g.at[0]).wait_send()
        for i, device in enumerate((to_core, to_core, to_y, to_x)):
            sv_copy(i, sv.at[0], device).wait_send()
        for o in range(1, others):
            svz_copy(o).wait_send()


def attn_bwd(
    n, db, qkv, att, lse, weights, qh, kn, x, d_resid, gain, small, sum_y, sum_own, got, rows, group
):
    tokens, model = n.shape
    stored = x.shape[1]
    pairs = qkv.shape[0]
    early, late = sum_y.shape[0], pairs // 2
    chunks = early + late
    others = group // 2
    wide = model // 2
    lines = small.shape[1]

    def of(shape):
        return pl.BlockSpec((None, *shape), lambda p: (jnp.maximum(pairs - 1 - p, 0), 0, 0))

    def unit(h):
        def at(p):
            u = 2 * jnp.maximum(pairs - 1 - p, 0) + h
            return u // late, u % late, 0, 0

        return pl.BlockSpec((None, None, CHUNK, model), at)

    anywhere = pl.BlockSpec(memory_space=pl.ANY)
    sems = pltpu.SemaphoreType.DMA
    between = max(others - 1, 1)
    many = (chunks, between)
    return pl.pallas_call(
        functools.partial(bwd_kernel, rows=rows, pairs=pairs, group=group),
        grid=(pairs + 1,),
        in_specs=[
            once((tokens, model)), once((tokens, model)), of((tokens, 3 * LANES)),
            of((tokens, LANES)), of((2, tokens)), unit(0), unit(1),
            once((tokens, LANES)), once((tokens, LANES)), once((tokens, stored)),
            once((tokens, model)), full((1, model)), full(small.shape),
            anywhere, anywhere, anywhere,
        ],
        out_specs=[once((tokens, stored)), anywhere, once((lines, model))],
        out_shape=[
            jax.ShapeDtypeStruct((tokens, stored), BF16),
            jax.ShapeDtypeStruct((chunks, CHUNK, model), BF16),
            jax.ShapeDtypeStruct((lines, model), F32),
        ],
        scratch_shapes=[
            pltpu.VMEM((3 * LANES, model), BF16),
            pltpu.VMEM((LANES, model), BF16),
            pltpu.VMEM((tokens, LANES), BF16),
            pltpu.VMEM((tokens, 3 * LANES), BF16),
            pltpu.VMEM((tokens, LANES), F32),
            pltpu.VMEM((tokens, LANES), F32),
            pltpu.VMEM((tokens, model), F32),
            pltpu.VMEM((CHUNK, model), F32),
            pltpu.VMEM((chunks + 3 * late, 2, CHUNK, wide), BF16),
            pltpu.VMEM((2, late, 2, CHUNK, wide), BF16),
            pltpu.VMEM((chunks, 2, CHUNK, wide), BF16),
            pltpu.VMEM((chunks, CHUNK, wide), BF16),
            pltpu.VMEM((*many, CHUNK // others, wide), BF16),
            pltpu.VMEM((chunks, CHUNK, wide), BF16),
            pltpu.VMEM((chunks, CHUNK, wide), BF16),
            pltpu.VMEM((4, lines, model), F32),
            pltpu.VMEM((4, lines, model), F32),
            pltpu.VMEM((others, lines, model), F32),
            sems((2, late)), sems((2, late)), sems((chunks,)), sems((chunks,)),
            sems((chunks,)), sems((chunks,)), sems(many), sems(many), sems(many), sems(many),
            sems((chunks,)), sems((chunks,)), sems((early,)), sems((got.shape[0],)),
            sems((chunks, 2)), sems((4,)), sems((4,)), sems((between,)), sems((between,)),
        ],
        compiler_params=params(60, collective_id=0, has_side_effects=True),
        name="attn_bwd",
    )(n, db, qkv, att, lse, weights, weights, qh, kn, x, d_resid, gain, small, sum_y, sum_own, got)


def solution(mesh):
    n_dp, n_tensor = mesh.shape["dp"], mesh.shape["tensor"]
    assert n_tensor == 4 and n_dp % 2 == 0 and n_dp & (n_dp - 1) == 0
    bits = [1 << i for i in range(n_dp.bit_length() - 1)]
    group = min(n_dp, 8)

    def to_dp(v, bit):
        return lax.ppermute(v, "dp", [(i, i ^ bit) for i in range(n_dp)])

    def local(
        layer_input, segments, cotangent, gain_one, w_qkv, b_qv, w_out, b_out, gain_two,
        w_up, b_up, w_down, b_down,
    ):
        rows = segments.shape[0]
        tokens, stored = layer_input.shape
        model = stored + 1
        heads = w_qkv.shape[2] // HEAD_DIM
        units = w_up.shape[1]

        def pad(v, size=model):
            return jnp.pad(v, [(0, 0)] * (v.ndim - 1) + [(0, size - v.shape[-1])])

        def line(v):
            return pad(v.astype(F32))[None]

        bias = b_qv.astype(F32).reshape(2, heads, HEAD_DIM)
        zeros = jnp.zeros((heads, HEAD_DIM), F32)
        places = [
            jnp.concatenate([bias[0], zeros, zeros, zeros, bias[1], zeros], axis=1),
            jnp.concatenate([zeros, bias[0], zeros, zeros, zeros, bias[1]], axis=1),
        ]
        misc = jnp.concatenate(
            [jnp.stack(places, axis=1), b_up.astype(F32).reshape(1, 2, units // 2)]
        )
        misc = jnp.broadcast_to(misc[:, :, None], (heads + 1, 2, 8, units // 2))

        gain_one_f, gain_two_f = line(gain_one), line(gain_two)
        lane = jnp.arange(LANES) % HEAD_DIM
        hot = segments.reshape(-1, 1) == lane[None, :]
        qh = jnp.where(hot, 1.0, 0.0).astype(BF16)
        kn = jnp.where(hot | (lane >= 8)[None, :], 0.0, MASKED_SCORE).astype(BF16)
        (
            n_one, cot, grad_bdown, qkv, att, lse, resid, n_two, w_attn, w_ffn, misc
        ) = forward(
            layer_input, cotangent, w_qkv.transpose(0, 2, 1), w_out, w_up, w_down, misc, gain_one_f,
            gain_two_f, line(b_out), qh, kn, rows,
        )
        bias_up = misc[:, heads, :, 0].reshape(4, 1, units)
        (
            sum_y, sum_own, got, g_bias, output, d_resid, d_branch, grad_gain_two, grad_bout
        ) = ffn(n_two, cot, resid, w_ffn, bias_up, line(b_down), gain_two_f, stored, 3)

        common = jnp.concatenate([grad_bdown, grad_bout, grad_gain_two], axis=0)[None]
        small = jnp.concatenate(
            [g_bias, jnp.broadcast_to(common, (4, 3, model)), jnp.zeros((4, 12, model), F32)], axis=1
        )
        input_grad, reduced, small = attn_bwd(
            n_one, d_branch, qkv, att, lse, w_attn, qh, kn, layer_input, d_resid, gain_one_f, small,
            sum_y, sum_own, got, rows, group,
        )
        for bit in bits:
            if bit >= group:
                small = small + to_dp(small, bit)
                reduced = (reduced.astype(F32) + to_dp(reduced, bit).astype(F32)).astype(BF16)
        each = model // CHUNK
        grad_up = reduced[:each].reshape(model, units)[:stored].astype(F32)
        grad_down = reduced[each : 2 * each].reshape(model, units).T[:, :stored].astype(F32)
        grad_heads = jnp.concatenate([reduced[2 * each + 1 :], reduced[2 * each : 2 * each + 1]])
        grad_heads = grad_heads.reshape(heads, 4, HEAD_DIM, model)[..., :stored].astype(F32)
        grad_qkv = grad_heads[:, :3].transpose(1, 0, 2, 3).reshape(3, heads * HEAD_DIM, stored)
        grad_qkv = grad_qkv.transpose(0, 2, 1)
        grad_out = grad_heads[:, 3].reshape(heads * HEAD_DIM, stored)
        per_head = small[8 : 8 + heads]
        grad_bqv = jnp.stack(
            [per_head[:, :HEAD_DIM].reshape(-1), per_head[:, 2 * LANES : 2 * LANES + HEAD_DIM].reshape(-1)]
        )
        return (
            output,
            input_grad,
            small[4, :stored],
            grad_qkv,
            grad_bqv,
            grad_out,
            small[2, :stored],
            small[3, :stored],
            grad_up,
            small[0],
            grad_down,
            small[1, :stored],
        )

    return jax.shard_map(
        local,
        mesh=mesh,
        in_specs=(
            P(("dp", "tensor"), None),
            P(("dp", "tensor"), None),
            P(("dp", "tensor"), None),
            P(),
            P(None, None, "tensor"),
            P(None, "tensor"),
            P("tensor", None),
            P(),
            P(),
            P(None, "tensor"),
            P("tensor"),
            P("tensor", None),
            P(),
        ),
        out_specs=(
            P(("dp", "tensor"), None),
            P(("dp", "tensor"), None),
            P(),
            P(None, None, "tensor"),
            P(None, "tensor"),
            P("tensor", None),
            P(),
            P(),
            P(None, "tensor"),
            P("tensor"),
            P("tensor", None),
            P(),
        ),
        check_vma=False,
    )
```

```python
import functools

import jax
import jax.numpy as jnp
from jax import lax
from jax.experimental import pallas as pl
from jax.experimental.pallas import tpu as pltpu
from jax.sharding import PartitionSpec as P

HEAD_DIM = 64
LANES = 128
EPSILON = 1e-05
MASKED_SCORE = -1e30
LONGEST = 512
BLOCK = 256
CHUNK = 256
F32 = jnp.float32
BF16 = jnp.bfloat16
NN = (((1,), (0,)), ((), ()))
NT = (((1,), (1,)), ((), ()))
TN = (((0,), (0,)), ((), ()))
GELU_A = 0.7978845608028654
GELU_B = 0.044715
MIB = 1024 * 1024
MESH = pl.DeviceIdType.MESH


def dot(a, b, dims=NN):
    return lax.dot_general(a, b, dims, preferred_element_type=F32)


def params(mib, **more):
    return pltpu.CompilerParams(vmem_limit_bytes=mib * MIB, **more)


def full(shape):
    return pl.BlockSpec(shape, lambda *_: (0,) * len(shape))


def once(shape):
    return pl.BlockSpec(shape, lambda *_: (0,) * len(shape), pipeline_mode=pl.Buffered(1))


def widen(ref, wide):
    wide[:, wide.shape[1] - LANES :] = jnp.zeros((wide.shape[0], LANES), F32)
    wide[:, : ref.shape[1]] = ref[...].astype(F32)
    return wide[...]


def norm_scale(values):
    total = jnp.sum(values, axis=-1, keepdims=True)
    square = jnp.sum(values * values, axis=-1, keepdims=True)
    return lax.rsqrt((square + total * total) / values.shape[-1] + EPSILON), total


def norm_back(values, gain, upstream):
    scale, total = norm_scale(values)
    weighted = upstream * values
    spread = jnp.sum(weighted * gain, axis=-1, keepdims=True)
    grad = upstream * gain * scale - (spread * scale * scale * scale / values.shape[-1]) * (
        values + total
    )
    return grad, jnp.sum(weighted * scale, axis=0, keepdims=True)


def scores_of(q_ref, k_ref, qh_ref, kn_ref, sel, at, span):
    q = q_ref[at, :] * 0.125
    qa = jnp.where(sel, q, qh_ref[at, :])
    ka = jnp.where(sel, k_ref[span, :], kn_ref[span, :])
    s = dot(ka, qa, NT)
    causal = lax.broadcasted_iota(jnp.int32, (BLOCK, BLOCK), 0) <= lax.broadcasted_iota(
        jnp.int32, (BLOCK, BLOCK), 1
    )
    early = s.shape[0] - BLOCK
    tail = jnp.where(causal, s[early:, :], MASKED_SCORE)
    return (tail if early == 0 else jnp.concatenate([s[:early, :], tail], axis=0)), q


def spans(length, row):
    for end in range(BLOCK, length + 1, BLOCK):
        start = max(0, end - BLOCK - LONGEST)
        base = row * length
        yield slice(base + end - BLOCK, base + end), slice(base + start, base + end)


def remote(src, dst, send, recv, device):
    return pltpu.make_async_remote_copy(
        src_ref=src, dst_ref=dst, send_sem=send, recv_sem=recv, device_id=device,
        device_id_type=MESH,
    )


def greet(partners):
    barrier = pltpu.get_barrier_semaphore()
    for device in partners:
        pl.semaphore_signal(barrier, inc=1, device_id=device, device_id_type=MESH)
    pl.semaphore_wait(barrier, len(partners))


def neighbours():
    dp, tensor = lax.axis_index("dp"), lax.axis_index("tensor")
    side = dp % 2
    to_core = (dp, tensor + 1 - 2 * (tensor % 2))
    return to_core, (dp, (tensor + 2) % 4), (dp + 1 - 2 * side, tensor), side


def pair_weights(even, odd, w, wo):
    for h, unit in enumerate((even, odd)):
        for i in range(3):
            at = LANES * i + HEAD_DIM * h
            w[at : at + HEAD_DIM, :] = unit[HEAD_DIM * i : HEAD_DIM * (i + 1), :]
        wo[HEAD_DIM * h : HEAD_DIM * (h + 1), :] = unit[3 * HEAD_DIM :, :]


def fwd_kernel(
    x_ref, c_ref, wqkv_ref, wout_ref, up_ref, down_ref, vec_ref, seg_ref,
    n_ref, cot_ref, c_sum_ref, qkv_ref, att_ref, lse_ref, resid_ref, n_two_ref, qh_ref, kn_ref,
    wa_ref, wf_ref, misc_all_ref,
    wa, stage, misc, w, wo, branch, wide,
    core_s, core_r, y_s, y_r, x_s, x_r, d_s, d_r, local_s, z_s, z_r, zz_s, zz_r,
    *, rows, pairs
):
    t = pl.program_id(0)
    tokens = x_ref.shape[0]
    length = tokens // rows
    heads = pairs // 2
    stored = x_ref.shape[1]
    model = stored + 1
    early, tail = heads, stage.shape[0]
    to_core, to_y, to_x, side = neighbours()
    last = early + tail
    dp = lax.axis_index("dp")
    level = dp // 2 % 2
    to_z = (dp + 2 - 4 * level, lax.axis_index("tensor"))

    def rows_of(k, across, along):
        if k < early:
            return pl.ds(pl.multiple_of(across * (CHUNK // 2), CHUNK // 2), CHUNK // 2)
        size = CHUNK // 4
        return pl.ds(pl.multiple_of((2 * across + along) * size, size), size)

    def held(quarter, k):
        if k == last:
            return misc.at[quarter]
        if k < early:
            return wa.at[quarter, k]
        return wf_ref.at[quarter, k - early]

    def own(k):
        return held(0, k) if k < early or k == last else stage.at[k - early]

    def core_copy(k):
        return remote(own(k), held(1, k), core_s.at[k], core_r.at[k], to_core)

    def y_copy(k):
        src, dst = own(k), held(2, k)
        if k < last:
            rows_ = rows_of(k, side, level)
            src, dst = src.at[rows_], dst.at[rows_]
        return remote(src, dst, y_s.at[k], y_r.at[k], to_y)

    def spread(k, across, along, send, recv, device):
        ref = held(2, k).at[rows_of(k, across, along)]
        return remote(ref, ref, send.at[k], recv.at[k], device)

    def x_copy(k, across):
        return spread(k, across, level, x_s, x_r, to_x)

    def z_copy(k, along):
        return spread(k, side, along, z_s, z_r, to_z)

    def zz_copy(k, along):
        return spread(k, 1 - side, along, zz_s, zz_r, to_z)

    def d_copy(k):
        return remote(held(2, k), held(3, k), d_s.at[k], d_r.at[k], to_core)

    def keep_copy(k):
        if k == last:
            return pltpu.make_async_copy(misc, misc_all_ref, local_s.at[k])
        if k < early:
            return pltpu.make_async_copy(wa.at[:, k], wa_ref.at[:, k], local_s.at[k])
        return pltpu.make_async_copy(stage.at[k - early], wf_ref.at[0, k - early], local_s.at[k])

    def x_on(k):
        y_copy(k).wait_recv()
        x_copy(k, side).start()
        if k >= early:
            z_copy(k, level).start()

    def z_on(k):
        x_copy(k, 1 - side).wait_recv()
        zz_copy(k, level).start()

    def d_on(k):
        if k == last:
            y_copy(k).wait_recv()
        elif k < early:
            x_copy(k, 1 - side).wait_recv()
        else:
            z_copy(k, 1 - level).wait_recv()
            zz_copy(k, 1 - level).wait_recv()
        d_copy(k).start()

    def start_y(k):
        y_copy(k).start()

    @pl.when(t == 0)
    def _():
        edge = slice(model - LANES, model)
        wa[0, :, :, edge] = jnp.zeros((early, CHUNK, LANES), BF16)
        for j in range(heads):
            head = slice(HEAD_DIM * j, HEAD_DIM * (j + 1))
            for i in range(3):
                wa[0, j, HEAD_DIM * i : HEAD_DIM * (i + 1), :stored] = wqkv_ref[i, head, :]
            wa[0, j, 3 * HEAD_DIM :, :stored] = wout_ref[head, :]
        misc[...] = jnp.zeros_like(misc)
        for p in range(2):
            for j in range(heads):
                for i, row in ((0, 5), (2, 6)):
                    at = LANES * i + HEAD_DIM * p
                    misc[0, j, p, :1, at : at + HEAD_DIM] = vec_ref[
                        row : row + 1, HEAD_DIM * j : HEAD_DIM * (j + 1)
                    ]
            units_half = misc.shape[4]
            misc[0, heads, p, :1, :] = vec_ref[4:5, units_half * p : units_half * (p + 1)]
        greet([to_core, to_y, to_x, to_z])
        for k in (last, *range(early)):
            core_copy(k).start()
            y_copy(k).start()
        count = tail // 2
        stage[:, :, edge] = jnp.zeros((tail, CHUNK, LANES), BF16)
        stage[count - 1, CHUNK - 16 :, :] = jnp.zeros((16, model), BF16)
        for i in range(count):
            end = min(CHUNK * (i + 1), stored)
            stage[i, : end - CHUNK * i, :] = up_ref[CHUNK * i : end, :]
            stage[count + i, :, :stored] = down_ref[CHUNK * i : CHUNK * (i + 1), :]
        for k in range(early, last):
            core_copy(k).start()
            keep_copy(k).start()
        branch[...] = jnp.zeros_like(branch)
        c_sum = jnp.zeros((1, model), F32)
        for i in range(0, tokens, CHUNK):
            r = slice(i, i + CHUNK)
            x = widen(x_ref.at[r, :], wide)
            n_ref[r, :] = (x * norm_scale(x)[0] * vec_ref[0:1, :model]).astype(BF16)
            c = widen(c_ref.at[r, :], wide)
            cot_ref[r, :] = c.astype(BF16)
            c_sum += jnp.sum(c, axis=0, keepdims=True)
        c_sum_ref[...] = c_sum
        lane = lax.broadcasted_iota(jnp.int32, (1, LANES), 1) % HEAD_DIM
        for row in range(rows):
            document = jnp.broadcast_to(seg_ref[row : row + 1, :].astype(F32), (LANES, length)).T
            hot = document == lane.astype(F32)
            r = slice(row * length, (row + 1) * length)
            qh_ref[r, :] = jnp.where(hot, 1.0, 0.0).astype(BF16)
            kn_ref[r, :] = jnp.where(hot | (lane >= 8), 0.0, MASKED_SCORE).astype(BF16)
        core_copy(last).wait_recv()

    events = {
        (0, 4): [(d_on, last)],
        (1, 1): [(x_on, 0)],
        (2, 1): [(x_on, 1)], (2, 3): [(d_on, 0), (start_y, early)], (2, 4): [(d_on, 1), (start_y, early + 1)],
        (3, 0): [(x_on, 2), (start_y, early + 2)], (3, 1): [(x_on, early), (start_y, early + 3)],
        (3, 2): [(start_y, early + 4)], (3, 3): [(x_on, early + 1), (start_y, early + 5)], (3, 4): [(d_on, 2)],
        (4, 0): [(x_on, early + 2)], (4, 1): [(z_on, early), (x_on, early + 3)], (4, 2): [(z_on, early + 1)],
        (4, 3): [(x_on, early + 4)], (4, 4): [(z_on, early + 2)],
        (5, 0): [(x_on, early + 5), (d_on, early)], (5, 1): [(z_on, early + 3), (d_on, early + 1)],
        (5, 2): [(z_on, early + 4)], (5, 3): [(d_on, early + 2)], (5, 4): [(z_on, early + 5)],
    }

    def run(slot):
        for (step, at), todo in events.items():
            if at == slot and todo:

                @pl.when(t == step)
                def _(todo=todo):
                    for event, k in todo:
                        event(k)

    for step in range(pairs):
        needed = {divmod(2 * step + h, heads) for h in range(2)}
        seen = {divmod(u, heads) for u in range(2 * step)}

        @pl.when(t == step)
        def _(needed=needed, seen=seen):
            for quarter, j in sorted(needed - seen):
                if quarter == 1:
                    core_copy(j).wait_recv()
                if quarter == 3:
                    d_copy(j).wait_recv()
            if any(quarter == 3 for quarter, _ in needed) and not any(q == 3 for q, _ in seen):
                d_copy(last).wait_recv()

    first = lax.broadcasted_iota(jnp.int32, (1, LANES), 1) < HEAD_DIM
    units = 2 * t, 2 * t + 1
    pair_weights(*(wa.at[u // heads, u % heads] for u in units), w, wo)
    bias = sum(misc[u // heads, u % heads, h, :1, :] for h, u in enumerate(units))
    qkv_ref[...] = (dot(n_ref[...], w[...], NT) + bias).astype(BF16)
    q_ref, k_ref, v_ref = (qkv_ref.at[:, j * LANES : (j + 1) * LANES] for j in range(3))
    run(0)
    slot = 1
    for row in range(rows):
        for at, span in spans(length, row):
            parts = []
            for h in range(2):
                sel = first if h == 0 else ~first
                s, _ = scores_of(q_ref, k_ref, qh_ref, kn_ref, sel, at, span)
                m = jnp.max(s, axis=0, keepdims=True)
                p = jnp.exp(s - m)
                total = jnp.sum(p, axis=0, keepdims=True)
                weights = (p * (1.0 / total)).astype(BF16)
                parts.append(dot(weights, v_ref[span, :], TN))
                lse_ref[h : h + 1, at] = m + jnp.log(total)
            att_ref[at, :] = jnp.where(first, parts[0], parts[1]).astype(BF16)
            if slot < 4:
                run(slot)
                slot += 1
    branch[...] += dot(att_ref[...], wo[...])
    run(4)

    @pl.when(t == pairs - 1)
    def _():
        for i in range(0, tokens, CHUNK):
            r = slice(i, i + CHUNK)
            resid = widen(x_ref.at[r, :], wide) + (branch[r, :] + vec_ref[2:3, :model])
            resid_ref[r, :] = resid
            n_two_ref[r, :] = (resid * norm_scale(resid)[0] * vec_ref[1:2, :model]).astype(BF16)
        for k in range(early + 3, last):
            d_on(k)
        for k in (*range(early), last):
            keep_copy(k).start()
        for k in range(early, last):
            core_copy(k).wait_recv()
            d_copy(k).wait_recv()
        for k in range(last + 1):
            core_copy(k).wait_send()
            y_copy(k).wait_send()
            if k < last:
                x_copy(k, side).wait_send()
            if early <= k < last:
                z_copy(k, level).wait_send()
                zz_copy(k, level).wait_send()
            d_copy(k).wait_send()
            keep_copy(k).wait()


def forward(x, c, wqkv, wout, up, down, vec, seg):
    tokens, stored = x.shape
    model = stored + 1
    heads = wqkv.shape[1] // HEAD_DIM
    pairs = 2 * heads
    tail = 2 * (model // CHUNK)

    def of(*shape):
        return pl.BlockSpec((None, *shape), lambda p: (p,) + (0,) * len(shape))

    anywhere = pl.BlockSpec(memory_space=pl.ANY)
    sems = pltpu.SemaphoreType.DMA((heads + tail + 1,))
    rows = seg.shape[0]
    misc = (heads + 1, 2, 8, model // 2)
    inputs = [x, c, wqkv, wout, up, down, vec, seg]
    big = once((tokens, model))
    outs = [
        (big, (tokens, model), BF16),
        (big, (tokens, model), BF16),
        (once((1, model)), (1, model), F32),
        (of(tokens, 3 * LANES), (pairs, tokens, 3 * LANES), BF16),
        (of(tokens, LANES), (pairs, tokens, LANES), BF16),
        (of(2, tokens), (pairs, 2, tokens), F32),
        (big, (tokens, model), F32),
        (big, (tokens, model), BF16),
        (once((tokens, LANES)), (tokens, LANES), BF16),
        (once((tokens, LANES)), (tokens, LANES), BF16),
        (anywhere, (4, heads, CHUNK, model), BF16),
        (anywhere, (4, tail, CHUNK, model), BF16),
        (anywhere, (4, *misc), F32),
    ]
    return pl.pallas_call(
        functools.partial(fwd_kernel, rows=rows, pairs=pairs),
        grid=(pairs,),
        in_specs=[once(v.shape) for v in inputs],
        out_specs=[spec for spec, _, _ in outs],
        out_shape=[jax.ShapeDtypeStruct(shape, dtype) for _, shape, dtype in outs],
        scratch_shapes=[
            pltpu.VMEM((4, heads, CHUNK, model), BF16),
            pltpu.VMEM((tail, CHUNK, model), BF16),
            pltpu.VMEM((4, *misc), F32),
            pltpu.VMEM((3 * LANES, model), BF16),
            pltpu.VMEM((LANES, model), BF16),
            pltpu.VMEM((tokens, model), F32),
            pltpu.VMEM((CHUNK, model), F32),
        ]
        + [sems] * 13,
        compiler_params=params(60, collective_id=1, has_side_effects=True),
        name="forward",
    )(*inputs)


def ffn_kernel(
    n_ref, c_ref, resid_ref, up_ref, down_ref, bias_ref, vec_ref,
    sum_y_ref, sum_own_ref, got_ref, gbias_ref, output_ref, d_resid_ref, d_branch_ref,
    gain_sum_ref, branch_sum_ref,
    out, back, nt, ct, g, core_in, core_s, core_r, y_s, y_r, out_s, *, chunk
):
    tokens = n_ref.shape[0]
    step, last = pl.program_id(0), pl.num_programs(0) - 1
    to_core, to_y, _, _ = neighbours()
    chunks, sent = core_in.shape[1], got_ref.shape[0]

    def core_copy(which, k):
        return remote(
            g.at[0, k], core_in.at[which, k], core_s.at[which, k], core_r.at[which, k], to_core
        )

    def y_copy(k):
        return remote(g.at[1, k], got_ref.at[k], y_s.at[k], y_r.at[k], to_y)

    def out_copy(which, k):
        dst = sum_own_ref if which else sum_y_ref
        return pltpu.make_async_copy(g.at[1 + which, k], dst.at[k], out_s.at[which, k])

    @pl.when(step == 0)
    def _():
        greet([to_core, to_y])
        out[...] = jnp.zeros_like(out)
        back[...] = jnp.zeros_like(back)
        for i in range(0, tokens, 256):
            nt[:, i : i + 256] = n_ref[i : i + 256, :].T
            ct[:, i : i + 256] = c_ref[i : i + 256, :].T

    model = n_ref.shape[1]
    up, down = (ref[...].reshape(-1, model) for ref in (up_ref, down_ref))
    bias = jnp.concatenate([bias_ref[h, :1, :] for h in range(2)], axis=1)
    gup = gdown = gbias = None
    for i in range(0, tokens, chunk):
        r = slice(i, i + chunk)
        pre = dot(n_ref[r, :], up) + bias
        dh = dot(c_ref[r, :], down, NT)
        sq = pre * pre
        th = jnp.tanh(pre * (GELU_A + (GELU_A * GELU_B) * sq))
        half = 0.5 + 0.5 * th
        hidden = (pre * half).astype(BF16)
        slope = half + (0.5 * pre) * (1.0 - th * th) * (GELU_A + (3.0 * GELU_A * GELU_B) * sq)
        dpre = (dh * slope).astype(BF16)
        out[r, :] += dot(hidden, down)
        back[r, :] += dot(dpre, up, NT)
        a, b = dot(nt[:, r], dpre), dot(ct[:, r], hidden)
        s = jnp.sum(dpre.astype(F32), axis=0, keepdims=True)
        gup, gdown, gbias = (a, b, s) if i == 0 else (gup + a, gdown + b, gbias + s)
    gbias_ref[...] = gbias

    @pl.when(step == 2)
    def _():
        for k in range(chunks):
            core_copy(0, k).wait_send()

    wide = g.shape[4]
    place = step % 2 * (1 + step // 2)
    for m, grad in enumerate((gup, gdown)):
        for i in range(chunks // 2):
            for h in range(2):
                at = slice(CHUNK * i, CHUNK * (i + 1)), slice(wide * h, wide * (h + 1))
                g[place, m * (chunks // 2) + i, h] = grad[at].astype(BF16)

    for which in range(2):

        @pl.when(step == 2 * which)
        def _(which=which):
            for k in range(chunks):
                core_copy(which, k).start()

        @pl.when(step == 2 * which + 1)
        def _(which=which):
            for k in range(chunks):
                core_copy(which, k).wait_recv()
                g[1 + which, k] = (
                    g[1 + which, k].astype(F32) + core_in[which, k].astype(F32)
                ).astype(BF16)
                if which == 0 and k < sent:
                    y_copy(k).start()
                else:
                    out_copy(which, k).start()

    @pl.when(step == last)
    def _():
        gain_sum_ref[...] = jnp.zeros_like(gain_sum_ref)
        branch_sum_ref[...] = jnp.zeros_like(branch_sum_ref)

        @pl.loop(0, tokens // 256)
        def _(i):
            r = pl.ds(pl.multiple_of(i * 256, 256), 256)
            resid = resid_ref[r, :]
            output = (resid + (out[r, :] + vec_ref[3:4, :model])).astype(BF16)
            output_ref[r, :] = output[:, : output_ref.shape[1]]
            d_norm, gain_sum = norm_back(resid, vec_ref[1:2, :model], back[r, :])
            d_resid = c_ref[r, :].astype(F32) + d_norm
            d_resid_ref[r, :] = d_resid
            d_branch = d_resid.astype(BF16)
            d_branch_ref[r, :] = d_branch
            gain_sum_ref[...] += gain_sum
            branch_sum_ref[...] += jnp.sum(d_branch.astype(F32), axis=0, keepdims=True)

        for k in range(chunks):
            core_copy(1, k).wait_send()
            out_copy(1, k).wait()
            if k < sent:
                y_copy(k).wait()
            else:
                out_copy(0, k).wait()


def ffn(n, c, resid, weights, misc, vec, stored, sent, chunk=512):
    tokens, model = n.shape
    count, entries, _, _, wide = misc.shape
    units = 2 * wide
    each = model // CHUNK

    def chunks(at):
        return pl.BlockSpec((None, each, CHUNK, model), lambda i: (count - 1 - i, at, 0, 0))

    line = pl.BlockSpec((None, 1, units), lambda i: (count - 1 - i, 0, 0))
    bias = pl.BlockSpec((None, None, 2, 8, wide), lambda i: (count - 1 - i, entries - 1, 0, 0, 0))
    anywhere = pl.BlockSpec(memory_space=pl.ANY)
    big, row = once((tokens, model)), full((1, model))
    sems = pltpu.SemaphoreType.DMA
    shape = jax.ShapeDtypeStruct
    return pl.pallas_call(
        functools.partial(ffn_kernel, chunk=chunk),
        grid=(count,),
        in_specs=[big, big, big, chunks(0), chunks(1), bias, full(vec.shape)],
        out_specs=[anywhere] * 3 + [line, once((tokens, stored)), big, big, row, row],
        out_shape=[
            shape((2 * each, 2, CHUNK, wide), BF16),
            shape((2 * each, 2, CHUNK, wide), BF16),
            shape((sent, 2, CHUNK, wide), BF16),
            shape((count, 1, units), F32),
            shape((tokens, stored), BF16),
            shape((tokens, model), F32),
            shape((tokens, model), BF16),
            shape((1, model), F32),
            shape((1, model), F32),
        ],
        scratch_shapes=[pltpu.VMEM((tokens, model), F32)] * 2
        + [pltpu.VMEM((model, tokens), BF16)] * 2
        + [
            pltpu.VMEM((3, 2 * each, 2, CHUNK, wide), BF16),
            pltpu.VMEM((2, 2 * each, 2, CHUNK, wide), BF16),
            sems((2, 2 * each)), sems((2, 2 * each)), sems((sent,)), sems((sent,)),
            sems((2, 2 * each)),
        ],
        compiler_params=params(62, collective_id=2, has_side_effects=True),
        name="ffn",
    )(n, c, resid, weights, weights, misc, vec)


def bwd_kernel(
    n_ref, db_ref, qkv_ref, att_ref, lse_ref, even_ref, odd_ref, qh_ref, kn_ref, x_ref, d_resid_ref,
    vec_ref, gbias_ref, c_sum_ref, branch_sum_ref, gain_two_sum_ref, sum_y_ref, sum_own_ref, got_ref,
    grad_in_ref, red_ref, red_qkv_ref, red_out_ref, total_ref,
    w, wo, da, dqkv, dk_acc, dv_acc, back, wide_x, g, core_in, y_in, x_in, z_in, ag, xag_in,
    sv, sv_in, sv_z,
    core_s, core_r, y_s, y_r, x_s, x_r, z_s, z_r, a_s, a_r, xa_s, xa_r, load_s, got_s, out_s,
    sv_s, sv_r, svz_s, svz_r,
    *, rows, pairs, group
):
    t = pl.program_id(0)
    tokens = n_ref.shape[0]
    length = tokens // rows
    early, done, late = sum_y_ref.shape[0], got_ref.shape[0], pairs // 2
    chunks = early + late
    others = group // 2
    keep = CHUNK // others
    half = g.shape[3]
    dp, tensor = lax.axis_index("dp"), lax.axis_index("tensor")
    place = (dp % group) // 2
    mine = pl.ds(pl.multiple_of(place * keep, keep), keep)
    to_core, to_y, to_x, side = neighbours()

    def place_of(o):
        return (place + o) % others

    def to_z(o):
        return (dp - dp % group + place_of(o) * 2 + side, tensor)

    def late_at(which, k):
        return chunks + late * which + k - early

    def core_copy(which, i, src):
        return remote(src, core_in.at[which, i], core_s.at[which, i], core_r.at[which, i], to_core)

    def y_copy(k, src):
        return remote(src, y_in.at[k], y_s.at[k], y_r.at[k], to_y)

    def x_copy(k):
        return remote(g.at[k, 1 - side], x_in.at[k], x_s.at[k], x_r.at[k], to_x)

    def z_copy(k, o):
        rows_of = pl.ds(pl.multiple_of(place_of(o) * keep, keep), keep)
        return remote(
            g.at[k, side, rows_of], z_in.at[k, o - 1], z_s.at[k, o - 1], z_r.at[k, o - 1], to_z(o)
        )

    def a_copy(k, o):
        return remote(ag.at[k, mine], ag.at[k, mine], a_s.at[k, o - 1], a_r.at[k, o - 1], to_z(o))

    def a_wait(k, o):
        rows_of = pl.ds(pl.multiple_of(place_of(others - o) * keep, keep), keep)
        part = ag.at[k, rows_of]
        remote(part, part, a_s.at[k, o - 1], a_r.at[k, o - 1], to_z(o)).wait_recv()

    def xa_copy(k):
        return remote(ag.at[k], xag_in.at[k], xa_s.at[k], xa_r.at[k], to_x)

    def out_copies(k, i, act):
        cols = pl.ds(pl.multiple_of((side + i - 2 * side * i) * half, LANES), half)
        src = xag_in if i else ag

        @pl.when(k < early)
        def _():
            at = jnp.minimum(k, early - 1)
            act(pltpu.make_async_copy(src.at[at], red_ref.at[at, :, cols], out_s.at[k, i, 0]))

        @pl.when(k >= early)
        def _():
            at = jnp.maximum(k, early)
            j = (at - early + late - 1) % late
            head = pl.ds(pl.multiple_of(j * HEAD_DIM, HEAD_DIM), HEAD_DIM)
            for p in range(4):
                part = src.at[at, HEAD_DIM * p : HEAD_DIM * (p + 1)]
                dst = red_out_ref.at[head, cols] if p == 3 else red_qkv_ref.at[p, head, cols]
                act(pltpu.make_async_copy(part, dst, out_s.at[k, i, p]))

    def load(k):
        return pltpu.make_async_copy(sum_own_ref.at[k], g.at[k], load_s.at[k])

    def got(k):
        return pltpu.make_async_copy(got_ref.at[k], y_in.at[k], got_s.at[k])

    def send_y(k):
        @pl.when(k < early)
        def _():
            y_copy(k, sum_y_ref.at[jnp.minimum(k, early - 1)]).start()

        @pl.when(k >= early)
        def _():
            at = jnp.maximum(k, early)
            core_copy(0, at - early, g.at[0]).wait_recv()
            i = late_at(0, at)
            g[i] = (g[i].astype(F32) + core_in[0, at - early].astype(F32)).astype(BF16)
            y_copy(at, g.at[i]).start()

    def send_x(k):
        @pl.when(k < early)
        def _():
            load(jnp.minimum(k, early - 1)).wait()

        @pl.when(k >= early)
        def _():
            at = jnp.maximum(k, early)
            core_copy(1, at - early, g.at[0]).wait_recv()
            g[at] = (g[at].astype(F32) + core_in[1, at - early].astype(F32)).astype(BF16)

        @pl.when(k < done)
        def _():
            got(jnp.minimum(k, done - 1)).wait()

        @pl.when(k >= done)
        def _():
            y_copy(jnp.maximum(k, done), g.at[0]).wait_recv()

        g[k] = (g[k].astype(F32) + y_in[k].astype(F32)).astype(BF16)
        x_copy(k).start()

    def send_z(k):
        x_copy(k).wait_recv()
        g[k, side] = (g[k, side].astype(F32) + x_in[k].astype(F32)).astype(BF16)
        for o in range(1, others):
            z_copy(k, o).start()

    def send_back(k):
        total = g[k, side, mine].astype(F32)
        for o in range(1, others):
            z_copy(k, o).wait_recv()
            total += z_in[k, o - 1].astype(F32)
        ag[k, mine] = total.astype(BF16)
        for o in range(1, others):
            a_copy(k, o).start()

    def send_back_x(k):
        for o in range(1, others):
            a_wait(k, o)
        xa_copy(k).start()
        out_copies(k, 0, lambda copy: copy.start())

    def finish(k):
        xa_copy(k).wait_recv()
        out_copies(k, 1, lambda copy: copy.start())

    schedule = [
        (finish, [{}, {3: 0, 4: 2, 5: 4}, {}, {5: 5}, {3: 1, 4: 3}]),
        (send_back_x, [{3: 1, 4: 3, 5: 5}, {2: 0}, {4: 4}, {3: 2}, {}]),
        (send_back, [{}, {2: 1, 3: 3}, {1: 0}, {4: 5}, {2: 2, 3: 4}]),
        (send_z, [{2: 2, 4: 5}, {1: 1, 3: 4}, {}, {2: 3}, {0: 0, 5: 6}]),
        (send_x, [{0: 0, 5: 6}, {0: 1, 1: 2}, {1: 3, 2: 4, 3: 5}, {}, {}]),
        (send_y, [{0: 3, 1: 4, 2: 5, 3: 6, 4: 7, 5: 8}, {}, {}, {}, {}]),
    ]

    def run(slot):
        for event, tables in schedule:
            table = tables[slot]
            if table:
                k = jnp.int32(-1)
                for step, at in table.items():
                    k = jnp.where(t == step, at, k)

                @pl.when(k >= 0)
                def _(event=event, k=k):
                    event(jnp.maximum(k, 0))

    def sv_copy(i, src, device):
        return remote(src, sv_in.at[i], sv_s.at[i], sv_r.at[i], device)

    def svz_copy(o):
        return remote(sv_z.at[place], sv_z.at[place], svz_s.at[o - 1], svz_r.at[o - 1], to_z(o))

    def small_y():
        for i in (0, 1):
            sv_copy(i, sv.at[3 - 2 * i], to_core).wait_recv()
        sv[2] += sv_in[0]
        sv_copy(2, sv.at[2], to_y).start()

    def small_x():
        sv_copy(2, sv.at[2], to_y).wait_recv()
        sv[0] = (sv[0] + sv_in[1]) + sv_in[2]
        sv_copy(3, sv.at[0], to_x).start()

    def small_z():
        sv_copy(3, sv.at[0], to_x).wait_recv()
        sv_z[place] = sv[0] + sv_in[3]
        for o in range(1, others):
            svz_copy(o).start()

    def small_end():
        for o in range(1, others):
            part = sv_z.at[place_of(others - o)]
            remote(part, part, svz_s.at[o - 1], svz_r.at[o - 1], to_z(o)).wait_recv()
        total = sv_z[0]
        for i in range(1, others):
            total += sv_z[i]
        total_ref[...] = total

    def norm_one():
        gain_sum = jnp.zeros((1, n_ref.shape[1]), F32)
        for i in range(0, tokens, CHUNK):
            r = slice(i, i + CHUNK)
            d_norm, part = norm_back(widen(x_ref.at[r, :], wide_x), vec_ref[0:1, : n_ref.shape[1]], back[r, :])
            grad = (d_resid_ref[r, :] + d_norm).astype(BF16)
            grad_in_ref[r, :] = grad[:, : grad_in_ref.shape[1]]
            gain_sum += part
        for i in range(4):
            sv[i, 4:5, :] = gain_sum
        for i in (0, 1):
            sv_copy(i, sv.at[3 - 2 * i], to_core).start()

    first = lax.broadcasted_iota(jnp.int32, (1, LANES), 1) < HEAD_DIM
    zero = jnp.zeros((), BF16)
    q_ref, k_ref, v_ref = (qkv_ref.at[:, j * LANES : (j + 1) * LANES] for j in range(3))

    def attend(at, span):
        dq = None
        for h in range(2):
            sel = first if h == 0 else ~first
            s, q = scores_of(q_ref, k_ref, qh_ref, kn_ref, sel, at, span)
            qm = jnp.where(sel, q, zero)
            km = jnp.where(sel, k_ref[span, :], zero)
            dom = jnp.where(sel, da[at, :], zero)
            p = jnp.exp(s - lse_ref[h : h + 1, at])
            dp_ = dot(v_ref[span, :], dom, NT)
            u = p * dp_
            inner = jnp.sum(u, axis=0, keepdims=True)
            ds = (u - p * inner).astype(BF16)
            dv_acc[span, :] += dot(p.astype(BF16), dom)
            dk_acc[span, :] += dot(ds, qm)
            part = dot(ds, km, TN)
            dq = part if dq is None else dq + part
        dqkv[at, :LANES] = (dq * 0.125).astype(BF16)

    @pl.when(t == 0)
    def _():
        greet([to_core, to_y, to_x] + [to_z(o) for o in range(1, others)])
        for k in range(early):
            load(k).start()
            if k < done:
                got(k).start()
        sv[...] = jnp.zeros_like(sv)
        sums = c_sum_ref, branch_sum_ref, gain_two_sum_ref
        for i in range(4):
            sv[i, 0:1, :] = gbias_ref[i]
            for j, ref in enumerate(sums):
                sv[i, 1 + j : 2 + j, :] = ref[...]
        back[...] = jnp.zeros_like(back)

    @pl.when(t < pairs)
    def _():
        pair_weights(even_ref, odd_ref, w, wo)
        da[...] = dot(db_ref[...], wo[...], NT).astype(BF16)
        dk_acc[...] = jnp.zeros_like(dk_acc)
        dv_acc[...] = jnp.zeros_like(dv_acc)
        run(0)
        slot = 1
        for row in range(rows):
            for at, span in spans(length, row):
                attend(at, span)
                if slot < 5:
                    run(slot)
                    slot += 1
        dqkv[:, LANES : 2 * LANES] = dk_acc[...].astype(BF16)
        dqkv[:, 2 * LANES :] = dv_acc[...].astype(BF16)
        sums = jnp.sum(dqkv[...].astype(F32), axis=0, keepdims=True)
        back[...] += dot(dqkv[...], w[...])
        grads = dot(dqkv[...], n_ref[...], TN).astype(BF16)
        grads_out = dot(att_ref[...], db_ref[...], TN).astype(BF16)
        for h in range(2):
            unit = 2 * (pairs - 1 - t) + h
            quarter, j = unit // late, unit % late
            for line in range(late):

                @pl.when(j == line)
                def _(line=8 + line, h=h):
                    for i in (0, 2):
                        part = sums[:, LANES * i + HEAD_DIM * h : LANES * i + HEAD_DIM * (h + 1)]
                        sv[quarter, line : line + 1, LANES * i : LANES * i + HEAD_DIM] = part

            i = (j + 1) % late
            odd = quarter % 2
            base = (1 - odd) * (early + (quarter // 2) * late) + odd * (
                chunks + late * (1 + quarter // 2)
            ) + i
            for side_ in range(2):
                cols = slice(side_ * half, (side_ + 1) * half)
                for p in range(3):
                    lines = slice(LANES * p + HEAD_DIM * h, LANES * p + HEAD_DIM * (h + 1))
                    g[base, side_, HEAD_DIM * p : HEAD_DIM * (p + 1), :] = grads[lines, cols]
                g[base, side_, 3 * HEAD_DIM :, :] = grads_out[
                    HEAD_DIM * h : HEAD_DIM * (h + 1), cols
                ]

            @pl.when(odd == 1)
            def _():
                core_copy(1 - quarter // 2, i, g.at[base]).start()

    @pl.when(t == pairs)
    def _():
        left = {
            event: sorted(set(range(done if event == send_y else 0, chunks)) - {k for table in tables for k in table.values()})
            for event, tables in schedule
        }

        def rest(event):
            for k in left[event]:
                event(k)

        rest(send_y)
        rest(send_x)
        norm_one()
        rest(send_z)
        small_y()
        rest(send_back)
        small_x()
        rest(send_back_x)
        small_z()
        rest(finish)
        small_end()

        @pl.loop(0, chunks)
        def _(k):
            x_copy(k).wait_send()
            for o in range(1, others):
                z_copy(k, o).wait_send()
                a_copy(k, o).wait_send()
            xa_copy(k).wait_send()
            for i in range(2):
                out_copies(k, i, lambda copy: copy.wait())

        for k in range(done, chunks):
            y_copy(k, g.at[0]).wait_send()
        for which in range(2):
            for i in range(late):
                core_copy(which, i, g.at[0]).wait_send()
        for i, device in enumerate((to_core, to_core, to_y, to_x)):
            sv_copy(i, sv.at[0], device).wait_send()
        for o in range(1, others):
            svz_copy(o).wait_send()


def attn_bwd(
    n, db, qkv, att, lse, weights, qh, kn, x, d_resid, vec, g_bias, c_sum, branch_sum, gain_two_sum,
    sum_y, sum_own, got, rows, group
):
    tokens, model = n.shape
    stored = x.shape[1]
    pairs = qkv.shape[0]
    early, late = sum_y.shape[0], pairs // 2
    chunks = early + late
    others = group // 2
    wide = model // 2
    lines = 16

    def of(shape):
        return pl.BlockSpec((None, *shape), lambda p: (jnp.maximum(pairs - 1 - p, 0), 0, 0))

    def unit(h):
        def at(p):
            u = 2 * jnp.maximum(pairs - 1 - p, 0) + h
            return u // late, u % late, 0, 0

        return pl.BlockSpec((None, None, CHUNK, model), at)

    anywhere = pl.BlockSpec(memory_space=pl.ANY)
    sems = pltpu.SemaphoreType.DMA
    between = max(others - 1, 1)
    many = (chunks, between)
    return pl.pallas_call(
        functools.partial(bwd_kernel, rows=rows, pairs=pairs, group=group),
        grid=(pairs + 1,),
        in_specs=[
            once((tokens, model)), once((tokens, model)), of((tokens, 3 * LANES)),
            of((tokens, LANES)), of((2, tokens)), unit(0), unit(1),
            once((tokens, LANES)), once((tokens, LANES)), once((tokens, stored)),
            once((tokens, model)), full(vec.shape), full(g_bias.shape),
            full((1, model)), full((1, model)), full((1, model)),
            anywhere, anywhere, anywhere,
        ],
        out_specs=[once((tokens, stored)), anywhere, anywhere, anywhere, once((lines, model))],
        out_shape=[
            jax.ShapeDtypeStruct((tokens, stored), BF16),
            jax.ShapeDtypeStruct((early, CHUNK, model), BF16),
            jax.ShapeDtypeStruct((3, late * HEAD_DIM, model), BF16),
            jax.ShapeDtypeStruct((late * HEAD_DIM, model), BF16),
            jax.ShapeDtypeStruct((lines, model), F32),
        ],
        scratch_shapes=[
            pltpu.VMEM((3 * LANES, model), BF16),
            pltpu.VMEM((LANES, model), BF16),
            pltpu.VMEM((tokens, LANES), BF16),
            pltpu.VMEM((tokens, 3 * LANES), BF16),
            pltpu.VMEM((tokens, LANES), F32),
            pltpu.VMEM((tokens, LANES), F32),
            pltpu.VMEM((tokens, model), F32),
            pltpu.VMEM((CHUNK, model), F32),
            pltpu.VMEM((chunks + 3 * late, 2, CHUNK, wide), BF16),
            pltpu.VMEM((2, late, 2, CHUNK, wide), BF16),
            pltpu.VMEM((chunks, 2, CHUNK, wide), BF16),
            pltpu.VMEM((chunks, CHUNK, wide), BF16),
            pltpu.VMEM((*many, CHUNK // others, wide), BF16),
            pltpu.VMEM((chunks, CHUNK, wide), BF16),
            pltpu.VMEM((chunks, CHUNK, wide), BF16),
            pltpu.VMEM((4, lines, model), F32),
            pltpu.VMEM((4, lines, model), F32),
            pltpu.VMEM((others, lines, model), F32),
            sems((2, late)), sems((2, late)), sems((chunks,)), sems((chunks,)),
            sems((chunks,)), sems((chunks,)), sems(many), sems(many), sems(many), sems(many),
            sems((chunks,)), sems((chunks,)), sems((early,)), sems((got.shape[0],)),
            sems((chunks, 2, 4)), sems((4,)), sems((4,)), sems((between,)), sems((between,)),
        ],
        compiler_params=params(60, collective_id=0, has_side_effects=True),
        name="attn_bwd",
    )(
        n, db, qkv, att, lse, weights, weights, qh, kn, x, d_resid, vec, g_bias, c_sum, branch_sum,
        gain_two_sum, sum_y, sum_own, got,
    )


def solution(mesh):
    n_dp, n_tensor = mesh.shape["dp"], mesh.shape["tensor"]
    assert n_tensor == 4 and n_dp % 4 == 0 and n_dp & (n_dp - 1) == 0
    bits = [1 << i for i in range(n_dp.bit_length() - 1)]
    group = min(n_dp, 8)

    def to_dp(v, bit):
        return lax.ppermute(v, "dp", [(i, i ^ bit) for i in range(n_dp)])

    def local(
        layer_input, segments, cotangent, gain_one, w_qkv, b_qv, w_out, b_out, gain_two,
        w_up, b_up, w_down, b_down,
    ):
        rows = segments.shape[0]
        tokens, stored = layer_input.shape
        model = stored + 1
        heads = w_qkv.shape[2] // HEAD_DIM
        units = w_up.shape[1]

        vec = [gain_one, gain_two, b_out, b_down, b_up, *b_qv]
        vec = jnp.concatenate([jnp.pad(v.astype(F32), (0, 1024 - v.shape[0])) for v in vec])
        vec = jnp.pad(vec, (0, 1024)).reshape(8, 1024)
        (
            n_one, cot, grad_bdown, qkv, att, lse, resid, n_two, qh, kn, w_attn, w_ffn, misc
        ) = forward(
            layer_input, cotangent, w_qkv.transpose(0, 2, 1), w_out, w_up, w_down, vec, segments
        )
        (
            sum_y, sum_own, got, g_bias, output, d_resid, d_branch, grad_gain_two, grad_bout
        ) = ffn(n_two, cot, resid, w_ffn, misc, vec, stored, 3)

        input_grad, *reduced, small = attn_bwd(
            n_one, d_branch, qkv, att, lse, w_attn, qh, kn, layer_input, d_resid, vec, g_bias,
            grad_bdown, grad_bout, grad_gain_two, sum_y, sum_own, got, rows, group,
        )
        for bit in bits:
            if bit >= group:
                small = small + to_dp(small, bit)
                reduced = [(v.astype(F32) + to_dp(v, bit).astype(F32)).astype(BF16) for v in reduced]
        grad_ffn, grad_qkv, grad_out = reduced
        grad_up, grad_down = grad_ffn.reshape(2, model, units)
        grad_up = grad_up[:stored].astype(F32)
        grad_down = grad_down.T[:, :stored].astype(F32)
        grad_qkv = grad_qkv[..., :stored].astype(F32).transpose(0, 2, 1)
        grad_out = grad_out[:, :stored].astype(F32)
        per_head = small[8 : 8 + heads]
        grad_bqv = jnp.stack(
            [per_head[:, :HEAD_DIM].reshape(-1), per_head[:, 2 * LANES : 2 * LANES + HEAD_DIM].reshape(-1)]
        )
        return (
            output,
            input_grad,
            small[4, :stored],
            grad_qkv,
            grad_bqv,
            grad_out,
            small[2, :stored],
            small[3, :stored],
            grad_up,
            small[0],
            grad_down,
            small[1, :stored],
        )

    return jax.shard_map(
        local,
        mesh=mesh,
        in_specs=(
            P(("dp", "tensor"), None),
            P(("dp", "tensor"), None),
            P(("dp", "tensor"), None),
            P(),
            P(None, None, "tensor"),
            P(None, "tensor"),
            P("tensor", None),
            P(),
            P(),
            P(None, "tensor"),
            P("tensor"),
            P("tensor", None),
            P(),
        ),
        out_specs=(
            P(("dp", "tensor"), None),
            P(("dp", "tensor"), None),
            P(),
            P(None, None, "tensor"),
            P(None, "tensor"),
            P("tensor", None),
            P(),
            P(),
            P(None, "tensor"),
            P("tensor"),
            P("tensor", None),
            P(),
        ),
        check_vma=False,
    )
```

```python
import functools

import jax
import jax.numpy as jnp
from jax import lax
from jax.experimental import pallas as pl
from jax.experimental.pallas import tpu as pltpu
from jax.sharding import PartitionSpec as P

HEAD_DIM = 64
LANES = 128
EPSILON = 1e-05
MASKED_SCORE = -1e30
LONGEST = 512
BLOCK = 256
CHUNK = 256
F32 = jnp.float32
BF16 = jnp.bfloat16
NN = (((1,), (0,)), ((), ()))
NT = (((1,), (1,)), ((), ()))
TN = (((0,), (0,)), ((), ()))
GELU_A = 0.7978845608028654
GELU_B = 0.044715
MIB = 1024 * 1024
MESH = pl.DeviceIdType.MESH


def dot(a, b, dims=NN):
    return lax.dot_general(a, b, dims, preferred_element_type=F32)


def params(mib, **more):
    return pltpu.CompilerParams(vmem_limit_bytes=mib * MIB, **more)


def full(shape):
    return pl.BlockSpec(shape, lambda *_: (0,) * len(shape))


def once(shape):
    return pl.BlockSpec(shape, lambda *_: (0,) * len(shape), pipeline_mode=pl.Buffered(1))


def widen(ref, wide):
    wide[:, wide.shape[1] - LANES :] = jnp.zeros((wide.shape[0], LANES), F32)
    wide[:, : ref.shape[1]] = ref[...].astype(F32)
    return wide[...]


def norm_scale(values):
    total = jnp.sum(values, axis=-1, keepdims=True)
    square = jnp.sum(values * values, axis=-1, keepdims=True)
    return lax.rsqrt((square + total * total) / values.shape[-1] + EPSILON), total


def norm_back(values, gain, upstream):
    scale, total = norm_scale(values)
    weighted = upstream * values
    spread = jnp.sum(weighted * gain, axis=-1, keepdims=True)
    grad = upstream * gain * scale - (spread * scale * scale * scale / values.shape[-1]) * (
        values + total
    )
    return grad, jnp.sum(weighted * scale, axis=0, keepdims=True)


def scores_of(q_ref, k_ref, qh_ref, kn_ref, sel, at, span):
    q = q_ref[at, :] * 0.125
    qa = jnp.where(sel, q, qh_ref[at, :])
    ka = jnp.where(sel, k_ref[span, :], kn_ref[span, :])
    s = dot(ka, qa, NT)
    causal = lax.broadcasted_iota(jnp.int32, (BLOCK, BLOCK), 0) <= lax.broadcasted_iota(
        jnp.int32, (BLOCK, BLOCK), 1
    )
    early = s.shape[0] - BLOCK
    tail = jnp.where(causal, s[early:, :], MASKED_SCORE)
    return (tail if early == 0 else jnp.concatenate([s[:early, :], tail], axis=0)), q


def spans(length, row):
    for end in range(BLOCK, length + 1, BLOCK):
        start = max(0, end - BLOCK - LONGEST)
        base = row * length
        yield slice(base + end - BLOCK, base + end), slice(base + start, base + end)


def remote(src, dst, send, recv, device):
    return pltpu.make_async_remote_copy(
        src_ref=src, dst_ref=dst, send_sem=send, recv_sem=recv, device_id=device,
        device_id_type=MESH,
    )


def greet(partners):
    barrier = pltpu.get_barrier_semaphore()
    for device in partners:
        pl.semaphore_signal(barrier, inc=1, device_id=device, device_id_type=MESH)
    pl.semaphore_wait(barrier, len(partners))


def neighbours():
    dp, tensor = lax.axis_index("dp"), lax.axis_index("tensor")
    side = dp % 2
    to_core = (dp, tensor + 1 - 2 * (tensor % 2))
    return to_core, (dp, (tensor + 2) % 4), (dp + 1 - 2 * side, tensor), side


def pair_weights(even, odd, w, wo):
    for h, unit in enumerate((even, odd)):
        for i in range(3):
            at = LANES * i + HEAD_DIM * h
            w[at : at + HEAD_DIM, :] = unit[HEAD_DIM * i : HEAD_DIM * (i + 1), :]
        wo[HEAD_DIM * h : HEAD_DIM * (h + 1), :] = unit[3 * HEAD_DIM :, :]


def fwd_kernel(
    x_ref, c_ref, wqkv_ref, wout_ref, up_ref, down_ref, vec_ref, seg_ref,
    n_ref, cot_ref, c_sum_ref, qkv_ref, att_ref, lse_ref, resid_ref, n_two_ref, qh_ref, kn_ref,
    wa_ref, wf_ref, misc_all_ref,
    wa, stage, misc, w, wo, branch, wide,
    core_s, core_r, y_s, y_r, x_s, x_r, d_s, d_r, local_s, z_s, z_r, zz_s, zz_r,
    *, rows, pairs
):
    t = pl.program_id(0)
    tokens = x_ref.shape[0]
    length = tokens // rows
    heads = pairs // 2
    stored = x_ref.shape[1]
    model = stored + 1
    early, tail = heads, stage.shape[0]
    to_core, to_y, to_x, side = neighbours()
    last = early + tail
    dp = lax.axis_index("dp")
    level = dp // 2 % 2
    to_z = (dp + 2 - 4 * level, lax.axis_index("tensor"))

    def rows_of(k, across, along):
        if k < early:
            return pl.ds(pl.multiple_of(across * (CHUNK // 2), CHUNK // 2), CHUNK // 2)
        size = CHUNK // 4
        return pl.ds(pl.multiple_of((2 * across + along) * size, size), size)

    def held(quarter, k):
        if k == last:
            return misc.at[quarter]
        if k < early:
            return wa.at[quarter, k]
        return wf_ref.at[quarter, k - early]

    def own(k):
        return held(0, k) if k < early or k == last else stage.at[k - early]

    def core_copy(k):
        return remote(own(k), held(1, k), core_s.at[k], core_r.at[k], to_core)

    def y_copy(k):
        src, dst = own(k), held(2, k)
        if k < last:
            rows_ = rows_of(k, side, level)
            src, dst = src.at[rows_], dst.at[rows_]
        return remote(src, dst, y_s.at[k], y_r.at[k], to_y)

    def spread(k, across, along, send, recv, device):
        ref = held(2, k).at[rows_of(k, across, along)]
        return remote(ref, ref, send.at[k], recv.at[k], device)

    def x_copy(k, across):
        return spread(k, across, level, x_s, x_r, to_x)

    def z_copy(k, along):
        return spread(k, side, along, z_s, z_r, to_z)

    def zz_copy(k, along):
        return spread(k, 1 - side, along, zz_s, zz_r, to_z)

    def d_copy(k):
        return remote(held(2, k), held(3, k), d_s.at[k], d_r.at[k], to_core)

    def keep_copy(k):
        if k == last:
            return pltpu.make_async_copy(misc, misc_all_ref, local_s.at[k])
        if k < early:
            return pltpu.make_async_copy(wa.at[:, k], wa_ref.at[:, k], local_s.at[k])
        return pltpu.make_async_copy(stage.at[k - early], wf_ref.at[0, k - early], local_s.at[k])

    def x_on(k):
        y_copy(k).wait_recv()
        x_copy(k, side).start()
        if k >= early:
            z_copy(k, level).start()

    def z_on(k):
        x_copy(k, 1 - side).wait_recv()
        zz_copy(k, level).start()

    def d_on(k):
        if k == last:
            y_copy(k).wait_recv()
        elif k < early:
            x_copy(k, 1 - side).wait_recv()
        else:
            z_copy(k, 1 - level).wait_recv()
            zz_copy(k, 1 - level).wait_recv()
        d_copy(k).start()

    def start_y(k):
        y_copy(k).start()

    def start_core(k):
        core_copy(k).start()

    @pl.when(t == 0)
    def _():
        edge = slice(model - LANES, model)
        wa[0, :, :, edge] = jnp.zeros((early, CHUNK, LANES), BF16)
        for j in range(heads):
            head = slice(HEAD_DIM * j, HEAD_DIM * (j + 1))
            for i in range(3):
                wa[0, j, HEAD_DIM * i : HEAD_DIM * (i + 1), :stored] = wqkv_ref[i, head, :]
            wa[0, j, 3 * HEAD_DIM :, :stored] = wout_ref[head, :]
        misc[...] = jnp.zeros_like(misc)
        for p in range(2):
            for j in range(heads):
                for i, row in ((0, 5), (2, 6)):
                    at = LANES * i + HEAD_DIM * p
                    misc[0, j, p, :1, at : at + HEAD_DIM] = vec_ref[
                        row : row + 1, HEAD_DIM * j : HEAD_DIM * (j + 1)
                    ]
            units_half = misc.shape[4]
            misc[0, heads, p, :1, :] = vec_ref[4:5, units_half * p : units_half * (p + 1)]
        greet([to_core, to_y, to_x, to_z])
        for k in (last, 0):
            core_copy(k).start()
            y_copy(k).start()
        for k in range(1, early):
            core_copy(k).start()
        count = tail // 2
        stage[:, :, edge] = jnp.zeros((tail, CHUNK, LANES), BF16)
        stage[count - 1, CHUNK - 16 :, :] = jnp.zeros((16, model), BF16)
        for i in range(count):
            end = min(CHUNK * (i + 1), stored)
            stage[i, : end - CHUNK * i, :] = up_ref[CHUNK * i : end, :]
            stage[count + i, :, :stored] = down_ref[CHUNK * i : CHUNK * (i + 1), :]
        for k in range(early, last):
            keep_copy(k).start()
        branch[...] = jnp.zeros_like(branch)
        c_sum = jnp.zeros((1, model), F32)
        for i in range(0, tokens, CHUNK):
            r = slice(i, i + CHUNK)
            x = widen(x_ref.at[r, :], wide)
            n_ref[r, :] = (x * norm_scale(x)[0] * vec_ref[0:1, :model]).astype(BF16)
            c = widen(c_ref.at[r, :], wide)
            cot_ref[r, :] = c.astype(BF16)
            c_sum += jnp.sum(c, axis=0, keepdims=True)
        c_sum_ref[...] = c_sum
        lane = lax.broadcasted_iota(jnp.int32, (1, LANES), 1) % HEAD_DIM
        for row in range(rows):
            document = jnp.broadcast_to(seg_ref[row : row + 1, :].astype(F32), (LANES, length)).T
            hot = document == lane.astype(F32)
            r = slice(row * length, (row + 1) * length)
            qh_ref[r, :] = jnp.where(hot, 1.0, 0.0).astype(BF16)
            kn_ref[r, :] = jnp.where(hot | (lane >= 8), 0.0, MASKED_SCORE).astype(BF16)
        core_copy(last).wait_recv()

    events = {
        (0, 0): [(start_y, 1)], (0, 2): [(d_on, last)], (0, 3): [(x_on, 0)], (0, 4): [(start_y, 2)],
        (1, 2): [(x_on, 1)], (1, 4): [(start_y, early), (start_core, early), (start_core, early + 1)],
        (2, 1): [(d_on, 0), (x_on, 2), (start_y, early + 1)],
        (2, 3): [(start_y, early + 2), (start_core, early + 2), (start_core, early + 3)],
        (2, 4): [(d_on, 1)],
        (3, 0): [(x_on, early), (start_y, early + 3)],
        (3, 1): [(x_on, early + 1)],
        (3, 2): [(start_y, early + 4), (start_core, early + 4), (start_core, early + 5)],
        (3, 3): [(d_on, 2), (x_on, early + 2)],
        (3, 4): [(start_y, early + 5), (z_on, early)],
        (4, 0): [(x_on, early + 3), (z_on, early + 1)],
        (4, 2): [(x_on, early + 4), (z_on, early + 2)],
        (4, 3): [(d_on, early)],
        (4, 4): [(x_on, early + 5), (z_on, early + 3)],
        (5, 1): [(z_on, early + 4), (d_on, early + 1)],
        (5, 3): [(z_on, early + 5), (d_on, early + 2)],
    }

    def run(slot):
        for (step, at), todo in events.items():
            if at == slot and todo:

                @pl.when(t == step)
                def _(todo=todo):
                    for event, k in todo:
                        event(k)

    for step in range(pairs):

        @pl.when(t == step)
        def _(far=step // heads, j=step % heads):
            (d_copy if far else core_copy)(j).wait_recv()
            if far and j == 0:
                d_copy(last).wait_recv()

    first = lax.broadcasted_iota(jnp.int32, (1, LANES), 1) < HEAD_DIM
    units = [(2 * (t // heads) + h, t % heads) for h in range(2)]
    pair_weights(*(wa.at[quarter, j] for quarter, j in units), w, wo)
    bias = sum(misc[quarter, j, h, :1, :] for h, (quarter, j) in enumerate(units))
    qkv_ref[...] = (dot(n_ref[...], w[...], NT) + bias).astype(BF16)
    q_ref, k_ref, v_ref = (qkv_ref.at[:, j * LANES : (j + 1) * LANES] for j in range(3))
    run(0)
    slot = 1
    for row in range(rows):
        for at, span in spans(length, row):
            parts = []
            for h in range(2):
                sel = first if h == 0 else ~first
                s, _ = scores_of(q_ref, k_ref, qh_ref, kn_ref, sel, at, span)
                m = jnp.max(s, axis=0, keepdims=True)
                p = jnp.exp(s - m)
                total = jnp.sum(p, axis=0, keepdims=True)
                weights = (p * (1.0 / total)).astype(BF16)
                parts.append(dot(weights, v_ref[span, :], TN))
                lse_ref[h : h + 1, at] = m + jnp.log(total)
            att_ref[at, :] = jnp.where(first, parts[0], parts[1]).astype(BF16)
            if slot < 4:
                run(slot)
                slot += 1
    branch[...] += dot(att_ref[...], wo[...])
    run(4)

    @pl.when(t == pairs - 1)
    def _():
        for i in range(0, tokens, CHUNK):
            r = slice(i, i + CHUNK)
            resid = widen(x_ref.at[r, :], wide) + (branch[r, :] + vec_ref[2:3, :model])
            resid_ref[r, :] = resid
            n_two_ref[r, :] = (resid * norm_scale(resid)[0] * vec_ref[1:2, :model]).astype(BF16)
        for k in range(early + 3, last):
            d_on(k)
        for k in (*range(early), last):
            keep_copy(k).start()
        for k in range(early, last):
            core_copy(k).wait_recv()
            d_copy(k).wait_recv()
        for k in range(last + 1):
            core_copy(k).wait_send()
            y_copy(k).wait_send()
            if k < last:
                x_copy(k, side).wait_send()
            if early <= k < last:
                z_copy(k, level).wait_send()
                zz_copy(k, level).wait_send()
            d_copy(k).wait_send()
            keep_copy(k).wait()


def forward(x, c, wqkv, wout, up, down, vec, seg):
    tokens, stored = x.shape
    model = stored + 1
    heads = wqkv.shape[1] // HEAD_DIM
    pairs = 2 * heads
    tail = 2 * (model // CHUNK)

    def of(*shape):
        return pl.BlockSpec((None, *shape), lambda p: (p,) + (0,) * len(shape))

    anywhere = pl.BlockSpec(memory_space=pl.ANY)
    sems = pltpu.SemaphoreType.DMA((heads + tail + 1,))
    rows = seg.shape[0]
    misc = (heads + 1, 2, 8, model // 2)
    inputs = [x, c, wqkv, wout, up, down, vec, seg]
    big = once((tokens, model))
    outs = [
        (big, (tokens, model), BF16),
        (big, (tokens, model), BF16),
        (once((1, model)), (1, model), F32),
        (of(tokens, 3 * LANES), (pairs, tokens, 3 * LANES), BF16),
        (of(tokens, LANES), (pairs, tokens, LANES), BF16),
        (of(2, tokens), (pairs, 2, tokens), F32),
        (big, (tokens, model), F32),
        (big, (tokens, model), BF16),
        (once((tokens, LANES)), (tokens, LANES), BF16),
        (once((tokens, LANES)), (tokens, LANES), BF16),
        (anywhere, (4, heads, CHUNK, model), BF16),
        (anywhere, (4, tail, CHUNK, model), BF16),
        (anywhere, (4, *misc), F32),
    ]
    return pl.pallas_call(
        functools.partial(fwd_kernel, rows=rows, pairs=pairs),
        grid=(pairs,),
        in_specs=[once(v.shape) for v in inputs],
        out_specs=[spec for spec, _, _ in outs],
        out_shape=[jax.ShapeDtypeStruct(shape, dtype) for _, shape, dtype in outs],
        scratch_shapes=[
            pltpu.VMEM((4, heads, CHUNK, model), BF16),
            pltpu.VMEM((tail, CHUNK, model), BF16),
            pltpu.VMEM((4, *misc), F32),
            pltpu.VMEM((3 * LANES, model), BF16),
            pltpu.VMEM((LANES, model), BF16),
            pltpu.VMEM((tokens, model), F32),
            pltpu.VMEM((CHUNK, model), F32),
        ]
        + [sems] * 13,
        compiler_params=params(60, collective_id=1, has_side_effects=True),
        name="forward",
    )(*inputs)


def ffn_kernel(
    n_ref, c_ref, resid_ref, up_ref, down_ref, bias_ref, vec_ref,
    sum_y_ref, sum_own_ref, got_ref, gbias_ref, output_ref, d_resid_ref, d_branch_ref,
    gain_sum_ref, branch_sum_ref,
    out, back, nt, ct, g, core_in, core_s, core_r, y_s, y_r, out_s, *, chunk
):
    tokens = n_ref.shape[0]
    step, last = pl.program_id(0), pl.num_programs(0) - 1
    to_core, to_y, _, _ = neighbours()
    chunks, sent = core_in.shape[1], got_ref.shape[0]

    def core_copy(which, k):
        return remote(
            g.at[0, k], core_in.at[which, k], core_s.at[which, k], core_r.at[which, k], to_core
        )

    def y_copy(k):
        return remote(g.at[1, k], got_ref.at[k], y_s.at[k], y_r.at[k], to_y)

    def out_copy(which, k):
        dst = sum_own_ref if which else sum_y_ref
        return pltpu.make_async_copy(g.at[1 + which, k], dst.at[k], out_s.at[which, k])

    @pl.when(step == 0)
    def _():
        greet([to_core, to_y])
        out[...] = jnp.zeros_like(out)
        back[...] = jnp.zeros_like(back)
        for i in range(0, tokens, 256):
            nt[:, i : i + 256] = n_ref[i : i + 256, :].T
            ct[:, i : i + 256] = c_ref[i : i + 256, :].T

    model = n_ref.shape[1]
    up, down = (ref[...].reshape(-1, model) for ref in (up_ref, down_ref))
    bias = jnp.concatenate([bias_ref[h, :1, :] for h in range(2)], axis=1)
    gup = gdown = gbias = None
    for i in range(0, tokens, chunk):
        r = slice(i, i + chunk)
        pre = dot(n_ref[r, :], up) + bias
        dh = dot(c_ref[r, :], down, NT)
        sq = pre * pre
        th = jnp.tanh(pre * (GELU_A + (GELU_A * GELU_B) * sq))
        half = 0.5 + 0.5 * th
        hidden = (pre * half).astype(BF16)
        slope = half + (0.5 * pre) * (1.0 - th * th) * (GELU_A + (3.0 * GELU_A * GELU_B) * sq)
        dpre = (dh * slope).astype(BF16)
        out[r, :] += dot(hidden, down)
        back[r, :] += dot(dpre, up, NT)
        a, b = dot(nt[:, r], dpre), dot(ct[:, r], hidden)
        s = jnp.sum(dpre.astype(F32), axis=0, keepdims=True)
        gup, gdown, gbias = (a, b, s) if i == 0 else (gup + a, gdown + b, gbias + s)
    gbias_ref[...] = gbias

    @pl.when(step == 2)
    def _():
        for k in range(chunks):
            core_copy(0, k).wait_send()

    wide = g.shape[4]
    place = step % 2 * (1 + step // 2)
    for m, grad in enumerate((gup, gdown)):
        for i in range(chunks // 2):
            for h in range(2):
                at = slice(CHUNK * i, CHUNK * (i + 1)), slice(wide * h, wide * (h + 1))
                g[place, m * (chunks // 2) + i, h] = grad[at].astype(BF16)

    for which in range(2):

        @pl.when(step == 2 * which)
        def _(which=which):
            for k in range(chunks):
                core_copy(which, k).start()

        @pl.when(step == 2 * which + 1)
        def _(which=which):
            for k in range(chunks):
                core_copy(which, k).wait_recv()
                g[1 + which, k] = (
                    g[1 + which, k].astype(F32) + core_in[which, k].astype(F32)
                ).astype(BF16)
                if which == 0 and k < sent:
                    y_copy(k).start()
                else:
                    out_copy(which, k).start()

    @pl.when(step == last)
    def _():
        gain_sum_ref[...] = jnp.zeros_like(gain_sum_ref)
        branch_sum_ref[...] = jnp.zeros_like(branch_sum_ref)

        @pl.loop(0, tokens // 256)
        def _(i):
            r = pl.ds(pl.multiple_of(i * 256, 256), 256)
            resid = resid_ref[r, :]
            output = (resid + (out[r, :] + vec_ref[3:4, :model])).astype(BF16)
            output_ref[r, :] = output[:, : output_ref.shape[1]]
            d_norm, gain_sum = norm_back(resid, vec_ref[1:2, :model], back[r, :])
            d_resid = c_ref[r, :].astype(F32) + d_norm
            d_resid_ref[r, :] = d_resid
            d_branch = d_resid.astype(BF16)
            d_branch_ref[r, :] = d_branch
            gain_sum_ref[...] += gain_sum
            branch_sum_ref[...] += jnp.sum(d_branch.astype(F32), axis=0, keepdims=True)

        for k in range(chunks):
            core_copy(1, k).wait_send()
            out_copy(1, k).wait()
            if k < sent:
                y_copy(k).wait()
            else:
                out_copy(0, k).wait()


def ffn(n, c, resid, weights, misc, vec, stored, sent, chunk=512):
    tokens, model = n.shape
    count, entries, _, _, wide = misc.shape
    units = 2 * wide
    each = model // CHUNK

    def chunks(at):
        return pl.BlockSpec((None, each, CHUNK, model), lambda i: (count - 1 - i, at, 0, 0))

    line = pl.BlockSpec((None, 1, units), lambda i: (count - 1 - i, 0, 0))
    bias = pl.BlockSpec((None, None, 2, 8, wide), lambda i: (count - 1 - i, entries - 1, 0, 0, 0))
    anywhere = pl.BlockSpec(memory_space=pl.ANY)
    big, row = once((tokens, model)), full((1, model))
    sems = pltpu.SemaphoreType.DMA
    shape = jax.ShapeDtypeStruct
    return pl.pallas_call(
        functools.partial(ffn_kernel, chunk=chunk),
        grid=(count,),
        in_specs=[big, big, big, chunks(0), chunks(1), bias, full(vec.shape)],
        out_specs=[anywhere] * 3 + [line, once((tokens, stored)), big, big, row, row],
        out_shape=[
            shape((2 * each, 2, CHUNK, wide), BF16),
            shape((2 * each, 2, CHUNK, wide), BF16),
            shape((sent, 2, CHUNK, wide), BF16),
            shape((count, 1, units), F32),
            shape((tokens, stored), BF16),
            shape((tokens, model), F32),
            shape((tokens, model), BF16),
            shape((1, model), F32),
            shape((1, model), F32),
        ],
        scratch_shapes=[pltpu.VMEM((tokens, model), F32)] * 2
        + [pltpu.VMEM((model, tokens), BF16)] * 2
        + [
            pltpu.VMEM((3, 2 * each, 2, CHUNK, wide), BF16),
            pltpu.VMEM((2, 2 * each, 2, CHUNK, wide), BF16),
            sems((2, 2 * each)), sems((2, 2 * each)), sems((sent,)), sems((sent,)),
            sems((2, 2 * each)),
        ],
        compiler_params=params(62, collective_id=2, has_side_effects=True),
        name="ffn",
    )(n, c, resid, weights, weights, misc, vec)


def bwd_kernel(
    n_ref, db_ref, qkv_ref, att_ref, lse_ref, even_ref, odd_ref, qh_ref, kn_ref, x_ref, d_resid_ref,
    vec_ref, gbias_ref, c_sum_ref, branch_sum_ref, gain_two_sum_ref, sum_y_ref, sum_own_ref, got_ref,
    grad_in_ref, red_ref, red_qkv_ref, red_out_ref, total_ref,
    w, wo, da, dqkv, dk_acc, dv_acc, back, wide_x, g, core_in, y_in, x_in, z_in, ag, xag_in,
    sv, sv_in, sv_z,
    core_s, core_r, y_s, y_r, x_s, x_r, z_s, z_r, a_s, a_r, xa_s, xa_r, load_s, got_s, out_s,
    sv_s, sv_r, svz_s, svz_r,
    *, rows, pairs, group
):
    t = pl.program_id(0)
    tokens = n_ref.shape[0]
    length = tokens // rows
    early, done, late = sum_y_ref.shape[0], got_ref.shape[0], pairs // 2
    chunks = early + late
    others = group // 2
    keep = CHUNK // others
    half = g.shape[3]
    dp, tensor = lax.axis_index("dp"), lax.axis_index("tensor")
    place = (dp % group) // 2
    mine = pl.ds(pl.multiple_of(place * keep, keep), keep)
    to_core, to_y, to_x, side = neighbours()

    def place_of(o):
        return (place + o) % others

    def to_z(o):
        return (dp - dp % group + place_of(o) * 2 + side, tensor)

    def late_at(which, k):
        return chunks + late * which + k - early

    def core_copy(which, i, src):
        return remote(src, core_in.at[which, i], core_s.at[which, i], core_r.at[which, i], to_core)

    def y_copy(k, src):
        return remote(src, y_in.at[k], y_s.at[k], y_r.at[k], to_y)

    def x_copy(k):
        return remote(g.at[k, 1 - side], x_in.at[k], x_s.at[k], x_r.at[k], to_x)

    def z_copy(k, o):
        rows_of = pl.ds(pl.multiple_of(place_of(o) * keep, keep), keep)
        return remote(
            g.at[k, side, rows_of], z_in.at[k, o - 1], z_s.at[k, o - 1], z_r.at[k, o - 1], to_z(o)
        )

    def a_copy(k, o):
        return remote(ag.at[k, mine], ag.at[k, mine], a_s.at[k, o - 1], a_r.at[k, o - 1], to_z(o))

    def a_wait(k, o):
        rows_of = pl.ds(pl.multiple_of(place_of(others - o) * keep, keep), keep)
        part = ag.at[k, rows_of]
        remote(part, part, a_s.at[k, o - 1], a_r.at[k, o - 1], to_z(o)).wait_recv()

    def xa_copy(k):
        return remote(ag.at[k], xag_in.at[k], xa_s.at[k], xa_r.at[k], to_x)

    def out_copies(k, i, act):
        cols = pl.ds(pl.multiple_of((side + i - 2 * side * i) * half, LANES), half)
        src = xag_in if i else ag

        @pl.when(k < early)
        def _():
            at = jnp.minimum(k, early - 1)
            act(pltpu.make_async_copy(src.at[at], red_ref.at[at, :, cols], out_s.at[k, i, 0]))

        @pl.when(k >= early)
        def _():
            at = jnp.maximum(k, early)
            j = chunks - 1 - at
            head = pl.ds(pl.multiple_of(j * HEAD_DIM, HEAD_DIM), HEAD_DIM)
            for p in range(4):
                part = src.at[at, HEAD_DIM * p : HEAD_DIM * (p + 1)]
                dst = red_out_ref.at[head, cols] if p == 3 else red_qkv_ref.at[p, head, cols]
                act(pltpu.make_async_copy(part, dst, out_s.at[k, i, p]))

    def load(k):
        return pltpu.make_async_copy(sum_own_ref.at[k], g.at[k], load_s.at[k])

    def got(k):
        return pltpu.make_async_copy(got_ref.at[k], y_in.at[k], got_s.at[k])

    def send_y(k):
        @pl.when(k < early)
        def _():
            y_copy(k, sum_y_ref.at[jnp.minimum(k, early - 1)]).start()

        @pl.when(k >= early)
        def _():
            at = jnp.maximum(k, early)
            core_copy(0, at - early, g.at[0]).wait_recv()
            i = late_at(0, at)
            g[i] = (g[i].astype(F32) + core_in[0, at - early].astype(F32)).astype(BF16)
            y_copy(at, g.at[i]).start()

    def send_x(k):
        @pl.when(k < early)
        def _():
            load(jnp.minimum(k, early - 1)).wait()

        @pl.when(k >= early)
        def _():
            at = jnp.maximum(k, early)
            core_copy(1, at - early, g.at[0]).wait_recv()
            g[at] = (g[at].astype(F32) + core_in[1, at - early].astype(F32)).astype(BF16)

        @pl.when(k < done)
        def _():
            got(jnp.minimum(k, done - 1)).wait()

        @pl.when(k >= done)
        def _():
            y_copy(jnp.maximum(k, done), g.at[0]).wait_recv()

        g[k] = (g[k].astype(F32) + y_in[k].astype(F32)).astype(BF16)
        x_copy(k).start()

    def send_z(k):
        x_copy(k).wait_recv()
        g[k, side] = (g[k, side].astype(F32) + x_in[k].astype(F32)).astype(BF16)
        for o in range(1, others):
            z_copy(k, o).start()

    def send_back(k):
        total = g[k, side, mine].astype(F32)
        for o in range(1, others):
            z_copy(k, o).wait_recv()
            total += z_in[k, o - 1].astype(F32)
        ag[k, mine] = total.astype(BF16)
        for o in range(1, others):
            a_copy(k, o).start()

    def send_back_x(k):
        for o in range(1, others):
            a_wait(k, o)
        xa_copy(k).start()
        out_copies(k, 0, lambda copy: copy.start())

    def finish(k):
        xa_copy(k).wait_recv()
        out_copies(k, 1, lambda copy: copy.start())

    times = [(0, 0), (0, 4), (1, 3), (2, 2), (3, 1), (4, 0), (4, 4), (5, 3)]
    stages = [finish, send_back_x, send_back, send_z, send_x]
    schedule = [
        (
            event,
            [
                {step: i - lag for i, (step, at) in enumerate(times) if at == slot and i >= lag}
                for slot in range(5)
            ],
        )
        for lag, event in zip((4, 3, 2, 1, 0), stages)
    ]
    schedule.append((send_y, [{0: 2, 5: 8}, {4: 7}, {3: 6}, {2: 5}, {0: 3, 1: 4}]))

    def run(slot):
        for event, tables in schedule:
            table = tables[slot]
            if table:
                k = jnp.int32(-1)
                for step, at in table.items():
                    k = jnp.where(t == step, at, k)

                @pl.when(k >= 0)
                def _(event=event, k=k):
                    event(jnp.maximum(k, 0))

    def sv_copy(i, src, device):
        return remote(src, sv_in.at[i], sv_s.at[i], sv_r.at[i], device)

    def svz_copy(o):
        return remote(sv_z.at[place], sv_z.at[place], svz_s.at[o - 1], svz_r.at[o - 1], to_z(o))

    def small_y():
        for i in (0, 1):
            sv_copy(i, sv.at[3 - 2 * i], to_core).wait_recv()
        sv[2] += sv_in[0]
        sv_copy(2, sv.at[2], to_y).start()

    def small_x():
        sv_copy(2, sv.at[2], to_y).wait_recv()
        sv[0] = (sv[0] + sv_in[1]) + sv_in[2]
        sv_copy(3, sv.at[0], to_x).start()

    def small_z():
        sv_copy(3, sv.at[0], to_x).wait_recv()
        sv_z[place] = sv[0] + sv_in[3]
        for o in range(1, others):
            svz_copy(o).start()

    def small_end():
        for o in range(1, others):
            part = sv_z.at[place_of(others - o)]
            remote(part, part, svz_s.at[o - 1], svz_r.at[o - 1], to_z(o)).wait_recv()
        total = sv_z[0]
        for i in range(1, others):
            total += sv_z[i]
        total_ref[...] = total

    def norm_one():
        gain_sum = jnp.zeros((1, n_ref.shape[1]), F32)
        for i in range(0, tokens, CHUNK):
            r = slice(i, i + CHUNK)
            d_norm, part = norm_back(widen(x_ref.at[r, :], wide_x), vec_ref[0:1, : n_ref.shape[1]], back[r, :])
            grad = (d_resid_ref[r, :] + d_norm).astype(BF16)
            grad_in_ref[r, :] = grad[:, : grad_in_ref.shape[1]]
            gain_sum += part
        for i in range(4):
            sv[i, 4:5, :] = gain_sum
        for i in (0, 1):
            sv_copy(i, sv.at[3 - 2 * i], to_core).start()

    first = lax.broadcasted_iota(jnp.int32, (1, LANES), 1) < HEAD_DIM
    zero = jnp.zeros((), BF16)
    q_ref, k_ref, v_ref = (qkv_ref.at[:, j * LANES : (j + 1) * LANES] for j in range(3))

    def attend(at, span):
        dq = None
        for h in range(2):
            sel = first if h == 0 else ~first
            s, q = scores_of(q_ref, k_ref, qh_ref, kn_ref, sel, at, span)
            qm = jnp.where(sel, q, zero)
            km = jnp.where(sel, k_ref[span, :], zero)
            dom = jnp.where(sel, da[at, :], zero)
            p = jnp.exp(s - lse_ref[h : h + 1, at])
            dp_ = dot(v_ref[span, :], dom, NT)
            u = p * dp_
            inner = jnp.sum(u, axis=0, keepdims=True)
            ds = (u - p * inner).astype(BF16)
            dv_acc[span, :] += dot(p.astype(BF16), dom)
            dk_acc[span, :] += dot(ds, qm)
            part = dot(ds, km, TN)
            dq = part if dq is None else dq + part
        dqkv[at, :LANES] = (dq * 0.125).astype(BF16)

    @pl.when(t == 0)
    def _():
        greet([to_core, to_y, to_x] + [to_z(o) for o in range(1, others)])
        for k in range(early):
            load(k).start()
            if k < done:
                got(k).start()
        sv[...] = jnp.zeros_like(sv)
        sums = c_sum_ref, branch_sum_ref, gain_two_sum_ref
        for i in range(4):
            sv[i, 0:1, :] = gbias_ref[i]
            for j, ref in enumerate(sums):
                sv[i, 1 + j : 2 + j, :] = ref[...]
        back[...] = jnp.zeros_like(back)

    @pl.when(t < pairs)
    def _():
        pair_weights(even_ref, odd_ref, w, wo)
        da[...] = dot(db_ref[...], wo[...], NT).astype(BF16)
        dk_acc[...] = jnp.zeros_like(dk_acc)
        dv_acc[...] = jnp.zeros_like(dv_acc)
        run(0)
        slot = 1
        for row in range(rows):
            for at, span in spans(length, row):
                attend(at, span)
                if slot < 5:
                    run(slot)
                    slot += 1
        dqkv[:, LANES : 2 * LANES] = dk_acc[...].astype(BF16)
        dqkv[:, 2 * LANES :] = dv_acc[...].astype(BF16)
        sums = jnp.sum(dqkv[...].astype(F32), axis=0, keepdims=True)
        back[...] += dot(dqkv[...], w[...])
        grads = dot(dqkv[...], n_ref[...], TN).astype(BF16)
        grads_out = dot(att_ref[...], db_ref[...], TN).astype(BF16)
        for h in range(2):
            pair = pairs - 1 - t
            quarter, j = 2 * (pair // late) + h, pair % late
            for line in range(late):

                @pl.when(j == line)
                def _(line=8 + line, h=h):
                    for i in (0, 2):
                        part = sums[:, LANES * i + HEAD_DIM * h : LANES * i + HEAD_DIM * (h + 1)]
                        sv[quarter, line : line + 1, LANES * i : LANES * i + HEAD_DIM] = part

            i = late - 1 - j
            far = pair // late
            base = i + ((chunks + late * (1 + far)) if h else (early + late * far))
            for side_ in range(2):
                cols = slice(side_ * half, (side_ + 1) * half)
                for p in range(3):
                    lines = slice(LANES * p + HEAD_DIM * h, LANES * p + HEAD_DIM * (h + 1))
                    g[base, side_, HEAD_DIM * p : HEAD_DIM * (p + 1), :] = grads[lines, cols]
                g[base, side_, 3 * HEAD_DIM :, :] = grads_out[
                    HEAD_DIM * h : HEAD_DIM * (h + 1), cols
                ]

            if h:
                core_copy(1 - far, i, g.at[base]).start()

    @pl.when(t == pairs)
    def _():
        def go_on(i):
            for lag, event in zip((4, 3, 2, 1, 0), stages):
                if 0 <= i - lag < chunks:
                    event(i - lag)

        start = len(times)
        norm_one()
        go_on(start)
        small_y()
        go_on(start + 1)
        small_x()
        go_on(start + 2)
        small_z()
        go_on(start + 3)
        small_end()
        for i in range(start + 4, chunks + 4):
            go_on(i)

        @pl.loop(0, chunks)
        def _(k):
            x_copy(k).wait_send()
            for o in range(1, others):
                z_copy(k, o).wait_send()
                a_copy(k, o).wait_send()
            xa_copy(k).wait_send()
            for i in range(2):
                out_copies(k, i, lambda copy: copy.wait())

        for k in range(done, chunks):
            y_copy(k, g.at[0]).wait_send()
        for which in range(2):
            for i in range(late):
                core_copy(which, i, g.at[0]).wait_send()
        for i, device in enumerate((to_core, to_core, to_y, to_x)):
            sv_copy(i, sv.at[0], device).wait_send()
        for o in range(1, others):
            svz_copy(o).wait_send()


def attn_bwd(
    n, db, qkv, att, lse, weights, qh, kn, x, d_resid, vec, g_bias, c_sum, branch_sum, gain_two_sum,
    sum_y, sum_own, got, rows, group
):
    tokens, model = n.shape
    stored = x.shape[1]
    pairs = qkv.shape[0]
    early, late = sum_y.shape[0], pairs // 2
    chunks = early + late
    others = group // 2
    wide = model // 2
    lines = 16

    def of(shape):
        return pl.BlockSpec((None, *shape), lambda p: (jnp.maximum(pairs - 1 - p, 0), 0, 0))

    def unit(h):
        def at(p):
            pair = jnp.maximum(pairs - 1 - p, 0)
            return 2 * (pair // late) + h, pair % late, 0, 0

        return pl.BlockSpec((None, None, CHUNK, model), at)

    anywhere = pl.BlockSpec(memory_space=pl.ANY)
    sems = pltpu.SemaphoreType.DMA
    between = max(others - 1, 1)
    many = (chunks, between)
    return pl.pallas_call(
        functools.partial(bwd_kernel, rows=rows, pairs=pairs, group=group),
        grid=(pairs + 1,),
        in_specs=[
            once((tokens, model)), once((tokens, model)), of((tokens, 3 * LANES)),
            of((tokens, LANES)), of((2, tokens)), unit(0), unit(1),
            once((tokens, LANES)), once((tokens, LANES)), once((tokens, stored)),
            once((tokens, model)), full(vec.shape), full(g_bias.shape),
            full((1, model)), full((1, model)), full((1, model)),
            anywhere, anywhere, anywhere,
        ],
        out_specs=[once((tokens, stored)), anywhere, anywhere, anywhere, once((lines, model))],
        out_shape=[
            jax.ShapeDtypeStruct((tokens, stored), BF16),
            jax.ShapeDtypeStruct((early, CHUNK, model), BF16),
            jax.ShapeDtypeStruct((3, late * HEAD_DIM, model), BF16),
            jax.ShapeDtypeStruct((late * HEAD_DIM, model), BF16),
            jax.ShapeDtypeStruct((lines, model), F32),
        ],
        scratch_shapes=[
            pltpu.VMEM((3 * LANES, model), BF16),
            pltpu.VMEM((LANES, model), BF16),
            pltpu.VMEM((tokens, LANES), BF16),
            pltpu.VMEM((tokens, 3 * LANES), BF16),
            pltpu.VMEM((tokens, LANES), F32),
            pltpu.VMEM((tokens, LANES), F32),
            pltpu.VMEM((tokens, model), F32),
            pltpu.VMEM((CHUNK, model), F32),
            pltpu.VMEM((chunks + 3 * late, 2, CHUNK, wide), BF16),
            pltpu.VMEM((2, late, 2, CHUNK, wide), BF16),
            pltpu.VMEM((chunks, 2, CHUNK, wide), BF16),
            pltpu.VMEM((chunks, CHUNK, wide), BF16),
            pltpu.VMEM((*many, CHUNK // others, wide), BF16),
            pltpu.VMEM((chunks, CHUNK, wide), BF16),
            pltpu.VMEM((chunks, CHUNK, wide), BF16),
            pltpu.VMEM((4, lines, model), F32),
            pltpu.VMEM((4, lines, model), F32),
            pltpu.VMEM((others, lines, model), F32),
            sems((2, late)), sems((2, late)), sems((chunks,)), sems((chunks,)),
            sems((chunks,)), sems((chunks,)), sems(many), sems(many), sems(many), sems(many),
            sems((chunks,)), sems((chunks,)), sems((early,)), sems((got.shape[0],)),
            sems((chunks, 2, 4)), sems((4,)), sems((4,)), sems((between,)), sems((between,)),
        ],
        compiler_params=params(60, collective_id=0, has_side_effects=True),
        name="attn_bwd",
    )(
        n, db, qkv, att, lse, weights, weights, qh, kn, x, d_resid, vec, g_bias, c_sum, branch_sum,
        gain_two_sum, sum_y, sum_own, got,
    )


def solution(mesh):
    n_dp, n_tensor = mesh.shape["dp"], mesh.shape["tensor"]
    assert n_tensor == 4 and n_dp % 4 == 0 and n_dp & (n_dp - 1) == 0
    bits = [1 << i for i in range(n_dp.bit_length() - 1)]
    group = min(n_dp, 8)

    def to_dp(v, bit):
        return lax.ppermute(v, "dp", [(i, i ^ bit) for i in range(n_dp)])

    def local(
        layer_input, segments, cotangent, gain_one, w_qkv, b_qv, w_out, b_out, gain_two,
        w_up, b_up, w_down, b_down,
    ):
        rows = segments.shape[0]
        tokens, stored = layer_input.shape
        model = stored + 1
        heads = w_qkv.shape[2] // HEAD_DIM
        units = w_up.shape[1]

        vec = [gain_one, gain_two, b_out, b_down, b_up, *b_qv]
        vec = jnp.concatenate([jnp.pad(v.astype(F32), (0, 1024 - v.shape[0])) for v in vec])
        vec = jnp.pad(vec, (0, 1024)).reshape(8, 1024)
        (
            n_one, cot, grad_bdown, qkv, att, lse, resid, n_two, qh, kn, w_attn, w_ffn, misc
        ) = forward(
            layer_input, cotangent, w_qkv.transpose(0, 2, 1), w_out, w_up, w_down, vec, segments
        )
        (
            sum_y, sum_own, got, g_bias, output, d_resid, d_branch, grad_gain_two, grad_bout
        ) = ffn(n_two, cot, resid, w_ffn, misc, vec, stored, 2)

        input_grad, *reduced, small = attn_bwd(
            n_one, d_branch, qkv, att, lse, w_attn, qh, kn, layer_input, d_resid, vec, g_bias,
            grad_bdown, grad_bout, grad_gain_two, sum_y, sum_own, got, rows, group,
        )
        for bit in bits:
            if bit >= group:
                small = small + to_dp(small, bit)
                reduced = [(v.astype(F32) + to_dp(v, bit).astype(F32)).astype(BF16) for v in reduced]
        grad_ffn, grad_qkv, grad_out = reduced
        grad_up, grad_down = grad_ffn.reshape(2, model, units)
        grad_up = grad_up[:stored].astype(F32)
        grad_down = grad_down.T[:, :stored].astype(F32)
        grad_qkv = grad_qkv[..., :stored].astype(F32).transpose(0, 2, 1)
        grad_out = grad_out[:, :stored].astype(F32)
        per_head = small[8 : 8 + heads]
        grad_bqv = jnp.stack(
            [per_head[:, :HEAD_DIM].reshape(-1), per_head[:, 2 * LANES : 2 * LANES + HEAD_DIM].reshape(-1)]
        )
        return (
            output,
            input_grad,
            small[4, :stored],
            grad_qkv,
            grad_bqv,
            grad_out,
            small[2, :stored],
            small[3, :stored],
            grad_up,
            small[0],
            grad_down,
            small[1, :stored],
        )

    return jax.shard_map(
        local,
        mesh=mesh,
        in_specs=(
            P(("dp", "tensor"), None),
            P(("dp", "tensor"), None),
            P(("dp", "tensor"), None),
            P(),
            P(None, None, "tensor"),
            P(None, "tensor"),
            P("tensor", None),
            P(),
            P(),
            P(None, "tensor"),
            P("tensor"),
            P("tensor", None),
            P(),
        ),
        out_specs=(
            P(("dp", "tensor"), None),
            P(("dp", "tensor"), None),
            P(),
            P(None, None, "tensor"),
            P(None, "tensor"),
            P("tensor", None),
            P(),
            P(),
            P(None, "tensor"),
            P("tensor"),
            P("tensor", None),
            P(),
        ),
        check_vma=False,
    )
```

```python
import functools

import jax
import jax.numpy as jnp
from jax import lax
from jax.experimental import pallas as pl
from jax.experimental.pallas import tpu as pltpu
from jax.sharding import PartitionSpec as P

HEAD_DIM = 64
LANES = 128
EPSILON = 1e-05
MASKED_SCORE = -1e30
LONGEST = 512
BLOCK = 256
CHUNK = 256
UNITS = 256
F32 = jnp.float32
BF16 = jnp.bfloat16
NN = (((1,), (0,)), ((), ()))
NT = (((1,), (1,)), ((), ()))
TN = (((0,), (0,)), ((), ()))
GELU_A = 0.7978845608028654
GELU_B = 0.044715
MIB = 1024 * 1024
MESH = pl.DeviceIdType.MESH


def dot(a, b, dims=NN):
    return lax.dot_general(a, b, dims, preferred_element_type=F32)


def params(mib, **more):
    return pltpu.CompilerParams(vmem_limit_bytes=mib * MIB, **more)


def full(shape):
    return pl.BlockSpec(shape, lambda *_: (0,) * len(shape))


def once(shape):
    return pl.BlockSpec(shape, lambda *_: (0,) * len(shape), pipeline_mode=pl.Buffered(1))


def widen(ref, wide):
    wide[:, wide.shape[1] - LANES :] = jnp.zeros((wide.shape[0], LANES), F32)
    wide[:, : ref.shape[1]] = ref[...].astype(F32)
    return wide[...]


def norm_scale(values):
    total = jnp.sum(values, axis=-1, keepdims=True)
    square = jnp.sum(values * values, axis=-1, keepdims=True)
    return lax.rsqrt((square + total * total) / values.shape[-1] + EPSILON), total


def norm_back(values, gain, upstream):
    scale, total = norm_scale(values)
    weighted = upstream * values
    spread = jnp.sum(weighted * gain, axis=-1, keepdims=True)
    grad = upstream * gain * scale - (spread * scale * scale * scale / values.shape[-1]) * (
        values + total
    )
    return grad, jnp.sum(weighted * scale, axis=0, keepdims=True)


def scores_of(q_ref, k_ref, qh_ref, kn_ref, sel, at, span):
    q = q_ref[at, :] * 0.125
    qa = jnp.where(sel, q, qh_ref[at, :])
    ka = jnp.where(sel, k_ref[span, :], kn_ref[span, :])
    s = dot(ka, qa, NT)
    causal = lax.broadcasted_iota(jnp.int32, (BLOCK, BLOCK), 0) <= lax.broadcasted_iota(
        jnp.int32, (BLOCK, BLOCK), 1
    )
    early = s.shape[0] - BLOCK
    tail = jnp.where(causal, s[early:, :], MASKED_SCORE)
    return (tail if early == 0 else jnp.concatenate([s[:early, :], tail], axis=0)), q


def spans(length, row):
    for end in range(BLOCK, length + 1, BLOCK):
        start = max(0, end - BLOCK - LONGEST)
        base = row * length
        yield slice(base + end - BLOCK, base + end), slice(base + start, base + end)


def remote(src, dst, send, recv, device):
    return pltpu.make_async_remote_copy(
        src_ref=src, dst_ref=dst, send_sem=send, recv_sem=recv, device_id=device,
        device_id_type=MESH,
    )


def greet(partners):
    barrier = pltpu.get_barrier_semaphore()
    for device in partners:
        pl.semaphore_signal(barrier, inc=1, device_id=device, device_id_type=MESH)
    pl.semaphore_wait(barrier, len(partners))


def neighbours():
    dp, tensor = lax.axis_index("dp"), lax.axis_index("tensor")
    side = dp % 2
    to_core = (dp, tensor + 1 - 2 * (tensor % 2))
    return to_core, (dp, (tensor + 2) % 4), (dp + 1 - 2 * side, tensor), side


def pair_weights(even, odd, w, wo):
    for h, unit in enumerate((even, odd)):
        for i in range(3):
            at = LANES * i + HEAD_DIM * h
            w[at : at + HEAD_DIM, :] = unit[HEAD_DIM * i : HEAD_DIM * (i + 1), :]
        wo[HEAD_DIM * h : HEAD_DIM * (h + 1), :] = unit[3 * HEAD_DIM :, :]


def fwd_kernel(
    x_ref, c_ref, wqkv_ref, wout_ref, up_ref, down_ref, vec_ref, seg_ref,
    n_ref, cot_ref, c_sum_ref, qkv_ref, att_ref, lse_ref, resid_ref, n_two_ref, qh_ref, kn_ref,
    wa_ref, wf_ref, misc_all_ref,
    wa, stage, misc, w, wo, branch, wide,
    core_s, core_r, y_s, y_r, x_s, x_r, d_s, d_r, local_s, z_s, z_r, zz_s, zz_r,
    *, rows, pairs
):
    t = pl.program_id(0)
    tokens = x_ref.shape[0]
    length = tokens // rows
    heads = pairs // 2
    stored = x_ref.shape[1]
    model = stored + 1
    early, tail = heads, stage.shape[0]
    to_core, to_y, to_x, side = neighbours()
    last = early + tail
    dp = lax.axis_index("dp")
    level = dp // 2 % 2
    to_z = (dp + 2 - 4 * level, lax.axis_index("tensor"))

    def rows_of(k, across, along):
        if k < early:
            return pl.ds(pl.multiple_of(across * (CHUNK // 2), CHUNK // 2), CHUNK // 2)
        size = CHUNK // 4
        return pl.ds(pl.multiple_of((2 * across + along) * size, size), size)

    def held(quarter, k):
        if k == last:
            return misc.at[quarter]
        if k < early:
            return wa.at[quarter, k]
        return wf_ref.at[quarter, k - early]

    def own(k):
        return held(0, k) if k < early or k == last else stage.at[k - early]

    def core_copy(k):
        return remote(own(k), held(1, k), core_s.at[k], core_r.at[k], to_core)

    def y_copy(k):
        src, dst = own(k), held(2, k)
        if k < last:
            rows_ = rows_of(k, side, level)
            src, dst = src.at[rows_], dst.at[rows_]
        return remote(src, dst, y_s.at[k], y_r.at[k], to_y)

    def spread(k, across, along, send, recv, device):
        ref = held(2, k).at[rows_of(k, across, along)]
        return remote(ref, ref, send.at[k], recv.at[k], device)

    def x_copy(k, across):
        return spread(k, across, level, x_s, x_r, to_x)

    def z_copy(k, along):
        return spread(k, side, along, z_s, z_r, to_z)

    def zz_copy(k, along):
        return spread(k, 1 - side, along, zz_s, zz_r, to_z)

    def d_copy(k):
        return remote(held(2, k), held(3, k), d_s.at[k], d_r.at[k], to_core)

    def keep_copy(k):
        if k == last:
            return pltpu.make_async_copy(misc, misc_all_ref, local_s.at[k])
        if k < early:
            return pltpu.make_async_copy(wa.at[:, k], wa_ref.at[:, k], local_s.at[k])
        return pltpu.make_async_copy(stage.at[k - early], wf_ref.at[0, k - early], local_s.at[k])

    def x_on(k):
        y_copy(k).wait_recv()
        x_copy(k, side).start()
        if k >= early:
            z_copy(k, level).start()

    def z_on(k):
        x_copy(k, 1 - side).wait_recv()
        zz_copy(k, level).start()

    def d_on(k):
        if k == last:
            y_copy(k).wait_recv()
        elif k < early:
            x_copy(k, 1 - side).wait_recv()
        else:
            z_copy(k, 1 - level).wait_recv()
            zz_copy(k, 1 - level).wait_recv()
        d_copy(k).start()

    def start_y(k):
        y_copy(k).start()

    def start_core(k):
        core_copy(k).start()

    @pl.when(t == 0)
    def _():
        edge = slice(model - LANES, model)
        wa[0, :, :, edge] = jnp.zeros((early, CHUNK, LANES), BF16)
        for j in range(heads):
            head = slice(HEAD_DIM * j, HEAD_DIM * (j + 1))
            for i in range(3):
                wa[0, j, HEAD_DIM * i : HEAD_DIM * (i + 1), :stored] = wqkv_ref[i, head, :]
            wa[0, j, 3 * HEAD_DIM :, :stored] = wout_ref[head, :]
        misc[...] = jnp.zeros_like(misc)
        for p in range(2):
            for j in range(heads):
                for i, row in ((0, 5), (2, 6)):
                    at = LANES * i + HEAD_DIM * p
                    misc[0, j, p, :1, at : at + HEAD_DIM] = vec_ref[
                        row : row + 1, HEAD_DIM * j : HEAD_DIM * (j + 1)
                    ]
            units_half = misc.shape[4]
            misc[0, heads, p, :1, :] = vec_ref[4:5, units_half * p : units_half * (p + 1)]
        greet([to_core, to_y, to_x, to_z])
        for k in (last, 0):
            core_copy(k).start()
            y_copy(k).start()
        for k in range(1, early):
            core_copy(k).start()
        count = tail // 2
        stage[:, :, edge] = jnp.zeros((tail, CHUNK, LANES), BF16)
        stage[count - 1, CHUNK - 16 :, :] = jnp.zeros((16, model), BF16)
        for i in range(count):
            end = min(CHUNK * (i + 1), stored)
            stage[i, : end - CHUNK * i, :] = up_ref[CHUNK * i : end, :]
            stage[count + i, :, :stored] = down_ref[CHUNK * i : CHUNK * (i + 1), :]
        for k in range(early, last):
            keep_copy(k).start()
        branch[...] = jnp.zeros_like(branch)
        c_sum = jnp.zeros((1, model), F32)
        for i in range(0, tokens, CHUNK):
            r = slice(i, i + CHUNK)
            x = widen(x_ref.at[r, :], wide)
            n_ref[r, :] = (x * norm_scale(x)[0] * vec_ref[0:1, :model]).astype(BF16)
            c = widen(c_ref.at[r, :], wide)
            cot_ref[r, :] = c.astype(BF16)
            c_sum += jnp.sum(c, axis=0, keepdims=True)
        c_sum_ref[...] = c_sum
        lane = lax.broadcasted_iota(jnp.int32, (1, LANES), 1) % HEAD_DIM
        for row in range(rows):
            document = jnp.broadcast_to(seg_ref[row : row + 1, :].astype(F32), (LANES, length)).T
            hot = document == lane.astype(F32)
            r = slice(row * length, (row + 1) * length)
            qh_ref[r, :] = jnp.where(hot, 1.0, 0.0).astype(BF16)
            kn_ref[r, :] = jnp.where(hot | (lane >= 8), 0.0, MASKED_SCORE).astype(BF16)
        core_copy(last).wait_recv()

    events = {
        (0, 0): [(start_y, 1)], (0, 2): [(d_on, last)], (0, 3): [(x_on, 0)], (0, 4): [(start_y, 2)],
        (1, 2): [(x_on, 1)], (1, 4): [(start_y, early), (start_core, early), (start_core, early + 1)],
        (2, 1): [(d_on, 0), (x_on, 2), (start_y, early + 1)],
        (2, 3): [(start_y, early + 2), (start_core, early + 2), (start_core, early + 3)],
        (2, 4): [(d_on, 1)],
        (3, 0): [(x_on, early), (start_y, early + 3)],
        (3, 1): [(x_on, early + 1)],
        (3, 2): [(start_y, early + 4), (start_core, early + 4), (start_core, early + 5)],
        (3, 3): [(d_on, 2), (x_on, early + 2)],
        (3, 4): [(start_y, early + 5), (z_on, early)],
        (4, 0): [(x_on, early + 3), (z_on, early + 1)],
        (4, 2): [(x_on, early + 4), (z_on, early + 2)],
        (4, 3): [(d_on, early)],
        (4, 4): [(x_on, early + 5), (z_on, early + 3)],
        (5, 1): [(z_on, early + 4), (d_on, early + 1)],
        (5, 3): [(z_on, early + 5), (d_on, early + 2)],
    }

    def run(slot):
        for (step, at), todo in events.items():
            if at == slot and todo:

                @pl.when(t == step)
                def _(todo=todo):
                    for event, k in todo:
                        event(k)

    for step in range(pairs):

        @pl.when(t == step)
        def _(far=step // heads, j=step % heads):
            (d_copy if far else core_copy)(j).wait_recv()
            if far and j == 0:
                d_copy(last).wait_recv()

    first = lax.broadcasted_iota(jnp.int32, (1, LANES), 1) < HEAD_DIM
    units = [(2 * (t // heads) + h, t % heads) for h in range(2)]
    pair_weights(*(wa.at[quarter, j] for quarter, j in units), w, wo)
    bias = sum(misc[quarter, j, h, :1, :] for h, (quarter, j) in enumerate(units))
    qkv_ref[...] = (dot(n_ref[...], w[...], NT) + bias).astype(BF16)
    q_ref, k_ref, v_ref = (qkv_ref.at[:, j * LANES : (j + 1) * LANES] for j in range(3))
    run(0)
    slot = 1
    for row in range(rows):
        for at, span in spans(length, row):
            parts = []
            for h in range(2):
                sel = first if h == 0 else ~first
                s, _ = scores_of(q_ref, k_ref, qh_ref, kn_ref, sel, at, span)
                m = jnp.max(s, axis=0, keepdims=True)
                p = jnp.exp(s - m)
                total = jnp.sum(p, axis=0, keepdims=True)
                weights = (p * (1.0 / total)).astype(BF16)
                parts.append(dot(weights, v_ref[span, :], TN))
                lse_ref[h : h + 1, at] = m + jnp.log(total)
            att_ref[at, :] = jnp.where(first, parts[0], parts[1]).astype(BF16)
            if slot < 4:
                run(slot)
                slot += 1
    branch[...] += dot(att_ref[...], wo[...])
    run(4)

    @pl.when(t == pairs - 1)
    def _():
        for i in range(0, tokens, CHUNK):
            r = slice(i, i + CHUNK)
            resid = widen(x_ref.at[r, :], wide) + (branch[r, :] + vec_ref[2:3, :model])
            resid_ref[r, :] = resid
            n_two_ref[r, :] = (resid * norm_scale(resid)[0] * vec_ref[1:2, :model]).astype(BF16)
        for k in range(early + 3, last):
            d_on(k)
        for k in (*range(early), last):
            keep_copy(k).start()
        for k in range(early, last):
            core_copy(k).wait_recv()
            d_copy(k).wait_recv()
        for k in range(last + 1):
            core_copy(k).wait_send()
            y_copy(k).wait_send()
            if k < last:
                x_copy(k, side).wait_send()
            if early <= k < last:
                z_copy(k, level).wait_send()
                zz_copy(k, level).wait_send()
            d_copy(k).wait_send()
            keep_copy(k).wait()


def forward(x, c, wqkv, wout, up, down, vec, seg):
    tokens, stored = x.shape
    model = stored + 1
    heads = wqkv.shape[1] // HEAD_DIM
    pairs = 2 * heads
    tail = 2 * (model // CHUNK)

    def of(*shape):
        return pl.BlockSpec((None, *shape), lambda p: (p,) + (0,) * len(shape))

    anywhere = pl.BlockSpec(memory_space=pl.ANY)
    sems = pltpu.SemaphoreType.DMA((heads + tail + 1,))
    rows = seg.shape[0]
    misc = (heads + 1, 2, 8, model // 2)
    inputs = [x, c, wqkv, wout, up, down, vec, seg]
    big = once((tokens, model))
    outs = [
        (big, (tokens, model), BF16),
        (big, (tokens, model), BF16),
        (once((1, model)), (1, model), F32),
        (of(tokens, 3 * LANES), (pairs, tokens, 3 * LANES), BF16),
        (of(tokens, LANES), (pairs, tokens, LANES), BF16),
        (of(2, tokens), (pairs, 2, tokens), F32),
        (big, (tokens, model), F32),
        (big, (tokens, model), BF16),
        (once((tokens, LANES)), (tokens, LANES), BF16),
        (once((tokens, LANES)), (tokens, LANES), BF16),
        (anywhere, (4, heads, CHUNK, model), BF16),
        (anywhere, (4, tail, CHUNK, model), BF16),
        (anywhere, (4, *misc), F32),
    ]
    return pl.pallas_call(
        functools.partial(fwd_kernel, rows=rows, pairs=pairs),
        grid=(pairs,),
        in_specs=[once(v.shape) for v in inputs],
        out_specs=[spec for spec, _, _ in outs],
        out_shape=[jax.ShapeDtypeStruct(shape, dtype) for _, shape, dtype in outs],
        scratch_shapes=[
            pltpu.VMEM((4, heads, CHUNK, model), BF16),
            pltpu.VMEM((tail, CHUNK, model), BF16),
            pltpu.VMEM((4, *misc), F32),
            pltpu.VMEM((3 * LANES, model), BF16),
            pltpu.VMEM((LANES, model), BF16),
            pltpu.VMEM((tokens, model), F32),
            pltpu.VMEM((CHUNK, model), F32),
        ]
        + [sems] * 13,
        compiler_params=params(60, collective_id=1, has_side_effects=True),
        name="forward",
    )(*inputs)


def backward_kernel(
    n_two_ref, c_ref, n_ref, x_ref, vec_ref, c_sum_ref, up_ref, down_ref, bias_ref,
    qkv_ref, att_ref, lse_ref, even_ref, odd_ref, qh_ref, kn_ref, resid_ref,
    output_ref, grad_in_ref, red_ref, red_late_ref, total_ref,
    out, back, d_resid, nt, ct, db, stage, bias_row, w, wo, da, dqkv, dk_acc, dv_acc, wide_x,
    g, core_in, y_in, x_in, z_in, ag, xag_in, sv, sv_in, sv_z,
    core_s, core_r, y_s, y_r, x_s, x_r, z_s, z_r, a_s, a_r, xa_s, xa_r, out_s,
    sv_s, sv_r, svz_s, svz_r, resid_s, rows_s,
    *, rows, pairs, group, blocks
):
    t = pl.program_id(0)
    tokens, model = n_ref.shape
    length = tokens // rows
    front = 4 * blocks
    early, late = 2 * blocks, pairs // 2
    chunks = early + late
    others = group // 2
    half, units = g.shape[2:]
    keep = half // others
    pieces = half // HEAD_DIM
    dp, tensor = lax.axis_index("dp"), lax.axis_index("tensor")
    place = (dp % group) // 2
    mine = pl.ds(pl.multiple_of(place * keep, keep), keep)
    to_core, to_y, to_x, side = neighbours()

    def place_of(o):
        return (place + o) % others

    def to_z(o):
        return (dp - dp % group + place_of(o) * 2 + side, tensor)

    box = 2 * chunks

    def core_copy(which, k, at, slot):
        return remote(
            g.at[box + at], core_in.at[which, slot], core_s.at[which, k], core_r.at[which, k], to_core
        )

    def early_core(which, k):
        return core_copy(which, k, k, k)

    def late_core(which, i):
        return core_copy(which, early + i, late * which + i, i)

    def y_copy(k):
        return remote(g.at[chunks + k], y_in.at[k], y_s.at[k], y_r.at[k], to_y)

    def x_copy(k):
        return remote(g.at[k, 1 - side], x_in.at[k], x_s.at[k], x_r.at[k], to_x)

    def z_copy(k, o):
        rows_of = pl.ds(pl.multiple_of(place_of(o) * keep, keep), keep)
        return remote(
            g.at[k, side, rows_of], z_in.at[k, o - 1], z_s.at[k, o - 1], z_r.at[k, o - 1], to_z(o)
        )

    def a_copy(k, o):
        return remote(ag.at[k, mine], ag.at[k, mine], a_s.at[k, o - 1], a_r.at[k, o - 1], to_z(o))

    def a_wait(k, o):
        rows_of = pl.ds(pl.multiple_of(place_of(others - o) * keep, keep), keep)
        part = ag.at[k, rows_of]
        remote(part, part, a_s.at[k, o - 1], a_r.at[k, o - 1], to_z(o)).wait_recv()

    def xa_copy(k):
        return remote(ag.at[k], xag_in.at[k], xa_s.at[k], xa_r.at[k], to_x)

    def out_copies(k, i, act):
        which = side + i - 2 * side * i
        src = xag_in if i else ag

        @pl.when(k < early)
        def _():
            at = jnp.minimum(k, early - 1)
            lines = pl.ds(pl.multiple_of(which * half, half), half)
            cols = pl.ds(pl.multiple_of(at // 2 * units, units), units)
            act(pltpu.make_async_copy(src.at[at], red_ref.at[at % 2, lines, cols], out_s.at[k, i, 0]))

        @pl.when(k >= early)
        def _():
            at = jnp.maximum(k, early)
            head = pl.ds(pl.multiple_of((chunks - 1 - at) * HEAD_DIM, HEAD_DIM), HEAD_DIM)
            for n in range(pieces):
                piece = which * pieces + n
                cols = pl.ds(pl.multiple_of(piece // 4 * units, units), units)
                act(
                    pltpu.make_async_copy(
                        src.at[at, HEAD_DIM * n : HEAD_DIM * (n + 1)],
                        red_late_ref.at[piece % 4, head, cols],
                        out_s.at[k, i, n],
                    )
                )

    def plus(at, value):
        g[at] = (g[at].astype(F32) + value.astype(F32)).astype(BF16)

    def send_y(k):
        @pl.when(k >= early)
        def _():
            i = jnp.maximum(k, early) - early
            late_core(0, i).wait_recv()
            plus(chunks + early + i, core_in[0, i])

        y_copy(k).start()

    def send_x(k):
        @pl.when(k >= early)
        def _():
            i = jnp.maximum(k, early) - early
            late_core(1, i).wait_recv()
            plus(early + i, core_in[1, i])

        y_copy(k).wait_recv()
        plus(k, y_in[k])
        x_copy(k).start()

    def send_z(k):
        x_copy(k).wait_recv()
        g[k, side] = (g[k, side].astype(F32) + x_in[k].astype(F32)).astype(BF16)
        for o in range(1, others):
            z_copy(k, o).start()

    def send_back(k):
        total = g[k, side, mine].astype(F32)
        for o in range(1, others):
            z_copy(k, o).wait_recv()
            total += z_in[k, o - 1].astype(F32)
        ag[k, mine] = total.astype(BF16)
        for o in range(1, others):
            a_copy(k, o).start()

    def send_back_x(k):
        for o in range(1, others):
            a_wait(k, o)
        xa_copy(k).start()
        out_copies(k, 0, lambda copy: copy.start())

    def finish(k):
        xa_copy(k).wait_recv()
        out_copies(k, 1, lambda copy: copy.start())

    plan = [
        (finish, [(13, 0), (14, 0), (15, 0), (16, 0), (17, 0)]),
        (send_back_x, [(12, 0), (13, 0), (14, 0), (15, 0), (16, 0), (17, 0)]),
        (send_back, [(10, 0), (12, 0), (13, 0), (14, 0), (15, 0), (16, 0), (17, 2)]),
        (send_z, [(8, 0), (10, 0), (12, 0), (13, 0), (14, 0), (15, 0), (16, 4), (17, 4)]),
        (send_x, [(6, 0), (8, 0), (10, 0), (12, 0), (13, 0), (14, 0), (16, 0), (17, 0)]),
        (send_y, [(2, 0), (4, 0), (6, 0), (8, 0), (10, 0), (12, 0), (13, 0), (14, 0), (15, 0)]),
    ]

    def run(slot, first, end):
        for event, times in plan:
            table = {
                step: k for k, (step, at) in enumerate(times) if at == slot and first <= step < end
            }
            if table:
                k = jnp.int32(-1)
                for step, at in table.items():
                    k = jnp.where(t == step, at, k)

                @pl.when(k >= 0)
                def _(event=event, k=k):
                    event(jnp.maximum(k, 0))

    def sv_copy(i, src, device):
        return remote(src, sv_in.at[i], sv_s.at[i], sv_r.at[i], device)

    def svz_copy(o):
        return remote(sv_z.at[place], sv_z.at[place], svz_s.at[o - 1], svz_r.at[o - 1], to_z(o))

    def small_y():
        for i in (0, 1):
            sv_copy(i, sv.at[3 - 2 * i], to_core).wait_recv()
        sv[2] += sv_in[0]
        sv_copy(2, sv.at[2], to_y).start()

    def small_x():
        sv_copy(2, sv.at[2], to_y).wait_recv()
        sv[0] = (sv[0] + sv_in[1]) + sv_in[2]
        sv_copy(3, sv.at[0], to_x).start()

    def small_z():
        sv_copy(3, sv.at[0], to_x).wait_recv()
        sv_z[place] = sv[0] + sv_in[3]
        for o in range(1, others):
            svz_copy(o).start()

    def small_end():
        for o in range(1, others):
            part = sv_z.at[place_of(others - o)]
            remote(part, part, svz_s.at[o - 1], svz_r.at[o - 1], to_z(o)).wait_recv()
        total = sv_z[0]
        for i in range(1, others):
            total += sv_z[i]
        total_ref[...] = total

    def resid_copy():
        return pltpu.make_async_copy(resid_ref, d_resid, resid_s)

    def grad_copy(i):
        r = slice(CHUNK * i, CHUNK * (i + 1))
        return pltpu.make_async_copy(db.at[r], grad_in_ref.at[r], rows_s.at[i])

    def output_copy(i):
        r = slice(CHUNK * i, CHUNK * (i + 1))
        return pltpu.make_async_copy(stage.at[i % 2], output_ref.at[r], rows_s.at[i])

    def feed_forward():
        b, quarter = t // 4, 3 - t % 4
        up = up_ref[...].reshape(model, units)
        down = down_ref[...]
        wide = bias_ref.shape[2]
        for h in range(2):
            bias_row[0:1, wide * h : wide * (h + 1)] = bias_ref[h, :1, :]
        lanes = pl.ds(pl.multiple_of(b * units, units), units)
        pre = dot(n_two_ref[...], up) + bias_row[0:1, lanes]
        dh = dot(c_ref[...], down, NT)
        sq = pre * pre
        th = jnp.tanh(pre * (GELU_A + (GELU_A * GELU_B) * sq))
        level = 0.5 + 0.5 * th
        hidden = (pre * level).astype(BF16)
        slope = level + (0.5 * pre) * (1.0 - th * th) * (GELU_A + (3.0 * GELU_A * GELU_B) * sq)
        dpre = (dh * slope).astype(BF16)
        out[...] += dot(hidden, down)
        back[...] += dot(dpre, up, NT)
        sv[quarter, 0:1, lanes] = jnp.sum(dpre.astype(F32), axis=0, keepdims=True)
        grads = dot(nt[...], dpre).astype(BF16), dot(ct[...], hidden).astype(BF16)

        @pl.when(t % 4 == 2)
        def _():
            for m in range(2):
                early_core(0, 2 * b + m).wait_send()

        base = jnp.where(quarter == 0, 0, jnp.where(quarter == 2, chunks, box)) + 2 * b
        for m in range(2):
            for h in range(2):
                g[base + m, h] = grads[m][half * h : half * (h + 1)]
        for m in range(2):
            k = 2 * b + m
            for which in range(2):

                @pl.when(t % 4 == 2 * which)
                def _(which=which, k=k):
                    early_core(which, k).start()

                @pl.when(t % 4 == 2 * which + 1)
                def _(which=which, k=k):
                    early_core(which, k).wait_recv()
                    plus((1 - which) * chunks + k, core_in[which, k])

    def turn():
        resid_copy().wait()
        gain_sum = branch_sum = jnp.zeros((1, model), F32)
        for i in range(tokens // CHUNK):
            r = slice(CHUNK * i, CHUNK * (i + 1))
            resid = d_resid[r, :]
            if i >= 2:
                output_copy(i - 2).wait()
            stage[i % 2] = (resid + (out[r, :] + vec_ref[3:4, :model])).astype(BF16)
            output_copy(i).start()
            out[r, :] = jnp.zeros((CHUNK, model), F32)
            d_norm, part = norm_back(resid, vec_ref[1:2, :model], back[r, :])
            d_rows = c_ref[r, :].astype(F32) + d_norm
            d_resid[r, :] = d_rows
            d_branch = d_rows.astype(BF16)
            db[r, :] = d_branch
            gain_sum += part
            branch_sum += jnp.sum(d_branch.astype(F32), axis=0, keepdims=True)
        for i in range(tokens // CHUNK - 2, tokens // CHUNK):
            output_copy(i).wait()
        for i in range(4):
            sv[i, 2:3, :] = branch_sum
            sv[i, 3:4, :] = gain_sum
        for k in range(early):
            early_core(1, k).wait_send()

    def norm_one():
        gain_sum = jnp.zeros((1, model), F32)
        for i in range(tokens // CHUNK):
            r = slice(CHUNK * i, CHUNK * (i + 1))
            d_norm, part = norm_back(widen(x_ref.at[r, :], wide_x), vec_ref[0:1, :model], out[r, :])
            db[r, :] = (d_resid[r, :] + d_norm).astype(BF16)
            grad_copy(i).start()
            gain_sum += part
        for i in range(4):
            sv[i, 4:5, :] = gain_sum
        for i in (0, 1):
            sv_copy(i, sv.at[3 - 2 * i], to_core).start()

    first = lax.broadcasted_iota(jnp.int32, (1, LANES), 1) < HEAD_DIM
    zero = jnp.zeros((), BF16)
    q_ref, k_ref, v_ref = (qkv_ref.at[:, j * LANES : (j + 1) * LANES] for j in range(3))

    def attend(at, span):
        dq = None
        for h in range(2):
            sel = first if h == 0 else ~first
            s, q = scores_of(q_ref, k_ref, qh_ref, kn_ref, sel, at, span)
            qm = jnp.where(sel, q, zero)
            km = jnp.where(sel, k_ref[span, :], zero)
            dom = jnp.where(sel, da[at, :], zero)
            p = jnp.exp(s - lse_ref[h : h + 1, at])
            dp_ = dot(v_ref[span, :], dom, NT)
            u = p * dp_
            inner = jnp.sum(u, axis=0, keepdims=True)
            ds = (u - p * inner).astype(BF16)
            dv_acc[span, :] += dot(p.astype(BF16), dom)
            dk_acc[span, :] += dot(ds, qm)
            part = dot(ds, km, TN)
            dq = part if dq is None else dq + part
        dqkv[at, :LANES] = (dq * 0.125).astype(BF16)

    def attention():
        pair_weights(even_ref, odd_ref, w, wo)
        da[...] = dot(db[...], wo[...], NT).astype(BF16)
        dk_acc[...] = jnp.zeros_like(dk_acc)
        dv_acc[...] = jnp.zeros_like(dv_acc)
        run(0, front, front + pairs)
        slot = 1
        for row in range(rows):
            for at, span in spans(length, row):
                attend(at, span)
                if slot < 5:
                    run(slot, front, front + pairs)
                    slot += 1
        dqkv[:, LANES : 2 * LANES] = dk_acc[...].astype(BF16)
        dqkv[:, 2 * LANES :] = dv_acc[...].astype(BF16)
        sums = jnp.sum(dqkv[...].astype(F32), axis=0, keepdims=True)
        out[...] += dot(dqkv[...], w[...])
        grads = dot(dqkv[...], n_ref[...], TN).astype(BF16)
        grads_out = dot(att_ref[...], db[...], TN).astype(BF16)
        pair = pairs - 1 - (t - front)
        far, j = pair // late, pair % late
        i = late - 1 - j
        for h in range(2):
            for line in range(late):

                @pl.when(j == line)
                def _(line=8 + line, h=h):
                    for part in (0, 2):
                        at = LANES * part + HEAD_DIM * h
                        sv[2 * far + h, line : line + 1, LANES * part : LANES * part + HEAD_DIM] = (
                            sums[:, at : at + HEAD_DIM]
                        )

            base = i + ((box + late * (1 - far)) if h else (early + chunks * far))
            for block in range(model // units):
                cols = slice(units * block, units * (block + 1))
                for p in range(4):
                    if p < 3:
                        lines = grads[LANES * p + HEAD_DIM * h : LANES * p + HEAD_DIM * (h + 1), cols]
                    else:
                        lines = grads_out[HEAD_DIM * h : HEAD_DIM * (h + 1), cols]
                    at = CHUNK * block + HEAD_DIM * p
                    g[base, at // half, at % half : at % half + HEAD_DIM, :] = lines
        late_core(1 - far, i).start()

    @pl.when(t == 0)
    def _():
        greet([to_core, to_y, to_x] + [to_z(o) for o in range(1, others)])
        out[...] = jnp.zeros_like(out)
        back[...] = jnp.zeros_like(back)
        sv[...] = jnp.zeros_like(sv)
        for i in range(4):
            sv[i, 1:2, :] = c_sum_ref[...]
        for i in range(0, tokens, CHUNK):
            nt[:, i : i + CHUNK] = n_two_ref[i : i + CHUNK, :].T
            ct[:, i : i + CHUNK] = c_ref[i : i + CHUNK, :].T

    @pl.when(t == front - 2)
    def _():
        resid_copy().start()

    @pl.when(t < front)
    def _():
        run(0, 0, front)
        feed_forward()

    pl.when(t == front - 1)(turn)
    pl.when((t >= front) & (t < front + pairs))(attention)

    @pl.when(t == front + pairs)
    def _():
        send_back_x(6)
        send_back(7)
        finish(5)
        send_x(8)
        norm_one()
        send_z(8)
        small_y()
        finish(6)
        send_back_x(7)
        send_back(8)
        small_x()
        finish(7)
        send_back_x(8)
        small_z()
        finish(8)
        small_end()

        @pl.loop(0, chunks)
        def _(k):
            y_copy(k).wait_send()
            x_copy(k).wait_send()
            for o in range(1, others):
                z_copy(k, o).wait_send()
                a_copy(k, o).wait_send()
            xa_copy(k).wait_send()
            for i in range(2):
                out_copies(k, i, lambda copy: copy.wait())

        for which in range(2):
            for i in range(late):
                late_core(which, i).wait_send()
        for i, device in enumerate((to_core, to_core, to_y, to_x)):
            sv_copy(i, sv.at[0], device).wait_send()
        for o in range(1, others):
            svz_copy(o).wait_send()
        for i in range(tokens // CHUNK):
            grad_copy(i).wait()


def backward(
    n_two, c, resid, w_ffn, misc, n, x, vec, c_sum, qkv, att, lse, w_attn, qh, kn, rows, group
):
    tokens, model = n.shape
    stored = x.shape[1]
    pairs = qkv.shape[0]
    blocks = model // UNITS
    front, early, late = 4 * blocks, 2 * blocks, pairs // 2
    chunks = early + late
    others = group // 2
    half = model // 2
    lines = 16
    entries, _, _, wide = misc.shape[1:]

    def unit_block(t):
        t = jnp.minimum(t, front - 1)
        return 3 - t % 4, t // 4

    def up_at(t):
        quarter, b = unit_block(t)
        return quarter, 0, 0, b

    def down_at(t):
        quarter, b = unit_block(t)
        return quarter, model // CHUNK + b, 0, 0

    def bias_at(t):
        return unit_block(t)[0], entries - 1, 0, 0, 0

    def pair_at(t):
        return pairs - 1 - jnp.clip(t - front, 0, pairs - 1)

    def of(shape):
        return pl.BlockSpec((None, *shape), lambda t: (pair_at(t), 0, 0))

    def unit(h):
        return pl.BlockSpec(
            (None, None, CHUNK, model),
            lambda t: (2 * (pair_at(t) // late) + h, pair_at(t) % late, 0, 0),
        )

    anywhere = pl.BlockSpec(memory_space=pl.ANY)
    sems = pltpu.SemaphoreType.DMA
    between = max(others - 1, 1)
    many = (chunks, between)
    big = once((tokens, model))
    return pl.pallas_call(
        functools.partial(backward_kernel, rows=rows, pairs=pairs, group=group, blocks=blocks),
        grid=(front + pairs + 1,),
        in_specs=[
            big, big, big, once((tokens, stored)), full(vec.shape), full((1, model)),
            pl.BlockSpec((None, model // CHUNK, CHUNK, UNITS), up_at),
            pl.BlockSpec((None, None, CHUNK, model), down_at),
            pl.BlockSpec((None, None, 2, 8, wide), bias_at),
            of((tokens, 3 * LANES)), of((tokens, LANES)), of((2, tokens)), unit(0), unit(1),
            once((tokens, LANES)), once((tokens, LANES)), anywhere,
        ],
        out_specs=[anywhere] * 4 + [once((lines, model))],
        out_shape=[
            jax.ShapeDtypeStruct((tokens, model), BF16),
            jax.ShapeDtypeStruct((tokens, model), BF16),
            jax.ShapeDtypeStruct((2, model, blocks * UNITS), BF16),
            jax.ShapeDtypeStruct((4, late * HEAD_DIM, model), BF16),
            jax.ShapeDtypeStruct((lines, model), F32),
        ],
        scratch_shapes=[pltpu.VMEM((tokens, model), F32)] * 3
        + [pltpu.VMEM((model, tokens), BF16)] * 2
        + [
            pltpu.VMEM((tokens, model), BF16),
            pltpu.VMEM((2, CHUNK, model), BF16),
            pltpu.VMEM((8, model), F32),
            pltpu.VMEM((3 * LANES, model), BF16),
            pltpu.VMEM((LANES, model), BF16),
            pltpu.VMEM((tokens, LANES), BF16),
            pltpu.VMEM((tokens, 3 * LANES), BF16),
            pltpu.VMEM((tokens, LANES), F32),
            pltpu.VMEM((tokens, LANES), F32),
            pltpu.VMEM((CHUNK, model), F32),
            pltpu.VMEM((2 * chunks + early, 2, half, UNITS), BF16),
            pltpu.VMEM((2, early, 2, half, UNITS), BF16),
            pltpu.VMEM((chunks, 2, half, UNITS), BF16),
            pltpu.VMEM((chunks, half, UNITS), BF16),
            pltpu.VMEM((*many, half // others, UNITS), BF16),
            pltpu.VMEM((chunks, half, UNITS), BF16),
            pltpu.VMEM((chunks, half, UNITS), BF16),
            pltpu.VMEM((4, lines, model), F32),
            pltpu.VMEM((4, lines, model), F32),
            pltpu.VMEM((others, lines, model), F32),
            sems((2, chunks)), sems((2, chunks)), sems((chunks,)), sems((chunks,)),
            sems((chunks,)), sems((chunks,)), sems(many), sems(many), sems(many), sems(many),
            sems((chunks,)), sems((chunks,)), sems((chunks, 2, half // HEAD_DIM)),
            sems((4,)), sems((4,)), sems((between,)), sems((between,)), sems, sems((tokens // CHUNK,)),
        ],
        compiler_params=params(63, collective_id=0, has_side_effects=True),
        name="backward",
    )(n_two, c, n, x, vec, c_sum, w_ffn, w_ffn, misc, qkv, att, lse, w_attn, w_attn, qh, kn, resid)


def solution(mesh):
    n_dp, n_tensor = mesh.shape["dp"], mesh.shape["tensor"]
    assert n_tensor == 4 and n_dp % 4 == 0 and n_dp & (n_dp - 1) == 0
    bits = [1 << i for i in range(n_dp.bit_length() - 1)]
    group = min(n_dp, 8)

    def to_dp(v, bit):
        return lax.ppermute(v, "dp", [(i, i ^ bit) for i in range(n_dp)])

    def local(
        layer_input, segments, cotangent, gain_one, w_qkv, b_qv, w_out, b_out, gain_two,
        w_up, b_up, w_down, b_down,
    ):
        rows = segments.shape[0]
        tokens, stored = layer_input.shape
        model = stored + 1
        heads = w_qkv.shape[2] // HEAD_DIM
        units = w_up.shape[1]

        vec = [gain_one, gain_two, b_out, b_down, b_up, *b_qv]
        vec = jnp.concatenate([jnp.pad(v.astype(F32), (0, 1024 - v.shape[0])) for v in vec])
        vec = jnp.pad(vec, (0, 1024)).reshape(8, 1024)
        (
            n_one, cot, grad_bdown, qkv, att, lse, resid, n_two, qh, kn, w_attn, w_ffn, misc
        ) = forward(
            layer_input, cotangent, w_qkv.transpose(0, 2, 1), w_out, w_up, w_down, vec, segments
        )
        output, input_grad, *reduced, small = backward(
            n_two, cot, resid, w_ffn, misc, n_one, layer_input, vec, grad_bdown, qkv, att, lse, w_attn,
            qh, kn, rows, group,
        )
        for bit in bits:
            if bit >= group:
                small = small + to_dp(small, bit)
                reduced = [(v.astype(F32) + to_dp(v, bit).astype(F32)).astype(BF16) for v in reduced]
        (grad_up, grad_down), grad_heads = reduced
        grad_up = grad_up[:stored].astype(F32)
        grad_down = grad_down.T[:, :stored].astype(F32)
        grad_qkv = grad_heads[:3, :, :stored].astype(F32).transpose(0, 2, 1)
        grad_out = grad_heads[3, :, :stored].astype(F32)
        per_head = small[8 : 8 + heads]
        grad_bqv = jnp.stack(
            [per_head[:, :HEAD_DIM].reshape(-1), per_head[:, 2 * LANES : 2 * LANES + HEAD_DIM].reshape(-1)]
        )
        return (
            output[:, :stored],
            input_grad[:, :stored],
            small[4, :stored],
            grad_qkv,
            grad_bqv,
            grad_out,
            small[2, :stored],
            small[3, :stored],
            grad_up,
            small[0],
            grad_down,
            small[1, :stored],
        )

    return jax.shard_map(
        local,
        mesh=mesh,
        in_specs=(
            P(("dp", "tensor"), None),
            P(("dp", "tensor"), None),
            P(("dp", "tensor"), None),
            P(),
            P(None, None, "tensor"),
            P(None, "tensor"),
            P("tensor", None),
            P(),
            P(),
            P(None, "tensor"),
            P("tensor"),
            P("tensor", None),
            P(),
        ),
        out_specs=(
            P(("dp", "tensor"), None),
            P(("dp", "tensor"), None),
            P(),
            P(None, None, "tensor"),
            P(None, "tensor"),
            P("tensor", None),
            P(),
            P(),
            P(None, "tensor"),
            P("tensor"),
            P("tensor", None),
            P(),
        ),
        check_vma=False,
    )
```

```python
import functools

import jax
import jax.numpy as jnp
from jax import lax
from jax.experimental import pallas as pl
from jax.experimental.pallas import tpu as pltpu
from jax.sharding import PartitionSpec as P

HEAD_DIM = 64
LANES = 128
EPSILON = 1e-05
MASKED_SCORE = -1e30
LONGEST = 512
BLOCK = 256
CHUNK = 256
UNITS = 256
QUARTERED = (0, 1, 3, 6, 7, 8)
F32 = jnp.float32
BF16 = jnp.bfloat16
NN = (((1,), (0,)), ((), ()))
NT = (((1,), (1,)), ((), ()))
TN = (((0,), (0,)), ((), ()))
GELU_A = 0.7978845608028654
GELU_B = 0.044715
MIB = 1024 * 1024
MESH = pl.DeviceIdType.MESH


def dot(a, b, dims=NN):
    return lax.dot_general(a, b, dims, preferred_element_type=F32)


def params(mib, **more):
    return pltpu.CompilerParams(vmem_limit_bytes=mib * MIB, **more)


def full(shape):
    return pl.BlockSpec(shape, lambda *_: (0,) * len(shape))


def once(shape):
    return pl.BlockSpec(shape, lambda *_: (0,) * len(shape), pipeline_mode=pl.Buffered(1))


def widen(ref, wide):
    wide[:, wide.shape[1] - LANES :] = jnp.zeros((wide.shape[0], LANES), F32)
    wide[:, : ref.shape[1]] = ref[...].astype(F32)
    return wide[...]


def norm_scale(values):
    total = jnp.sum(values, axis=-1, keepdims=True)
    square = jnp.sum(values * values, axis=-1, keepdims=True)
    return lax.rsqrt((square + total * total) / values.shape[-1] + EPSILON), total


def norm_back(values, gain, upstream):
    scale, total = norm_scale(values)
    weighted = upstream * values
    spread = jnp.sum(weighted * gain, axis=-1, keepdims=True)
    grad = upstream * gain * scale - (spread * scale * scale * scale / values.shape[-1]) * (
        values + total
    )
    return grad, jnp.sum(weighted * scale, axis=0, keepdims=True)


def scores_of(q_ref, k_ref, qh_ref, kn_ref, sel, at, span):
    q = q_ref[at, :] * 0.125
    qa = jnp.where(sel, q, qh_ref[at, :])
    ka = jnp.where(sel, k_ref[span, :], kn_ref[span, :])
    s = dot(ka, qa, NT)
    causal = lax.broadcasted_iota(jnp.int32, (BLOCK, BLOCK), 0) <= lax.broadcasted_iota(
        jnp.int32, (BLOCK, BLOCK), 1
    )
    early = s.shape[0] - BLOCK
    tail = jnp.where(causal, s[early:, :], MASKED_SCORE)
    return (tail if early == 0 else jnp.concatenate([s[:early, :], tail], axis=0)), q


def spans(length, row):
    for end in range(BLOCK, length + 1, BLOCK):
        start = max(0, end - BLOCK - LONGEST)
        base = row * length
        yield slice(base + end - BLOCK, base + end), slice(base + start, base + end)


def remote(src, dst, send, recv, device):
    return pltpu.make_async_remote_copy(
        src_ref=src, dst_ref=dst, send_sem=send, recv_sem=recv, device_id=device,
        device_id_type=MESH,
    )


def greet(partners):
    barrier = pltpu.get_barrier_semaphore()
    for device in partners:
        pl.semaphore_signal(barrier, inc=1, device_id=device, device_id_type=MESH)
    pl.semaphore_wait(barrier, len(partners))


def neighbours():
    dp, tensor = lax.axis_index("dp"), lax.axis_index("tensor")
    side = dp % 2
    to_core = (dp, tensor + 1 - 2 * (tensor % 2))
    return to_core, (dp, (tensor + 2) % 4), (dp + 1 - 2 * side, tensor), side


def pair_weights(even, odd, w, wo):
    for h, unit in enumerate((even, odd)):
        for i in range(3):
            at = LANES * i + HEAD_DIM * h
            w[at : at + HEAD_DIM, :] = unit[HEAD_DIM * i : HEAD_DIM * (i + 1), :]
        wo[HEAD_DIM * h : HEAD_DIM * (h + 1), :] = unit[3 * HEAD_DIM :, :]


def fwd_kernel(
    x_ref, c_ref, wqkv_ref, wout_ref, up_ref, down_ref, vec_ref, seg_ref,
    n_ref, cot_ref, c_sum_ref, qkv_ref, att_ref, lse_ref, resid_ref, n_two_ref, qh_ref, kn_ref,
    wa_ref, wf_ref, misc_all_ref,
    wa, stage, misc, w, wo, branch, wide,
    core_s, core_r, y_s, y_r, x_s, x_r, d_s, d_r, local_s, z_s, z_r, zz_s, zz_r,
    *, rows, pairs
):
    t = pl.program_id(0)
    tokens = x_ref.shape[0]
    length = tokens // rows
    heads = pairs // 2
    stored = x_ref.shape[1]
    model = stored + 1
    early, tail = heads, stage.shape[0]
    to_core, to_y, to_x, side = neighbours()
    last = early + tail
    dp = lax.axis_index("dp")
    level = dp // 2 % 2
    to_z = (dp + 2 - 4 * level, lax.axis_index("tensor"))

    def rows_of(k, across, along):
        if k not in QUARTERED:
            return pl.ds(pl.multiple_of(across * (CHUNK // 2), CHUNK // 2), CHUNK // 2)
        size = CHUNK // 4
        return pl.ds(pl.multiple_of((2 * across + along) * size, size), size)

    def held(quarter, k):
        if k == last:
            return misc.at[quarter]
        if k < early:
            return wa.at[quarter, k]
        return wf_ref.at[quarter, k - early]

    def own(k):
        return held(0, k) if k < early or k == last else stage.at[k - early]

    def core_copy(k):
        return remote(own(k), held(1, k), core_s.at[k], core_r.at[k], to_core)

    def y_copy(k):
        src, dst = own(k), held(2, k)
        if k < last:
            rows_ = rows_of(k, side, level)
            src, dst = src.at[rows_], dst.at[rows_]
        return remote(src, dst, y_s.at[k], y_r.at[k], to_y)

    def spread(k, across, along, send, recv, device):
        ref = held(2, k).at[rows_of(k, across, along)]
        return remote(ref, ref, send.at[k], recv.at[k], device)

    def x_copy(k, across):
        return spread(k, across, level, x_s, x_r, to_x)

    def z_copy(k, along):
        return spread(k, side, along, z_s, z_r, to_z)

    def zz_copy(k, along):
        return spread(k, 1 - side, along, zz_s, zz_r, to_z)

    def d_copy(k):
        return remote(held(2, k), held(3, k), d_s.at[k], d_r.at[k], to_core)

    def keep_copy(k):
        if k == last:
            return pltpu.make_async_copy(misc, misc_all_ref, local_s.at[k])
        if k < early:
            return pltpu.make_async_copy(wa.at[:, k], wa_ref.at[:, k], local_s.at[k])
        return pltpu.make_async_copy(stage.at[k - early], wf_ref.at[0, k - early], local_s.at[k])

    def x_on(k):
        y_copy(k).wait_recv()
        x_copy(k, side).start()
        if k in QUARTERED:
            z_copy(k, level).start()

    def z_on(k):
        x_copy(k, 1 - side).wait_recv()
        zz_copy(k, level).start()

    def d_on(k):
        if k == last:
            y_copy(k).wait_recv()
        elif k not in QUARTERED:
            x_copy(k, 1 - side).wait_recv()
        else:
            z_copy(k, 1 - level).wait_recv()
            zz_copy(k, 1 - level).wait_recv()
        d_copy(k).start()

    def start_y(k):
        y_copy(k).start()

    def start_core(k):
        core_copy(k).start()

    @pl.when(t == 0)
    def _():
        edge = slice(model - LANES, model)
        wa[0, :, :, edge] = jnp.zeros((early, CHUNK, LANES), BF16)
        for j in range(heads):
            head = slice(HEAD_DIM * j, HEAD_DIM * (j + 1))
            for i in range(3):
                wa[0, j, HEAD_DIM * i : HEAD_DIM * (i + 1), :stored] = wqkv_ref[i, head, :]
            wa[0, j, 3 * HEAD_DIM :, :stored] = wout_ref[head, :]
        misc[0] = jnp.zeros_like(misc[0])
        for p in range(2):
            for j in range(heads):
                for i, row in ((0, 5), (2, 6)):
                    at = LANES * i + HEAD_DIM * p
                    misc[0, p, j : j + 1, at : at + HEAD_DIM] = vec_ref[
                        row : row + 1, HEAD_DIM * j : HEAD_DIM * (j + 1)
                    ]
            wide_half = misc.shape[3]
            misc[0, p, heads : heads + 1, :] = vec_ref[4:5, wide_half * p : wide_half * (p + 1)]
        greet([to_core, to_y, to_x, to_z])
        for k in (last, 0):
            core_copy(k).start()
            y_copy(k).start()
        for k in range(1, early):
            core_copy(k).start()
        count = tail // 2
        stage[:, :, edge] = jnp.zeros((tail, CHUNK, LANES), BF16)
        stage[count - 1, CHUNK - 16 :, :] = jnp.zeros((16, model), BF16)
        for i in range(count):
            end = min(CHUNK * (i + 1), stored)
            stage[i, : end - CHUNK * i, :] = up_ref[CHUNK * i : end, :]
            stage[count + i, :, :stored] = down_ref[CHUNK * i : CHUNK * (i + 1), :]
        for k in range(early, last):
            keep_copy(k).start()
        branch[...] = jnp.zeros_like(branch)
        c_sum = jnp.zeros((1, model), F32)
        for i in range(0, tokens, CHUNK):
            r = slice(i, i + CHUNK)
            x = widen(x_ref.at[r, :], wide)
            n_ref[r, :] = (x * norm_scale(x)[0] * vec_ref[0:1, :model]).astype(BF16)
            c = widen(c_ref.at[r, :], wide)
            cot_ref[r, :] = c.astype(BF16)
            c_sum += jnp.sum(c, axis=0, keepdims=True)
        c_sum_ref[...] = c_sum
        lane = lax.broadcasted_iota(jnp.int32, (1, LANES), 1) % HEAD_DIM
        for row in range(rows):
            document = jnp.broadcast_to(seg_ref[row : row + 1, :].astype(F32), (LANES, length)).T
            hot = document == lane.astype(F32)
            r = slice(row * length, (row + 1) * length)
            qh_ref[r, :] = jnp.where(hot, 1.0, 0.0).astype(BF16)
            kn_ref[r, :] = jnp.where(hot | (lane >= 8), 0.0, MASKED_SCORE).astype(BF16)
        core_copy(last).wait_recv()

    events = {
        (0, 0): [(start_y, 6)],
        (0, 1): [(x_on, 0), (start_y, 1)],
        (0, 2): [(z_on, 0), (start_y, 8)],
        (0, 4): [(x_on, 1), (start_y, 2)],
        (1, 0): [(x_on, 6)],
        (1, 1): [(d_on, 0)],
        (1, 2): [(x_on, 8)],
        (1, 3): [(d_on, last)],
        (1, 4): [(z_on, 1), (start_y, 3)],
        (2, 0): [(x_on, 2), (start_y, 7)],
        (2, 2): [(z_on, 6)],
        (2, 3): [(start_y, 5), (start_core, 6)],
        (2, 4): [(x_on, 3), (start_core, 4)],
        (3, 0): [(d_on, 1), (x_on, 7), (start_core, 3)],
        (3, 1): [(z_on, 8)],
        (3, 2): [(start_y, 4), (start_core, 5)],
        (3, 4): [(d_on, 2), (x_on, 5)],
        (4, 0): [(start_core, 7)],
        (4, 1): [(z_on, 7)],
        (4, 2): [(d_on, 6)],
        (4, 3): [(x_on, 4), (start_core, 8)],
        (4, 4): [(z_on, 3)],
        (5, 0): [(d_on, 5), (d_on, 8)],
        (5, 2): [(d_on, 7)],
        (5, 3): [(d_on, 3)],
        (5, 4): [(d_on, 4)],
    }
    rest = []

    def run(slot):
        for (step, at), todo in events.items():
            if at == slot and todo:

                @pl.when(t == step)
                def _(todo=todo):
                    for event, k in todo:
                        event(k)

    for step in range(pairs):

        @pl.when(t == step)
        def _(far=step // heads, j=step % heads):
            (d_copy if far else core_copy)(j).wait_recv()
            if far and j == 0:
                d_copy(last).wait_recv()

    first = lax.broadcasted_iota(jnp.int32, (1, LANES), 1) < HEAD_DIM
    units = [(2 * (t // heads) + h, t % heads) for h in range(2)]
    pair_weights(*(wa.at[quarter, j] for quarter, j in units), w, wo)
    bias = sum(
        jnp.where(j == row, misc[quarter, h, row : row + 1, :], 0.0)
        for h, (quarter, j) in enumerate(units)
        for row in range(heads)
    )
    qkv_ref[...] = (dot(n_ref[...], w[...], NT) + bias).astype(BF16)
    q_ref, k_ref, v_ref = (qkv_ref.at[:, j * LANES : (j + 1) * LANES] for j in range(3))
    run(0)
    slot = 1
    for row in range(rows):
        for at, span in spans(length, row):
            parts = []
            for h in range(2):
                sel = first if h == 0 else ~first
                s, _ = scores_of(q_ref, k_ref, qh_ref, kn_ref, sel, at, span)
                m = jnp.max(s, axis=0, keepdims=True)
                p = jnp.exp(s - m)
                total = jnp.sum(p, axis=0, keepdims=True)
                weights = (p * (1.0 / total)).astype(BF16)
                parts.append(dot(weights, v_ref[span, :], TN))
                lse_ref[h : h + 1, at] = m + jnp.log(total)
            att_ref[at, :] = jnp.where(first, parts[0], parts[1]).astype(BF16)
            if slot < 4:
                run(slot)
                slot += 1
    branch[...] += dot(att_ref[...], wo[...])
    run(4)

    @pl.when(t == pairs - 1)
    def _():
        for i in range(0, tokens, CHUNK):
            r = slice(i, i + CHUNK)
            resid = widen(x_ref.at[r, :], wide) + (branch[r, :] + vec_ref[2:3, :model])
            resid_ref[r, :] = resid
            n_two_ref[r, :] = (resid * norm_scale(resid)[0] * vec_ref[1:2, :model]).astype(BF16)
        for event, k in rest:
            event(k)
        for k in (*range(early), last):
            keep_copy(k).start()
        for k in range(early, last):
            core_copy(k).wait_recv()
            d_copy(k).wait_recv()
        for k in range(last + 1):
            core_copy(k).wait_send()
            y_copy(k).wait_send()
            if k < last:
                x_copy(k, side).wait_send()
            if k in QUARTERED:
                z_copy(k, level).wait_send()
                zz_copy(k, level).wait_send()
            d_copy(k).wait_send()
            keep_copy(k).wait()


def forward(x, c, wqkv, wout, up, down, vec, seg):
    tokens, stored = x.shape
    model = stored + 1
    heads = wqkv.shape[1] // HEAD_DIM
    pairs = 2 * heads
    tail = 2 * (model // CHUNK)

    def of(*shape):
        return pl.BlockSpec((None, *shape), lambda p: (p,) + (0,) * len(shape))

    anywhere = pl.BlockSpec(memory_space=pl.ANY)
    sems = pltpu.SemaphoreType.DMA((heads + tail + 1,))
    rows = seg.shape[0]
    misc = (2, 8, model // 2)
    inputs = [x, c, wqkv, wout, up, down, vec, seg]
    big = once((tokens, model))
    outs = [
        (big, (tokens, model), BF16),
        (big, (tokens, model), BF16),
        (once((1, model)), (1, model), F32),
        (of(tokens, 3 * LANES), (pairs, tokens, 3 * LANES), BF16),
        (of(tokens, LANES), (pairs, tokens, LANES), BF16),
        (of(2, tokens), (pairs, 2, tokens), F32),
        (big, (tokens, model), F32),
        (big, (tokens, model), BF16),
        (once((tokens, LANES)), (tokens, LANES), BF16),
        (once((tokens, LANES)), (tokens, LANES), BF16),
        (anywhere, (4, heads, CHUNK, model), BF16),
        (anywhere, (4, tail, CHUNK, model), BF16),
        (anywhere, (4, *misc), F32),
    ]
    return pl.pallas_call(
        functools.partial(fwd_kernel, rows=rows, pairs=pairs),
        grid=(pairs,),
        in_specs=[once(v.shape) for v in inputs],
        out_specs=[spec for spec, _, _ in outs],
        out_shape=[jax.ShapeDtypeStruct(shape, dtype) for _, shape, dtype in outs],
        scratch_shapes=[
            pltpu.VMEM((4, heads, CHUNK, model), BF16),
            pltpu.VMEM((tail, CHUNK, model), BF16),
            pltpu.VMEM((4, *misc), F32),
            pltpu.VMEM((3 * LANES, model), BF16),
            pltpu.VMEM((LANES, model), BF16),
            pltpu.VMEM((tokens, model), F32),
            pltpu.VMEM((CHUNK, model), F32),
        ]
        + [sems] * 13,
        compiler_params=params(60, collective_id=1, has_side_effects=True),
        name="forward",
    )(*inputs)


def backward_kernel(
    n_two_ref, c_ref, n_ref, x_ref, vec_ref, c_sum_ref, up_ref, down_ref, bias_ref,
    qkv_ref, att_ref, lse_ref, even_ref, odd_ref, qh_ref, kn_ref, resid_ref,
    output_ref, grad_in_ref, red_ref, red_late_ref, total_ref,
    out, back, d_resid, nt, ct, db, stage, bias_row, w, wo, da, dqkv, dk_acc, dv_acc, wide_x,
    g, core_in, y_in, x_in, z_in, ag, xag_in, sv, sv_in, sv_z,
    core_s, core_r, y_s, y_r, x_s, x_r, z_s, z_r, a_s, a_r, xa_s, xa_r, out_s,
    sv_s, sv_r, svz_s, svz_r, resid_s, rows_s,
    *, rows, pairs, group, blocks
):
    t = pl.program_id(0)
    tokens, model = n_ref.shape
    length = tokens // rows
    front = 4 * blocks
    early, late = 2 * blocks, pairs // 2
    chunks = early + late
    others = group // 2
    half, units = g.shape[2:]
    keep = half // others
    pieces = half // HEAD_DIM
    dp, tensor = lax.axis_index("dp"), lax.axis_index("tensor")
    place = (dp % group) // 2
    mine = pl.ds(pl.multiple_of(place * keep, keep), keep)
    to_core, to_y, to_x, side = neighbours()

    def place_of(o):
        return (place + o) % others

    def to_z(o):
        return (dp - dp % group + place_of(o) * 2 + side, tensor)

    box = 2 * chunks

    def core_copy(which, k, at, slot):
        return remote(
            g.at[box + at], core_in.at[which, slot], core_s.at[which, k], core_r.at[which, k], to_core
        )

    def early_core(which, k):
        return core_copy(which, k, k, k)

    def late_core(which, i):
        return core_copy(which, early + i, late * which + i, i)

    def y_copy(k):
        return remote(g.at[chunks + k], y_in.at[k], y_s.at[k], y_r.at[k], to_y)

    def x_copy(k):
        return remote(g.at[k, 1 - side], x_in.at[k], x_s.at[k], x_r.at[k], to_x)

    def z_copy(k, o):
        rows_of = pl.ds(pl.multiple_of(place_of(o) * keep, keep), keep)
        return remote(
            g.at[k, side, rows_of], z_in.at[k, o - 1], z_s.at[k, o - 1], z_r.at[k, o - 1], to_z(o)
        )

    def a_copy(k, o):
        return remote(ag.at[k, mine], ag.at[k, mine], a_s.at[k, o - 1], a_r.at[k, o - 1], to_z(o))

    def a_wait(k, o):
        rows_of = pl.ds(pl.multiple_of(place_of(others - o) * keep, keep), keep)
        part = ag.at[k, rows_of]
        remote(part, part, a_s.at[k, o - 1], a_r.at[k, o - 1], to_z(o)).wait_recv()

    def xa_copy(k):
        return remote(ag.at[k], xag_in.at[k], xa_s.at[k], xa_r.at[k], to_x)

    def out_copies(k, i, act):
        which = side + i - 2 * side * i
        src = xag_in if i else ag

        @pl.when(k < early)
        def _():
            at = jnp.minimum(k, early - 1)
            lines = pl.ds(pl.multiple_of(which * half, half), half)
            cols = pl.ds(pl.multiple_of(at // 2 * units, units), units)
            act(pltpu.make_async_copy(src.at[at], red_ref.at[at % 2, lines, cols], out_s.at[k, i, 0]))

        @pl.when(k >= early)
        def _():
            at = jnp.maximum(k, early)
            head = pl.ds(pl.multiple_of((chunks - 1 - at) * HEAD_DIM, HEAD_DIM), HEAD_DIM)
            for n in range(pieces):
                piece = which * pieces + n
                cols = pl.ds(pl.multiple_of(piece // 4 * units, units), units)
                act(
                    pltpu.make_async_copy(
                        src.at[at, HEAD_DIM * n : HEAD_DIM * (n + 1)],
                        red_late_ref.at[piece % 4, head, cols],
                        out_s.at[k, i, n],
                    )
                )

    def plus(at, value):
        g[at] = (g[at].astype(F32) + value.astype(F32)).astype(BF16)

    def send_y(k):
        @pl.when(k >= early)
        def _():
            i = jnp.maximum(k, early) - early
            late_core(0, i).wait_recv()
            plus(chunks + early + i, core_in[0, i])

        y_copy(k).start()

    def send_x(k):
        @pl.when(k >= early)
        def _():
            i = jnp.maximum(k, early) - early
            late_core(1, i).wait_recv()
            plus(early + i, core_in[1, i])

        y_copy(k).wait_recv()
        plus(k, y_in[k])
        x_copy(k).start()

    def send_z(k):
        x_copy(k).wait_recv()
        g[k, side] = (g[k, side].astype(F32) + x_in[k].astype(F32)).astype(BF16)
        for o in range(1, others):
            z_copy(k, o).start()

    def send_back(k):
        total = g[k, side, mine].astype(F32)
        for o in range(1, others):
            z_copy(k, o).wait_recv()
            total += z_in[k, o - 1].astype(F32)
        ag[k, mine] = total.astype(BF16)
        for o in range(1, others):
            a_copy(k, o).start()

    def send_back_x(k):
        for o in range(1, others):
            a_wait(k, o)
        xa_copy(k).start()
        out_copies(k, 0, lambda copy: copy.start())

    def finish(k):
        xa_copy(k).wait_recv()
        out_copies(k, 1, lambda copy: copy.start())

    plan = [
        (finish, [(16, 2), (16, 4), (17, 0), (17, 4), (17, 4)]),
        (send_back_x, [(12, 3), (14, 3), (14, 4), (15, 4), (16, 4), (17, 4)]),
        (send_back, [(11, 0), (12, 0), (13, 2), (14, 3), (16, 0), (16, 2), (17, 2)]),
        (send_z, [(9, 0), (10, 0), (12, 2), (13, 0), (14, 0), (15, 1), (16, 4), (17, 4)]),
        (send_x, [(7, 0), (8, 0), (10, 0), (12, 0), (12, 3), (14, 1), (16, 1), (17, 1)]),
        (send_y, [(2, 0), (3, 0), (6, 0), (8, 0), (10, 0), (12, 2), (14, 0), (16, 0), (17, 0)]),
    ]

    def run(slot, first, end):
        for event, times in plan:
            now = [(step, k) for k, (step, at) in enumerate(times) if at == slot and first <= step < end]
            while now:
                table = dict(now[::-1])
                now = [(step, k) for step, k in now if table[step] != k]
                k = jnp.int32(-1)
                for step, at in table.items():
                    k = jnp.where(t == step, at, k)

                @pl.when(k >= 0)
                def _(event=event, k=k):
                    event(jnp.maximum(k, 0))

    def sv_copy(i, src, device):
        return remote(src, sv_in.at[i], sv_s.at[i], sv_r.at[i], device)

    def svz_copy(o):
        return remote(sv_z.at[place], sv_z.at[place], svz_s.at[o - 1], svz_r.at[o - 1], to_z(o))

    def small_y():
        for i in (0, 1):
            sv_copy(i, sv.at[3 - 2 * i], to_core).wait_recv()
        sv[2] += sv_in[0]
        sv_copy(2, sv.at[2], to_y).start()

    def small_x():
        sv_copy(2, sv.at[2], to_y).wait_recv()
        sv[0] = (sv[0] + sv_in[1]) + sv_in[2]
        sv_copy(3, sv.at[0], to_x).start()

    def small_z():
        sv_copy(3, sv.at[0], to_x).wait_recv()
        sv_z[place] = sv[0] + sv_in[3]
        for o in range(1, others):
            svz_copy(o).start()

    def small_end():
        for o in range(1, others):
            part = sv_z.at[place_of(others - o)]
            remote(part, part, svz_s.at[o - 1], svz_r.at[o - 1], to_z(o)).wait_recv()
        total = sv_z[0]
        for i in range(1, others):
            total += sv_z[i]
        total_ref[...] = total

    def resid_copy():
        return pltpu.make_async_copy(resid_ref, d_resid, resid_s)

    def grad_copy(i):
        r = slice(CHUNK * i, CHUNK * (i + 1))
        return pltpu.make_async_copy(db.at[r], grad_in_ref.at[r], rows_s.at[i])

    def output_copy(i):
        r = slice(CHUNK * i, CHUNK * (i + 1))
        return pltpu.make_async_copy(stage.at[i % 2], output_ref.at[r], rows_s.at[i])

    def feed_forward():
        b, quarter = t // 4, 3 - t % 4
        up = up_ref[...].reshape(model, units)
        down = down_ref[...]
        wide = bias_ref.shape[2]
        for h in range(2):
            bias_row[0:1, wide * h : wide * (h + 1)] = bias_ref[h, late : late + 1, :]
        lanes = pl.ds(pl.multiple_of(b * units, units), units)
        pre = dot(n_two_ref[...], up) + bias_row[0:1, lanes]
        dh = dot(c_ref[...], down, NT)
        sq = pre * pre
        th = jnp.tanh(pre * (GELU_A + (GELU_A * GELU_B) * sq))
        level = 0.5 + 0.5 * th
        hidden = (pre * level).astype(BF16)
        slope = level + (0.5 * pre) * (1.0 - th * th) * (GELU_A + (3.0 * GELU_A * GELU_B) * sq)
        dpre = (dh * slope).astype(BF16)
        out[...] += dot(hidden, down)
        back[...] += dot(dpre, up, NT)
        sv[quarter, 0:1, lanes] = jnp.sum(dpre.astype(F32), axis=0, keepdims=True)
        grads = dot(nt[...], dpre).astype(BF16), dot(ct[...], hidden).astype(BF16)

        @pl.when(t % 4 == 2)
        def _():
            for m in range(2):
                early_core(0, 2 * b + m).wait_send()

        base = jnp.where(quarter == 0, 0, jnp.where(quarter == 2, chunks, box)) + 2 * b
        for m in range(2):
            for h in range(2):
                g[base + m, h] = grads[m][half * h : half * (h + 1)]
        for m in range(2):
            k = 2 * b + m
            for which in range(2):

                @pl.when(t % 4 == 2 * which)
                def _(which=which, k=k):
                    early_core(which, k).start()

                @pl.when(t % 4 == 2 * which + 1)
                def _(which=which, k=k):
                    early_core(which, k).wait_recv()
                    plus((1 - which) * chunks + k, core_in[which, k])

    def turn():
        resid_copy().wait()
        gain_sum = branch_sum = jnp.zeros((1, model), F32)
        for i in range(tokens // CHUNK):
            r = slice(CHUNK * i, CHUNK * (i + 1))
            resid = d_resid[r, :]
            if i >= 2:
                output_copy(i - 2).wait()
            stage[i % 2] = (resid + (out[r, :] + vec_ref[3:4, :model])).astype(BF16)
            output_copy(i).start()
            out[r, :] = jnp.zeros((CHUNK, model), F32)
            d_norm, part = norm_back(resid, vec_ref[1:2, :model], back[r, :])
            d_rows = c_ref[r, :].astype(F32) + d_norm
            d_resid[r, :] = d_rows
            d_branch = d_rows.astype(BF16)
            db[r, :] = d_branch
            gain_sum += part
            branch_sum += jnp.sum(d_branch.astype(F32), axis=0, keepdims=True)
        for i in range(tokens // CHUNK - 2, tokens // CHUNK):
            output_copy(i).wait()
        for i in range(4):
            sv[i, 2:3, :] = branch_sum
            sv[i, 3:4, :] = gain_sum
        for k in range(early):
            early_core(1, k).wait_send()

    def norm_one():
        gain_sum = jnp.zeros((1, model), F32)
        for i in range(tokens // CHUNK):
            r = slice(CHUNK * i, CHUNK * (i + 1))
            d_norm, part = norm_back(widen(x_ref.at[r, :], wide_x), vec_ref[0:1, :model], out[r, :])
            db[r, :] = (d_resid[r, :] + d_norm).astype(BF16)
            grad_copy(i).start()
            gain_sum += part
        for i in range(4):
            sv[i, 4:5, :] = gain_sum
        for i in (0, 1):
            sv_copy(i, sv.at[3 - 2 * i], to_core).start()

    first = lax.broadcasted_iota(jnp.int32, (1, LANES), 1) < HEAD_DIM
    zero = jnp.zeros((), BF16)
    q_ref, k_ref, v_ref = (qkv_ref.at[:, j * LANES : (j + 1) * LANES] for j in range(3))

    def attend(at, span):
        dq = None
        for h in range(2):
            sel = first if h == 0 else ~first
            s, q = scores_of(q_ref, k_ref, qh_ref, kn_ref, sel, at, span)
            qm = jnp.where(sel, q, zero)
            km = jnp.where(sel, k_ref[span, :], zero)
            dom = jnp.where(sel, da[at, :], zero)
            p = jnp.exp(s - lse_ref[h : h + 1, at])
            dp_ = dot(v_ref[span, :], dom, NT)
            u = p * dp_
            inner = jnp.sum(u, axis=0, keepdims=True)
            ds = (u - p * inner).astype(BF16)
            dv_acc[span, :] += dot(p.astype(BF16), dom)
            dk_acc[span, :] += dot(ds, qm)
            part = dot(ds, km, TN)
            dq = part if dq is None else dq + part
        dqkv[at, :LANES] = (dq * 0.125).astype(BF16)

    def attention():
        pair_weights(even_ref, odd_ref, w, wo)
        da[...] = dot(db[...], wo[...], NT).astype(BF16)
        dk_acc[...] = jnp.zeros_like(dk_acc)
        dv_acc[...] = jnp.zeros_like(dv_acc)
        run(0, front, front + pairs)
        slot = 1
        for row in range(rows):
            for at, span in spans(length, row):
                attend(at, span)
                if slot < 5:
                    run(slot, front, front + pairs)
                    slot += 1
        dqkv[:, LANES : 2 * LANES] = dk_acc[...].astype(BF16)
        dqkv[:, 2 * LANES :] = dv_acc[...].astype(BF16)
        grads = dot(dqkv[...], n_ref[...], TN).astype(BF16)
        grads_out = dot(att_ref[...], db[...], TN).astype(BF16)
        pair = pairs - 1 - (t - front)
        far, j = pair // late, pair % late
        i = late - 1 - j
        for h in range(2):
            base = i + ((box + late * (1 - far)) if h else (early + chunks * far))
            for block in range(model // units):
                cols = slice(units * block, units * (block + 1))
                for p in range(4):
                    if p < 3:
                        lines = grads[LANES * p + HEAD_DIM * h : LANES * p + HEAD_DIM * (h + 1), cols]
                    else:
                        lines = grads_out[HEAD_DIM * h : HEAD_DIM * (h + 1), cols]
                    at = CHUNK * block + HEAD_DIM * p
                    g[base, at // half, at % half : at % half + HEAD_DIM, :] = lines
        late_core(1 - far, i).start()
        out[...] += dot(dqkv[...], w[...])
        sums = jnp.sum(dqkv[...].astype(F32), axis=0, keepdims=True)
        for h in range(2):
            for line in range(late):

                @pl.when(j == line)
                def _(line=8 + line, h=h):
                    for part in (0, 2):
                        at = LANES * part + HEAD_DIM * h
                        sv[2 * far + h, line : line + 1, LANES * part : LANES * part + HEAD_DIM] = (
                            sums[:, at : at + HEAD_DIM]
                        )

    @pl.when(t == 0)
    def _():
        greet([to_core, to_y, to_x] + [to_z(o) for o in range(1, others)])
        out[...] = jnp.zeros_like(out)
        back[...] = jnp.zeros_like(back)
        sv[...] = jnp.zeros_like(sv)
        for i in range(4):
            sv[i, 1:2, :] = c_sum_ref[...]
        for i in range(0, tokens, CHUNK):
            nt[:, i : i + CHUNK] = n_two_ref[i : i + CHUNK, :].T
            ct[:, i : i + CHUNK] = c_ref[i : i + CHUNK, :].T

    @pl.when(t == front - 2)
    def _():
        resid_copy().start()

    @pl.when(t < front)
    def _():
        run(0, 0, front)
        feed_forward()

    pl.when(t == front - 1)(turn)
    pl.when((t >= front) & (t < front + pairs))(attention)

    @pl.when(t == front + pairs)
    def _():
        send_x(8)
        finish(5)
        send_back(7)
        norm_one()
        send_back_x(6)
        send_z(8)
        small_y()
        send_back_x(7)
        small_x()
        send_back(8)
        send_back_x(8)
        small_z()
        finish(6)
        small_end()
        finish(7)
        finish(8)

        @pl.loop(0, chunks)
        def _(k):
            y_copy(k).wait_send()
            x_copy(k).wait_send()
            for o in range(1, others):
                z_copy(k, o).wait_send()
                a_copy(k, o).wait_send()
            xa_copy(k).wait_send()
            for i in range(2):
                out_copies(k, i, lambda copy: copy.wait())

        for which in range(2):
            for i in range(late):
                late_core(which, i).wait_send()
        for i, device in enumerate((to_core, to_core, to_y, to_x)):
            sv_copy(i, sv.at[0], device).wait_send()
        for o in range(1, others):
            svz_copy(o).wait_send()
        for i in range(tokens // CHUNK):
            grad_copy(i).wait()


def backward(
    n_two, c, resid, w_ffn, misc, n, x, vec, c_sum, qkv, att, lse, w_attn, qh, kn, rows, group
):
    tokens, model = n.shape
    stored = x.shape[1]
    pairs = qkv.shape[0]
    blocks = model // UNITS
    front, early, late = 4 * blocks, 2 * blocks, pairs // 2
    chunks = early + late
    others = group // 2
    half = model // 2
    lines = 16
    wide = misc.shape[3]

    def unit_block(t):
        t = jnp.minimum(t, front - 1)
        return 3 - t % 4, t // 4

    def up_at(t):
        quarter, b = unit_block(t)
        return quarter, 0, 0, b

    def down_at(t):
        quarter, b = unit_block(t)
        return quarter, model // CHUNK + b, 0, 0

    def bias_at(t):
        return unit_block(t)[0], 0, 0, 0

    def pair_at(t):
        return pairs - 1 - jnp.clip(t - front, 0, pairs - 1)

    def of(shape):
        return pl.BlockSpec((None, *shape), lambda t: (pair_at(t), 0, 0))

    def unit(h):
        return pl.BlockSpec(
            (None, None, CHUNK, model),
            lambda t: (2 * (pair_at(t) // late) + h, pair_at(t) % late, 0, 0),
        )

    anywhere = pl.BlockSpec(memory_space=pl.ANY)
    sems = pltpu.SemaphoreType.DMA
    between = max(others - 1, 1)
    many = (chunks, between)
    big = once((tokens, model))
    return pl.pallas_call(
        functools.partial(backward_kernel, rows=rows, pairs=pairs, group=group, blocks=blocks),
        grid=(front + pairs + 1,),
        in_specs=[
            big, big, big, once((tokens, stored)), full(vec.shape), full((1, model)),
            pl.BlockSpec((None, model // CHUNK, CHUNK, UNITS), up_at),
            pl.BlockSpec((None, None, CHUNK, model), down_at),
            pl.BlockSpec((None, 2, 8, wide), bias_at),
            of((tokens, 3 * LANES)), of((tokens, LANES)), of((2, tokens)), unit(0), unit(1),
            once((tokens, LANES)), once((tokens, LANES)), anywhere,
        ],
        out_specs=[anywhere] * 4 + [once((lines, model))],
        out_shape=[
            jax.ShapeDtypeStruct((tokens, model), BF16),
            jax.ShapeDtypeStruct((tokens, model), BF16),
            jax.ShapeDtypeStruct((2, model, blocks * UNITS), BF16),
            jax.ShapeDtypeStruct((4, late * HEAD_DIM, model), BF16),
            jax.ShapeDtypeStruct((lines, model), F32),
        ],
        scratch_shapes=[pltpu.VMEM((tokens, model), F32)] * 3
        + [pltpu.VMEM((model, tokens), BF16)] * 2
        + [
            pltpu.VMEM((tokens, model), BF16),
            pltpu.VMEM((2, CHUNK, model), BF16),
            pltpu.VMEM((8, model), F32),
            pltpu.VMEM((3 * LANES, model), BF16),
            pltpu.VMEM((LANES, model), BF16),
            pltpu.VMEM((tokens, LANES), BF16),
            pltpu.VMEM((tokens, 3 * LANES), BF16),
            pltpu.VMEM((tokens, LANES), F32),
            pltpu.VMEM((tokens, LANES), F32),
            pltpu.VMEM((CHUNK, model), F32),
            pltpu.VMEM((2 * chunks + early, 2, half, UNITS), BF16),
            pltpu.VMEM((2, early, 2, half, UNITS), BF16),
            pltpu.VMEM((chunks, 2, half, UNITS), BF16),
            pltpu.VMEM((chunks, half, UNITS), BF16),
            pltpu.VMEM((*many, half // others, UNITS), BF16),
            pltpu.VMEM((chunks, half, UNITS), BF16),
            pltpu.VMEM((chunks, half, UNITS), BF16),
            pltpu.VMEM((4, lines, model), F32),
            pltpu.VMEM((4, lines, model), F32),
            pltpu.VMEM((others, lines, model), F32),
            sems((2, chunks)), sems((2, chunks)), sems((chunks,)), sems((chunks,)),
            sems((chunks,)), sems((chunks,)), sems(many), sems(many), sems(many), sems(many),
            sems((chunks,)), sems((chunks,)), sems((chunks, 2, half // HEAD_DIM)),
            sems((4,)), sems((4,)), sems((between,)), sems((between,)), sems, sems((tokens // CHUNK,)),
        ],
        compiler_params=params(63, collective_id=0, has_side_effects=True),
        name="backward",
    )(n_two, c, n, x, vec, c_sum, w_ffn, w_ffn, misc, qkv, att, lse, w_attn, w_attn, qh, kn, resid)


def solution(mesh):
    n_dp, n_tensor = mesh.shape["dp"], mesh.shape["tensor"]
    assert n_tensor == 4 and n_dp % 4 == 0 and n_dp & (n_dp - 1) == 0
    bits = [1 << i for i in range(n_dp.bit_length() - 1)]
    group = min(n_dp, 8)

    def to_dp(v, bit):
        return lax.ppermute(v, "dp", [(i, i ^ bit) for i in range(n_dp)])

    def local(
        layer_input, segments, cotangent, gain_one, w_qkv, b_qv, w_out, b_out, gain_two,
        w_up, b_up, w_down, b_down,
    ):
        rows = segments.shape[0]
        tokens, stored = layer_input.shape
        model = stored + 1
        heads = w_qkv.shape[2] // HEAD_DIM
        units = w_up.shape[1]

        vec = [gain_one, gain_two, b_out, b_down, b_up, *b_qv]
        vec = jnp.concatenate([jnp.pad(v.astype(F32), (0, 1024 - v.shape[0])) for v in vec])
        vec = jnp.pad(vec, (0, 1024)).reshape(8, 1024)
        (
            n_one, cot, grad_bdown, qkv, att, lse, resid, n_two, qh, kn, w_attn, w_ffn, misc
        ) = forward(
            layer_input, cotangent, w_qkv.transpose(0, 2, 1), w_out, w_up, w_down, vec, segments
        )
        output, input_grad, *reduced, small = backward(
            n_two, cot, resid, w_ffn, misc, n_one, layer_input, vec, grad_bdown, qkv, att, lse, w_attn,
            qh, kn, rows, group,
        )
        for bit in bits:
            if bit >= group:
                small = small + to_dp(small, bit)
                reduced = [(v.astype(F32) + to_dp(v, bit).astype(F32)).astype(BF16) for v in reduced]
        (grad_up, grad_down), grad_heads = reduced
        grad_up = grad_up[:stored].astype(F32)
        grad_down = grad_down.T[:, :stored].astype(F32)
        grad_qkv = grad_heads[:3, :, :stored].astype(F32).transpose(0, 2, 1)
        grad_out = grad_heads[3, :, :stored].astype(F32)
        per_head = small[8 : 8 + heads]
        grad_bqv = jnp.stack(
            [per_head[:, :HEAD_DIM].reshape(-1), per_head[:, 2 * LANES : 2 * LANES + HEAD_DIM].reshape(-1)]
        )
        return (
            output[:, :stored],
            input_grad[:, :stored],
            small[4, :stored],
            grad_qkv,
            grad_bqv,
            grad_out,
            small[2, :stored],
            small[3, :stored],
            grad_up,
            small[0],
            grad_down,
            small[1, :stored],
        )

    return jax.shard_map(
        local,
        mesh=mesh,
        in_specs=(
            P(("dp", "tensor"), None),
            P(("dp", "tensor"), None),
            P(("dp", "tensor"), None),
            P(),
            P(None, None, "tensor"),
            P(None, "tensor"),
            P("tensor", None),
            P(),
            P(),
            P(None, "tensor"),
            P("tensor"),
            P("tensor", None),
            P(),
        ),
        out_specs=(
            P(("dp", "tensor"), None),
            P(("dp", "tensor"), None),
            P(),
            P(None, None, "tensor"),
            P(None, "tensor"),
            P("tensor", None),
            P(),
            P(),
            P(None, "tensor"),
            P("tensor"),
            P("tensor", None),
            P(),
        ),
        check_vma=False,
    )
```

```python
import functools

import jax
import jax.numpy as jnp
from jax import lax
from jax.experimental import pallas as pl
from jax.experimental.pallas import tpu as pltpu
from jax.sharding import PartitionSpec as P

HEAD_DIM = 64
LANES = 128
EPSILON = 1e-05
MASKED_SCORE = -1e30
LONGEST = 512
BLOCK = 256
CHUNK = 256
UNITS = 256
QUARTERED = (0, 1, 3, 6, 7, 8)
F32 = jnp.float32
BF16 = jnp.bfloat16
NN = (((1,), (0,)), ((), ()))
NT = (((1,), (1,)), ((), ()))
TN = (((0,), (0,)), ((), ()))
GELU_A = 0.7978845608028654
GELU_B = 0.044715
MIB = 1024 * 1024
MESH = pl.DeviceIdType.MESH


def dot(a, b, dims=NN):
    return lax.dot_general(a, b, dims, preferred_element_type=F32)


def params(mib, **more):
    return pltpu.CompilerParams(vmem_limit_bytes=mib * MIB, **more)


def full(shape):
    return pl.BlockSpec(shape, lambda *_: (0,) * len(shape))


def once(shape):
    return pl.BlockSpec(shape, lambda *_: (0,) * len(shape), pipeline_mode=pl.Buffered(1))


def widen(ref, wide):
    wide[:, wide.shape[1] - LANES :] = jnp.zeros((wide.shape[0], LANES), F32)
    wide[:, : ref.shape[1]] = ref[...].astype(F32)
    return wide[...]


def norm_scale(values):
    total = jnp.sum(values, axis=-1, keepdims=True)
    square = jnp.sum(values * values, axis=-1, keepdims=True)
    return lax.rsqrt((square + total * total) / values.shape[-1] + EPSILON), total


def norm_back(values, gain, upstream):
    scale, total = norm_scale(values)
    weighted = upstream * values
    spread = jnp.sum(weighted * gain, axis=-1, keepdims=True)
    grad = upstream * gain * scale - (spread * scale * scale * scale / values.shape[-1]) * (
        values + total
    )
    return grad, jnp.sum(weighted * scale, axis=0, keepdims=True)


def scores_of(q_ref, k_ref, qh_ref, kn_ref, sel, at, span):
    q = q_ref[at, :] * 0.125
    qa = jnp.where(sel, q, qh_ref[at, :])
    ka = jnp.where(sel, k_ref[span, :], kn_ref[span, :])
    s = dot(ka, qa, NT)
    causal = lax.broadcasted_iota(jnp.int32, (BLOCK, BLOCK), 0) <= lax.broadcasted_iota(
        jnp.int32, (BLOCK, BLOCK), 1
    )
    early = s.shape[0] - BLOCK
    tail = jnp.where(causal, s[early:, :], MASKED_SCORE)
    return (tail if early == 0 else jnp.concatenate([s[:early, :], tail], axis=0)), q


def spans(length, row):
    for end in range(BLOCK, length + 1, BLOCK):
        start = max(0, end - BLOCK - LONGEST)
        base = row * length
        yield slice(base + end - BLOCK, base + end), slice(base + start, base + end)


def remote(src, dst, send, recv, device):
    return pltpu.make_async_remote_copy(
        src_ref=src, dst_ref=dst, send_sem=send, recv_sem=recv, device_id=device,
        device_id_type=MESH,
    )


def greet(partners):
    barrier = pltpu.get_barrier_semaphore()
    for device in partners:
        pl.semaphore_signal(barrier, inc=1, device_id=device, device_id_type=MESH)
    pl.semaphore_wait(barrier, len(partners))


def neighbours():
    dp, tensor = lax.axis_index("dp"), lax.axis_index("tensor")
    side = dp % 2
    to_core = (dp, tensor + 1 - 2 * (tensor % 2))
    return to_core, (dp, (tensor + 2) % 4), (dp + 1 - 2 * side, tensor), side


def pair_weights(even, odd, w, wo):
    for h, unit in enumerate((even, odd)):
        for i in range(3):
            at = LANES * i + HEAD_DIM * h
            w[at : at + HEAD_DIM, :] = unit[HEAD_DIM * i : HEAD_DIM * (i + 1), :]
        wo[HEAD_DIM * h : HEAD_DIM * (h + 1), :] = unit[3 * HEAD_DIM :, :]


def fwd_kernel(
    x_ref, c_ref, wqkv_ref, wout_ref, up_ref, down_ref, gain_one_ref, gain_two_ref, bias_out_ref,
    bias_down_ref, bias_up_ref, bias_qv_ref, seg_ref,
    vec_ref, n_ref, cot_ref, c_sum_ref, qkv_ref, att_ref, lse_ref, resid_ref, n_two_ref, qh_ref, kn_ref,
    wa_ref, wf_ref, misc_all_ref,
    wa, stage, misc, w, wo, branch, wide,
    core_s, core_r, y_s, y_r, x_s, x_r, d_s, d_r, local_s, z_s, z_r, zz_s, zz_r,
    *, rows, pairs
):
    t = pl.program_id(0)
    tokens = x_ref.shape[0]
    length = tokens // rows
    heads = pairs // 2
    stored = x_ref.shape[1]
    model = stored + 1
    early, tail = heads, stage.shape[0]
    to_core, to_y, to_x, side = neighbours()
    last = early + tail
    dp = lax.axis_index("dp")
    level = dp // 2 % 2
    to_z = (dp + 2 - 4 * level, lax.axis_index("tensor"))

    def rows_of(k, across, along):
        if k not in QUARTERED:
            return pl.ds(pl.multiple_of(across * (CHUNK // 2), CHUNK // 2), CHUNK // 2)
        size = CHUNK // 4
        return pl.ds(pl.multiple_of((2 * across + along) * size, size), size)

    def held(quarter, k):
        if k == last:
            return misc.at[quarter]
        if k < early:
            return wa.at[quarter, k]
        return wf_ref.at[quarter, k - early]

    def own(k):
        return held(0, k) if k < early or k == last else stage.at[k - early]

    def core_copy(k):
        return remote(own(k), held(1, k), core_s.at[k], core_r.at[k], to_core)

    def y_copy(k):
        src, dst = own(k), held(2, k)
        if k < last:
            rows_ = rows_of(k, side, level)
            src, dst = src.at[rows_], dst.at[rows_]
        return remote(src, dst, y_s.at[k], y_r.at[k], to_y)

    def spread(k, across, along, send, recv, device):
        ref = held(2, k).at[rows_of(k, across, along)]
        return remote(ref, ref, send.at[k], recv.at[k], device)

    def x_copy(k, across):
        return spread(k, across, level, x_s, x_r, to_x)

    def z_copy(k, along):
        return spread(k, side, along, z_s, z_r, to_z)

    def zz_copy(k, along):
        return spread(k, 1 - side, along, zz_s, zz_r, to_z)

    def d_copy(k):
        return remote(held(2, k), held(3, k), d_s.at[k], d_r.at[k], to_core)

    def keep_copy(k):
        if k == last:
            return pltpu.make_async_copy(misc, misc_all_ref, local_s.at[k])
        if k < early:
            return pltpu.make_async_copy(wa.at[:, k], wa_ref.at[:, k], local_s.at[k])
        return pltpu.make_async_copy(stage.at[k - early], wf_ref.at[0, k - early], local_s.at[k])

    def x_on(k):
        y_copy(k).wait_recv()
        x_copy(k, side).start()
        if k in QUARTERED:
            z_copy(k, level).start()

    def z_on(k):
        x_copy(k, 1 - side).wait_recv()
        zz_copy(k, level).start()

    def d_on(k):
        if k == last:
            y_copy(k).wait_recv()
        elif k not in QUARTERED:
            x_copy(k, 1 - side).wait_recv()
        else:
            z_copy(k, 1 - level).wait_recv()
            zz_copy(k, 1 - level).wait_recv()
        d_copy(k).start()

    def start_y(k):
        y_copy(k).start()

    def start_core(k):
        core_copy(k).start()

    @pl.when(t == 0)
    def _():
        edge = slice(model - LANES, model)
        wa[0, :, :, edge] = jnp.zeros((early, CHUNK, LANES), BF16)
        for j in range(heads):
            head = slice(HEAD_DIM * j, HEAD_DIM * (j + 1))
            for i in range(3):
                wa[0, j, HEAD_DIM * i : HEAD_DIM * (i + 1), :stored] = wqkv_ref[i, head, :]
            wa[0, j, 3 * HEAD_DIM :, :stored] = wout_ref[head, :]
        vec_ref[...] = jnp.zeros_like(vec_ref)
        vectors = gain_one_ref, gain_two_ref, bias_out_ref, bias_down_ref, bias_up_ref
        for i, ref in enumerate(vectors):
            vec_ref[i : i + 1, : ref.shape[0]] = ref[...].astype(F32).reshape(1, ref.shape[0])
        vec_ref[5:7, : bias_qv_ref.shape[1]] = bias_qv_ref[...].astype(F32)
        misc[0] = jnp.zeros_like(misc[0])
        for p in range(2):
            for j in range(heads):
                for i, row in ((0, 5), (2, 6)):
                    at = LANES * i + HEAD_DIM * p
                    misc[0, p, j : j + 1, at : at + HEAD_DIM] = vec_ref[
                        row : row + 1, HEAD_DIM * j : HEAD_DIM * (j + 1)
                    ]
            wide_half = misc.shape[3]
            misc[0, p, heads : heads + 1, :] = vec_ref[4:5, wide_half * p : wide_half * (p + 1)]
        greet([to_core, to_y, to_x, to_z])
        for k in (last, 0):
            core_copy(k).start()
            y_copy(k).start()
        for k in range(1, early):
            core_copy(k).start()
        count = tail // 2
        stage[:, :, edge] = jnp.zeros((tail, CHUNK, LANES), BF16)
        stage[count - 1, CHUNK - 16 :, :] = jnp.zeros((16, model), BF16)
        for i in range(count):
            end = min(CHUNK * (i + 1), stored)
            stage[i, : end - CHUNK * i, :] = up_ref[CHUNK * i : end, :]
            stage[count + i, :, :stored] = down_ref[CHUNK * i : CHUNK * (i + 1), :]
        for k in range(early, last):
            keep_copy(k).start()
        branch[...] = jnp.zeros_like(branch)
        c_sum = jnp.zeros((1, model), F32)
        for i in range(0, tokens, CHUNK):
            r = slice(i, i + CHUNK)
            x = widen(x_ref.at[r, :], wide)
            n_ref[r, :] = (x * norm_scale(x)[0] * vec_ref[0:1, :model]).astype(BF16)
            c = widen(c_ref.at[r, :], wide)
            cot_ref[r, :] = c.astype(BF16)
            c_sum += jnp.sum(c, axis=0, keepdims=True)
        c_sum_ref[...] = c_sum
        lane = lax.broadcasted_iota(jnp.int32, (1, LANES), 1) % HEAD_DIM
        for row in range(rows):
            document = jnp.broadcast_to(seg_ref[row : row + 1, :].astype(F32), (LANES, length)).T
            hot = document == lane.astype(F32)
            r = slice(row * length, (row + 1) * length)
            qh_ref[r, :] = jnp.where(hot, 1.0, 0.0).astype(BF16)
            kn_ref[r, :] = jnp.where(hot | (lane >= 8), 0.0, MASKED_SCORE).astype(BF16)
        core_copy(last).wait_recv()

    events = {
        (0, 0): [(start_y, 6)],
        (0, 1): [(x_on, 0), (start_y, 1)],
        (0, 2): [(z_on, 0), (start_y, 8)],
        (0, 4): [(x_on, 1), (start_y, 2)],
        (1, 0): [(x_on, 6)],
        (1, 1): [(d_on, 0)],
        (1, 2): [(x_on, 8)],
        (1, 3): [(d_on, last)],
        (1, 4): [(z_on, 1), (start_y, 3)],
        (2, 0): [(x_on, 2), (start_y, 7)],
        (2, 2): [(z_on, 6)],
        (2, 3): [(start_y, 5), (start_core, 6)],
        (2, 4): [(x_on, 3), (start_core, 4)],
        (3, 0): [(d_on, 1), (x_on, 7), (start_core, 3)],
        (3, 1): [(z_on, 8)],
        (3, 2): [(start_y, 4), (start_core, 5)],
        (3, 4): [(d_on, 2), (x_on, 5)],
        (4, 0): [(start_core, 7)],
        (4, 1): [(z_on, 7)],
        (4, 2): [(d_on, 6)],
        (4, 3): [(x_on, 4), (start_core, 8)],
        (4, 4): [(z_on, 3)],
        (5, 0): [(d_on, 5), (d_on, 8)],
        (5, 2): [(d_on, 7)],
        (5, 3): [(d_on, 3)],
        (5, 4): [(d_on, 4)],
    }
    rest = []

    def run(slot):
        for (step, at), todo in events.items():
            if at == slot and todo:

                @pl.when(t == step)
                def _(todo=todo):
                    for event, k in todo:
                        event(k)

    for step in range(pairs):

        @pl.when(t == step)
        def _(far=step // heads, j=step % heads):
            (d_copy if far else core_copy)(j).wait_recv()
            if far and j == 0:
                d_copy(last).wait_recv()

    first = lax.broadcasted_iota(jnp.int32, (1, LANES), 1) < HEAD_DIM
    units = [(2 * (t // heads) + h, t % heads) for h in range(2)]
    pair_weights(*(wa.at[quarter, j] for quarter, j in units), w, wo)
    bias = sum(
        jnp.where(j == row, misc[quarter, h, row : row + 1, :], 0.0)
        for h, (quarter, j) in enumerate(units)
        for row in range(heads)
    )
    qkv_ref[...] = (dot(n_ref[...], w[...], NT) + bias).astype(BF16)
    q_ref, k_ref, v_ref = (qkv_ref.at[:, j * LANES : (j + 1) * LANES] for j in range(3))
    run(0)
    slot = 1
    for row in range(rows):
        for at, span in spans(length, row):
            parts = []
            for h in range(2):
                sel = first if h == 0 else ~first
                s, _ = scores_of(q_ref, k_ref, qh_ref, kn_ref, sel, at, span)
                m = jnp.max(s, axis=0, keepdims=True)
                p = jnp.exp(s - m)
                total = jnp.sum(p, axis=0, keepdims=True)
                weights = (p * (1.0 / total)).astype(BF16)
                parts.append(dot(weights, v_ref[span, :], TN))
                lse_ref[h : h + 1, at] = m + jnp.log(total)
            att_ref[at, :] = jnp.where(first, parts[0], parts[1]).astype(BF16)
            if slot < 4:
                run(slot)
                slot += 1
    branch[...] += dot(att_ref[...], wo[...])
    run(4)

    @pl.when(t == pairs - 1)
    def _():
        for i in range(0, tokens, CHUNK):
            r = slice(i, i + CHUNK)
            resid = widen(x_ref.at[r, :], wide) + (branch[r, :] + vec_ref[2:3, :model])
            resid_ref[r, :] = resid
            n_two_ref[r, :] = (resid * norm_scale(resid)[0] * vec_ref[1:2, :model]).astype(BF16)
        for event, k in rest:
            event(k)
        for k in (*range(early), last):
            keep_copy(k).start()
        for k in range(early, last):
            core_copy(k).wait_recv()
            d_copy(k).wait_recv()
        for k in range(last + 1):
            core_copy(k).wait_send()
            y_copy(k).wait_send()
            if k < last:
                x_copy(k, side).wait_send()
            if k in QUARTERED:
                z_copy(k, level).wait_send()
                zz_copy(k, level).wait_send()
            d_copy(k).wait_send()
            keep_copy(k).wait()


def forward(x, c, wqkv, wout, up, down, gain_one, gain_two, bias_out, bias_down, bias_up, bias_qv, seg):
    tokens, stored = x.shape
    model = stored + 1
    heads = wqkv.shape[1] // HEAD_DIM
    pairs = 2 * heads
    tail = 2 * (model // CHUNK)

    def of(*shape):
        return pl.BlockSpec((None, *shape), lambda p: (p,) + (0,) * len(shape))

    anywhere = pl.BlockSpec(memory_space=pl.ANY)
    sems = pltpu.SemaphoreType.DMA((heads + tail + 1,))
    rows = seg.shape[0]
    misc = (2, 8, model // 2)
    inputs = [
        x, c, wqkv, wout, up, down, gain_one, gain_two, bias_out, bias_down, bias_up, bias_qv, seg
    ]
    big = once((tokens, model))
    outs = [
        (once((8, 1024)), (8, 1024), F32),
        (big, (tokens, model), BF16),
        (big, (tokens, model), BF16),
        (once((1, model)), (1, model), F32),
        (of(tokens, 3 * LANES), (pairs, tokens, 3 * LANES), BF16),
        (of(tokens, LANES), (pairs, tokens, LANES), BF16),
        (of(2, tokens), (pairs, 2, tokens), F32),
        (big, (tokens, model), F32),
        (big, (tokens, model), BF16),
        (once((tokens, LANES)), (tokens, LANES), BF16),
        (once((tokens, LANES)), (tokens, LANES), BF16),
        (anywhere, (4, heads, CHUNK, model), BF16),
        (anywhere, (4, tail, CHUNK, model), BF16),
        (anywhere, (4, *misc), F32),
    ]
    return pl.pallas_call(
        functools.partial(fwd_kernel, rows=rows, pairs=pairs),
        grid=(pairs,),
        in_specs=[once(v.shape) for v in inputs],
        out_specs=[spec for spec, _, _ in outs],
        out_shape=[jax.ShapeDtypeStruct(shape, dtype) for _, shape, dtype in outs],
        scratch_shapes=[
            pltpu.VMEM((4, heads, CHUNK, model), BF16),
            pltpu.VMEM((tail, CHUNK, model), BF16),
            pltpu.VMEM((4, *misc), F32),
            pltpu.VMEM((3 * LANES, model), BF16),
            pltpu.VMEM((LANES, model), BF16),
            pltpu.VMEM((tokens, model), F32),
            pltpu.VMEM((CHUNK, model), F32),
        ]
        + [sems] * 13,
        compiler_params=params(60, collective_id=1, has_side_effects=True),
        name="forward",
    )(*inputs)


def backward_kernel(
    n_two_ref, c_ref, n_ref, x_ref, vec_ref, c_sum_ref, up_ref, down_ref, bias_ref,
    qkv_ref, att_ref, lse_ref, even_ref, odd_ref, qh_ref, kn_ref, resid_ref,
    output_ref, grad_in_ref, red_ref, red_late_ref, total_ref,
    out, back, d_resid, nt, ct, db, stage, bias_row, w, wo, da, dqkv, dk_acc, dv_acc, wide_x,
    g, core_in, y_in, x_in, z_in, ag, xag_in, sv, sv_in, sv_z,
    core_s, core_r, y_s, y_r, x_s, x_r, z_s, z_r, a_s, a_r, xa_s, xa_r, out_s,
    sv_s, sv_r, svz_s, svz_r, resid_s, rows_s,
    *, rows, pairs, group, blocks
):
    t = pl.program_id(0)
    tokens, model = n_ref.shape
    length = tokens // rows
    front = 4 * blocks
    early, late = 2 * blocks, pairs // 2
    chunks = early + late
    others = group // 2
    half, units = g.shape[2:]
    keep = half // others
    pieces = half // HEAD_DIM
    dp, tensor = lax.axis_index("dp"), lax.axis_index("tensor")
    place = (dp % group) // 2
    mine = pl.ds(pl.multiple_of(place * keep, keep), keep)
    to_core, to_y, to_x, side = neighbours()

    def place_of(o):
        return (place + o) % others

    def to_z(o):
        return (dp - dp % group + place_of(o) * 2 + side, tensor)

    box = 2 * chunks

    def core_copy(which, k, at, slot):
        return remote(
            g.at[box + at], core_in.at[which, slot], core_s.at[which, k], core_r.at[which, k], to_core
        )

    def early_core(which, k):
        return core_copy(which, k, k, k)

    def late_core(which, i):
        return core_copy(which, early + i, late * which + i, i)

    def y_copy(k):
        return remote(g.at[chunks + k], y_in.at[k], y_s.at[k], y_r.at[k], to_y)

    def x_copy(k):
        return remote(g.at[k, 1 - side], x_in.at[k], x_s.at[k], x_r.at[k], to_x)

    def z_copy(k, o):
        rows_of = pl.ds(pl.multiple_of(place_of(o) * keep, keep), keep)
        return remote(
            g.at[k, side, rows_of], z_in.at[k, o - 1], z_s.at[k, o - 1], z_r.at[k, o - 1], to_z(o)
        )

    def a_copy(k, o):
        return remote(ag.at[k, mine], ag.at[k, mine], a_s.at[k, o - 1], a_r.at[k, o - 1], to_z(o))

    def a_wait(k, o):
        rows_of = pl.ds(pl.multiple_of(place_of(others - o) * keep, keep), keep)
        part = ag.at[k, rows_of]
        remote(part, part, a_s.at[k, o - 1], a_r.at[k, o - 1], to_z(o)).wait_recv()

    def xa_copy(k):
        return remote(ag.at[k], xag_in.at[k], xa_s.at[k], xa_r.at[k], to_x)

    def out_copies(k, i, act):
        which = side + i - 2 * side * i
        src = xag_in if i else ag

        @pl.when(k < early)
        def _():
            at = jnp.minimum(k, early - 1)
            lines = pl.ds(pl.multiple_of(which * half, half), half)
            cols = pl.ds(pl.multiple_of(at // 2 * units, units), units)
            act(pltpu.make_async_copy(src.at[at], red_ref.at[at % 2, lines, cols], out_s.at[k, i, 0]))

        @pl.when(k >= early)
        def _():
            at = jnp.maximum(k, early)
            head = pl.ds(pl.multiple_of((chunks - 1 - at) * HEAD_DIM, HEAD_DIM), HEAD_DIM)
            for n in range(pieces):
                piece = which * pieces + n
                cols = pl.ds(pl.multiple_of(piece // 4 * units, units), units)
                act(
                    pltpu.make_async_copy(
                        src.at[at, HEAD_DIM * n : HEAD_DIM * (n + 1)],
                        red_late_ref.at[piece % 4, head, cols],
                        out_s.at[k, i, n],
                    )
                )

    def plus(at, value):
        g[at] = (g[at].astype(F32) + value.astype(F32)).astype(BF16)

    def send_y(k):
        @pl.when(k >= early)
        def _():
            i = jnp.maximum(k, early) - early
            late_core(0, i).wait_recv()
            plus(chunks + early + i, core_in[0, i])

        y_copy(k).start()

    def send_x(k):
        @pl.when(k >= early)
        def _():
            i = jnp.maximum(k, early) - early
            late_core(1, i).wait_recv()
            plus(early + i, core_in[1, i])

        y_copy(k).wait_recv()
        plus(k, y_in[k])
        x_copy(k).start()

    def send_z(k):
        x_copy(k).wait_recv()
        g[k, side] = (g[k, side].astype(F32) + x_in[k].astype(F32)).astype(BF16)
        for o in range(1, others):
            z_copy(k, o).start()

    def send_back(k):
        total = g[k, side, mine].astype(F32)
        for o in range(1, others):
            z_copy(k, o).wait_recv()
            total += z_in[k, o - 1].astype(F32)
        ag[k, mine] = total.astype(BF16)
        for o in range(1, others):
            a_copy(k, o).start()

    def send_back_x(k):
        for o in range(1, others):
            a_wait(k, o)
        xa_copy(k).start()
        out_copies(k, 0, lambda copy: copy.start())

    def finish(k):
        xa_copy(k).wait_recv()
        out_copies(k, 1, lambda copy: copy.start())

    plan = [
        (finish, [(16, 2), (16, 4), (17, 0), (17, 4), (17, 4)]),
        (send_back_x, [(12, 3), (14, 3), (14, 4), (15, 4), (16, 4), (17, 4)]),
        (send_back, [(11, 0), (12, 0), (13, 2), (14, 3), (16, 0), (16, 2), (17, 2)]),
        (send_z, [(9, 0), (10, 0), (12, 2), (13, 0), (14, 0), (15, 1), (16, 4), (17, 4)]),
        (send_x, [(7, 0), (8, 0), (10, 0), (12, 0), (12, 3), (14, 1), (16, 1), (17, 1)]),
        (send_y, [(2, 0), (3, 0), (6, 0), (8, 0), (10, 0), (12, 2), (14, 0), (16, 0), (17, 0)]),
    ]

    def run(slot, first, end):
        for event, times in plan:
            now = [(step, k) for k, (step, at) in enumerate(times) if at == slot and first <= step < end]
            while now:
                table = dict(now[::-1])
                now = [(step, k) for step, k in now if table[step] != k]
                k = jnp.int32(-1)
                for step, at in table.items():
                    k = jnp.where(t == step, at, k)

                @pl.when(k >= 0)
                def _(event=event, k=k):
                    event(jnp.maximum(k, 0))

    def sv_copy(i, src, device):
        return remote(src, sv_in.at[i], sv_s.at[i], sv_r.at[i], device)

    def svz_copy(o):
        return remote(sv_z.at[place], sv_z.at[place], svz_s.at[o - 1], svz_r.at[o - 1], to_z(o))

    def small_y():
        for i in (0, 1):
            sv_copy(i, sv.at[3 - 2 * i], to_core).wait_recv()
        sv[2] += sv_in[0]
        sv_copy(2, sv.at[2], to_y).start()

    def small_x():
        sv_copy(2, sv.at[2], to_y).wait_recv()
        sv[0] = (sv[0] + sv_in[1]) + sv_in[2]
        sv_copy(3, sv.at[0], to_x).start()

    def small_z():
        sv_copy(3, sv.at[0], to_x).wait_recv()
        sv_z[place] = sv[0] + sv_in[3]
        for o in range(1, others):
            svz_copy(o).start()

    def small_end():
        for o in range(1, others):
            part = sv_z.at[place_of(others - o)]
            remote(part, part, svz_s.at[o - 1], svz_r.at[o - 1], to_z(o)).wait_recv()
        total = sv_z[0]
        for i in range(1, others):
            total += sv_z[i]
        total_ref[...] = total

    def resid_copy():
        return pltpu.make_async_copy(resid_ref, d_resid, resid_s)

    def grad_copy(i):
        r = slice(CHUNK * i, CHUNK * (i + 1))
        return pltpu.make_async_copy(db.at[r], grad_in_ref.at[r], rows_s.at[i])

    def output_copy(i):
        r = slice(CHUNK * i, CHUNK * (i + 1))
        return pltpu.make_async_copy(stage.at[i % 2], output_ref.at[r], rows_s.at[i])

    def feed_forward():
        b, quarter = t // 4, 3 - t % 4
        up = up_ref[...].reshape(model, units)
        down = down_ref[...]
        wide = bias_ref.shape[2]
        for h in range(2):
            bias_row[0:1, wide * h : wide * (h + 1)] = bias_ref[h, late : late + 1, :]
        lanes = pl.ds(pl.multiple_of(b * units, units), units)
        pre = dot(n_two_ref[...], up) + bias_row[0:1, lanes]
        dh = dot(c_ref[...], down, NT)
        sq = pre * pre
        th = jnp.tanh(pre * (GELU_A + (GELU_A * GELU_B) * sq))
        level = 0.5 + 0.5 * th
        hidden = (pre * level).astype(BF16)
        slope = level + (0.5 * pre) * (1.0 - th * th) * (GELU_A + (3.0 * GELU_A * GELU_B) * sq)
        dpre = (dh * slope).astype(BF16)
        out[...] += dot(hidden, down)
        back[...] += dot(dpre, up, NT)
        sv[quarter, 0:1, lanes] = jnp.sum(dpre.astype(F32), axis=0, keepdims=True)
        grads = dot(nt[...], dpre).astype(BF16), dot(ct[...], hidden).astype(BF16)

        @pl.when(t % 4 == 2)
        def _():
            for m in range(2):
                early_core(0, 2 * b + m).wait_send()

        base = jnp.where(quarter == 0, 0, jnp.where(quarter == 2, chunks, box)) + 2 * b
        for m in range(2):
            for h in range(2):
                g[base + m, h] = grads[m][half * h : half * (h + 1)]
        for m in range(2):
            k = 2 * b + m
            for which in range(2):

                @pl.when(t % 4 == 2 * which)
                def _(which=which, k=k):
                    early_core(which, k).start()

                @pl.when(t % 4 == 2 * which + 1)
                def _(which=which, k=k):
                    early_core(which, k).wait_recv()
                    plus((1 - which) * chunks + k, core_in[which, k])

    def turn():
        resid_copy().wait()
        gain_sum = branch_sum = jnp.zeros((1, model), F32)
        for i in range(tokens // CHUNK):
            r = slice(CHUNK * i, CHUNK * (i + 1))
            resid = d_resid[r, :]
            if i >= 2:
                output_copy(i - 2).wait()
            stage[i % 2] = (resid + (out[r, :] + vec_ref[3:4, :model])).astype(BF16)
            output_copy(i).start()
            out[r, :] = jnp.zeros((CHUNK, model), F32)
            d_norm, part = norm_back(resid, vec_ref[1:2, :model], back[r, :])
            d_rows = c_ref[r, :].astype(F32) + d_norm
            d_resid[r, :] = d_rows
            d_branch = d_rows.astype(BF16)
            db[r, :] = d_branch
            gain_sum += part
            branch_sum += jnp.sum(d_branch.astype(F32), axis=0, keepdims=True)
        for i in range(tokens // CHUNK - 2, tokens // CHUNK):
            output_copy(i).wait()
        for i in range(4):
            sv[i, 2:3, :] = branch_sum
            sv[i, 3:4, :] = gain_sum
        for k in range(early):
            early_core(1, k).wait_send()

    def norm_one():
        gain_sum = jnp.zeros((1, model), F32)
        for i in range(tokens // CHUNK):
            r = slice(CHUNK * i, CHUNK * (i + 1))
            d_norm, part = norm_back(widen(x_ref.at[r, :], wide_x), vec_ref[0:1, :model], out[r, :])
            db[r, :] = (d_resid[r, :] + d_norm).astype(BF16)
            grad_copy(i).start()
            gain_sum += part
        for i in range(4):
            sv[i, 4:5, :] = gain_sum
        for i in (0, 1):
            sv_copy(i, sv.at[3 - 2 * i], to_core).start()

    first = lax.broadcasted_iota(jnp.int32, (1, LANES), 1) < HEAD_DIM
    zero = jnp.zeros((), BF16)
    q_ref, k_ref, v_ref = (qkv_ref.at[:, j * LANES : (j + 1) * LANES] for j in range(3))

    def attend(at, span):
        dq = None
        for h in range(2):
            sel = first if h == 0 else ~first
            s, q = scores_of(q_ref, k_ref, qh_ref, kn_ref, sel, at, span)
            qm = jnp.where(sel, q, zero)
            km = jnp.where(sel, k_ref[span, :], zero)
            dom = jnp.where(sel, da[at, :], zero)
            p = jnp.exp(s - lse_ref[h : h + 1, at])
            dp_ = dot(v_ref[span, :], dom, NT)
            u = p * dp_
            inner = jnp.sum(u, axis=0, keepdims=True)
            ds = (u - p * inner).astype(BF16)
            dv_acc[span, :] += dot(p.astype(BF16), dom)
            dk_acc[span, :] += dot(ds, qm)
            part = dot(ds, km, TN)
            dq = part if dq is None else dq + part
        dqkv[at, :LANES] = (dq * 0.125).astype(BF16)

    def attention():
        pair_weights(even_ref, odd_ref, w, wo)
        da[...] = dot(db[...], wo[...], NT).astype(BF16)
        dk_acc[...] = jnp.zeros_like(dk_acc)
        dv_acc[...] = jnp.zeros_like(dv_acc)
        run(0, front, front + pairs)
        slot = 1
        for row in range(rows):
            for at, span in spans(length, row):
                attend(at, span)
                if slot < 5:
                    run(slot, front, front + pairs)
                    slot += 1
        dqkv[:, LANES : 2 * LANES] = dk_acc[...].astype(BF16)
        dqkv[:, 2 * LANES :] = dv_acc[...].astype(BF16)
        grads = dot(dqkv[...], n_ref[...], TN).astype(BF16)
        grads_out = dot(att_ref[...], db[...], TN).astype(BF16)
        pair = pairs - 1 - (t - front)
        far, j = pair // late, pair % late
        i = late - 1 - j
        for h in range(2):
            base = i + ((box + late * (1 - far)) if h else (early + chunks * far))
            for block in range(model // units):
                cols = slice(units * block, units * (block + 1))
                for p in range(4):
                    if p < 3:
                        lines = grads[LANES * p + HEAD_DIM * h : LANES * p + HEAD_DIM * (h + 1), cols]
                    else:
                        lines = grads_out[HEAD_DIM * h : HEAD_DIM * (h + 1), cols]
                    at = CHUNK * block + HEAD_DIM * p
                    g[base, at // half, at % half : at % half + HEAD_DIM, :] = lines
        late_core(1 - far, i).start()
        out[...] += dot(dqkv[...], w[...])
        sums = jnp.sum(dqkv[...].astype(F32), axis=0, keepdims=True)
        for h in range(2):
            for line in range(late):

                @pl.when(j == line)
                def _(line=8 + line, h=h):
                    for part in (0, 2):
                        at = LANES * part + HEAD_DIM * h
                        sv[2 * far + h, line : line + 1, LANES * part : LANES * part + HEAD_DIM] = (
                            sums[:, at : at + HEAD_DIM]
                        )

    @pl.when(t == 0)
    def _():
        greet([to_core, to_y, to_x] + [to_z(o) for o in range(1, others)])
        out[...] = jnp.zeros_like(out)
        back[...] = jnp.zeros_like(back)
        sv[...] = jnp.zeros_like(sv)
        for i in range(4):
            sv[i, 1:2, :] = c_sum_ref[...]
        for i in range(0, tokens, CHUNK):
            nt[:, i : i + CHUNK] = n_two_ref[i : i + CHUNK, :].T
            ct[:, i : i + CHUNK] = c_ref[i : i + CHUNK, :].T

    @pl.when(t == front - 2)
    def _():
        resid_copy().start()

    @pl.when(t < front)
    def _():
        run(0, 0, front)
        feed_forward()

    pl.when(t == front - 1)(turn)
    pl.when((t >= front) & (t < front + pairs))(attention)

    @pl.when(t == front + pairs)
    def _():
        send_x(8)
        finish(5)
        send_back(7)
        norm_one()
        send_back_x(6)
        send_z(8)
        small_y()
        send_back_x(7)
        small_x()
        send_back(8)
        send_back_x(8)
        small_z()
        finish(6)
        small_end()
        finish(7)
        finish(8)

        @pl.loop(0, chunks)
        def _(k):
            y_copy(k).wait_send()
            x_copy(k).wait_send()
            for o in range(1, others):
                z_copy(k, o).wait_send()
                a_copy(k, o).wait_send()
            xa_copy(k).wait_send()
            for i in range(2):
                out_copies(k, i, lambda copy: copy.wait())

        for which in range(2):
            for i in range(late):
                late_core(which, i).wait_send()
        for i, device in enumerate((to_core, to_core, to_y, to_x)):
            sv_copy(i, sv.at[0], device).wait_send()
        for o in range(1, others):
            svz_copy(o).wait_send()
        for i in range(tokens // CHUNK):
            grad_copy(i).wait()


def backward(
    n_two, c, resid, w_ffn, misc, n, x, vec, c_sum, qkv, att, lse, w_attn, qh, kn, rows, group
):
    tokens, model = n.shape
    stored = x.shape[1]
    pairs = qkv.shape[0]
    blocks = model // UNITS
    front, early, late = 4 * blocks, 2 * blocks, pairs // 2
    chunks = early + late
    others = group // 2
    half = model // 2
    lines = 16
    wide = misc.shape[3]

    def unit_block(t):
        t = jnp.minimum(t, front - 1)
        return 3 - t % 4, t // 4

    def up_at(t):
        quarter, b = unit_block(t)
        return quarter, 0, 0, b

    def down_at(t):
        quarter, b = unit_block(t)
        return quarter, model // CHUNK + b, 0, 0

    def bias_at(t):
        return unit_block(t)[0], 0, 0, 0

    def pair_at(t):
        return pairs - 1 - jnp.clip(t - front, 0, pairs - 1)

    def of(shape):
        return pl.BlockSpec((None, *shape), lambda t: (pair_at(t), 0, 0))

    def unit(h):
        return pl.BlockSpec(
            (None, None, CHUNK, model),
            lambda t: (2 * (pair_at(t) // late) + h, pair_at(t) % late, 0, 0),
        )

    anywhere = pl.BlockSpec(memory_space=pl.ANY)
    sems = pltpu.SemaphoreType.DMA
    between = max(others - 1, 1)
    many = (chunks, between)
    big = once((tokens, model))
    return pl.pallas_call(
        functools.partial(backward_kernel, rows=rows, pairs=pairs, group=group, blocks=blocks),
        grid=(front + pairs + 1,),
        in_specs=[
            big, big, big, once((tokens, stored)), full(vec.shape), full((1, model)),
            pl.BlockSpec((None, model // CHUNK, CHUNK, UNITS), up_at),
            pl.BlockSpec((None, None, CHUNK, model), down_at),
            pl.BlockSpec((None, 2, 8, wide), bias_at),
            of((tokens, 3 * LANES)), of((tokens, LANES)), of((2, tokens)), unit(0), unit(1),
            once((tokens, LANES)), once((tokens, LANES)), anywhere,
        ],
        out_specs=[anywhere] * 4 + [once((lines, model))],
        out_shape=[
            jax.ShapeDtypeStruct((tokens, model), BF16),
            jax.ShapeDtypeStruct((tokens, model), BF16),
            jax.ShapeDtypeStruct((2, model, blocks * UNITS), BF16),
            jax.ShapeDtypeStruct((4, late * HEAD_DIM, model), BF16),
            jax.ShapeDtypeStruct((lines, model), F32),
        ],
        scratch_shapes=[pltpu.VMEM((tokens, model), F32)] * 3
        + [pltpu.VMEM((model, tokens), BF16)] * 2
        + [
            pltpu.VMEM((tokens, model), BF16),
            pltpu.VMEM((2, CHUNK, model), BF16),
            pltpu.VMEM((8, model), F32),
            pltpu.VMEM((3 * LANES, model), BF16),
            pltpu.VMEM((LANES, model), BF16),
            pltpu.VMEM((tokens, LANES), BF16),
            pltpu.VMEM((tokens, 3 * LANES), BF16),
            pltpu.VMEM((tokens, LANES), F32),
            pltpu.VMEM((tokens, LANES), F32),
            pltpu.VMEM((CHUNK, model), F32),
            pltpu.VMEM((2 * chunks + early, 2, half, UNITS), BF16),
            pltpu.VMEM((2, early, 2, half, UNITS), BF16),
            pltpu.VMEM((chunks, 2, half, UNITS), BF16),
            pltpu.VMEM((chunks, half, UNITS), BF16),
            pltpu.VMEM((*many, half // others, UNITS), BF16),
            pltpu.VMEM((chunks, half, UNITS), BF16),
            pltpu.VMEM((chunks, half, UNITS), BF16),
            pltpu.VMEM((4, lines, model), F32),
            pltpu.VMEM((4, lines, model), F32),
            pltpu.VMEM((others, lines, model), F32),
            sems((2, chunks)), sems((2, chunks)), sems((chunks,)), sems((chunks,)),
            sems((chunks,)), sems((chunks,)), sems(many), sems(many), sems(many), sems(many),
            sems((chunks,)), sems((chunks,)), sems((chunks, 2, half // HEAD_DIM)),
            sems((4,)), sems((4,)), sems((between,)), sems((between,)), sems, sems((tokens // CHUNK,)),
        ],
        compiler_params=params(63, collective_id=0, has_side_effects=True),
        name="backward",
    )(n_two, c, n, x, vec, c_sum, w_ffn, w_ffn, misc, qkv, att, lse, w_attn, w_attn, qh, kn, resid)


def last_kernel(
    output_ref, grad_ref, up_ref, down_ref, qkv_ref, out_ref, sums_ref,
    output_to, grad_to, up_to, down_to, qkv_to, out_to, bqv_to, *vectors
):
    stored = output_to.shape[1]
    output_to[...] = output_ref[:, :stored]
    grad_to[...] = grad_ref[:, :stored]
    up_to[...] = up_ref[...].astype(F32)
    down_to[...] = down_ref[...].T.astype(F32)[:, :stored]
    qkv_to[...] = qkv_ref[...].astype(F32)[:, :stored]

    @pl.when(pl.program_id(0) == 0)
    def _():
        out_to[...] = out_ref[...].astype(F32)[:, :stored]
        for j in range(bqv_to.shape[1] // HEAD_DIM):
            for i in range(2):
                part = sums_ref[8 + j : 9 + j, 2 * LANES * i : 2 * LANES * i + HEAD_DIM]
                bqv_to[i : i + 1, HEAD_DIM * j : HEAD_DIM * (j + 1)] = part
        for i, ref in enumerate(vectors):
            ref[...] = sums_ref[i : i + 1, : ref.shape[0]].reshape(ref.shape[0])


def results(output, grad, ffn, heads, sums, stored):
    tokens, model = output.shape
    units, rows = ffn.shape[2], heads.shape[1]
    steps = tokens // CHUNK
    most = model // CHUNK - 1
    assert steps > most

    def block(shape, at):
        return pl.BlockSpec(shape, at)

    def lesser(i):
        return jnp.minimum(i, most)

    lengths = [units, stored, stored, stored, stored]
    shape = jax.ShapeDtypeStruct
    return pl.pallas_call(
        last_kernel,
        grid=(steps,),
        in_specs=[
            block((CHUNK, model), lambda i: (i, 0)),
            block((CHUNK, model), lambda i: (i, 0)),
            block((None, CHUNK, units), lambda i: (0, lesser(i), 0)),
            block((None, model, CHUNK), lambda i: (1, 0, lesser(i))),
            block((None, rows, model), lambda i: (lesser(i), 0, 0)),
            block((None, rows, model), lambda i: (3, 0, 0)),
            full(sums.shape),
        ],
        out_specs=[
            block((CHUNK, stored), lambda i: (i, 0)),
            block((CHUNK, stored), lambda i: (i, 0)),
            block((CHUNK, units), lambda i: (lesser(i), 0)),
            block((CHUNK, stored), lambda i: (lesser(i), 0)),
            block((None, rows, stored), lambda i: (lesser(i), 0, 0)),
            full((rows, stored)),
            full((2, rows)),
        ]
        + [full((n,)) for n in lengths],
        out_shape=[
            shape((tokens, stored), BF16),
            shape((tokens, stored), BF16),
            shape((stored, units), F32),
            shape((units, stored), F32),
            shape((3, rows, stored), F32),
            shape((rows, stored), F32),
            shape((2, rows), F32),
        ]
        + [shape((n,), F32) for n in lengths],
        compiler_params=params(60),
        name="results",
    )(output, grad, ffn, ffn, heads, heads, sums)


def solution(mesh):
    n_dp, n_tensor = mesh.shape["dp"], mesh.shape["tensor"]
    assert n_tensor == 4 and n_dp % 4 == 0 and n_dp & (n_dp - 1) == 0
    bits = [1 << i for i in range(n_dp.bit_length() - 1)]
    group = min(n_dp, 8)

    def to_dp(v, bit):
        return lax.ppermute(v, "dp", [(i, i ^ bit) for i in range(n_dp)])

    def local(
        layer_input, segments, cotangent, gain_one, w_qkv, b_qv, w_out, b_out, gain_two,
        w_up, b_up, w_down, b_down,
    ):
        rows = segments.shape[0]
        tokens, stored = layer_input.shape
        model = stored + 1
        heads = w_qkv.shape[2] // HEAD_DIM
        units = w_up.shape[1]

        (
            vec, n_one, cot, grad_bdown, qkv, att, lse, resid, n_two, qh, kn, w_attn, w_ffn, misc
        ) = forward(
            layer_input, cotangent, w_qkv.transpose(0, 2, 1), w_out, w_up, w_down, gain_one, gain_two,
            b_out, b_down, b_up, b_qv, segments,
        )
        output, input_grad, *reduced, small = backward(
            n_two, cot, resid, w_ffn, misc, n_one, layer_input, vec, grad_bdown, qkv, att, lse, w_attn,
            qh, kn, rows, group,
        )
        for bit in bits:
            if bit >= group:
                small = small + to_dp(small, bit)
                reduced = [(v.astype(F32) + to_dp(v, bit).astype(F32)).astype(BF16) for v in reduced]
        (
            output, input_grad, grad_up, grad_down, grad_qkv, grad_out, grad_bqv,
            grad_bup, grad_bdown, grad_bout, grad_gain_two, grad_gain_one,
        ) = results(output, input_grad, *reduced, small, stored)
        return (
            output, input_grad, grad_gain_one, grad_qkv.transpose(0, 2, 1), grad_bqv, grad_out, grad_bout,
            grad_gain_two, grad_up, grad_bup, grad_down, grad_bdown,
        )

    return jax.shard_map(
        local,
        mesh=mesh,
        in_specs=(
            P(("dp", "tensor"), None),
            P(("dp", "tensor"), None),
            P(("dp", "tensor"), None),
            P(),
            P(None, None, "tensor"),
            P(None, "tensor"),
            P("tensor", None),
            P(),
            P(),
            P(None, "tensor"),
            P("tensor"),
            P("tensor", None),
            P(),
        ),
        out_specs=(
            P(("dp", "tensor"), None),
            P(("dp", "tensor"), None),
            P(),
            P(None, None, "tensor"),
            P(None, "tensor"),
            P("tensor", None),
            P(),
            P(),
            P(None, "tensor"),
            P("tensor"),
            P("tensor", None),
            P(),
        ),
        check_vma=False,
    )
```

```python
import functools

import jax
import jax.numpy as jnp
from jax import lax
from jax.experimental import pallas as pl
from jax.experimental.pallas import tpu as pltpu
from jax.sharding import PartitionSpec as P

HEAD_DIM = 64
LANES = 128
EPSILON = 1e-05
MASKED_SCORE = -1e30
LONGEST = 512
BLOCK = 256
CHUNK = 256
UNITS = 256
QUARTERED = (0, 1, 3, 6, 7, 8)
F32 = jnp.float32
BF16 = jnp.bfloat16
NN = (((1,), (0,)), ((), ()))
NT = (((1,), (1,)), ((), ()))
TN = (((0,), (0,)), ((), ()))
GELU_A = 0.7978845608028654
GELU_B = 0.044715
MIB = 1024 * 1024
MESH = pl.DeviceIdType.MESH


def dot(a, b, dims=NN):
    return lax.dot_general(a, b, dims, preferred_element_type=F32)


def params(mib, **more):
    return pltpu.CompilerParams(vmem_limit_bytes=mib * MIB, **more)


def full(shape):
    return pl.BlockSpec(shape, lambda *_: (0,) * len(shape))


def once(shape):
    return pl.BlockSpec(shape, lambda *_: (0,) * len(shape), pipeline_mode=pl.Buffered(1))


def widen(ref, wide):
    wide[:, wide.shape[1] - LANES :] = jnp.zeros((wide.shape[0], LANES), F32)
    wide[:, : ref.shape[1]] = ref[...].astype(F32)
    return wide[...]


def norm_scale(values):
    total = jnp.sum(values, axis=-1, keepdims=True)
    square = jnp.sum(values * values, axis=-1, keepdims=True)
    return lax.rsqrt((square + total * total) / values.shape[-1] + EPSILON), total


def norm_back(values, gain, upstream):
    scale, total = norm_scale(values)
    weighted = upstream * values
    spread = jnp.sum(weighted * gain, axis=-1, keepdims=True)
    grad = upstream * gain * scale - (spread * scale * scale * scale / values.shape[-1]) * (
        values + total
    )
    return grad, jnp.sum(weighted * scale, axis=0, keepdims=True)


def scores_of(q_ref, k_ref, qh_ref, kn_ref, sel, at, span):
    q = q_ref[at, :] * 0.125
    qa = jnp.where(sel, q, qh_ref[at, :])
    ka = jnp.where(sel, k_ref[span, :], kn_ref[span, :])
    s = dot(ka, qa, NT)
    causal = lax.broadcasted_iota(jnp.int32, (BLOCK, BLOCK), 0) <= lax.broadcasted_iota(
        jnp.int32, (BLOCK, BLOCK), 1
    )
    early = s.shape[0] - BLOCK
    tail = jnp.where(causal, s[early:, :], MASKED_SCORE)
    return (tail if early == 0 else jnp.concatenate([s[:early, :], tail], axis=0)), q


def spans(length, row):
    for end in range(BLOCK, length + 1, BLOCK):
        start = max(0, end - BLOCK - LONGEST)
        base = row * length
        yield slice(base + end - BLOCK, base + end), slice(base + start, base + end)


def remote(src, dst, send, recv, device):
    return pltpu.make_async_remote_copy(
        src_ref=src, dst_ref=dst, send_sem=send, recv_sem=recv, device_id=device,
        device_id_type=MESH,
    )


def greet(partners):
    barrier = pltpu.get_barrier_semaphore()
    for device in partners:
        pl.semaphore_signal(barrier, inc=1, device_id=device, device_id_type=MESH)
    pl.semaphore_wait(barrier, len(partners))


def neighbours():
    dp, tensor = lax.axis_index("dp"), lax.axis_index("tensor")
    side = dp % 2
    to_core = (dp, tensor + 1 - 2 * (tensor % 2))
    return to_core, (dp, (tensor + 2) % 4), (dp + 1 - 2 * side, tensor), side


def pair_weights(even, odd, w, wo):
    for h, unit in enumerate((even, odd)):
        for i in range(3):
            at = LANES * i + HEAD_DIM * h
            w[at : at + HEAD_DIM, :] = unit[HEAD_DIM * i : HEAD_DIM * (i + 1), :]
        wo[HEAD_DIM * h : HEAD_DIM * (h + 1), :] = unit[3 * HEAD_DIM :, :]


def fwd_kernel(
    x_from, c_from, wqkv_ref, wout_ref, up_from, down_from, gain_one_ref, gain_two_ref, bias_out_ref,
    bias_down_ref, bias_up_ref, bias_qv_ref, seg_ref,
    vec_ref, n_to, cot_to, c_sum_ref, qkv_ref, att_ref, lse_ref, resid_to, n_two_to, qh_ref, kn_ref,
    wa_ref, wf_ref, misc_all_ref,
    wa, stage, misc, w, wo, branch, wide,
    core_s, core_r, y_s, y_r, x_s, x_r, d_s, d_r, local_s, z_s, z_r, zz_s, zz_r,
    x_ref, c_ref, up_ref, down_ref, n_ref, cot_ref, resid_ref, n_two_ref, in_s, to_s,
    *, rows, pairs
):
    t = pl.program_id(0)
    tokens, stored = x_ref.shape
    length = tokens // rows
    heads = pairs // 2
    model = stored + 1
    early, tail = heads, stage.shape[0]
    to_core, to_y, to_x, side = neighbours()
    last = early + tail
    dp = lax.axis_index("dp")
    level = dp // 2 % 2
    to_z = (dp + 2 - 4 * level, lax.axis_index("tensor"))

    def rows_of(k, across, along):
        if k not in QUARTERED:
            return pl.ds(pl.multiple_of(across * (CHUNK // 2), CHUNK // 2), CHUNK // 2)
        size = CHUNK // 4
        return pl.ds(pl.multiple_of((2 * across + along) * size, size), size)

    def held(quarter, k):
        if k == last:
            return misc.at[quarter]
        if k < early:
            return wa.at[quarter, k]
        return wf_ref.at[quarter, k - early]

    def own(k):
        return held(0, k) if k < early or k == last else stage.at[k - early]

    def core_copy(k):
        return remote(own(k), held(1, k), core_s.at[k], core_r.at[k], to_core)

    def y_copy(k):
        src, dst = own(k), held(2, k)
        if k < last:
            rows_ = rows_of(k, side, level)
            src, dst = src.at[rows_], dst.at[rows_]
        return remote(src, dst, y_s.at[k], y_r.at[k], to_y)

    def spread(k, across, along, send, recv, device):
        ref = held(2, k).at[rows_of(k, across, along)]
        return remote(ref, ref, send.at[k], recv.at[k], device)

    def x_copy(k, across):
        return spread(k, across, level, x_s, x_r, to_x)

    def z_copy(k, along):
        return spread(k, side, along, z_s, z_r, to_z)

    def zz_copy(k, along):
        return spread(k, 1 - side, along, zz_s, zz_r, to_z)

    def d_copy(k):
        return remote(held(2, k), held(3, k), d_s.at[k], d_r.at[k], to_core)

    def keep_copy(k):
        if k == last:
            return pltpu.make_async_copy(misc, misc_all_ref, local_s.at[k])
        if k < early:
            return pltpu.make_async_copy(wa.at[:, k], wa_ref.at[:, k], local_s.at[k])
        return pltpu.make_async_copy(stage.at[k - early], wf_ref.at[0, k - early], local_s.at[k])

    def x_on(k):
        y_copy(k).wait_recv()
        x_copy(k, side).start()
        if k in QUARTERED:
            z_copy(k, level).start()

    def z_on(k):
        x_copy(k, 1 - side).wait_recv()
        zz_copy(k, level).start()

    def d_on(k):
        if k == last:
            y_copy(k).wait_recv()
        elif k not in QUARTERED:
            x_copy(k, 1 - side).wait_recv()
        else:
            z_copy(k, 1 - level).wait_recv()
            zz_copy(k, 1 - level).wait_recv()
        d_copy(k).start()

    def start_y(k):
        y_copy(k).start()

    def start_core(k):
        core_copy(k).start()

    def taken():
        pairs_of = (up_from, up_ref), (down_from, down_ref), (x_from, x_ref), (c_from, c_ref)
        return [pltpu.make_async_copy(*refs, in_s.at[i]) for i, refs in enumerate(pairs_of)]

    def given(i):
        pairs_of = (n_ref, n_to), (cot_ref, cot_to), (resid_ref, resid_to), (n_two_ref, n_two_to)
        return pltpu.make_async_copy(*pairs_of[i], to_s.at[i])

    @pl.when(t == 0)
    def _():
        for copy in taken():
            copy.start()
        edge = slice(model - LANES, model)
        wa[0, :, :, edge] = jnp.zeros((early, CHUNK, LANES), BF16)
        for j in range(heads):
            head = slice(HEAD_DIM * j, HEAD_DIM * (j + 1))
            for i in range(3):
                wa[0, j, HEAD_DIM * i : HEAD_DIM * (i + 1), :stored] = wqkv_ref[i, head, :]
            wa[0, j, 3 * HEAD_DIM :, :stored] = wout_ref[head, :]
        vec_ref[...] = jnp.zeros_like(vec_ref)
        vectors = gain_one_ref, gain_two_ref, bias_out_ref, bias_down_ref, bias_up_ref
        for i, ref in enumerate(vectors):
            vec_ref[i : i + 1, : ref.shape[0]] = ref[...].astype(F32).reshape(1, ref.shape[0])
        vec_ref[5:7, : bias_qv_ref.shape[1]] = bias_qv_ref[...].astype(F32)
        misc[0] = jnp.zeros_like(misc[0])
        for p in range(2):
            for j in range(heads):
                for i, row in ((0, 5), (2, 6)):
                    at = LANES * i + HEAD_DIM * p
                    misc[0, p, j : j + 1, at : at + HEAD_DIM] = vec_ref[
                        row : row + 1, HEAD_DIM * j : HEAD_DIM * (j + 1)
                    ]
            wide_half = misc.shape[3]
            misc[0, p, heads : heads + 1, :] = vec_ref[4:5, wide_half * p : wide_half * (p + 1)]
        greet([to_core, to_y, to_x, to_z])
        for k in (last, 0):
            core_copy(k).start()
            y_copy(k).start()
        for k in range(1, early):
            core_copy(k).start()
        for copy in taken():
            copy.wait()
        count = tail // 2
        stage[:, :, edge] = jnp.zeros((tail, CHUNK, LANES), BF16)
        stage[count - 1, CHUNK - 16 :, :] = jnp.zeros((16, model), BF16)
        for i in range(count):
            end = min(CHUNK * (i + 1), stored)
            stage[i, : end - CHUNK * i, :] = up_ref[CHUNK * i : end, :]
            stage[count + i, :, :stored] = down_ref[CHUNK * i : CHUNK * (i + 1), :]
        for k in range(early, last):
            keep_copy(k).start()
        branch[...] = jnp.zeros_like(branch)
        c_sum = jnp.zeros((1, model), F32)
        for i in range(0, tokens, CHUNK):
            r = slice(i, i + CHUNK)
            x = widen(x_ref.at[r, :], wide)
            n_ref[r, :] = (x * norm_scale(x)[0] * vec_ref[0:1, :model]).astype(BF16)
            c = widen(c_ref.at[r, :], wide)
            cot_ref[r, :] = c.astype(BF16)
            c_sum += jnp.sum(c, axis=0, keepdims=True)
        c_sum_ref[...] = c_sum
        for i in range(2):
            given(i).start()
        lane = lax.broadcasted_iota(jnp.int32, (1, LANES), 1) % HEAD_DIM
        for row in range(rows):
            document = jnp.broadcast_to(seg_ref[row : row + 1, :].astype(F32), (LANES, length)).T
            hot = document == lane.astype(F32)
            r = slice(row * length, (row + 1) * length)
            qh_ref[r, :] = jnp.where(hot, 1.0, 0.0).astype(BF16)
            kn_ref[r, :] = jnp.where(hot | (lane >= 8), 0.0, MASKED_SCORE).astype(BF16)
        core_copy(last).wait_recv()

    events = {
        (0, 0): [(start_y, 6)],
        (0, 1): [(x_on, 0), (start_y, 1)],
        (0, 2): [(z_on, 0), (start_y, 8)],
        (0, 4): [(x_on, 1), (start_y, 2)],
        (1, 0): [(x_on, 6)],
        (1, 1): [(d_on, 0)],
        (1, 2): [(x_on, 8)],
        (1, 3): [(d_on, last)],
        (1, 4): [(z_on, 1), (start_y, 3)],
        (2, 0): [(x_on, 2), (start_y, 7)],
        (2, 2): [(z_on, 6)],
        (2, 3): [(start_y, 5), (start_core, 6)],
        (2, 4): [(x_on, 3), (start_core, 4)],
        (3, 0): [(d_on, 1), (x_on, 7), (start_core, 3)],
        (3, 1): [(z_on, 8)],
        (3, 2): [(start_y, 4), (start_core, 5)],
        (3, 4): [(d_on, 2), (x_on, 5)],
        (4, 0): [(start_core, 7)],
        (4, 1): [(z_on, 7)],
        (4, 2): [(d_on, 6)],
        (4, 3): [(x_on, 4), (start_core, 8)],
        (4, 4): [(z_on, 3)],
        (5, 0): [(d_on, 5), (d_on, 8)],
        (5, 2): [(d_on, 7)],
        (5, 3): [(d_on, 3)],
        (5, 4): [(d_on, 4)],
    }
    rest = []

    def run(slot):
        for (step, at), todo in events.items():
            if at == slot and todo:

                @pl.when(t == step)
                def _(todo=todo):
                    for event, k in todo:
                        event(k)

    for step in range(pairs):

        @pl.when(t == step)
        def _(far=step // heads, j=step % heads):
            (d_copy if far else core_copy)(j).wait_recv()
            if far and j == 0:
                d_copy(last).wait_recv()

    first = lax.broadcasted_iota(jnp.int32, (1, LANES), 1) < HEAD_DIM
    units = [(2 * (t // heads) + h, t % heads) for h in range(2)]
    pair_weights(*(wa.at[quarter, j] for quarter, j in units), w, wo)
    bias = sum(
        jnp.where(j == row, misc[quarter, h, row : row + 1, :], 0.0)
        for h, (quarter, j) in enumerate(units)
        for row in range(heads)
    )
    qkv_ref[...] = (dot(n_ref[...], w[...], NT) + bias).astype(BF16)
    q_ref, k_ref, v_ref = (qkv_ref.at[:, j * LANES : (j + 1) * LANES] for j in range(3))
    run(0)
    slot = 1
    for row in range(rows):
        for at, span in spans(length, row):
            parts = []
            for h in range(2):
                sel = first if h == 0 else ~first
                s, _ = scores_of(q_ref, k_ref, qh_ref, kn_ref, sel, at, span)
                m = jnp.max(s, axis=0, keepdims=True)
                p = jnp.exp(s - m)
                total = jnp.sum(p, axis=0, keepdims=True)
                weights = (p * (1.0 / total)).astype(BF16)
                parts.append(dot(weights, v_ref[span, :], TN))
                lse_ref[h : h + 1, at] = m + jnp.log(total)
            att_ref[at, :] = jnp.where(first, parts[0], parts[1]).astype(BF16)
            if slot < 4:
                run(slot)
                slot += 1
    branch[...] += dot(att_ref[...], wo[...])
    run(4)

    @pl.when(t == pairs - 1)
    def _():
        for i in range(0, tokens, CHUNK):
            r = slice(i, i + CHUNK)
            resid = widen(x_ref.at[r, :], wide) + (branch[r, :] + vec_ref[2:3, :model])
            resid_ref[r, :] = resid
            n_two_ref[r, :] = (resid * norm_scale(resid)[0] * vec_ref[1:2, :model]).astype(BF16)
        for i in range(2, 4):
            given(i).start()
        for event, k in rest:
            event(k)
        for k in (*range(early), last):
            keep_copy(k).start()
        for k in range(early, last):
            core_copy(k).wait_recv()
            d_copy(k).wait_recv()
        for k in range(last + 1):
            core_copy(k).wait_send()
            y_copy(k).wait_send()
            if k < last:
                x_copy(k, side).wait_send()
            if k in QUARTERED:
                z_copy(k, level).wait_send()
                zz_copy(k, level).wait_send()
            d_copy(k).wait_send()
            keep_copy(k).wait()
        for i in range(4):
            given(i).wait()


def forward(x, c, wqkv, wout, up, down, gain_one, gain_two, bias_out, bias_down, bias_up, bias_qv, seg):
    tokens, stored = x.shape
    model = stored + 1
    heads = wqkv.shape[1] // HEAD_DIM
    pairs = 2 * heads
    tail = 2 * (model // CHUNK)

    def of(*shape):
        return pl.BlockSpec((None, *shape), lambda p: (p,) + (0,) * len(shape))

    anywhere = pl.BlockSpec(memory_space=pl.ANY)
    sems = pltpu.SemaphoreType.DMA((heads + tail + 1,))
    rows = seg.shape[0]
    misc = (2, 8, model // 2)
    inputs = [
        x, c, wqkv, wout, up, down, gain_one, gain_two, bias_out, bias_down, bias_up, bias_qv, seg
    ]
    outs = [
        (once((8, 1024)), (8, 1024), F32),
        (anywhere, (tokens, model), BF16),
        (anywhere, (tokens, model), BF16),
        (once((1, model)), (1, model), F32),
        (of(tokens, 3 * LANES), (pairs, tokens, 3 * LANES), BF16),
        (of(tokens, LANES), (pairs, tokens, LANES), BF16),
        (of(2, tokens), (pairs, 2, tokens), F32),
        (anywhere, (tokens, model), F32),
        (anywhere, (tokens, model), BF16),
        (once((tokens, LANES)), (tokens, LANES), BF16),
        (once((tokens, LANES)), (tokens, LANES), BF16),
        (anywhere, (4, heads, CHUNK, model), BF16),
        (anywhere, (4, tail, CHUNK, model), BF16),
        (anywhere, (4, *misc), F32),
    ]
    return pl.pallas_call(
        functools.partial(fwd_kernel, rows=rows, pairs=pairs),
        grid=(pairs,),
        in_specs=[anywhere if i in (0, 1, 4, 5) else once(v.shape) for i, v in enumerate(inputs)],
        out_specs=[spec for spec, _, _ in outs],
        out_shape=[jax.ShapeDtypeStruct(shape, dtype) for _, shape, dtype in outs],
        scratch_shapes=[
            pltpu.VMEM((4, heads, CHUNK, model), BF16),
            pltpu.VMEM((tail, CHUNK, model), BF16),
            pltpu.VMEM((4, *misc), F32),
            pltpu.VMEM((3 * LANES, model), BF16),
            pltpu.VMEM((LANES, model), BF16),
            pltpu.VMEM((tokens, model), F32),
            pltpu.VMEM((CHUNK, model), F32),
        ]
        + [sems] * 13
        + [
            pltpu.VMEM(x.shape, BF16),
            pltpu.VMEM(c.shape, BF16),
            pltpu.VMEM(up.shape, BF16),
            pltpu.VMEM(down.shape, BF16),
            pltpu.VMEM((tokens, model), BF16),
            pltpu.VMEM((tokens, model), BF16),
            pltpu.VMEM((tokens, model), F32),
            pltpu.VMEM((tokens, model), BF16),
            pltpu.SemaphoreType.DMA((4,)),
            pltpu.SemaphoreType.DMA((4,)),
        ],
        compiler_params=params(60, collective_id=1, has_side_effects=True),
        name="forward",
    )(*inputs)


def backward_kernel(
    n_two_ref, c_ref, n_from, x_from, vec_ref, c_sum_ref, up_ref, down_ref, bias_ref,
    qkv_ref, att_ref, lse_ref, even_ref, odd_ref, qh_ref, kn_ref, resid_ref,
    output_ref, grad_in_ref, red_ref, red_late_ref, total_ref,
    out, back, d_resid, nt, ct, db, stage, bias_row, w, wo, da, dqkv, dk_acc, dv_acc, wide_x,
    g, core_in, y_in, x_in, z_in, ag, xag_in, sv, sv_in, sv_z,
    core_s, core_r, y_s, y_r, x_s, x_r, z_s, z_r, a_s, a_r, xa_s, xa_r, out_s,
    sv_s, sv_r, svz_s, svz_r, resid_s, rows_s, n_ref, x_ref, late_s,
    *, rows, pairs, group, blocks
):
    t = pl.program_id(0)
    tokens, model = n_ref.shape
    length = tokens // rows
    front = 4 * blocks
    early, late = 2 * blocks, pairs // 2
    chunks = early + late
    others = group // 2
    half, units = g.shape[2:]
    keep = half // others
    pieces = half // HEAD_DIM
    dp, tensor = lax.axis_index("dp"), lax.axis_index("tensor")
    place = (dp % group) // 2
    mine = pl.ds(pl.multiple_of(place * keep, keep), keep)
    to_core, to_y, to_x, side = neighbours()

    def place_of(o):
        return (place + o) % others

    def to_z(o):
        return (dp - dp % group + place_of(o) * 2 + side, tensor)

    box = 2 * chunks

    def core_copy(which, k, at, slot):
        return remote(
            g.at[box + at], core_in.at[which, slot], core_s.at[which, k], core_r.at[which, k], to_core
        )

    def early_core(which, k):
        return core_copy(which, k, k, k)

    def late_core(which, i):
        return core_copy(which, early + i, late * which + i, i)

    def y_copy(k):
        return remote(g.at[chunks + k], y_in.at[k], y_s.at[k], y_r.at[k], to_y)

    def x_copy(k):
        return remote(g.at[k, 1 - side], x_in.at[k], x_s.at[k], x_r.at[k], to_x)

    def z_copy(k, o):
        rows_of = pl.ds(pl.multiple_of(place_of(o) * keep, keep), keep)
        return remote(
            g.at[k, side, rows_of], z_in.at[k, o - 1], z_s.at[k, o - 1], z_r.at[k, o - 1], to_z(o)
        )

    def a_copy(k, o):
        return remote(ag.at[k, mine], ag.at[k, mine], a_s.at[k, o - 1], a_r.at[k, o - 1], to_z(o))

    def a_wait(k, o):
        rows_of = pl.ds(pl.multiple_of(place_of(others - o) * keep, keep), keep)
        part = ag.at[k, rows_of]
        remote(part, part, a_s.at[k, o - 1], a_r.at[k, o - 1], to_z(o)).wait_recv()

    def xa_copy(k):
        return remote(ag.at[k], xag_in.at[k], xa_s.at[k], xa_r.at[k], to_x)

    def out_copies(k, i, act):
        which = side + i - 2 * side * i
        src = xag_in if i else ag

        @pl.when(k < early)
        def _():
            at = jnp.minimum(k, early - 1)
            lines = pl.ds(pl.multiple_of(which * half, half), half)
            cols = pl.ds(pl.multiple_of(at // 2 * units, units), units)
            act(pltpu.make_async_copy(src.at[at], red_ref.at[at % 2, lines, cols], out_s.at[k, i, 0]))

        @pl.when(k >= early)
        def _():
            at = jnp.maximum(k, early)
            head = pl.ds(pl.multiple_of((chunks - 1 - at) * HEAD_DIM, HEAD_DIM), HEAD_DIM)
            for n in range(pieces):
                piece = which * pieces + n
                cols = pl.ds(pl.multiple_of(piece // 4 * units, units), units)
                act(
                    pltpu.make_async_copy(
                        src.at[at, HEAD_DIM * n : HEAD_DIM * (n + 1)],
                        red_late_ref.at[piece % 4, head, cols],
                        out_s.at[k, i, n],
                    )
                )

    def plus(at, value):
        g[at] = (g[at].astype(F32) + value.astype(F32)).astype(BF16)

    def send_y(k):
        @pl.when(k >= early)
        def _():
            i = jnp.maximum(k, early) - early
            late_core(0, i).wait_recv()
            plus(chunks + early + i, core_in[0, i])

        y_copy(k).start()

    def send_x(k):
        @pl.when(k >= early)
        def _():
            i = jnp.maximum(k, early) - early
            late_core(1, i).wait_recv()
            plus(early + i, core_in[1, i])

        y_copy(k).wait_recv()
        plus(k, y_in[k])
        x_copy(k).start()

    def send_z(k):
        x_copy(k).wait_recv()
        g[k, side] = (g[k, side].astype(F32) + x_in[k].astype(F32)).astype(BF16)
        for o in range(1, others):
            z_copy(k, o).start()

    def send_back(k):
        total = g[k, side, mine].astype(F32)
        for o in range(1, others):
            z_copy(k, o).wait_recv()
            total += z_in[k, o - 1].astype(F32)
        ag[k, mine] = total.astype(BF16)
        for o in range(1, others):
            a_copy(k, o).start()

    def send_back_x(k):
        for o in range(1, others):
            a_wait(k, o)
        xa_copy(k).start()
        out_copies(k, 0, lambda copy: copy.start())

    def finish(k):
        xa_copy(k).wait_recv()
        out_copies(k, 1, lambda copy: copy.start())

    plan = [
        (finish, [(16, 2), (16, 4), (17, 0), (17, 4), (17, 4)]),
        (send_back_x, [(12, 3), (14, 3), (14, 4), (15, 4), (16, 4), (17, 4)]),
        (send_back, [(11, 0), (12, 0), (13, 2), (14, 3), (16, 0), (16, 2), (17, 2)]),
        (send_z, [(9, 0), (10, 0), (12, 2), (13, 0), (14, 0), (15, 1), (16, 4), (17, 4)]),
        (send_x, [(7, 0), (8, 0), (10, 0), (12, 0), (12, 3), (14, 1), (16, 1), (17, 1)]),
        (send_y, [(2, 0), (3, 0), (6, 0), (8, 0), (10, 0), (12, 2), (14, 0), (16, 0), (17, 0)]),
    ]

    def run(slot, first, end):
        for event, times in plan:
            now = [(step, k) for k, (step, at) in enumerate(times) if at == slot and first <= step < end]
            while now:
                table = dict(now[::-1])
                now = [(step, k) for step, k in now if table[step] != k]
                k = jnp.int32(-1)
                for step, at in table.items():
                    k = jnp.where(t == step, at, k)

                @pl.when(k >= 0)
                def _(event=event, k=k):
                    event(jnp.maximum(k, 0))

    def sv_copy(i, src, device):
        return remote(src, sv_in.at[i], sv_s.at[i], sv_r.at[i], device)

    def svz_copy(o):
        return remote(sv_z.at[place], sv_z.at[place], svz_s.at[o - 1], svz_r.at[o - 1], to_z(o))

    def small_y():
        for i in (0, 1):
            sv_copy(i, sv.at[3 - 2 * i], to_core).wait_recv()
        sv[2] += sv_in[0]
        sv_copy(2, sv.at[2], to_y).start()

    def small_x():
        sv_copy(2, sv.at[2], to_y).wait_recv()
        sv[0] = (sv[0] + sv_in[1]) + sv_in[2]
        sv_copy(3, sv.at[0], to_x).start()

    def small_z():
        sv_copy(3, sv.at[0], to_x).wait_recv()
        sv_z[place] = sv[0] + sv_in[3]
        for o in range(1, others):
            svz_copy(o).start()

    def small_end():
        for o in range(1, others):
            part = sv_z.at[place_of(others - o)]
            remote(part, part, svz_s.at[o - 1], svz_r.at[o - 1], to_z(o)).wait_recv()
        total = sv_z[0]
        for i in range(1, others):
            total += sv_z[i]
        total_ref[...] = total

    def late_copies():
        return (
            pltpu.make_async_copy(n_from, n_ref, late_s.at[0]),
            pltpu.make_async_copy(x_from, x_ref, late_s.at[1]),
        )

    def resid_copy():
        return pltpu.make_async_copy(resid_ref, d_resid, resid_s)

    def grad_copy(i):
        r = slice(CHUNK * i, CHUNK * (i + 1))
        return pltpu.make_async_copy(db.at[r], grad_in_ref.at[r], rows_s.at[i])

    def output_copy(i):
        r = slice(CHUNK * i, CHUNK * (i + 1))
        return pltpu.make_async_copy(stage.at[i % 2], output_ref.at[r], rows_s.at[i])

    def feed_forward():
        b, quarter = t // 4, 3 - t % 4
        up = up_ref[...].reshape(model, units)
        down = down_ref[...]
        wide = bias_ref.shape[2]
        for h in range(2):
            bias_row[0:1, wide * h : wide * (h + 1)] = bias_ref[h, late : late + 1, :]
        lanes = pl.ds(pl.multiple_of(b * units, units), units)
        pre = dot(n_two_ref[...], up) + bias_row[0:1, lanes]
        dh = dot(c_ref[...], down, NT)
        sq = pre * pre
        th = jnp.tanh(pre * (GELU_A + (GELU_A * GELU_B) * sq))
        level = 0.5 + 0.5 * th
        hidden = (pre * level).astype(BF16)
        slope = level + (0.5 * pre) * (1.0 - th * th) * (GELU_A + (3.0 * GELU_A * GELU_B) * sq)
        dpre = (dh * slope).astype(BF16)
        out[...] += dot(hidden, down)
        back[...] += dot(dpre, up, NT)
        sv[quarter, 0:1, lanes] = jnp.sum(dpre.astype(F32), axis=0, keepdims=True)
        grads = dot(nt[...], dpre).astype(BF16), dot(ct[...], hidden).astype(BF16)

        @pl.when(t % 4 == 2)
        def _():
            for m in range(2):
                early_core(0, 2 * b + m).wait_send()

        base = jnp.where(quarter == 0, 0, jnp.where(quarter == 2, chunks, box)) + 2 * b
        for m in range(2):
            for h in range(2):
                g[base + m, h] = grads[m][half * h : half * (h + 1)]
        for m in range(2):
            k = 2 * b + m
            for which in range(2):

                @pl.when(t % 4 == 2 * which)
                def _(which=which, k=k):
                    early_core(which, k).start()

                @pl.when(t % 4 == 2 * which + 1)
                def _(which=which, k=k):
                    early_core(which, k).wait_recv()
                    plus((1 - which) * chunks + k, core_in[which, k])

    def turn():
        resid_copy().wait()
        for copy in late_copies():
            copy.wait()
        gain_sum = branch_sum = jnp.zeros((1, model), F32)
        for i in range(tokens // CHUNK):
            r = slice(CHUNK * i, CHUNK * (i + 1))
            resid = d_resid[r, :]
            if i >= 2:
                output_copy(i - 2).wait()
            stage[i % 2] = (resid + (out[r, :] + vec_ref[3:4, :model])).astype(BF16)
            output_copy(i).start()
            out[r, :] = jnp.zeros((CHUNK, model), F32)
            d_norm, part = norm_back(resid, vec_ref[1:2, :model], back[r, :])
            d_rows = c_ref[r, :].astype(F32) + d_norm
            d_resid[r, :] = d_rows
            d_branch = d_rows.astype(BF16)
            db[r, :] = d_branch
            gain_sum += part
            branch_sum += jnp.sum(d_branch.astype(F32), axis=0, keepdims=True)
        for i in range(tokens // CHUNK - 2, tokens // CHUNK):
            output_copy(i).wait()
        for i in range(4):
            sv[i, 2:3, :] = branch_sum
            sv[i, 3:4, :] = gain_sum
        for k in range(early):
            early_core(1, k).wait_send()

    def norm_one():
        gain_sum = jnp.zeros((1, model), F32)
        for i in range(tokens // CHUNK):
            r = slice(CHUNK * i, CHUNK * (i + 1))
            d_norm, part = norm_back(widen(x_ref.at[r, :], wide_x), vec_ref[0:1, :model], out[r, :])
            db[r, :] = (d_resid[r, :] + d_norm).astype(BF16)
            grad_copy(i).start()
            gain_sum += part
        for i in range(4):
            sv[i, 4:5, :] = gain_sum
        for i in (0, 1):
            sv_copy(i, sv.at[3 - 2 * i], to_core).start()

    first = lax.broadcasted_iota(jnp.int32, (1, LANES), 1) < HEAD_DIM
    zero = jnp.zeros((), BF16)
    q_ref, k_ref, v_ref = (qkv_ref.at[:, j * LANES : (j + 1) * LANES] for j in range(3))

    def attend(d_ref, at, span):
        dq = None
        for h in range(2):
            sel = first if h == 0 else ~first
            s, q = scores_of(q_ref, k_ref, qh_ref, kn_ref, sel, at, span)
            qm = jnp.where(sel, q, zero)
            km = jnp.where(sel, k_ref[span, :], zero)
            dom = jnp.where(sel, da[at, :], zero)
            p = jnp.exp(s - lse_ref[h : h + 1, at])
            dp_ = dot(v_ref[span, :], dom, NT)
            u = p * dp_
            inner = jnp.sum(u, axis=0, keepdims=True)
            ds = (u - p * inner).astype(BF16)
            dv_acc[span, :] += dot(p.astype(BF16), dom)
            dk_acc[span, :] += dot(ds, qm)
            part = dot(ds, km, TN)
            dq = part if dq is None else dq + part
        d_ref[at, :LANES] = (dq * 0.125).astype(BF16)

    def attention():
        slot_of = jnp.maximum(t - front - late, 0)
        pair_weights(even_ref, odd_ref, w.at[slot_of], wo)
        da[...] = dot(db[...], wo[...], NT).astype(BF16)
        dk_acc[...] = jnp.zeros_like(dk_acc)
        dv_acc[...] = jnp.zeros_like(dv_acc)
        run(0, front, front + pairs)
        slot = 1
        for row in range(rows):
            for at, span in spans(length, row):
                attend(dqkv.at[slot_of], at, span)
                if slot < 5:
                    run(slot, front, front + pairs)
                    slot += 1
        dqkv[slot_of, :, LANES : 2 * LANES] = dk_acc[...].astype(BF16)
        dqkv[slot_of, :, 2 * LANES :] = dv_acc[...].astype(BF16)
        grads = dot(dqkv[slot_of], n_ref[...], TN).astype(BF16)
        grads_out = dot(att_ref[...], db[...], TN).astype(BF16)
        pair = pairs - 1 - (t - front)
        far, j = pair // late, pair % late
        i = late - 1 - j
        for h in range(2):
            base = i + ((box + late * (1 - far)) if h else (early + chunks * far))
            for block in range(model // units):
                cols = slice(units * block, units * (block + 1))
                for p in range(4):
                    if p < 3:
                        lines = grads[LANES * p + HEAD_DIM * h : LANES * p + HEAD_DIM * (h + 1), cols]
                    else:
                        lines = grads_out[HEAD_DIM * h : HEAD_DIM * (h + 1), cols]
                    at = CHUNK * block + HEAD_DIM * p
                    g[base, at // half, at % half : at % half + HEAD_DIM, :] = lines
        late_core(1 - far, i).start()

        for j_far in range(late):
            pl.when(t == front + late - 1 - j_far)(functools.partial(add_back, 0, 1, j_far))

    def add_back(slot, far, j):
        out[...] += dot(dqkv[slot], w[slot])
        sums = jnp.sum(dqkv[slot].astype(F32), axis=0, keepdims=True)
        for h in range(2):
            for part in (0, 2):
                at = LANES * part + HEAD_DIM * h
                sv[2 * far + h, 8 + j : 9 + j, LANES * part : LANES * part + HEAD_DIM] = (
                    sums[:, at : at + HEAD_DIM]
                )

    @pl.when(t == 0)
    def _():
        greet([to_core, to_y, to_x] + [to_z(o) for o in range(1, others)])
        out[...] = jnp.zeros_like(out)
        back[...] = jnp.zeros_like(back)
        sv[...] = jnp.zeros_like(sv)
        for i in range(4):
            sv[i, 1:2, :] = c_sum_ref[...]
        for i in range(0, tokens, CHUNK):
            nt[:, i : i + CHUNK] = n_two_ref[i : i + CHUNK, :].T
            ct[:, i : i + CHUNK] = c_ref[i : i + CHUNK, :].T

    @pl.when(t == front - 2)
    def _():
        resid_copy().start()
        for copy in late_copies():
            copy.start()

    @pl.when(t < front)
    def _():
        run(0, 0, front)
        feed_forward()

    pl.when(t == front - 1)(turn)
    pl.when((t >= front) & (t < front + pairs))(attention)

    @pl.when(t == front + pairs)
    def _():
        add_back(0, 0, late - 1)
        send_x(8)
        add_back(1, 0, late - 2)
        finish(5)
        send_back(7)
        add_back(2, 0, late - 3)
        norm_one()
        send_back_x(6)
        send_z(8)
        small_y()
        send_back_x(7)
        small_x()
        send_back(8)
        send_back_x(8)
        small_z()
        finish(6)
        small_end()
        finish(7)
        finish(8)

        @pl.loop(0, chunks)
        def _(k):
            y_copy(k).wait_send()
            x_copy(k).wait_send()
            for o in range(1, others):
                z_copy(k, o).wait_send()
                a_copy(k, o).wait_send()
            xa_copy(k).wait_send()
            for i in range(2):
                out_copies(k, i, lambda copy: copy.wait())

        for which in range(2):
            for i in range(late):
                late_core(which, i).wait_send()
        for i, device in enumerate((to_core, to_core, to_y, to_x)):
            sv_copy(i, sv.at[0], device).wait_send()
        for o in range(1, others):
            svz_copy(o).wait_send()
        for i in range(tokens // CHUNK):
            grad_copy(i).wait()


def backward(
    n_two, c, resid, w_ffn, misc, n, x, vec, c_sum, qkv, att, lse, w_attn, qh, kn, rows, group
):
    tokens, model = n.shape
    stored = x.shape[1]
    pairs = qkv.shape[0]
    blocks = model // UNITS
    front, early, late = 4 * blocks, 2 * blocks, pairs // 2
    chunks = early + late
    others = group // 2
    half = model // 2
    lines = 16
    wide = misc.shape[3]

    def unit_block(t):
        t = jnp.minimum(t, front - 1)
        return 3 - t % 4, t // 4

    def up_at(t):
        quarter, b = unit_block(t)
        return quarter, 0, 0, b

    def down_at(t):
        quarter, b = unit_block(t)
        return quarter, model // CHUNK + b, 0, 0

    def bias_at(t):
        return unit_block(t)[0], 0, 0, 0

    def pair_at(t):
        return pairs - 1 - jnp.clip(t - front, 0, pairs - 1)

    def of(shape):
        return pl.BlockSpec((None, *shape), lambda t: (pair_at(t), 0, 0))

    def unit(h):
        return pl.BlockSpec(
            (None, None, CHUNK, model),
            lambda t: (2 * (pair_at(t) // late) + h, pair_at(t) % late, 0, 0),
        )

    anywhere = pl.BlockSpec(memory_space=pl.ANY)
    sems = pltpu.SemaphoreType.DMA
    between = max(others - 1, 1)
    many = (chunks, between)
    big = once((tokens, model))
    return pl.pallas_call(
        functools.partial(backward_kernel, rows=rows, pairs=pairs, group=group, blocks=blocks),
        grid=(front + pairs + 1,),
        in_specs=[
            big, big, anywhere, anywhere, full(vec.shape), full((1, model)),
            pl.BlockSpec((None, model // CHUNK, CHUNK, UNITS), up_at),
            pl.BlockSpec((None, None, CHUNK, model), down_at),
            pl.BlockSpec((None, 2, 8, wide), bias_at),
            of((tokens, 3 * LANES)), of((tokens, LANES)), of((2, tokens)), unit(0), unit(1),
            once((tokens, LANES)), once((tokens, LANES)), anywhere,
        ],
        out_specs=[anywhere] * 4 + [once((lines, model))],
        out_shape=[
            jax.ShapeDtypeStruct((tokens, model), BF16),
            jax.ShapeDtypeStruct((tokens, model), BF16),
            jax.ShapeDtypeStruct((2, model, blocks * UNITS), BF16),
            jax.ShapeDtypeStruct((4, late * HEAD_DIM, model), BF16),
            jax.ShapeDtypeStruct((lines, model), F32),
        ],
        scratch_shapes=[pltpu.VMEM((tokens, model), F32)] * 3
        + [pltpu.VMEM((model, tokens), BF16)] * 2
        + [
            pltpu.VMEM((tokens, model), BF16),
            pltpu.VMEM((2, CHUNK, model), BF16),
            pltpu.VMEM((8, model), F32),
            pltpu.VMEM((late, 3 * LANES, model), BF16),
            pltpu.VMEM((LANES, model), BF16),
            pltpu.VMEM((tokens, LANES), BF16),
            pltpu.VMEM((late, tokens, 3 * LANES), BF16),
            pltpu.VMEM((tokens, LANES), F32),
            pltpu.VMEM((tokens, LANES), F32),
            pltpu.VMEM((CHUNK, model), F32),
            pltpu.VMEM((2 * chunks + early, 2, half, UNITS), BF16),
            pltpu.VMEM((2, early, 2, half, UNITS), BF16),
            pltpu.VMEM((chunks, 2, half, UNITS), BF16),
            pltpu.VMEM((chunks, half, UNITS), BF16),
            pltpu.VMEM((*many, half // others, UNITS), BF16),
            pltpu.VMEM((chunks, half, UNITS), BF16),
            pltpu.VMEM((chunks, half, UNITS), BF16),
            pltpu.VMEM((4, lines, model), F32),
            pltpu.VMEM((4, lines, model), F32),
            pltpu.VMEM((others, lines, model), F32),
            sems((2, chunks)), sems((2, chunks)), sems((chunks,)), sems((chunks,)),
            sems((chunks,)), sems((chunks,)), sems(many), sems(many), sems(many), sems(many),
            sems((chunks,)), sems((chunks,)), sems((chunks, 2, half // HEAD_DIM)),
            sems((4,)), sems((4,)), sems((between,)), sems((between,)), sems, sems((tokens // CHUNK,)),
            pltpu.VMEM((tokens, model), BF16), pltpu.VMEM((tokens, stored), BF16), sems((2,)),
        ],
        compiler_params=params(63, collective_id=0, has_side_effects=True),
        name="backward",
    )(n_two, c, n, x, vec, c_sum, w_ffn, w_ffn, misc, qkv, att, lse, w_attn, w_attn, qh, kn, resid)


def last_kernel(
    output_ref, grad_ref, up_ref, down_ref, qkv_ref, out_ref, sums_ref,
    output_to, grad_to, up_to, down_to, qkv_to, out_to, bqv_to, *vectors
):
    stored = output_to.shape[1]
    output_to[...] = output_ref[:, :stored]
    grad_to[...] = grad_ref[:, :stored]
    up_to[...] = up_ref[...].astype(F32)
    down_to[...] = down_ref[...].T.astype(F32)[:, :stored]
    qkv_to[...] = qkv_ref[...].astype(F32)[:, :stored]

    @pl.when(pl.program_id(0) == 0)
    def _():
        out_to[...] = out_ref[...].astype(F32)[:, :stored]
        for j in range(bqv_to.shape[1] // HEAD_DIM):
            for i in range(2):
                part = sums_ref[8 + j : 9 + j, 2 * LANES * i : 2 * LANES * i + HEAD_DIM]
                bqv_to[i : i + 1, HEAD_DIM * j : HEAD_DIM * (j + 1)] = part
        for i, ref in enumerate(vectors):
            ref[...] = sums_ref[i : i + 1, : ref.shape[0]].reshape(ref.shape[0])


def results(output, grad, ffn, heads, sums, stored):
    tokens, model = output.shape
    units, rows = ffn.shape[2], heads.shape[1]
    steps = tokens // CHUNK
    most = model // CHUNK - 1
    assert steps > most

    def block(shape, at):
        return pl.BlockSpec(shape, at)

    def lesser(i):
        return jnp.minimum(i, most)

    lengths = [units, stored, stored, stored, stored]
    shape = jax.ShapeDtypeStruct
    return pl.pallas_call(
        last_kernel,
        grid=(steps,),
        in_specs=[
            block((CHUNK, model), lambda i: (i, 0)),
            block((CHUNK, model), lambda i: (i, 0)),
            block((None, CHUNK, units), lambda i: (0, lesser(i), 0)),
            block((None, model, CHUNK), lambda i: (1, 0, lesser(i))),
            block((None, rows, model), lambda i: (lesser(i), 0, 0)),
            block((None, rows, model), lambda i: (3, 0, 0)),
            full(sums.shape),
        ],
        out_specs=[
            block((CHUNK, stored), lambda i: (i, 0)),
            block((CHUNK, stored), lambda i: (i, 0)),
            block((CHUNK, units), lambda i: (lesser(i), 0)),
            block((CHUNK, stored), lambda i: (lesser(i), 0)),
            block((None, rows, stored), lambda i: (lesser(i), 0, 0)),
            full((rows, stored)),
            full((2, rows)),
        ]
        + [full((n,)) for n in lengths],
        out_shape=[
            shape((tokens, stored), BF16),
            shape((tokens, stored), BF16),
            shape((stored, units), F32),
            shape((units, stored), F32),
            shape((3, rows, stored), F32),
            shape((rows, stored), F32),
            shape((2, rows), F32),
        ]
        + [shape((n,), F32) for n in lengths],
        compiler_params=params(60),
        name="results",
    )(output, grad, ffn, ffn, heads, heads, sums)


def solution(mesh):
    n_dp, n_tensor = mesh.shape["dp"], mesh.shape["tensor"]
    assert n_tensor == 4 and n_dp % 4 == 0 and n_dp & (n_dp - 1) == 0
    bits = [1 << i for i in range(n_dp.bit_length() - 1)]
    group = min(n_dp, 8)

    def to_dp(v, bit):
        return lax.ppermute(v, "dp", [(i, i ^ bit) for i in range(n_dp)])

    def local(
        layer_input, segments, cotangent, gain_one, w_qkv, b_qv, w_out, b_out, gain_two,
        w_up, b_up, w_down, b_down,
    ):
        rows = segments.shape[0]
        tokens, stored = layer_input.shape
        model = stored + 1
        heads = w_qkv.shape[2] // HEAD_DIM
        units = w_up.shape[1]

        (
            vec, n_one, cot, grad_bdown, qkv, att, lse, resid, n_two, qh, kn, w_attn, w_ffn, misc
        ) = forward(
            layer_input, cotangent, w_qkv.transpose(0, 2, 1), w_out, w_up, w_down, gain_one, gain_two,
            b_out, b_down, b_up, b_qv, segments,
        )
        output, input_grad, *reduced, small = backward(
            n_two, cot, resid, w_ffn, misc, n_one, layer_input, vec, grad_bdown, qkv, att, lse, w_attn,
            qh, kn, rows, group,
        )
        for bit in bits:
            if bit >= group:
                small = small + to_dp(small, bit)
                reduced = [(v.astype(F32) + to_dp(v, bit).astype(F32)).astype(BF16) for v in reduced]
        (
            output, input_grad, grad_up, grad_down, grad_qkv, grad_out, grad_bqv,
            grad_bup, grad_bdown, grad_bout, grad_gain_two, grad_gain_one,
        ) = results(output, input_grad, *reduced, small, stored)
        return (
            output, input_grad, grad_gain_one, grad_qkv.transpose(0, 2, 1), grad_bqv, grad_out, grad_bout,
            grad_gain_two, grad_up, grad_bup, grad_down, grad_bdown,
        )

    return jax.shard_map(
        local,
        mesh=mesh,
        in_specs=(
            P(("dp", "tensor"), None),
            P(("dp", "tensor"), None),
            P(("dp", "tensor"), None),
            P(),
            P(None, None, "tensor"),
            P(None, "tensor"),
            P("tensor", None),
            P(),
            P(),
            P(None, "tensor"),
            P("tensor"),
            P("tensor", None),
            P(),
        ),
        out_specs=(
            P(("dp", "tensor"), None),
            P(("dp", "tensor"), None),
            P(),
            P(None, None, "tensor"),
            P(None, "tensor"),
            P("tensor", None),
            P(),
            P(),
            P(None, "tensor"),
            P("tensor"),
            P("tensor", None),
            P(),
        ),
        check_vma=False,
    )
```

```python
import functools

import jax
import jax.numpy as jnp
from jax import lax
from jax.experimental import pallas as pl
from jax.experimental.pallas import tpu as pltpu
from jax.sharding import PartitionSpec as P

HEAD_DIM = 64
LANES = 128
EPSILON = 1e-05
MASKED_SCORE = -1e30
LONGEST = 512
BLOCK = 256
CHUNK = 256
UNITS = 256
QUARTERED = (1, 2, 3, 6, 7)
F32 = jnp.float32
BF16 = jnp.bfloat16
NN = (((1,), (0,)), ((), ()))
NT = (((1,), (1,)), ((), ()))
TN = (((0,), (0,)), ((), ()))
GELU_A = 0.7978845608028654
GELU_B = 0.044715
MIB = 1024 * 1024
MESH = pl.DeviceIdType.MESH


def dot(a, b, dims=NN):
    return lax.dot_general(a, b, dims, preferred_element_type=F32)


def params(mib, **more):
    return pltpu.CompilerParams(vmem_limit_bytes=mib * MIB, **more)


def full(shape):
    return pl.BlockSpec(shape, lambda *_: (0,) * len(shape))


def once(shape):
    return pl.BlockSpec(shape, lambda *_: (0,) * len(shape), pipeline_mode=pl.Buffered(1))


def widen(ref, wide):
    wide[:, wide.shape[1] - LANES :] = jnp.zeros((wide.shape[0], LANES), F32)
    wide[:, : ref.shape[1]] = ref[...].astype(F32)
    return wide[...]


def norm_scale(values):
    total = jnp.sum(values, axis=-1, keepdims=True)
    square = jnp.sum(values * values, axis=-1, keepdims=True)
    return lax.rsqrt((square + total * total) / values.shape[-1] + EPSILON), total


def norm_back(values, gain, upstream):
    scale, total = norm_scale(values)
    weighted = upstream * values
    spread = jnp.sum(weighted * gain, axis=-1, keepdims=True)
    grad = upstream * gain * scale - (spread * scale * scale * scale / values.shape[-1]) * (
        values + total
    )
    return grad, jnp.sum(weighted * scale, axis=0, keepdims=True)


def scores_of(q_ref, k_ref, qh_ref, kn_ref, sel, at, span):
    q = q_ref[at, :] * 0.125
    qa = jnp.where(sel, q, qh_ref[at, :])
    ka = jnp.where(sel, k_ref[span, :], kn_ref[span, :])
    s = dot(ka, qa, NT)
    causal = lax.broadcasted_iota(jnp.int32, (BLOCK, BLOCK), 0) <= lax.broadcasted_iota(
        jnp.int32, (BLOCK, BLOCK), 1
    )
    early = s.shape[0] - BLOCK
    tail = jnp.where(causal, s[early:, :], MASKED_SCORE)
    return (tail if early == 0 else jnp.concatenate([s[:early, :], tail], axis=0)), q


def spans(length, row):
    for end in range(BLOCK, length + 1, BLOCK):
        start = max(0, end - BLOCK - LONGEST)
        base = row * length
        yield slice(base + end - BLOCK, base + end), slice(base + start, base + end)


def remote(src, dst, send, recv, device):
    return pltpu.make_async_remote_copy(
        src_ref=src, dst_ref=dst, send_sem=send, recv_sem=recv, device_id=device,
        device_id_type=MESH,
    )


def greet(partners):
    barrier = pltpu.get_barrier_semaphore()
    for device in partners:
        pl.semaphore_signal(barrier, inc=1, device_id=device, device_id_type=MESH)
    pl.semaphore_wait(barrier, len(partners))


def neighbours():
    dp, tensor = lax.axis_index("dp"), lax.axis_index("tensor")
    side = dp % 2
    to_core = (dp, tensor + 1 - 2 * (tensor % 2))
    return to_core, (dp, (tensor + 2) % 4), (dp + 1 - 2 * side, tensor), side


def pair_weights(even, odd, w, wo):
    for h, unit in enumerate((even, odd)):
        for i in range(3):
            at = LANES * i + HEAD_DIM * h
            w[at : at + HEAD_DIM, :] = unit[HEAD_DIM * i : HEAD_DIM * (i + 1), :]
        wo[HEAD_DIM * h : HEAD_DIM * (h + 1), :] = unit[3 * HEAD_DIM :, :]


def fwd_kernel(
    x_from, c_from, wqkv_ref, wout_ref, up_from, down_from, gain_one_ref, gain_two_ref, bias_out_ref,
    bias_down_ref, bias_up_ref, bias_qv_ref, seg_ref,
    vec_ref, n_to, cot_to, c_sum_ref, qkv_ref, att_ref, lse_ref, resid_to, n_two_to, qh_ref, kn_ref,
    wa_ref, wf_ref, misc_all_ref,
    wa, stage, misc, w, wo, branch, wide,
    core_s, core_r, y_s, y_r, x_s, x_r, d_s, d_r, local_s, z_s, z_r, zz_s, zz_r,
    x_ref, c_ref, up_ref, down_ref, n_ref, cot_ref, resid_ref, n_two_ref, in_s, to_s,
    *, rows, pairs
):
    t = pl.program_id(0)
    tokens, stored = x_ref.shape
    length = tokens // rows
    heads = pairs // 2
    model = stored + 1
    early, tail = heads, stage.shape[0]
    to_core, to_y, to_x, side = neighbours()
    last = early + tail
    dp = lax.axis_index("dp")
    level = dp // 2 % 2
    to_z = (dp + 2 - 4 * level, lax.axis_index("tensor"))

    def rows_of(k, across, along):
        if k not in QUARTERED:
            return pl.ds(pl.multiple_of(across * (CHUNK // 2), CHUNK // 2), CHUNK // 2)
        size = CHUNK // 4
        return pl.ds(pl.multiple_of((2 * across + along) * size, size), size)

    def held(quarter, k):
        if k == last:
            return misc.at[quarter]
        if k < early:
            return wa.at[quarter, k]
        return wf_ref.at[quarter, k - early]

    def own(k):
        return held(0, k) if k < early or k == last else stage.at[k - early]

    def core_copy(k):
        return remote(own(k), held(1, k), core_s.at[k], core_r.at[k], to_core)

    def y_copy(k):
        src, dst = own(k), held(2, k)
        if k < last:
            rows_ = rows_of(k, side, level)
            src, dst = src.at[rows_], dst.at[rows_]
        return remote(src, dst, y_s.at[k], y_r.at[k], to_y)

    def spread(k, across, along, send, recv, device):
        ref = held(2, k).at[rows_of(k, across, along)]
        return remote(ref, ref, send.at[k], recv.at[k], device)

    def x_copy(k, across):
        return spread(k, across, level, x_s, x_r, to_x)

    def z_copy(k, along):
        return spread(k, side, along, z_s, z_r, to_z)

    def zz_copy(k, along):
        return spread(k, 1 - side, along, zz_s, zz_r, to_z)

    def d_copy(k):
        return remote(held(2, k), held(3, k), d_s.at[k], d_r.at[k], to_core)

    def keep_copy(k):
        if k == last:
            return pltpu.make_async_copy(misc, misc_all_ref, local_s.at[k])
        if k < early:
            return pltpu.make_async_copy(wa.at[:, k], wa_ref.at[:, k], local_s.at[k])
        return pltpu.make_async_copy(stage.at[k - early], wf_ref.at[0, k - early], local_s.at[k])

    def x_on(k):
        y_copy(k).wait_recv()
        x_copy(k, side).start()
        if k in QUARTERED:
            z_copy(k, level).start()

    def z_on(k):
        x_copy(k, 1 - side).wait_recv()
        zz_copy(k, level).start()

    def d_on(k):
        if k == last:
            y_copy(k).wait_recv()
        elif k not in QUARTERED:
            x_copy(k, 1 - side).wait_recv()
        else:
            z_copy(k, 1 - level).wait_recv()
            zz_copy(k, 1 - level).wait_recv()
        d_copy(k).start()

    def start_y(k):
        y_copy(k).start()

    def start_core(k):
        core_copy(k).start()

    def taken():
        pairs_of = (up_from, up_ref), (down_from, down_ref), (x_from, x_ref), (c_from, c_ref)
        return [pltpu.make_async_copy(*refs, in_s.at[i]) for i, refs in enumerate(pairs_of)]

    def given(i):
        pairs_of = (n_ref, n_to), (cot_ref, cot_to), (resid_ref, resid_to), (n_two_ref, n_two_to)
        return pltpu.make_async_copy(*pairs_of[i], to_s.at[i])

    @pl.when(t == 0)
    def _():
        for copy in taken():
            copy.start()
        edge = slice(model - LANES, model)
        wa[0, :, :, edge] = jnp.zeros((early, CHUNK, LANES), BF16)
        for j in range(heads):
            head = slice(HEAD_DIM * j, HEAD_DIM * (j + 1))
            for i in range(3):
                wa[0, j, HEAD_DIM * i : HEAD_DIM * (i + 1), :stored] = wqkv_ref[i, head, :]
            wa[0, j, 3 * HEAD_DIM :, :stored] = wout_ref[head, :]
        vec_ref[...] = jnp.zeros_like(vec_ref)
        vectors = gain_one_ref, gain_two_ref, bias_out_ref, bias_down_ref, bias_up_ref
        for i, ref in enumerate(vectors):
            vec_ref[i : i + 1, : ref.shape[0]] = ref[...].astype(F32).reshape(1, ref.shape[0])
        vec_ref[5:7, : bias_qv_ref.shape[1]] = bias_qv_ref[...].astype(F32)
        misc[0] = jnp.zeros_like(misc[0])
        for p in range(2):
            for j in range(heads):
                for i, row in ((0, 5), (2, 6)):
                    at = LANES * i + HEAD_DIM * p
                    misc[0, p, j : j + 1, at : at + HEAD_DIM] = vec_ref[
                        row : row + 1, HEAD_DIM * j : HEAD_DIM * (j + 1)
                    ]
            wide_half = misc.shape[3]
            misc[0, p, heads : heads + 1, :] = vec_ref[4:5, wide_half * p : wide_half * (p + 1)]
        greet([to_core, to_y, to_x, to_z])
        for k in (last, 0):
            core_copy(k).start()
            y_copy(k).start()
        for k in range(1, early):
            core_copy(k).start()
        for copy in taken():
            copy.wait()
        count = tail // 2
        stage[:, :, edge] = jnp.zeros((tail, CHUNK, LANES), BF16)
        stage[count - 1, CHUNK - 16 :, :] = jnp.zeros((16, model), BF16)
        for i in range(count):
            end = min(CHUNK * (i + 1), stored)
            stage[i, : end - CHUNK * i, :] = up_ref[CHUNK * i : end, :]
            stage[count + i, :, :stored] = down_ref[CHUNK * i : CHUNK * (i + 1), :]
        for k in range(early, last):
            keep_copy(k).start()
        branch[...] = jnp.zeros_like(branch)
        c_sum = jnp.zeros((1, model), F32)
        for i in range(0, tokens, CHUNK):
            r = slice(i, i + CHUNK)
            x = widen(x_ref.at[r, :], wide)
            n_ref[r, :] = (x * norm_scale(x)[0] * vec_ref[0:1, :model]).astype(BF16)
            c = widen(c_ref.at[r, :], wide)
            cot_ref[r, :] = c.astype(BF16)
            c_sum += jnp.sum(c, axis=0, keepdims=True)
        c_sum_ref[...] = c_sum
        for i in range(2):
            given(i).start()
        lane = lax.broadcasted_iota(jnp.int32, (1, LANES), 1) % HEAD_DIM
        for row in range(rows):
            document = jnp.broadcast_to(seg_ref[row : row + 1, :].astype(F32), (LANES, length)).T
            hot = document == lane.astype(F32)
            r = slice(row * length, (row + 1) * length)
            qh_ref[r, :] = jnp.where(hot, 1.0, 0.0).astype(BF16)
            kn_ref[r, :] = jnp.where(hot | (lane >= 8), 0.0, MASKED_SCORE).astype(BF16)
        core_copy(last).wait_recv()

    events = {
        (0, 0): [(start_y, 1), (start_core, 6)],
        (0, 1): [(x_on, 0)],
        (0, 2): [(start_y, 2), (start_core, 7)],
        (0, 4): [(start_y, 3)],
        (1, 0): [(x_on, 1)],
        (1, 2): [(start_y, 8), (start_core, 5)],
        (1, 4): [(d_on, 0), (d_on, last), (x_on, 3)],
        (2, 0): [(x_on, 2), (start_core, 4)],
        (2, 1): [(z_on, 1), (start_y, 6)],
        (2, 2): [(start_y, 7)],
        (2, 3): [(start_core, 3)],
        (2, 4): [(x_on, 8), (start_core, 8)],
        (3, 0): [(start_y, 5)],
        (3, 1): [(z_on, 2)],
        (3, 2): [(d_on, 1), (x_on, 6), (x_on, 7)],
        (3, 4): [(start_y, 4)],
        (4, 0): [(d_on, 2), (x_on, 5)],
        (4, 2): [(z_on, 3)],
        (4, 4): [(d_on, 8), (z_on, 7)],
        (5, 0): [(z_on, 6), (x_on, 4)],
        (5, 1): [(d_on, 3)],
        (5, 4): [(d_on, 5), (d_on, 7)],
    }
    rest = [(d_on, 6), (d_on, 4)]

    def run(slot):
        for (step, at), todo in events.items():
            if at == slot and todo:

                @pl.when(t == step)
                def _(todo=todo):
                    for event, k in todo:
                        event(k)

    for step in range(pairs):

        @pl.when(t == step)
        def _(far=step // heads, j=step % heads):
            (d_copy if far else core_copy)(j).wait_recv()
            if far and j == 0:
                d_copy(last).wait_recv()

    first = lax.broadcasted_iota(jnp.int32, (1, LANES), 1) < HEAD_DIM
    units = [(2 * (t // heads) + h, t % heads) for h in range(2)]
    pair_weights(*(wa.at[quarter, j] for quarter, j in units), w, wo)
    bias = sum(
        jnp.where(j == row, misc[quarter, h, row : row + 1, :], 0.0)
        for h, (quarter, j) in enumerate(units)
        for row in range(heads)
    )
    qkv_ref[...] = (dot(n_ref[...], w[...], NT) + bias).astype(BF16)
    q_ref, k_ref, v_ref = (qkv_ref.at[:, j * LANES : (j + 1) * LANES] for j in range(3))
    run(0)
    slot = 1
    for row in range(rows):
        for at, span in spans(length, row):
            parts = []
            for h in range(2):
                sel = first if h == 0 else ~first
                s, _ = scores_of(q_ref, k_ref, qh_ref, kn_ref, sel, at, span)
                m = jnp.max(s, axis=0, keepdims=True)
                p = jnp.exp(s - m)
                total = jnp.sum(p, axis=0, keepdims=True)
                weights = (p * (1.0 / total)).astype(BF16)
                parts.append(dot(weights, v_ref[span, :], TN))
                lse_ref[h : h + 1, at] = m + jnp.log(total)
            att_ref[at, :] = jnp.where(first, parts[0], parts[1]).astype(BF16)
            if slot < 4:
                run(slot)
                slot += 1
    branch[...] += dot(att_ref[...], wo[...])
    run(4)

    @pl.when(t == pairs - 1)
    def _():
        for i in range(0, tokens, CHUNK):
            r = slice(i, i + CHUNK)
            resid = widen(x_ref.at[r, :], wide) + (branch[r, :] + vec_ref[2:3, :model])
            resid_ref[r, :] = resid
            n_two_ref[r, :] = (resid * norm_scale(resid)[0] * vec_ref[1:2, :model]).astype(BF16)
        for i in range(2, 4):
            given(i).start()
        for event, k in rest:
            event(k)
        for k in (*range(early), last):
            keep_copy(k).start()
        for k in range(early, last):
            core_copy(k).wait_recv()
            d_copy(k).wait_recv()
        for k in range(last + 1):
            core_copy(k).wait_send()
            y_copy(k).wait_send()
            if k < last:
                x_copy(k, side).wait_send()
            if k in QUARTERED:
                z_copy(k, level).wait_send()
                zz_copy(k, level).wait_send()
            d_copy(k).wait_send()
            keep_copy(k).wait()
        for i in range(4):
            given(i).wait()


def forward(x, c, wqkv, wout, up, down, gain_one, gain_two, bias_out, bias_down, bias_up, bias_qv, seg):
    tokens, stored = x.shape
    model = stored + 1
    heads = wqkv.shape[1] // HEAD_DIM
    pairs = 2 * heads
    tail = 2 * (model // CHUNK)

    def of(*shape):
        return pl.BlockSpec((None, *shape), lambda p: (p,) + (0,) * len(shape))

    anywhere = pl.BlockSpec(memory_space=pl.ANY)
    sems = pltpu.SemaphoreType.DMA((heads + tail + 1,))
    rows = seg.shape[0]
    misc = (2, 8, model // 2)
    inputs = [
        x, c, wqkv, wout, up, down, gain_one, gain_two, bias_out, bias_down, bias_up, bias_qv, seg
    ]
    outs = [
        (once((8, 1024)), (8, 1024), F32),
        (anywhere, (tokens, model), BF16),
        (anywhere, (tokens, model), BF16),
        (once((1, model)), (1, model), F32),
        (of(tokens, 3 * LANES), (pairs, tokens, 3 * LANES), BF16),
        (of(tokens, LANES), (pairs, tokens, LANES), BF16),
        (of(2, tokens), (pairs, 2, tokens), F32),
        (anywhere, (tokens, model), F32),
        (anywhere, (tokens, model), BF16),
        (once((tokens, LANES)), (tokens, LANES), BF16),
        (once((tokens, LANES)), (tokens, LANES), BF16),
        (anywhere, (4, heads, CHUNK, model), BF16),
        (anywhere, (4, tail, CHUNK, model), BF16),
        (anywhere, (4, *misc), F32),
    ]
    return pl.pallas_call(
        functools.partial(fwd_kernel, rows=rows, pairs=pairs),
        grid=(pairs,),
        in_specs=[anywhere if i in (0, 1, 4, 5) else once(v.shape) for i, v in enumerate(inputs)],
        out_specs=[spec for spec, _, _ in outs],
        out_shape=[jax.ShapeDtypeStruct(shape, dtype) for _, shape, dtype in outs],
        scratch_shapes=[
            pltpu.VMEM((4, heads, CHUNK, model), BF16),
            pltpu.VMEM((tail, CHUNK, model), BF16),
            pltpu.VMEM((4, *misc), F32),
            pltpu.VMEM((3 * LANES, model), BF16),
            pltpu.VMEM((LANES, model), BF16),
            pltpu.VMEM((tokens, model), F32),
            pltpu.VMEM((CHUNK, model), F32),
        ]
        + [sems] * 13
        + [
            pltpu.VMEM(x.shape, BF16),
            pltpu.VMEM(c.shape, BF16),
            pltpu.VMEM(up.shape, BF16),
            pltpu.VMEM(down.shape, BF16),
            pltpu.VMEM((tokens, model), BF16),
            pltpu.VMEM((tokens, model), BF16),
            pltpu.VMEM((tokens, model), F32),
            pltpu.VMEM((tokens, model), BF16),
            pltpu.SemaphoreType.DMA((4,)),
            pltpu.SemaphoreType.DMA((4,)),
        ],
        compiler_params=params(60, collective_id=1, has_side_effects=True),
        name="forward",
    )(*inputs)


def backward_kernel(
    n_two_ref, c_ref, n_from, x_from, vec_ref, c_sum_ref, up_ref, down_ref, bias_ref,
    qkv_ref, att_ref, lse_ref, even_ref, odd_ref, qh_ref, kn_ref, resid_ref,
    output_ref, grad_in_ref, red_ref, red_late_ref, total_ref,
    out, back, d_resid, nt, ct, db, stage, bias_row, w, wo, da, dqkv, dk_acc, dv_acc, wide_x,
    g, core_in, y_in, x_in, z_in, ag, xag_in, sv, sv_in, sv_z,
    core_s, core_r, y_s, y_r, x_s, x_r, z_s, z_r, a_s, a_r, xa_s, xa_r, out_s,
    sv_s, sv_r, svz_s, svz_r, resid_s, rows_s, n_ref, x_ref, late_s,
    *, rows, pairs, group, blocks
):
    t = pl.program_id(0)
    tokens, model = n_ref.shape
    length = tokens // rows
    front = 4 * blocks
    early, late = 2 * blocks, pairs // 2
    chunks = early + late
    others = group // 2
    half, units = g.shape[2:]
    keep = half // others
    pieces = half // HEAD_DIM
    dp, tensor = lax.axis_index("dp"), lax.axis_index("tensor")
    place = (dp % group) // 2
    mine = pl.ds(pl.multiple_of(place * keep, keep), keep)
    to_core, to_y, to_x, side = neighbours()

    def place_of(o):
        return (place + o) % others

    def to_z(o):
        return (dp - dp % group + place_of(o) * 2 + side, tensor)

    box = 2 * chunks

    def core_copy(which, k, at, slot):
        return remote(
            g.at[box + at], core_in.at[which, slot], core_s.at[which, k], core_r.at[which, k], to_core
        )

    def early_core(which, k):
        return core_copy(which, k, k, k)

    def late_core(which, i):
        return core_copy(which, early + i, late * which + i, i)

    def y_copy(k):
        return remote(g.at[chunks + k], y_in.at[k], y_s.at[k], y_r.at[k], to_y)

    def x_copy(k):
        return remote(g.at[k, 1 - side], x_in.at[k], x_s.at[k], x_r.at[k], to_x)

    def z_copy(k, o):
        rows_of = pl.ds(pl.multiple_of(place_of(o) * keep, keep), keep)
        return remote(
            g.at[k, side, rows_of], z_in.at[k, o - 1], z_s.at[k, o - 1], z_r.at[k, o - 1], to_z(o)
        )

    def a_copy(k, o):
        return remote(ag.at[k, mine], ag.at[k, mine], a_s.at[k, o - 1], a_r.at[k, o - 1], to_z(o))

    def a_wait(k, o):
        rows_of = pl.ds(pl.multiple_of(place_of(others - o) * keep, keep), keep)
        part = ag.at[k, rows_of]
        remote(part, part, a_s.at[k, o - 1], a_r.at[k, o - 1], to_z(o)).wait_recv()

    def xa_copy(k):
        return remote(ag.at[k], xag_in.at[k], xa_s.at[k], xa_r.at[k], to_x)

    def out_copies(k, i, act):
        which = side + i - 2 * side * i
        src = xag_in if i else ag

        @pl.when(k < early)
        def _():
            at = jnp.minimum(k, early - 1)
            lines = pl.ds(pl.multiple_of(which * half, half), half)
            cols = pl.ds(pl.multiple_of(at // 2 * units, units), units)
            act(pltpu.make_async_copy(src.at[at], red_ref.at[at % 2, lines, cols], out_s.at[k, i, 0]))

        @pl.when(k >= early)
        def _():
            at = jnp.maximum(k, early)
            head = pl.ds(pl.multiple_of((chunks - 1 - at) * HEAD_DIM, HEAD_DIM), HEAD_DIM)
            for n in range(pieces):
                piece = which * pieces + n
                cols = pl.ds(pl.multiple_of(piece // 4 * units, units), units)
                act(
                    pltpu.make_async_copy(
                        src.at[at, HEAD_DIM * n : HEAD_DIM * (n + 1)],
                        red_late_ref.at[piece % 4, head, cols],
                        out_s.at[k, i, n],
                    )
                )

    def plus(at, value):
        g[at] = (g[at].astype(F32) + value.astype(F32)).astype(BF16)

    def send_y(k):
        @pl.when(k >= early)
        def _():
            i = jnp.maximum(k, early) - early
            late_core(0, i).wait_recv()
            plus(chunks + early + i, core_in[0, i])

        y_copy(k).start()

    def send_x(k):
        @pl.when(k >= early)
        def _():
            i = jnp.maximum(k, early) - early
            late_core(1, i).wait_recv()
            plus(early + i, core_in[1, i])

        y_copy(k).wait_recv()
        plus(k, y_in[k])
        x_copy(k).start()

    def send_z(k):
        x_copy(k).wait_recv()
        g[k, side] = (g[k, side].astype(F32) + x_in[k].astype(F32)).astype(BF16)
        for o in range(1, others):
            z_copy(k, o).start()

    def send_back(k):
        total = g[k, side, mine].astype(F32)
        for o in range(1, others):
            z_copy(k, o).wait_recv()
            total += z_in[k, o - 1].astype(F32)
        ag[k, mine] = total.astype(BF16)
        for o in range(1, others):
            a_copy(k, o).start()

    def send_back_x(k):
        for o in range(1, others):
            a_wait(k, o)
        xa_copy(k).start()
        out_copies(k, 0, lambda copy: copy.start())

    def finish(k):
        xa_copy(k).wait_recv()
        out_copies(k, 1, lambda copy: copy.start())

    plan = [
        (finish, [(16, 2), (16, 4), (17, 0), (17, 4), (17, 4)]),
        (send_back_x, [(12, 3), (14, 3), (14, 4), (15, 4), (16, 4), (17, 4)]),
        (send_back, [(11, 0), (12, 0), (13, 2), (14, 3), (16, 0), (16, 2), (17, 2)]),
        (send_z, [(9, 0), (10, 0), (12, 2), (13, 0), (14, 0), (15, 1), (16, 4), (17, 4)]),
        (send_x, [(7, 0), (8, 0), (10, 0), (12, 0), (12, 3), (14, 1), (16, 1), (17, 1)]),
        (send_y, [(2, 0), (3, 0), (6, 0), (8, 0), (10, 0), (12, 2), (14, 0), (16, 0), (17, 0)]),
    ]

    def run(slot, first, end):
        for event, times in plan:
            now = [(step, k) for k, (step, at) in enumerate(times) if at == slot and first <= step < end]
            while now:
                table = dict(now[::-1])
                now = [(step, k) for step, k in now if table[step] != k]
                k = jnp.int32(-1)
                for step, at in table.items():
                    k = jnp.where(t == step, at, k)

                @pl.when(k >= 0)
                def _(event=event, k=k):
                    event(jnp.maximum(k, 0))

    def sv_copy(i, src, device):
        return remote(src, sv_in.at[i], sv_s.at[i], sv_r.at[i], device)

    def svz_copy(o):
        return remote(sv_z.at[place], sv_z.at[place], svz_s.at[o - 1], svz_r.at[o - 1], to_z(o))

    def small_y():
        for i in (0, 1):
            sv_copy(i, sv.at[3 - 2 * i], to_core).wait_recv()
        sv[2] += sv_in[0]
        sv_copy(2, sv.at[2], to_y).start()

    def small_x():
        sv_copy(2, sv.at[2], to_y).wait_recv()
        sv[0] = (sv[0] + sv_in[1]) + sv_in[2]
        sv_copy(3, sv.at[0], to_x).start()

    def small_z():
        sv_copy(3, sv.at[0], to_x).wait_recv()
        sv_z[place] = sv[0] + sv_in[3]
        for o in range(1, others):
            svz_copy(o).start()

    def small_end():
        for o in range(1, others):
            part = sv_z.at[place_of(others - o)]
            remote(part, part, svz_s.at[o - 1], svz_r.at[o - 1], to_z(o)).wait_recv()
        total = sv_z[0]
        for i in range(1, others):
            total += sv_z[i]
        total_ref[...] = total

    def late_copies():
        return (
            pltpu.make_async_copy(n_from, n_ref, late_s.at[0]),
            pltpu.make_async_copy(x_from, x_ref, late_s.at[1]),
        )

    def resid_copy():
        return pltpu.make_async_copy(resid_ref, d_resid, resid_s)

    def grad_copy(i):
        r = slice(CHUNK * i, CHUNK * (i + 1))
        return pltpu.make_async_copy(db.at[r], grad_in_ref.at[r], rows_s.at[i])

    def output_copy(i):
        r = slice(CHUNK * i, CHUNK * (i + 1))
        return pltpu.make_async_copy(stage.at[i % 2], output_ref.at[r], rows_s.at[i])

    def feed_forward():
        b, quarter = t // 4, 3 - t % 4
        up = up_ref[...].reshape(model, units)
        down = down_ref[...]
        wide = bias_ref.shape[2]
        for h in range(2):
            bias_row[0:1, wide * h : wide * (h + 1)] = bias_ref[h, late : late + 1, :]
        lanes = pl.ds(pl.multiple_of(b * units, units), units)
        pre = dot(n_two_ref[...], up) + bias_row[0:1, lanes]
        dh = dot(c_ref[...], down, NT)
        sq = pre * pre
        th = jnp.tanh(pre * (GELU_A + (GELU_A * GELU_B) * sq))
        level = 0.5 + 0.5 * th
        hidden = (pre * level).astype(BF16)
        slope = level + (0.5 * pre) * (1.0 - th * th) * (GELU_A + (3.0 * GELU_A * GELU_B) * sq)
        dpre = (dh * slope).astype(BF16)
        out[...] += dot(hidden, down)
        back[...] += dot(dpre, up, NT)
        sv[quarter, 0:1, lanes] = jnp.sum(dpre.astype(F32), axis=0, keepdims=True)
        grads = dot(nt[...], dpre).astype(BF16), dot(ct[...], hidden).astype(BF16)

        @pl.when(t % 4 == 2)
        def _():
            for m in range(2):
                early_core(0, 2 * b + m).wait_send()

        base = jnp.where(quarter == 0, 0, jnp.where(quarter == 2, chunks, box)) + 2 * b
        for m in range(2):
            for h in range(2):
                g[base + m, h] = grads[m][half * h : half * (h + 1)]
        for m in range(2):
            k = 2 * b + m
            for which in range(2):

                @pl.when(t % 4 == 2 * which)
                def _(which=which, k=k):
                    early_core(which, k).start()

                @pl.when(t % 4 == 2 * which + 1)
                def _(which=which, k=k):
                    early_core(which, k).wait_recv()
                    plus((1 - which) * chunks + k, core_in[which, k])

    def turn():
        resid_copy().wait()
        for copy in late_copies():
            copy.wait()
        gain_sum = branch_sum = jnp.zeros((1, model), F32)
        for i in range(tokens // CHUNK):
            r = slice(CHUNK * i, CHUNK * (i + 1))
            resid = d_resid[r, :]
            if i >= 2:
                output_copy(i - 2).wait()
            stage[i % 2] = (resid + (out[r, :] + vec_ref[3:4, :model])).astype(BF16)
            output_copy(i).start()
            out[r, :] = jnp.zeros((CHUNK, model), F32)
            d_norm, part = norm_back(resid, vec_ref[1:2, :model], back[r, :])
            d_rows = c_ref[r, :].astype(F32) + d_norm
            d_resid[r, :] = d_rows
            d_branch = d_rows.astype(BF16)
            db[r, :] = d_branch
            gain_sum += part
            branch_sum += jnp.sum(d_branch.astype(F32), axis=0, keepdims=True)
        for i in range(tokens // CHUNK - 2, tokens // CHUNK):
            output_copy(i).wait()
        for i in range(4):
            sv[i, 2:3, :] = branch_sum
            sv[i, 3:4, :] = gain_sum
        for k in range(early):
            early_core(1, k).wait_send()

    def norm_one():
        gain_sum = jnp.zeros((1, model), F32)
        for i in range(tokens // CHUNK):
            r = slice(CHUNK * i, CHUNK * (i + 1))
            d_norm, part = norm_back(widen(x_ref.at[r, :], wide_x), vec_ref[0:1, :model], out[r, :])
            db[r, :] = (d_resid[r, :] + d_norm).astype(BF16)
            grad_copy(i).start()
            gain_sum += part
        for i in range(4):
            sv[i, 4:5, :] = gain_sum
        for i in (0, 1):
            sv_copy(i, sv.at[3 - 2 * i], to_core).start()

    first = lax.broadcasted_iota(jnp.int32, (1, LANES), 1) < HEAD_DIM
    zero = jnp.zeros((), BF16)
    q_ref, k_ref, v_ref = (qkv_ref.at[:, j * LANES : (j + 1) * LANES] for j in range(3))

    def attend(d_ref, at, span):
        dq = None
        for h in range(2):
            sel = first if h == 0 else ~first
            s, q = scores_of(q_ref, k_ref, qh_ref, kn_ref, sel, at, span)
            qm = jnp.where(sel, q, zero)
            km = jnp.where(sel, k_ref[span, :], zero)
            dom = jnp.where(sel, da[at, :], zero)
            p = jnp.exp(s - lse_ref[h : h + 1, at])
            dp_ = dot(v_ref[span, :], dom, NT)
            u = p * dp_
            inner = jnp.sum(u, axis=0, keepdims=True)
            ds = (u - p * inner).astype(BF16)
            dv_acc[span, :] += dot(p.astype(BF16), dom)
            dk_acc[span, :] += dot(ds, qm)
            part = dot(ds, km, TN)
            dq = part if dq is None else dq + part
        d_ref[at, :LANES] = (dq * 0.125).astype(BF16)

    def attention():
        slot_of = jnp.maximum(t - front - late, 0)
        pair_weights(even_ref, odd_ref, w.at[slot_of], wo)
        da[...] = dot(db[...], wo[...], NT).astype(BF16)
        dk_acc[...] = jnp.zeros_like(dk_acc)
        dv_acc[...] = jnp.zeros_like(dv_acc)
        run(0, front, front + pairs)
        slot = 1
        for row in range(rows):
            for at, span in spans(length, row):
                attend(dqkv.at[slot_of], at, span)
                if slot < 5:
                    run(slot, front, front + pairs)
                    slot += 1
        dqkv[slot_of, :, LANES : 2 * LANES] = dk_acc[...].astype(BF16)
        dqkv[slot_of, :, 2 * LANES :] = dv_acc[...].astype(BF16)
        grads = dot(dqkv[slot_of], n_ref[...], TN).astype(BF16)
        grads_out = dot(att_ref[...], db[...], TN).astype(BF16)
        pair = pairs - 1 - (t - front)
        far, j = pair // late, pair % late
        i = late - 1 - j
        for h in range(2):
            base = i + ((box + late * (1 - far)) if h else (early + chunks * far))
            for block in range(model // units):
                cols = slice(units * block, units * (block + 1))
                for p in range(4):
                    if p < 3:
                        lines = grads[LANES * p + HEAD_DIM * h : LANES * p + HEAD_DIM * (h + 1), cols]
                    else:
                        lines = grads_out[HEAD_DIM * h : HEAD_DIM * (h + 1), cols]
                    at = CHUNK * block + HEAD_DIM * p
                    g[base, at // half, at % half : at % half + HEAD_DIM, :] = lines
        late_core(1 - far, i).start()

        for j_far in range(late):
            pl.when(t == front + late - 1 - j_far)(functools.partial(add_back, 0, 1, j_far))

    def add_back(slot, far, j):
        out[...] += dot(dqkv[slot], w[slot])
        sums = jnp.sum(dqkv[slot].astype(F32), axis=0, keepdims=True)
        for h in range(2):
            for part in (0, 2):
                at = LANES * part + HEAD_DIM * h
                sv[2 * far + h, 8 + j : 9 + j, LANES * part : LANES * part + HEAD_DIM] = (
                    sums[:, at : at + HEAD_DIM]
                )

    @pl.when(t == 0)
    def _():
        greet([to_core, to_y, to_x] + [to_z(o) for o in range(1, others)])
        out[...] = jnp.zeros_like(out)
        back[...] = jnp.zeros_like(back)
        sv[...] = jnp.zeros_like(sv)
        for i in range(4):
            sv[i, 1:2, :] = c_sum_ref[...]
        for i in range(0, tokens, CHUNK):
            nt[:, i : i + CHUNK] = n_two_ref[i : i + CHUNK, :].T
            ct[:, i : i + CHUNK] = c_ref[i : i + CHUNK, :].T

    @pl.when(t == front - 2)
    def _():
        resid_copy().start()
        for copy in late_copies():
            copy.start()

    @pl.when(t < front)
    def _():
        run(0, 0, front)
        feed_forward()

    pl.when(t == front - 1)(turn)
    pl.when((t >= front) & (t < front + pairs))(attention)

    @pl.when(t == front + pairs)
    def _():
        add_back(0, 0, late - 1)
        send_x(8)
        add_back(1, 0, late - 2)
        finish(5)
        send_back(7)
        add_back(2, 0, late - 3)
        norm_one()
        send_back_x(6)
        send_z(8)
        small_y()
        send_back_x(7)
        small_x()
        send_back(8)
        send_back_x(8)
        small_z()
        finish(6)
        small_end()
        finish(7)
        finish(8)

        @pl.loop(0, chunks)
        def _(k):
            y_copy(k).wait_send()
            x_copy(k).wait_send()
            for o in range(1, others):
                z_copy(k, o).wait_send()
                a_copy(k, o).wait_send()
            xa_copy(k).wait_send()
            for i in range(2):
                out_copies(k, i, lambda copy: copy.wait())

        for which in range(2):
            for i in range(late):
                late_core(which, i).wait_send()
        for i, device in enumerate((to_core, to_core, to_y, to_x)):
            sv_copy(i, sv.at[0], device).wait_send()
        for o in range(1, others):
            svz_copy(o).wait_send()
        for i in range(tokens // CHUNK):
            grad_copy(i).wait()


def backward(
    n_two, c, resid, w_ffn, misc, n, x, vec, c_sum, qkv, att, lse, w_attn, qh, kn, rows, group
):
    tokens, model = n.shape
    stored = x.shape[1]
    pairs = qkv.shape[0]
    blocks = model // UNITS
    front, early, late = 4 * blocks, 2 * blocks, pairs // 2
    chunks = early + late
    others = group // 2
    half = model // 2
    lines = 16
    wide = misc.shape[3]

    def unit_block(t):
        t = jnp.minimum(t, front - 1)
        return 3 - t % 4, t // 4

    def up_at(t):
        quarter, b = unit_block(t)
        return quarter, 0, 0, b

    def down_at(t):
        quarter, b = unit_block(t)
        return quarter, model // CHUNK + b, 0, 0

    def bias_at(t):
        return unit_block(t)[0], 0, 0, 0

    def pair_at(t):
        return pairs - 1 - jnp.clip(t - front, 0, pairs - 1)

    def of(shape):
        return pl.BlockSpec((None, *shape), lambda t: (pair_at(t), 0, 0))

    def unit(h):
        return pl.BlockSpec(
            (None, None, CHUNK, model),
            lambda t: (2 * (pair_at(t) // late) + h, pair_at(t) % late, 0, 0),
        )

    anywhere = pl.BlockSpec(memory_space=pl.ANY)
    sems = pltpu.SemaphoreType.DMA
    between = max(others - 1, 1)
    many = (chunks, between)
    big = once((tokens, model))
    return pl.pallas_call(
        functools.partial(backward_kernel, rows=rows, pairs=pairs, group=group, blocks=blocks),
        grid=(front + pairs + 1,),
        in_specs=[
            big, big, anywhere, anywhere, full(vec.shape), full((1, model)),
            pl.BlockSpec((None, model // CHUNK, CHUNK, UNITS), up_at),
            pl.BlockSpec((None, None, CHUNK, model), down_at),
            pl.BlockSpec((None, 2, 8, wide), bias_at),
            of((tokens, 3 * LANES)), of((tokens, LANES)), of((2, tokens)), unit(0), unit(1),
            once((tokens, LANES)), once((tokens, LANES)), anywhere,
        ],
        out_specs=[anywhere] * 4 + [once((lines, model))],
        out_shape=[
            jax.ShapeDtypeStruct((tokens, model), BF16),
            jax.ShapeDtypeStruct((tokens, model), BF16),
            jax.ShapeDtypeStruct((2, model, blocks * UNITS), BF16),
            jax.ShapeDtypeStruct((4, late * HEAD_DIM, model), BF16),
            jax.ShapeDtypeStruct((lines, model), F32),
        ],
        scratch_shapes=[pltpu.VMEM((tokens, model), F32)] * 3
        + [pltpu.VMEM((model, tokens), BF16)] * 2
        + [
            pltpu.VMEM((tokens, model), BF16),
            pltpu.VMEM((2, CHUNK, model), BF16),
            pltpu.VMEM((8, model), F32),
            pltpu.VMEM((late, 3 * LANES, model), BF16),
            pltpu.VMEM((LANES, model), BF16),
            pltpu.VMEM((tokens, LANES), BF16),
            pltpu.VMEM((late, tokens, 3 * LANES), BF16),
            pltpu.VMEM((tokens, LANES), F32),
            pltpu.VMEM((tokens, LANES), F32),
            pltpu.VMEM((CHUNK, model), F32),
            pltpu.VMEM((2 * chunks + early, 2, half, UNITS), BF16),
            pltpu.VMEM((2, early, 2, half, UNITS), BF16),
            pltpu.VMEM((chunks, 2, half, UNITS), BF16),
            pltpu.VMEM((chunks, half, UNITS), BF16),
            pltpu.VMEM((*many, half // others, UNITS), BF16),
            pltpu.VMEM((chunks, half, UNITS), BF16),
            pltpu.VMEM((chunks, half, UNITS), BF16),
            pltpu.VMEM((4, lines, model), F32),
            pltpu.VMEM((4, lines, model), F32),
            pltpu.VMEM((others, lines, model), F32),
            sems((2, chunks)), sems((2, chunks)), sems((chunks,)), sems((chunks,)),
            sems((chunks,)), sems((chunks,)), sems(many), sems(many), sems(many), sems(many),
            sems((chunks,)), sems((chunks,)), sems((chunks, 2, half // HEAD_DIM)),
            sems((4,)), sems((4,)), sems((between,)), sems((between,)), sems, sems((tokens // CHUNK,)),
            pltpu.VMEM((tokens, model), BF16), pltpu.VMEM((tokens, stored), BF16), sems((2,)),
        ],
        compiler_params=params(63, collective_id=0, has_side_effects=True),
        name="backward",
    )(n_two, c, n, x, vec, c_sum, w_ffn, w_ffn, misc, qkv, att, lse, w_attn, w_attn, qh, kn, resid)


def last_kernel(
    output_ref, grad_ref, up_ref, down_ref, qkv_ref, out_ref, sums_ref,
    output_to, grad_to, up_to, down_to, qkv_to, out_to, bqv_to, *vectors
):
    stored = output_to.shape[1]
    output_to[...] = output_ref[:, :stored]
    grad_to[...] = grad_ref[:, :stored]

    @pl.when(pl.program_id(0) < 3)
    def _():
        up_to[...] = up_ref[...].astype(F32)
        down_to[...] = down_ref[...].T.astype(F32)[:, :stored]
        qkv_to[...] = qkv_ref[...].astype(F32)[:, :stored]

    @pl.when(pl.program_id(0) == 0)
    def _():
        out_to[...] = out_ref[...].astype(F32)[:, :stored]
        for j in range(bqv_to.shape[1] // HEAD_DIM):
            for i in range(2):
                part = sums_ref[8 + j : 9 + j, 2 * LANES * i : 2 * LANES * i + HEAD_DIM]
                bqv_to[i : i + 1, HEAD_DIM * j : HEAD_DIM * (j + 1)] = part
        for i, ref in enumerate(vectors):
            ref[...] = sums_ref[i : i + 1, : ref.shape[0]].reshape(ref.shape[0])


def results(output, grad, ffn, heads, sums, stored):
    tokens, model = output.shape
    units, rows = ffn.shape[2], heads.shape[1]
    steps = tokens // CHUNK
    most = model // CHUNK - 1
    assert steps > most

    def block(shape, at):
        return pl.BlockSpec(shape, at)

    def lesser(i):
        return jnp.minimum(i, most)

    lengths = [units, stored, stored, stored, stored]
    shape = jax.ShapeDtypeStruct
    return pl.pallas_call(
        last_kernel,
        grid=(steps,),
        in_specs=[
            block((CHUNK, model), lambda i: (i, 0)),
            block((CHUNK, model), lambda i: (i, 0)),
            block((None, CHUNK, units), lambda i: (0, lesser(i), 0)),
            block((None, model, CHUNK), lambda i: (1, 0, lesser(i))),
            block((None, rows, model), lambda i: (lesser(i), 0, 0)),
            block((None, rows, model), lambda i: (3, 0, 0)),
            full(sums.shape),
        ],
        out_specs=[
            block((CHUNK, stored), lambda i: (i, 0)),
            block((CHUNK, stored), lambda i: (i, 0)),
            block((CHUNK, units), lambda i: (lesser(i), 0)),
            block((CHUNK, stored), lambda i: (lesser(i), 0)),
            block((None, rows, stored), lambda i: (lesser(i), 0, 0)),
            full((rows, stored)),
            full((2, rows)),
        ]
        + [full((n,)) for n in lengths],
        out_shape=[
            shape((tokens, stored), BF16),
            shape((tokens, stored), BF16),
            shape((stored, units), F32),
            shape((units, stored), F32),
            shape((3, rows, stored), F32),
            shape((rows, stored), F32),
            shape((2, rows), F32),
        ]
        + [shape((n,), F32) for n in lengths],
        compiler_params=params(60),
        name="results",
    )(output, grad, ffn, ffn, heads, heads, sums)


def solution(mesh):
    n_dp, n_tensor = mesh.shape["dp"], mesh.shape["tensor"]
    assert n_tensor == 4 and n_dp % 4 == 0 and n_dp & (n_dp - 1) == 0
    bits = [1 << i for i in range(n_dp.bit_length() - 1)]
    group = min(n_dp, 8)

    def to_dp(v, bit):
        return lax.ppermute(v, "dp", [(i, i ^ bit) for i in range(n_dp)])

    def local(
        layer_input, segments, cotangent, gain_one, w_qkv, b_qv, w_out, b_out, gain_two,
        w_up, b_up, w_down, b_down,
    ):
        rows = segments.shape[0]
        tokens, stored = layer_input.shape
        model = stored + 1
        heads = w_qkv.shape[2] // HEAD_DIM
        units = w_up.shape[1]

        (
            vec, n_one, cot, grad_bdown, qkv, att, lse, resid, n_two, qh, kn, w_attn, w_ffn, misc
        ) = forward(
            layer_input, cotangent, w_qkv.transpose(0, 2, 1), w_out, w_up, w_down, gain_one, gain_two,
            b_out, b_down, b_up, b_qv, segments,
        )
        output, input_grad, *reduced, small = backward(
            n_two, cot, resid, w_ffn, misc, n_one, layer_input, vec, grad_bdown, qkv, att, lse, w_attn,
            qh, kn, rows, group,
        )
        for bit in bits:
            if bit >= group:
                small = small + to_dp(small, bit)
                reduced = [(v.astype(F32) + to_dp(v, bit).astype(F32)).astype(BF16) for v in reduced]
        (
            output, input_grad, grad_up, grad_down, grad_qkv, grad_out, grad_bqv,
            grad_bup, grad_bdown, grad_bout, grad_gain_two, grad_gain_one,
        ) = results(output, input_grad, *reduced, small, stored)
        return (
            output, input_grad, grad_gain_one, grad_qkv.transpose(0, 2, 1), grad_bqv, grad_out, grad_bout,
            grad_gain_two, grad_up, grad_bup, grad_down, grad_bdown,
        )

    return jax.shard_map(
        local,
        mesh=mesh,
        in_specs=(
            P(("dp", "tensor"), None),
            P(("dp", "tensor"), None),
            P(("dp", "tensor"), None),
            P(),
            P(None, None, "tensor"),
            P(None, "tensor"),
            P("tensor", None),
            P(),
            P(),
            P(None, "tensor"),
            P("tensor"),
            P("tensor", None),
            P(),
        ),
        out_specs=(
            P(("dp", "tensor"), None),
            P(("dp", "tensor"), None),
            P(),
            P(None, None, "tensor"),
            P(None, "tensor"),
            P("tensor", None),
            P(),
            P(),
            P(None, "tensor"),
            P("tensor"),
            P("tensor", None),
            P(),
        ),
        check_vma=False,
    )
```
